32 devices in a mesh: dp: 4 (over y, core), seq: 8 (over z, x).
Axes of the slice: x: 2, y: 2, z: 4, core: 2. Of those that a mesh axis runs over, the one named last changes fastest.
Arguments:
- tokens: bfloat16 [4, 16, 64, 192], P('dp', 'seq'), may hold values from -6 to 6
- heights: int32 [4, 4], P('dp'), may hold values from 1 to 8, 16 in all within a row
- cotangent: bfloat16 [4, 16, 64, 192], P('dp', 'seq'), may hold values from -6 to 6
- norm_gain: float32 [192], replicated, may hold values from 0.5 to 1.5
- norm_bias: float32 [192], replicated, may hold values from -1 to 1
- in_weight: bfloat16 [192, 768], replicated, may hold values from -0.4375 to 0.4375
- conv_kernel: float32 [3, 3, 384], replicated, may hold values from -3.5 to 3.5
- conv_bias: float32 [384], replicated, may hold values from -1 to 1
- select_weight: bfloat16 [384, 44], replicated, may hold values from -0.3125 to 0.3125
- step_weight: float32 [12, 384], replicated, may hold values from -1.75 to 1.75
- step_bias: float32 [384], replicated, may hold values from -6.9 to -2.3
- decay_log: float32 [384, 16], replicated, may hold values from 0 to 2.77
- skip_gain: float32 [384], replicated, may hold values from 0.5 to 1.5
- out_weight: bfloat16 [384, 192], replicated, may hold values from -0.3125 to 0.3125
Outputs:
- layer_out: bfloat16 [4, 16, 64, 192], P('dp', 'seq')
- tokens_grad: bfloat16 [4, 16, 64, 192], P('dp', 'seq')
- gain_grad: float32 [192], replicated
- shift_grad: float32 [192], replicated
- inproj_grad: float32 [192, 768], replicated
- kernel_grad: float32 [3, 3, 384], replicated
- offset_grad: float32 [384], replicated
- select_grad: float32 [384, 44], replicated
- stepproj_grad: float32 [12, 384], replicated
- stepbias_grad: float32 [384], replicated
- decay_grad: float32 [384, 16], replicated
- skip_grad: float32 [384], replicated
- outproj_grad: float32 [384, 192], replicated
The draws below stay inside these ranges and needn't reach their ends.
Inputs may be any that keep to these rules, and one draw needn't show every extreme that they name: The 4 heights of each sequence add up to 16, and one of them is exactly 8.
All inputs are finite; a program needn't handle non-finite values.
Results may differ from the reference program's by a relative error of at most 0.01.
Values sent between devices are 32-bit elements; how exact they have to be, the bound alone decides.
No kernel may reach another device: no remote copies, remote signals or barrier semaphores. Data moves between devices by JAX's collectives and lax.ppermute only.
A program may use at most 64 MiB of HBM per device.

```python
import math
import jax
import jax.numpy as jnp
import numpy as np
from jax import lax

D = 192
E = 384
STATE = 16
RANK = 12
COLS = 64
IMAGES = 4
BLOCK = 8
ROWS = 16
SEQUENCES = 4


def block_levels(own_key, dims, cuts, low, top_value):
    def one(dim, parts):
        draws = jax.random.uniform(jax.random.fold_in(jax.random.fold_in(own_key, 6), dim), (parts,), jnp.float32, low / len(cuts), top_value / len(cuts))
        return jnp.repeat(jnp.exp(draws), dims[dim] // parts).reshape((-1,) + (1,) * (len(dims) - dim - 1))

    gain = one(*cuts[0])
    for cut in cuts[1:]:
        gain = gain * one(*cut)
    return gain


def profile(amount, total, most, slope):
    loads = [(1 << 20) // math.isqrt(standing ** slope) + 1 for standing in range(2, amount + 1)]
    spare, given = total - most - (amount - 1), [1] * (amount - 1)
    while spare > 0:
        candidates = [i for i in range(amount - 1) if given[i] < most]
        whole, left = sum([loads[i] for i in candidates]), spare
        for i in candidates:
            addition = min(most - given[i], max(1, left * loads[i] // whole), spare)
            given[i] = given[i] + addition
            spare = spare - addition
    return np.array([most] + given)


def ragged(rng, amount, total, limit, slope):
    if amount == 2:
        one = jax.random.randint(rng, (), max(1, total - limit), min(limit, total - 1) + 1)
        return jnp.stack([one, total - one])
    sizes = jnp.asarray(profile(amount, total, limit, slope), jnp.int32)
    pairs = (amount - 1) // 2
    giver, taker = sizes[1:1 + 2 * pairs:2], sizes[2:2 + 2 * pairs:2]
    slack = jnp.minimum(giver - 1, limit - taker)
    passed = jax.random.randint(jax.random.fold_in(rng, 1), (pairs,), 0, 1 << 20) % (slack + 1)
    sizes = sizes.at[1:1 + 2 * pairs:2].set(giver - passed).at[2:2 + 2 * pairs:2].set(taker + passed)
    return sizes[jax.random.permutation(jax.random.fold_in(rng, 2), amount)]


def scatter_about(own_key, shape, scale, limit, shards=(), kind=jnp.bfloat16):
    values = scale * jax.random.normal(own_key, shape, jnp.float32)
    if shards:
        values = values * block_levels(own_key, shape, shards, -0.22, 0.18)
    return jnp.clip(values, -limit, limit).astype(kind)


def setup_inputs(seed: int = 0) -> dict:
    key_of = jax.random.split(jax.random.key(seed), 15)
    return {
        "tokens": scatter_about(key_of[0], (SEQUENCES, ROWS, COLS, D), 1.0, 6.0, ((0, 4), (1, 8))),
        "heights": jax.vmap(lambda own: ragged(own, IMAGES, ROWS, ROWS // 2, 2))(jax.random.split(key_of[1], SEQUENCES)).reshape((SEQUENCES, IMAGES)).astype(jnp.int32),
        "cotangent": scatter_about(key_of[2], (SEQUENCES, ROWS, COLS, D), 1.0, 6.0, ((0, 4), (1, 8))),
        "norm_gain": jnp.clip(1.0 + 0.1 * jax.random.normal(key_of[3], (D,), jnp.float32), 0.5, 1.5),
        "norm_bias": scatter_about(key_of[4], (D,), 0.2, 1.0, (), jnp.float32),
        "in_weight": scatter_about(key_of[5], (D, 2 * E), D ** -0.5, 0.4375),
        "conv_kernel": scatter_about(key_of[6], (3, 3, E), 3 ** -0.5, 3.5, (), jnp.float32),
        "conv_bias": scatter_about(key_of[7], (E,), 0.2, 1.0, (), jnp.float32),
        "select_weight": scatter_about(key_of[8], (E, RANK + 2 * STATE), E ** -0.5, 0.3125),
        "step_weight": scatter_about(key_of[9], (RANK, E), RANK ** -0.5, 1.75, (), jnp.float32),
        "step_bias": jnp.clip(jax.random.uniform(key_of[10], (E,), jnp.float32, -6.9, -2.3), -6.9, -2.3),
        "decay_log": jnp.clip(jax.random.uniform(key_of[11], (E, STATE), jnp.float32, 0.0, 2.77), 0.0, 2.77),
        "skip_gain": jnp.clip(jax.random.uniform(key_of[12], (E,), jnp.float32, 0.5, 1.5), 0.5, 1.5),
        "out_weight": scatter_about(key_of[13], (E, D), E ** -0.5, 0.3125),
    }


epsilon = 1e-05

@jax.custom_vjp
def low(v):
    return lax.optimization_barrier(v.astype(jnp.bfloat16)).astype(jnp.float32)

@jax.custom_vjp
def low_back(v):
    return v

def low_keep(v):
    return (low(v), None)

def low_pass(kept, grad):
    return (grad,)

def back_keep(v):
    return (v, None)

def back_low(kept, grad):
    return (low(grad),)
low.defvjp(low_keep, low_pass)
low_back.defvjp(back_keep, back_low)

def chain_run(initial, step_size, values, in_coef, out_coef, keep_flag, decay_log):
    decay_rate = -jnp.exp(decay_log)
    chains = step_size.shape[0]
    length = step_size.shape[1]
    blocks = length // BLOCK

    def to_blocks(array):
        shaped = array.reshape((chains, blocks, BLOCK) + array.shape[2:])
        return jnp.moveaxis(shaped, 1, 0)

    def advance(carried, block_in):
        step_d, step_v, step_b, step_c, step_k = block_in
        state = carried
        outputs = []
        for position in range(BLOCK):
            delta_now = step_d[:, position]
            factor = jnp.exp(delta_now[..., None] * decay_rate) * step_k[:, position][:, None, None]
            source = (delta_now * step_v[:, position])[..., None] * step_b[:, position][:, None, :]
            state = factor * state + source
            outputs.append(lax.optimization_barrier(jnp.sum(state * step_c[:, position][:, None, :], axis=-1)))
        return (state, jnp.stack(outputs, axis=1))
    pieces = tuple((to_blocks(array) for array in (step_size, values, in_coef, out_coef, keep_flag)))
    final_state, emitted = lax.scan(jax.checkpoint(advance), initial, pieces)
    emitted = jnp.moveaxis(emitted, 0, 1).reshape(chains, length, emitted.shape[-1])
    return (emitted, final_state)

def row_links(image_heights):
    row_ends = jnp.cumsum(image_heights)
    positions = jnp.arange(ROWS, dtype=jnp.int32)
    image_of = lax.optimization_barrier(jnp.sum((row_ends[None, :] <= positions[:, None]).astype(jnp.int32), axis=1))
    equal_up = image_of[1:] == image_of[:-1]
    prev_same = jnp.concatenate([jnp.zeros((1,), jnp.bool_), equal_up]).astype(jnp.float32)
    next_same = jnp.concatenate([equal_up, jnp.zeros((1,), jnp.bool_)]).astype(jnp.float32)
    return (prev_same, next_same)

def conv_grid(field_in, kernel, offset, prev_same, next_same):
    padded = jnp.pad(field_in, ((1, 1), (1, 1), (0, 0)))
    row_masks = (prev_same, jnp.ones_like(prev_same), next_same)
    result = offset + jnp.zeros_like(field_in)
    for tap_row in range(3):
        for tap_col in range(3):
            window = padded[tap_row:tap_row + ROWS, tap_col:tap_col + COLS]
            result = result + kernel[tap_row, tap_col] * row_masks[tap_row][:, None, None] * window
    return result

def snake_grid(array):
    odd_rows = jnp.arange(ROWS) % 2 == 1
    return jnp.where(odd_rows[:, None, None], jnp.flip(array, 1), array)

def four_scans(step_size, values, in_coef, out_coef, prev_same, next_same, decay_log):
    col_pos = jnp.arange(COLS)
    keep_snake = jnp.where(col_pos[None, :] == 0, prev_same[:, None], 1.0).reshape(1, ROWS * COLS)
    keep_back = jnp.where(col_pos[None, :] == COLS - 1, next_same[:, None], 1.0).reshape(1, ROWS * COLS)

    def lined(array):
        return snake_grid(array).reshape(1, ROWS * COLS, array.shape[-1])
    forward_in = tuple((lined(array) for array in (step_size, values, in_coef, out_coef)))
    anchor = jnp.zeros((1, E, STATE), jnp.float32)
    ahead = chain_run(anchor, *forward_in, keep_snake, decay_log)[0]
    backward_in = tuple((jnp.flip(array, 1) for array in forward_in))
    behind = jnp.flip(chain_run(anchor, *backward_in, jnp.flip(keep_back, 1), decay_log)[0], 1)
    along_rows = snake_grid((ahead + behind).reshape(ROWS, COLS, E))
    column_in = tuple((jnp.moveaxis(array, 1, 0) for array in (step_size, values, in_coef, out_coef)))
    keep_down = jnp.broadcast_to(prev_same[None, :], (COLS, ROWS))
    keep_up = jnp.broadcast_to(next_same[None, :], (COLS, ROWS))
    anchor_cols = jnp.zeros((COLS, E, STATE), jnp.float32)
    downward = chain_run(anchor_cols, *column_in, keep_down, decay_log)[0]
    flipped = tuple((jnp.flip(array, 1) for array in column_in))
    upward = jnp.flip(chain_run(anchor_cols, *flipped, jnp.flip(keep_up, 1), decay_log)[0], 1)
    return along_rows + jnp.moveaxis(downward + upward, 0, 1)

def forward(params, canvas, prev_same, next_same):
    norm_gain, norm_bias, in_weight, conv_kernel, conv_bias, select_weight, step_weight, step_bias, decay_log, skip_gain, out_weight = params
    highest = lax.Precision.HIGHEST
    centred = canvas - lax.optimization_barrier(jnp.mean(canvas, axis=-1, keepdims=True))
    variance = lax.optimization_barrier(jnp.mean(centred * centred, axis=-1, keepdims=True))
    normed = centred * lax.rsqrt(variance + epsilon) * norm_gain + norm_bias
    both_halves = low_back(jnp.einsum('rcd,de->rce', low(normed), in_weight, precision=highest))
    conv_in = both_halves[..., :E]
    gate_half = both_halves[..., E:]
    inner_act = low(jax.nn.silu(conv_grid(conv_in, conv_kernel, conv_bias, prev_same, next_same)))
    projected = low_back(jnp.einsum('rce,ek->rck', inner_act, select_weight, precision=highest))
    pre_step = jnp.einsum('rck,ke->rce', projected[..., :RANK], step_weight, precision=highest) + step_bias
    step_size = jax.nn.softplus(pre_step)
    mixed = four_scans(step_size, inner_act, projected[..., RANK:RANK + STATE], projected[..., RANK + STATE:], prev_same, next_same, decay_log)
    gated_out = (mixed + skip_gain * inner_act) * jax.nn.silu(gate_half)
    return canvas + jnp.einsum('rce,ed->rcd', low(gated_out), out_weight, precision=highest)

def reference(tokens, heights, cotangent, norm_gain, norm_bias, in_weight, conv_kernel, conv_bias, select_weight, step_weight, step_bias, decay_log, skip_gain, out_weight):
    params = tuple((array.astype(jnp.float32) for array in (norm_gain, norm_bias, in_weight, conv_kernel, conv_bias, select_weight, step_weight, step_bias, decay_log, skip_gain, out_weight)))

    def per_sequence(totals, inputs):
        canvas, image_heights, seed_grad = inputs
        prev_same, next_same = row_links(image_heights)

        def applied(weights, grid_in):
            return forward(weights, grid_in, prev_same, next_same)
        layer_seq, pull_back = jax.vjp(applied, params, canvas)
        weight_grads, canvas_grad = pull_back(seed_grad)
        totals = tuple((acc_part + new_part for acc_part, new_part in zip(totals, weight_grads)))
        return (totals, (layer_seq.astype(jnp.bfloat16), canvas_grad.astype(jnp.bfloat16)))
    zero_grads = tuple((jnp.zeros_like(array) for array in params))
    totals, stacked = lax.scan(per_sequence, zero_grads, (tokens.astype(jnp.float32), heights, cotangent.astype(jnp.float32)))
    return (stacked[0], stacked[1], totals[0], totals[1], totals[2], totals[3], totals[4], totals[5], totals[6], totals[7], totals[8], totals[9], totals[10])
```

```python
import functools

import jax
import jax.numpy as jnp
from jax import lax
from jax.experimental import pallas as pl
from jax.experimental.pallas import tpu as pltpu
from jax.sharding import PartitionSpec as P

epsilon = 1e-05
exact = lax.Precision.HIGHEST
f32, bf16 = (jnp.float32, jnp.bfloat16)
ONE, IN, OUT, PROJ = (12, 16, 32, 48)
VMEM_LIMIT = 60 * 1024 * 1024


def dot(a, b, over, precision=None):
    return lax.dot_general(
        a, b, (((over[0],), (over[1],)), ((), ())), precision=precision, preferred_element_type=f32
    )


def iota(shape, dim):
    return lax.broadcasted_iota(jnp.int32, shape, dim)


def sigmoid(v):
    return 1.0 / (1.0 + jnp.exp(-v))


def links_up(heights, row):
    end = jnp.int32(0)
    same = row > 0
    for k in range(heights.shape[1]):
        end = end + heights[0, k]
        same = same & (end != row)
    return jnp.where(same, 1.0, 0.0).astype(f32)


def swap_columns(pos):
    new, old = (iota((pos, pos), 0), iota((pos, pos), 1))
    source = (new & ~63) | ((new & 7) << 3) | ((new >> 3) & 7)
    return source == old


def rows_around(own, halo, lane):
    upper = pltpu.roll(jnp.where(lane < 64, own, halo), 64, 1)
    lower = pltpu.roll(jnp.where(lane < 64, halo, own), 64, 1)
    return (upper, lower)


def conv_taps(upper, own, lower, taps, lane):
    out = None
    for b in range(3):
        part = taps[0][b] * upper + taps[1][b] * own + taps[2][b] * lower
        if b == 0:
            part = jnp.where((lane & 63) == 0, 0.0, pltpu.roll(part, 1, 1))
        if b == 2:
            part = jnp.where((lane & 63) == 63, 0.0, pltpu.roll(part, part.shape[1] - 1, 1))
        out = part if out is None else out + part
    return out


def row_links(heights, place, lane):
    first = 2 * place
    flags = [links_up(heights, first + k) for k in range(3)]
    prev = jnp.where(lane < 64, flags[0], flags[1])
    following = jnp.where(lane < 64, flags[1], flags[2])
    return (prev, following)


def normalized(x):
    centred = x - jnp.mean(x, axis=0, keepdims=True)
    inverse = lax.rsqrt(jnp.mean(centred * centred, axis=0, keepdims=True) + epsilon)
    return (centred * inverse, inverse)


def entry_kernel(
    heights, place, tok, above, below, cot, in_t, out_w, select_t, chan, norm,
    send, conv_own, conv_halo, pre_out, gate_out, grad_out,
):
    inner_width = out_w.shape[0]
    devices = send.shape[0]
    part = inner_width // devices
    lane = iota((1, tok.shape[1]), 1)
    gain, shift = (norm[:, 0:1], norm[:, 1:2])
    halo = jnp.where(lane < 64, below[...], above[...])
    low_own = (normalized(tok[...])[0] * gain + shift).astype(bf16)
    low_halo = (normalized(halo)[0] * gain + shift).astype(bf16)
    both = dot(in_t[...], low_own, (1, 0))
    conv_in, gate = (both[:inner_width], both[inner_width:])
    around = dot(in_t[:inner_width], low_halo, (1, 0))
    gated_grad = dot(out_w[...], cot[...], (1, 1))
    prev, following = row_links(heights, place[0], lane)
    upper, lower = rows_around(conv_in, around, lane)
    taps = [[chan[:, 3 * a + b : 3 * a + b + 1] for b in range(3)] for a in range(3)]
    pre_act = chan[:, 9:10] + conv_taps(upper * prev, conv_in, lower * following, taps, lane)
    inner = (pre_act * sigmoid(pre_act)).astype(bf16)
    mix_grad = gated_grad * (gate * sigmoid(gate))
    proj = dot(select_t[...], inner, (1, 0))
    proj = jnp.where(iota(proj.shape, 0) == ONE, 1.0, proj)
    conv_own[...] = conv_in
    conv_halo[...] = around
    pre_out[...] = pre_act
    gate_out[...] = gate
    grad_out[...] = gated_grad
    inner = inner.astype(f32)
    for k in range(devices):
        send[k, :part] = inner[k * part : (k + 1) * part]
        send[k, part : 2 * part] = mix_grad[k * part : (k + 1) * part]
        send[k, 2 * part :] = proj


def spread_matrices(part, states, width):
    lane = iota((1, width), 1)
    state = jnp.floor((lane.astype(f32) + 0.5) * (1.0 / part)).astype(jnp.int32)
    channel = lane - state * part
    live = state < states
    return (channel, state, live)


def scan_kernel(
    heights, place, got, decay, step_in, send, small,
    a_ref, s_ref, g_ref, down_ref, up_ref, col_h, col_m,
    prod, end_lr, end_rl, back_lr, back_rl, in_lr, in_rl, tail_lr, tail_rl,
    lhs_d, lhs_u, lhs_m, lhs_p, step_keep, decay_acc, stp_acc, *, part, states, span,
):
    devices, _, pos = got.shape
    rows = 2 * devices
    width = a_ref.shape[1]
    tiles = width // span
    swap = swap_columns(pos)
    swap_low, swap_f = (swap.astype(bf16), swap.astype(f32))
    channel, state, live = spread_matrices(part, states, width)
    twice = iota((2 * part, 1), 0)
    twice = jnp.where(twice >= part, twice - part, twice)
    spread_e = ((twice == channel) & live).astype(bf16)
    coef = iota((2 * PROJ, 1), 0)
    coef = jnp.where(coef >= PROJ, coef - PROJ, coef)
    spread_b = ((coef - IN == state) & live).astype(bf16)
    spread_c = ((coef - OUT == state) & live).astype(bf16)
    first = pl.multiple_of(place[0] * part, 4)
    rate = -jnp.exp(decay[pl.ds(first, part), :])
    step_rows = step_in[pl.ds(first, part), :]
    by_state = dot(rate, ((iota((states, 1), 0) == state) & live).astype(f32), (1, 0), exact)
    rate_row = jnp.sum(
        jnp.where((iota((part, 1), 0) == channel) & live, by_state, 0.0), axis=0, keepdims=True
    )
    step_twice = jnp.concatenate([step_rows, step_rows], axis=0)
    high_lane = iota((1, 2 * part), 1) < part
    high_proj = iota((1, 2 * PROJ), 1) < PROJ

    def halves(value, high):
        whole = value.astype(bf16).astype(f32)
        return jnp.where(high, whole, value - whole).astype(bf16)

    def prepare(tile, carry):
        lines = pl.ds(pl.multiple_of(tile * pos, pos), pos)
        block = got[tile]
        inner = block[:part].astype(bf16)
        mix = block[part : 2 * part]
        proj = block[2 * part :]
        inner = dot(swap_low, jnp.concatenate([inner, inner], axis=0), (1, 1))
        mix = dot(swap_f, jnp.concatenate([mix, mix], axis=0), (1, 1), exact)
        proj = dot(swap_f, jnp.concatenate([proj, proj], axis=0), (1, 1), exact)
        pre_step = dot(proj[:, :PROJ], step_twice, (1, 1), exact)
        tail = jnp.exp(-jnp.abs(pre_step))
        tail = jnp.where(tail < 1e-3, tail * (1.0 - 0.5 * tail), jnp.log(1.0 + tail))
        delta = jnp.maximum(pre_step, 0.0) + tail
        of_delta = halves(delta, high_lane)
        of_source = halves(delta * inner, high_lane)
        of_mix = halves(mix, high_lane)
        of_proj = halves(proj, high_proj)
        lhs_d[lines, :] = of_delta
        lhs_u[lines, :] = of_source
        lhs_m[lines, :] = of_mix
        lhs_p[lines, :] = of_proj
        step_keep[0, lines, :] = pre_step[:, :part]
        step_keep[1, lines, :] = delta[:, :part]
        step_keep[2, lines, :] = inner[:, :part]
        for k in range(tiles):
            lanes = slice(k * span, (k + 1) * span)
            a_ref[lines, lanes] = jnp.exp(dot(of_delta, spread_e[:, lanes], (1, 0)) * rate_row[:, lanes])
            s_ref[lines, lanes] = dot(of_source, spread_e[:, lanes], (1, 0)) * dot(
                of_proj, spread_b[:, lanes], (1, 0)
            )
            g_ref[lines, lanes] = dot(of_mix, spread_e[:, lanes], (1, 0)) * dot(
                of_proj, spread_c[:, lanes], (1, 0)
            )
        return carry

    lax.fori_loop(0, devices, prepare, 0)
    col_h[...] = jnp.zeros_like(col_h)
    col_m[...] = jnp.zeros_like(col_m)

    def ascend(row, carry):
        keep = links_up(heights, row)
        for k in range(width // 128):
            lanes = slice(k * 128, (k + 1) * 128)
            whole = lr = rl = mlr = mrl = None
            for c in range(8):
                lines = pl.ds(pl.multiple_of(row * 64 + c * 8, 8), 8)
                spot = slice(c * 8, c * 8 + 8)
                a, s, g = (a_ref[lines, lanes], s_ref[lines, lanes], g_ref[lines, lanes])
                state_h = a * (col_h[spot, lanes] * keep) + s
                col_h[spot, lanes] = state_h
                down_ref[lines, lanes] = state_h
                lam = g + col_m[spot, lanes] * keep
                col_m[spot, lanes] = a * lam
                up_ref[lines, lanes] = lam
                if c == 0:
                    whole, lr, rl, mlr, mrl = (a, s, s, a * g, a * g)
                else:
                    lr = a * lr + s
                    rl = rl + whole * s
                    whole = whole * a
                    mlr = mlr + whole * g
                    mrl = a * (mrl + g)
            lines = pl.ds(pl.multiple_of(row * 8, 8), 8)
            prod[lines, lanes] = whole
            end_lr[lines, lanes] = lr
            end_rl[lines, lanes] = rl
            back_lr[lines, lanes] = mlr
            back_rl[lines, lanes] = mrl
        return carry

    lax.fori_loop(0, rows, ascend, 0)

    def chain(state_in, row, order, ends, starts):
        for c in order:
            line = pl.ds(row * 8 + c, 1)
            starts[line, :] = state_in
            state_in = prod[line, :] * state_in + ends[line, :]
        return state_in

    def carries(pair, held):
        ahead, behind, back_ahead, back_behind = held
        right, left = (range(8), range(7, -1, -1))
        low = 2 * pair
        high = rows - 2 - low
        ahead = chain(ahead * links_up(heights, low), low, right, end_lr, in_lr)
        back_behind = chain(back_behind, low, right, back_rl, tail_rl)
        back_behind = back_behind * links_up(heights, low + 1)
        ahead = chain(ahead * links_up(heights, low + 1), low + 1, left, end_rl, in_rl)
        back_behind = chain(back_behind, low + 1, left, back_lr, tail_lr)
        back_behind = back_behind * links_up(heights, low + 2)
        behind = chain(behind * links_up(heights, high + 2), high + 1, right, end_lr, in_lr)
        back_ahead = chain(back_ahead, high + 1, right, back_rl, tail_rl)
        back_ahead = back_ahead * links_up(heights, high + 1)
        behind = chain(behind * links_up(heights, high + 1), high, left, end_rl, in_rl)
        back_ahead = chain(back_ahead, high, left, back_lr, tail_lr)
        back_ahead = back_ahead * links_up(heights, high)
        return (ahead, behind, back_ahead, back_behind)

    nothing = jnp.zeros((1, width), f32)
    lax.fori_loop(0, devices, carries, (nothing,) * 4)
    col_h[...] = jnp.zeros_like(col_h)
    col_m[...] = jnp.zeros_like(col_m)

    def descend(step, carry):
        row = rows - 1 - step
        keep = links_up(heights, row + 1)
        edge = pl.ds(pl.multiple_of(row * 8, 8), 8)
        for k in range(width // 128):
            lanes = slice(k * 128, (k + 1) * 128)
            h_right, m_left = (in_lr[edge, lanes], tail_rl[edge, lanes])
            rights, lams = ([], [])
            for c in range(8):
                lines = pl.ds(pl.multiple_of(row * 64 + c * 8, 8), 8)
                a, s, g = (a_ref[lines, lanes], s_ref[lines, lanes], g_ref[lines, lanes])
                h_right = a * h_right + s
                lam = g + m_left
                m_left = a * lam
                rights.append(h_right)
                lams.append(lam)
            h_left, m_right = (in_rl[edge, lanes], tail_lr[edge, lanes])
            for c in range(7, -1, -1):
                lines = pl.ds(pl.multiple_of(row * 64 + c * 8, 8), 8)
                spot = slice(c * 8, c * 8 + 8)
                a, s, g = (a_ref[lines, lanes], s_ref[lines, lanes], g_ref[lines, lanes])
                h_left = a * h_left + s
                lam_lr = g + m_right
                m_right = a * lam_lr
                h_down, lam_up = (down_ref[lines, lanes], up_ref[lines, lanes])
                h_up = a * (col_h[spot, lanes] * keep) + s
                col_h[spot, lanes] = h_up
                lam_down = g + col_m[spot, lanes] * keep
                col_m[spot, lanes] = a * lam_down
                h_right, lam_rl = (rights[c], lams[c])
                lam_sum = (lam_lr + lam_rl) + (lam_down + lam_up)
                down_ref[lines, lanes] = (h_right + h_left) + (h_down + h_up)
                up_ref[lines, lanes] = lam_sum
                g_ref[lines, lanes] = (
                    (lam_lr * h_right + lam_rl * h_left)
                    + (lam_down * h_down + lam_up * h_up)
                    - s * lam_sum
                )
        return carry

    lax.fori_loop(0, rows, descend, 0)
    decay_acc[...] = jnp.zeros_like(decay_acc)
    stp_acc[...] = jnp.zeros_like(stp_acc)
    channel_col = iota((1, part), 1)
    proj_col = iota((1, PROJ), 1)

    def column(row_value):
        return jnp.transpose(jnp.broadcast_to(row_value, (8, width)).astype(f32))[:, 0:1]

    channel_c, state_c = (column(channel), column(jnp.where(live, state, -1)))
    gather_e = ((channel_c == channel_col.astype(f32)) & (state_c >= 0)).astype(bf16)
    gather_b = ((state_c + IN == proj_col.astype(f32)) & (state_c >= 0)).astype(bf16)
    gather_c = ((state_c + OUT == proj_col.astype(f32)) & (state_c >= 0)).astype(bf16)

    def finish(tile, carry):
        lines = pl.ds(pl.multiple_of(tile * pos, pos), pos)
        y = steps = sums = coefs = None
        of_delta, of_source, of_mix, of_proj = (
            lhs_d[lines, :], lhs_u[lines, :], lhs_m[lines, :], lhs_p[lines, :]
        )
        for k in range(tiles):
            lanes = slice(k * span, (k + 1) * span)
            h_sum, lam_sum = (down_ref[lines, lanes], up_ref[lines, lanes])
            scaled = g_ref[lines, lanes] * rate_row[:, lanes]
            of_b = dot(of_proj, spread_b[:, lanes], (1, 0))
            of_c = dot(of_proj, spread_c[:, lanes], (1, 0))
            spread_d = dot(of_delta, spread_e[:, lanes], (1, 0))
            spread_u = dot(of_source, spread_e[:, lanes], (1, 0))
            spread_m = dot(of_mix, spread_e[:, lanes], (1, 0))
            decay_acc[:, lanes] += jnp.sum((scaled * spread_d).reshape(pos // 8, 8, span), axis=0)
            parts = (
                dot((h_sum * of_c).astype(bf16), gather_e[lanes], (1, 0)),
                dot(scaled.astype(bf16), gather_e[lanes], (1, 0)),
                dot((lam_sum * of_b).astype(bf16), gather_e[lanes], (1, 0)),
                dot((lam_sum * spread_u).astype(bf16), gather_b[lanes], (1, 0))
                + dot((h_sum * spread_m).astype(bf16), gather_c[lanes], (1, 0)),
            )
            if k == 0:
                y, steps, sums, coefs = parts
            else:
                y, steps, sums, coefs = [x + z for x, z in zip((y, steps, sums, coefs), parts)]
        pre_step, delta, inner = (step_keep[0, lines, :], step_keep[1, lines, :], step_keep[2, lines, :])
        pre_grad = (steps + inner * sums) * sigmoid(pre_step)
        coefs = coefs + dot(pre_grad, step_rows, (1, 0), exact)
        proj = of_proj[:, :PROJ].astype(f32) + of_proj[:, PROJ:].astype(f32)
        stp_acc[...] += dot(proj, pre_grad, (0, 0), exact)
        send[tile, :part] = dot(y, swap_f, (0, 0), exact)
        send[tile, part : 2 * part] = dot(delta * sums, swap_f, (0, 0), exact)
        send[tile, 2 * part :] = dot(coefs, swap_f, (0, 0), exact)
        return carry

    lax.fori_loop(0, devices, finish, 0)
    total = jnp.sum(decay_acc[...], axis=0, keepdims=True)
    by_state = jnp.where((iota((states, 1), 0) == state) & live, total, 0.0)
    decay_grad = dot(by_state, gather_e.astype(f32), (1, 0), exact)
    spot = (iota((part, small.shape[1]), 1) == iota((part, small.shape[1]), 0) + place[0] * part).astype(f32)
    small[:16] = dot(stp_acc[:16], spot, (1, 0), exact)
    small[16:] = dot(decay_grad, spot, (1, 0), exact)


def lane_sums(value):
    return dot(jnp.ones((8, value.shape[1]), f32), value, (1, 1), exact)[0:1]


def put_lanes(ref, start, value):
    for k in range(value.shape[1] // 128):
        ref[start + k * value.shape[0] : start + (k + 1) * value.shape[0]] = value[:, k * 128 : (k + 1) * 128]


def mix_kernel(
    heights, place, got, small_in, tok, tok_rows, cot_t, conv_own, conv_halo, pre, gate_in, grad_in,
    chan, norm, select, out_w,
    layer_out, act_out, up, down, gate_grad_out, grads,
):
    devices, length, pos = got.shape
    inner_width = out_w.shape[0]
    part = inner_width // devices
    lane = iota((1, pos), 1)
    y = jnp.concatenate([got[k, :part] for k in range(devices)], axis=0)
    inner_grad = jnp.concatenate([got[k, part : 2 * part] for k in range(devices)], axis=0)
    proj_grad = got[0, 2 * part :]
    for k in range(1, devices):
        proj_grad = proj_grad + got[k, 2 * part :]
    proj_grad = proj_grad.astype(bf16)
    pre_act, gate, gated_grad = (pre[...], gate_in[...], grad_in[...])
    skip = chan[:, 10:11]
    sig_pre, sig_gate = (sigmoid(pre_act), sigmoid(gate))
    inner = (pre_act * sig_pre).astype(bf16)
    inner_f = inner.astype(f32)
    y_all = y + skip * inner_f
    silu_gate = gate * sig_gate
    gated = (y_all * silu_gate).astype(bf16)
    mix_grad = gated_grad * silu_gate
    layer_out[...] = (tok_rows[...].astype(f32) + dot(gated, out_w[...], (0, 0))).astype(bf16)
    gate_grad = (gated_grad * y_all * (sig_gate * (1.0 + gate * (1.0 - sig_gate)))).astype(bf16)
    gate_grad_out[...] = gate_grad
    inner_grad = inner_grad + mix_grad * skip + dot(select[...], proj_grad, (1, 0))
    act_grad = inner_grad * (sig_pre * (1.0 + pre_act * (1.0 - sig_pre)))
    act_out[...] = act_grad
    half = inner_width // 2
    top, bottom = (act_grad[:half], act_grad[half:])
    up[...] = jnp.where(lane < 64, top, pltpu.roll(bottom, 64, 1))
    down[...] = jnp.where(lane < 64, pltpu.roll(top, 64, 1), bottom)
    low = (normalized(tok[...])[0] * norm[:, 0:1] + norm[:, 1:2]).astype(bf16)
    model = low.shape[0]
    put_lanes(grads, 0, dot(low, gate_grad, (1, 1)))
    put_lanes(grads, inner_width // 128 * model, dot(cot_t[...], gated, (1, 1)))
    prev, following = row_links(heights, place[0], lane)
    upper, lower = rows_around(conv_own[...], conv_halo[...], lane)
    tap_sums = []
    for rows_in in (upper * prev, conv_own[...], lower * following):
        for b in range(3):
            shifted = rows_in
            if b == 0:
                shifted = jnp.where((lane & 63) == 0, 0.0, pltpu.roll(rows_in, 1, 1))
            if b == 2:
                shifted = jnp.where((lane & 63) == 63, 0.0, pltpu.roll(rows_in, pos - 1, 1))
            tap_sums.append(lane_sums(act_grad * shifted))
    tap_sums.append(lane_sums(act_grad))
    tap_sums.append(lane_sums(mix_grad * inner_f))
    tap_sums.append(jnp.zeros((16 - len(tap_sums), inner_width), f32))
    smalls = jnp.concatenate(
        [dot(proj_grad, inner, (1, 1)), small_in[...], jnp.concatenate(tap_sums, axis=0)], axis=0
    )
    put_lanes(grads, 2 * (inner_width // 128) * model, smalls)


def exit_kernel(
    heights, place, act, from_above, from_below, gate_grad, grads_in, tok, cot_t, chan, norm, in_w,
    tokens_grad, grads,
):
    inner_width, pos = act.shape
    model = tok.shape[0]
    half = inner_width // 2
    lane = iota((1, pos), 1)
    above, below = (from_above[...], from_below[...])
    halo_top = jnp.where(lane < 64, below, pltpu.roll(above, 64, 1))
    halo_bottom = jnp.where(lane < 64, pltpu.roll(below, 64, 1), above)
    act_grad = act[...]
    prev, following = row_links(heights, place[0], lane)
    upper, lower = rows_around(act_grad, jnp.concatenate([halo_top, halo_bottom], axis=0), lane)
    taps = [[chan[:, 8 - 3 * a - b : 9 - 3 * a - b] for b in range(3)] for a in range(3)]
    conv_grad = conv_taps(upper * prev, act_grad, lower * following, taps, lane).astype(bf16)
    halves = jnp.concatenate([conv_grad, gate_grad[...]], axis=0)
    normed_grad = dot(in_w[...], halves, (1, 0))
    xhat, inverse = normalized(tok[...])
    gain = norm[:, 0:1]
    low = (xhat * gain + norm[:, 1:2]).astype(bf16)
    scaled = normed_grad * gain
    x_grad = (
        scaled
        - jnp.mean(scaled, axis=0, keepdims=True)
        - xhat * jnp.mean(scaled * xhat, axis=0, keepdims=True)
    ) * inverse
    tokens_grad[...] = jnp.transpose(x_grad + cot_t[...].astype(f32)).astype(bf16)
    count = inner_width // 128 * model
    put_lanes(grads, 0, dot(low, conv_grad, (1, 1)))
    grads[count : count + grads_in.shape[0]] = grads_in[...]
    used = count + grads_in.shape[0]
    norm_sums = jnp.concatenate([lane_sums(normed_grad * xhat), lane_sums(normed_grad)], axis=1)
    small_rows = (grads_in.shape[0] - 2 * count) // (inner_width // 128)
    for k in range(inner_width // 128):
        line = 3 * count + k * small_rows + small_rows - 1
        grads[line : line + 1] = norm_sums[:, k * 128 : (k + 1) * 128]
    grads[used:] = jnp.zeros((grads.shape[0] - used, 128), f32)


def deal_kernel(
    core, mine, other, gain_grad, shift_grad, inproj, kernel_grad, offset, select, stepproj, stepbias,
    decay, skip, outproj,
):
    model, inner_width = (outproj.shape[1], outproj.shape[0])
    blocks = inner_width // 128
    own = core[0] == 0
    half = mine.shape[0]

    def rows(start, count):
        pieces = []
        while count:
            side, offset_in = divmod(start, half)
            length = min(count, half - offset_in)
            a, b = (mine[offset_in : offset_in + length], other[offset_in : offset_in + length])
            pieces.append(jnp.where(own, a, b) if side == 0 else jnp.where(own, b, a))
            start, count = (start + length, count - length)
        return pieces[0] if len(pieces) == 1 else jnp.concatenate(pieces, axis=0)

    for k in range(2 * blocks):
        inproj[:, k * 128 : (k + 1) * 128] = rows(k * model, model)
    start = 2 * blocks * model
    for k in range(blocks):
        outproj[k * 128 : (k + 1) * 128, :] = jnp.transpose(rows(start + k * model, model))
    start = start + blocks * model
    count = 96
    small = jnp.concatenate([rows(start + k * count, count) for k in range(blocks)], axis=1)
    select_t = jnp.transpose(small[:PROJ])
    rank = stepproj.shape[0]
    select[:, :rank] = select_t[:, :rank]
    select[:, rank:] = select_t[:, IN:]
    stepproj[...] = small[PROJ : PROJ + rank]
    stepbias[...] = small[PROJ + ONE : PROJ + ONE + 1]
    decay[...] = jnp.transpose(small[PROJ + 16 : PROJ + 32])
    rest = small[PROJ + 32 :]
    for k in range(3):
        kernel_grad[k] = rest[3 * k : 3 * k + 3]
    offset[...] = rest[9:10]
    skip[...] = rest[10:11]
    gain_grad[...] = rest[15:16, :model]
    shift_grad[...] = rest[15:16, model:]


def vmem_call(kernel, out_shape, scalars, arrays, scratch=()):
    return pl.pallas_call(
        kernel,
        out_shape=out_shape,
        in_specs=[pl.BlockSpec(memory_space=pltpu.SMEM)] * len(scalars)
        + [pl.BlockSpec(memory_space=pltpu.VMEM)] * len(arrays),
        out_specs=[pl.BlockSpec(memory_space=pltpu.VMEM)] * len(out_shape),
        scratch_shapes=list(scratch),
        compiler_params=pltpu.CompilerParams(vmem_limit_bytes=VMEM_LIMIT),
    )(*scalars, *arrays)


def struct(*shape, dtype=f32):
    return jax.ShapeDtypeStruct(shape, dtype)


def on_device(
    tokens, heights, cotangent, norm_gain, norm_bias, in_weight, conv_kernel, conv_bias, select_weight,
    step_weight, step_bias, decay_log, skip_gain, out_weight,
):
    _, tile_rows, grid_cols, model = tokens.shape
    inner_width = out_weight.shape[0]
    states = decay_log.shape[1]
    rank = step_weight.shape[0]
    devices = lax.axis_size("seq")
    groups = lax.axis_size("dp")
    place = lax.axis_index("seq").reshape(1)
    core = (lax.axis_index("dp") % 2).reshape(1)
    pos = tile_rows * grid_cols
    part = inner_width // devices
    length = 2 * part + PROJ
    width = -(-part * states // 128) * 128
    up_pairs = [(i, i + 1) for i in range(devices - 1)]
    down_pairs = [(i + 1, i) for i in range(devices - 1)]

    tok_rows = tokens.reshape(pos, model)
    cot = cotangent.reshape(pos, model)
    tok = tok_rows.T.astype(f32)
    cot_t = cot.T
    above = lax.ppermute(tok, "seq", up_pairs)
    below = lax.ppermute(tok, "seq", down_pairs)
    in_t = in_weight.T
    gap = jnp.zeros((inner_width, IN - rank), bf16)
    select = jnp.concatenate([select_weight[:, :rank], gap, select_weight[:, rank:]], axis=1)
    chan = jnp.concatenate(
        [conv_kernel.reshape(9, inner_width), conv_bias[None], skip_gain[None], jnp.zeros((5, inner_width), f32)]
    ).T
    step_in = jnp.concatenate(
        [step_weight, step_bias[None], jnp.zeros((PROJ - rank - 1, inner_width), f32)]
    ).T
    norm = jnp.stack([norm_gain, norm_bias], axis=1)

    channels = struct(inner_width, pos)
    sent, conv_own, conv_halo, pre_act, gate, gated_grad = vmem_call(
        entry_kernel,
        [struct(devices, length, pos)] + [channels] * 5,
        [heights, place],
        [tok, above, below, cot, in_t, out_weight, select.T, chan, norm],
    )
    got = lax.all_to_all(sent, "seq", 0, 0, tiled=True)
    total = devices * pos
    big = pltpu.VMEM((total, width), f32)
    line = pltpu.VMEM((total // 8, width), f32)
    column = pltpu.VMEM((grid_cols, width), f32)
    span = 256 if width % 256 == 0 else 128
    sent, small = vmem_call(
        functools.partial(scan_kernel, part=part, states=states, span=span),
        [struct(devices, length, pos), struct(32, inner_width)],
        [heights, place],
        [got, decay_log, step_in],
        [big] * 5
        + [column] * 2
        + [pltpu.VMEM((total // 8, width), f32)] * 0
        + [pltpu.VMEM((2 * devices * 8, width), f32)] * 9
        + [pltpu.VMEM((total, 2 * part), bf16)] * 3
        + [
            pltpu.VMEM((total, 2 * PROJ), bf16),
            pltpu.VMEM((3, total, part), f32),
            pltpu.VMEM((8, width), f32),
            pltpu.VMEM((PROJ, part), f32),
        ],
    )
    got = lax.all_to_all(sent, "seq", 0, 0, tiled=True)
    blocks = inner_width // 128
    early = 2 * blocks * model + blocks * 96
    layer_out, act_grad, up, down, gate_grad, grads = vmem_call(
        mix_kernel,
        [
            struct(pos, model, dtype=bf16),
            channels,
            struct(inner_width // 2, pos),
            struct(inner_width // 2, pos),
            struct(inner_width, pos, dtype=bf16),
            struct(early, 128),
        ],
        [heights, place],
        [got, small, tok, tok_rows, cot_t, conv_own, conv_halo, pre_act, gate, gated_grad, chan, norm, select, out_weight],
    )
    from_above = lax.ppermute(down, "seq", up_pairs)
    from_below = lax.ppermute(up, "seq", down_pairs)
    whole = -(-(early + blocks * model) // 2048) * 2048
    tokens_grad, grads = vmem_call(
        exit_kernel,
        [struct(pos, model, dtype=bf16), struct(whole, 128)],
        [heights, place],
        [act_grad, from_above, from_below, gate_grad, grads, tok, cot_t, chan, norm, in_weight],
    )
    half = whole // 2
    grads = grads.reshape(2, half, 128)
    swap = [(i, i ^ 1) for i in range(groups)]
    kept = lax.dynamic_index_in_dim(grads, core[0], 0, False)
    kept = kept + lax.ppermute(lax.dynamic_index_in_dim(grads, 1 - core[0], 0, False), "dp", swap)
    peers = groups // 2 * devices
    same_core = [
        [d * devices + s for d in range(c, groups, 2) for s in range(devices)] for c in range(2)
    ]
    shares = lax.all_to_all(
        kept.reshape(peers, half // peers, 128), ("dp", "seq"), 0, 0, tiled=True, axis_index_groups=same_core
    )
    share = jnp.sum(shares, axis=0)
    mine = lax.all_to_all(
        jnp.broadcast_to(share, shares.shape), ("dp", "seq"), 0, 0, tiled=True, axis_index_groups=same_core
    ).reshape(half, 128)
    other = lax.ppermute(mine, "dp", swap)
    sums = vmem_call(
        deal_kernel,
        [
            struct(1, model), struct(1, model), struct(model, 2 * inner_width), struct(3, 3, inner_width),
            struct(1, inner_width), struct(inner_width, rank + 2 * states), struct(rank, inner_width),
            struct(1, inner_width), struct(inner_width, states), struct(1, inner_width),
            struct(inner_width, model),
        ],
        [core],
        [mine, other],
    )
    sums = [x.reshape(-1) if x.shape[0] == 1 else x for x in sums]
    shape = tokens.shape
    return (layer_out.reshape(shape), tokens_grad.reshape(shape)) + tuple(sums)


def solution(mesh):
    tile, whole = (P("dp", "seq", None, None), P())
    return jax.shard_map(
        on_device,
        mesh=mesh,
        in_specs=(tile, P("dp", None), tile) + (whole,) * 11,
        out_specs=(tile, tile) + (whole,) * 11,
        check_vma=False,
    )
```

```python
import functools

import jax
import jax.numpy as jnp
from jax import lax
from jax.experimental import pallas as pl
from jax.experimental.pallas import tpu as pltpu
from jax.sharding import PartitionSpec as P

epsilon = 1e-05
f32, bf16 = (jnp.float32, jnp.bfloat16)
ONE, IN, OUT, PROJ = (12, 16, 32, 48)
BIAS, SKIP, STEP, DECAY, TABLE = (9, 10, 16, 32, 48)
STEP_AT, DECAY_AT, TAPS_AT, OFFSET_AT, SKIP_AT, NORM_AT, SMALL = (48, 64, 80, 89, 90, 95, 96)


def dot(a, b, over):
    return lax.dot_general(a, b, (((over[0],), (over[1],)), ((), ())), preferred_element_type=f32)


def split(value):
    high = value.astype(bf16)
    return (high, (value - high.astype(f32)).astype(bf16))


def fine_dot(a, b, over):
    (a_high, a_low), (b_high, b_low) = (split(a), split(b))
    return dot(a_high, b_high, over) + (dot(a_low, b_high, over) + dot(a_high, b_low, over))


def iota(shape, dim):
    return lax.broadcasted_iota(jnp.int32, shape, dim)


def sigmoid(v):
    return 1.0 / (1.0 + jnp.exp(-v))


def links_up(heights, row):
    end = jnp.int32(0)
    same = row > 0
    for k in range(heights.shape[1]):
        end = end + heights[0, k]
        same = same & (end != row)
    return jnp.where(same, 1.0, 0.0).astype(f32)


def row_masks(heights, place):
    lane = iota((1, 128), 1)
    flags = [links_up(heights, 2 * place + k) for k in range(3)]
    return (jnp.where(lane < 64, flags[0], flags[1]), jnp.where(lane < 64, flags[1], flags[2]))


def rows_around(own, halo):
    lane = iota((1, 128), 1)
    upper = pltpu.roll(jnp.where(lane < 64, own, halo), 64, 1)
    lower = pltpu.roll(jnp.where(lane < 64, halo, own), 64, 1)
    return (upper, lower)


def from_left(tile):
    place = iota((1, 128), 1) & 63
    wrapped = jnp.where(place == 0, 0.0, pltpu.roll(tile, 73, 1))
    return jnp.where(place < 8, wrapped, pltpu.roll(tile, 8, 1))


def from_right(tile):
    place = iota((1, 128), 1) & 63
    wrapped = jnp.where(place == 63, 0.0, pltpu.roll(tile, 55, 1))
    return jnp.where(place >= 56, wrapped, pltpu.roll(tile, 120, 1))


def conv_tile(upper, own, lower, taps):
    left, middle, right = [
        taps[0][b] * upper + taps[1][b] * own + taps[2][b] * lower for b in range(3)
    ]
    return middle + (from_left(left) + from_right(right))


def normalized(x):
    centred = x - jnp.mean(x, axis=0, keepdims=True)
    inverse = lax.rsqrt(jnp.mean(centred * centred, axis=0, keepdims=True) + epsilon)
    return (centred * inverse, inverse)


def as_column(vector):
    return jnp.transpose(jnp.broadcast_to(vector.reshape(1, -1), (8, vector.shape[0])))[:, 0:1]


def patch_sums(value):
    high, low = split(value)
    ones = jnp.ones((8, value.shape[1]), bf16)
    return (dot(ones, high, (1, 1)) + dot(ones, low, (1, 1)))[0:1]


def put_blocks(ref, start, value):
    for k in range(value.shape[1] // 128):
        ref[start + k * value.shape[0] : start + (k + 1) * value.shape[0]] = value[:, k * 128 : (k + 1) * 128]


def column_order(pos):
    new, old = (iota((pos, pos), 0), iota((pos, pos), 1))
    source = (new & ~63) | ((new & 7) << 3) | ((new >> 3) & 7)
    return (source == old).astype(bf16)


def lane_maps(part, states, width):
    lane = iota((1, width), 1)
    state = jnp.floor((lane.astype(f32) + 0.5) * (1.0 / part)).astype(jnp.int32)
    channel = lane - state * part
    return (channel, state, state < states)


def entry_kernel(
    heights, place, tok, above, below, cot, in_w, out_t, select_t, conv_kernel, conv_bias, step_weight,
    step_bias, decay_t, skip_gain, norm_gain, norm_bias,
    send, conv_out, halo_out, pre_out, gate_out, grad_out, low_out, low_halo_out, cot_out, select_rows, table,
    table_t,
):
    devices = send.shape[0]
    inner_width = out_t.shape[1]
    part = inner_width // devices
    states = decay_t.shape[0]
    rank = step_weight.shape[0]
    in_rows = jnp.transpose(in_w[...].astype(f32)).astype(bf16)
    out_rows = jnp.transpose(out_t[...].astype(f32)).astype(bf16)
    chosen = iota((PROJ, select_t.shape[0]), 0)
    chosen = jnp.where(chosen < rank, chosen, jnp.where(chosen < IN, -1, chosen - IN + rank))
    chosen = (chosen == iota((PROJ, select_t.shape[0]), 1)).astype(bf16)
    select = dot(chosen, select_t[...], (1, 0))
    select_rows[...] = jnp.transpose(select).astype(bf16)
    table_t[...] = jnp.zeros_like(table_t)
    for k in range(3):
        table_t[3 * k : 3 * k + 3] = conv_kernel[k]
    table_t[BIAS : BIAS + 1] = conv_bias[...].reshape(1, inner_width)
    table_t[SKIP : SKIP + 1] = skip_gain[...].reshape(1, inner_width)
    table_t[STEP : STEP + rank] = step_weight[...]
    table_t[STEP + ONE : STEP + ONE + 1] = step_bias[...].reshape(1, inner_width)
    table_t[DECAY : DECAY + states] = decay_t[...]
    columns = jnp.transpose(table_t[...])
    table[...] = columns

    order = column_order(tok.shape[0])
    gain, shift = (as_column(norm_gain[...]), as_column(norm_bias[...]))

    def entered(rows):
        return dot(jnp.transpose(rows).astype(bf16), order, (1, 0))

    halo = jnp.concatenate([below[:64], above[64:]], axis=0)
    low = (normalized(entered(tok[...].astype(f32)))[0] * gain + shift).astype(bf16)
    low_halo = (normalized(entered(halo))[0] * gain + shift).astype(bf16)
    cot_in = entered(cot[...].astype(f32)).astype(bf16)
    low_out[...] = low
    low_halo_out[...] = low_halo
    cot_out[...] = cot_in
    both = dot(in_rows, low, (1, 0))
    conv_in, gate = (both[:inner_width], both[inner_width:])
    around = dot(in_rows[:inner_width], low_halo, (1, 0))
    gated_grad = dot(out_rows, cot_in, (1, 0))
    prev, following = row_masks(heights, place[0])
    upper, lower = rows_around(conv_in, around)
    taps = [[columns[:, 3 * a + b : 3 * a + b + 1] for b in range(3)] for a in range(3)]
    pre_act = columns[:, BIAS : BIAS + 1] + conv_tile(upper * prev, conv_in, lower * following, taps)
    inner = (pre_act * sigmoid(pre_act)).astype(bf16)
    mix_grad = gated_grad * (gate * sigmoid(gate))
    proj = dot(select.astype(bf16), inner, (1, 0))
    proj = jnp.where(iota(proj.shape, 0) == ONE, 1.0, proj)
    conv_out[...] = conv_in
    halo_out[...] = around
    pre_out[...] = pre_act
    gate_out[...] = gate
    grad_out[...] = gated_grad
    inner = inner.astype(f32)
    for k in range(devices):
        send[k, :part] = inner[k * part : (k + 1) * part]
        send[k, part : 2 * part] = mix_grad[k * part : (k + 1) * part]
        send[k, 2 * part :] = proj


def scan_kernel(
    heights, place, got, table,
    send, small,
    a_ref, s_ref, g_ref, down_ref, up_ref, col_h, col_m, row_h, row_m,
    prod, end_lr, end_rl, back_lr, back_rl, in_lr, in_rl, tail_lr, tail_rl,
    lhs_u, lhs_m, lhs_p, step_keep, delta_keep, decay_acc, step_acc, *, part, states, span, group,
):
    devices, _, pos = got.shape
    rows = 2 * devices
    width = a_ref.shape[1]
    own_rows = table[pl.ds(pl.multiple_of(place[0] * part, 4), part), :]
    channel, state, live = lane_maps(part, states, width)
    twice = iota((2 * part, 1), 0)
    twice = jnp.where(twice >= part, twice - part, twice)
    spread_e = ((twice == channel) & live).astype(bf16)
    coef = iota((2 * PROJ, 1), 0)
    coef = jnp.where(coef >= PROJ, coef - PROJ, coef)
    spread_b = ((coef - IN == state) & live).astype(bf16)
    spread_c = ((coef - OUT == state) & live).astype(bf16)
    by_state = ((iota((states, 1), 0) == state) & live).astype(bf16)
    rate = -jnp.exp(own_rows[:, DECAY : DECAY + states])
    one_channel = (iota((part, 1), 0) == channel) & live
    rate_high, rate_low = split(rate)
    rate_rest = split(rate - rate_high.astype(f32) - rate_low.astype(f32))[0]
    rate_row = sum(dot(piece, by_state, (1, 0)) for piece in (rate_high, rate_low, rate_rest))
    rate_row = jnp.sum(jnp.where(one_channel, rate_row, 0.0), axis=0, keepdims=True)
    rate_two = rate_row * 1.4426950408889634
    step_own = own_rows[:, STEP : STEP + 16]
    eye = (iota((pos, pos), 0) == iota((pos, pos), 1)).astype(bf16)

    def turned(value):
        return dot(eye, jnp.concatenate(split(value), axis=0), (1, 1)).astype(bf16)

    def prepare(tile, carry):
        lines = pl.ds(pl.multiple_of(tile * pos, pos), pos)
        inner_own = got[tile, :part]
        proj = got[tile, 2 * part :]
        pre_step = fine_dot(step_own, proj[:16], (1, 0))
        tail = jnp.exp(-jnp.abs(pre_step))
        tail = jnp.where(tail < 1e-3, tail * (1.0 - 0.5 * tail), jnp.log(1.0 + tail))
        delta = jnp.maximum(pre_step, 0.0) + tail
        step_keep[tile] = pre_step
        delta_keep[tile] = delta
        of_delta, of_source, of_mix, of_proj = [
            turned(value) for value in (delta, delta * inner_own, got[tile, part : 2 * part], proj)
        ]
        lhs_u[lines, :] = of_source
        lhs_m[lines, :] = of_mix
        lhs_p[lines, :] = of_proj
        for k in range(width // span):
            lanes = slice(k * span, (k + 1) * span)
            a_ref[lines, lanes] = jnp.exp2(dot(of_delta, spread_e[:, lanes], (1, 0)) * rate_two[:, lanes])
            s_ref[lines, lanes] = dot(of_source, spread_e[:, lanes], (1, 0)) * dot(
                of_proj, spread_b[:, lanes], (1, 0)
            )
            g_ref[lines, lanes] = dot(of_mix, spread_e[:, lanes], (1, 0)) * dot(
                of_proj, spread_c[:, lanes], (1, 0)
            )
        return carry

    lax.fori_loop(0, devices, prepare, 0)
    col_h[...] = jnp.zeros_like(col_h)
    col_m[...] = jnp.zeros_like(col_m)

    def ascend(row, carry):
        keep = links_up(heights, row)
        for k in range(width // group):
            lanes = slice(k * group, (k + 1) * group)
            whole = lr = rl = mlr = mrl = None
            for c in range(8):
                lines = pl.ds(pl.multiple_of(row * 64 + c * 8, 8), 8)
                spot = slice(c * 8, c * 8 + 8)
                a, s, g = (a_ref[lines, lanes], s_ref[lines, lanes], g_ref[lines, lanes])
                state_h = a * (col_h[spot, lanes] * keep) + s
                col_h[spot, lanes] = state_h
                down_ref[lines, lanes] = state_h
                lam = g + col_m[spot, lanes] * keep
                col_m[spot, lanes] = a * lam
                up_ref[lines, lanes] = lam
                if c == 0:
                    whole, lr, rl, mlr, mrl = (a, s, s, a * g, a * g)
                else:
                    lr = a * lr + s
                    rl = rl + whole * s
                    whole = whole * a
                    mlr = mlr + whole * g
                    mrl = a * (mrl + g)
            lines = pl.ds(pl.multiple_of(row * 8, 8), 8)
            prod[lines, lanes] = whole
            end_lr[lines, lanes] = lr
            end_rl[lines, lanes] = rl
            back_lr[lines, lanes] = mlr
            back_rl[lines, lanes] = mrl
        return carry

    lax.fori_loop(0, rows, ascend, 0)

    def chain(state_in, row, order, ends, starts):
        for c in order:
            line = pl.ds(row * 8 + c, 1)
            starts[line, :] = state_in
            state_in = prod[line, :] * state_in + ends[line, :]
        return state_in

    def carries(pair, held):
        ahead, behind, back_ahead, back_behind = held
        right, left = (range(8), range(7, -1, -1))
        low = 2 * pair
        high = rows - 2 - low
        ahead = chain(ahead * links_up(heights, low), low, right, end_lr, in_lr)
        back_behind = chain(back_behind, low, right, back_rl, tail_rl)
        back_behind = back_behind * links_up(heights, low + 1)
        ahead = chain(ahead * links_up(heights, low + 1), low + 1, left, end_rl, in_rl)
        back_behind = chain(back_behind, low + 1, left, back_lr, tail_lr)
        back_behind = back_behind * links_up(heights, low + 2)
        behind = chain(behind * links_up(heights, high + 2), high + 1, right, end_lr, in_lr)
        back_ahead = chain(back_ahead, high + 1, right, back_rl, tail_rl)
        back_ahead = back_ahead * links_up(heights, high + 1)
        behind = chain(behind * links_up(heights, high + 1), high, left, end_rl, in_rl)
        back_ahead = chain(back_ahead, high, left, back_lr, tail_lr)
        back_ahead = back_ahead * links_up(heights, high)
        return (ahead, behind, back_ahead, back_behind)

    nothing = jnp.zeros((1, width), f32)
    lax.fori_loop(0, devices, carries, (nothing,) * 4)
    col_h[...] = jnp.zeros_like(col_h)
    col_m[...] = jnp.zeros_like(col_m)

    def descend(step, carry):
        row = rows - 1 - step
        keep = links_up(heights, row + 1)
        edge = pl.ds(pl.multiple_of(row * 8, 8), 8)
        for k in range(width // group):
            lanes = slice(k * group, (k + 1) * group)
            h_right, m_left = (in_lr[edge, lanes], tail_rl[edge, lanes])
            for c in range(8):
                lines = pl.ds(pl.multiple_of(row * 64 + c * 8, 8), 8)
                spot = slice(c * 8, c * 8 + 8)
                a, s, g = (a_ref[lines, lanes], s_ref[lines, lanes], g_ref[lines, lanes])
                h_right = a * h_right + s
                lam = g + m_left
                m_left = a * lam
                row_h[spot, lanes] = h_right
                row_m[spot, lanes] = lam
            h_left, m_right = (in_rl[edge, lanes], tail_lr[edge, lanes])
            for c in range(7, -1, -1):
                lines = pl.ds(pl.multiple_of(row * 64 + c * 8, 8), 8)
                spot = slice(c * 8, c * 8 + 8)
                a, s, g = (a_ref[lines, lanes], s_ref[lines, lanes], g_ref[lines, lanes])
                h_left = a * h_left + s
                lam_lr = g + m_right
                m_right = a * lam_lr
                h_down, lam_up = (down_ref[lines, lanes], up_ref[lines, lanes])
                h_up = a * (col_h[spot, lanes] * keep) + s
                col_h[spot, lanes] = h_up
                lam_down = g + col_m[spot, lanes] * keep
                col_m[spot, lanes] = a * lam_down
                h_right, lam_rl = (row_h[spot, lanes], row_m[spot, lanes])
                lam_sum = (lam_lr + lam_rl) + (lam_down + lam_up)
                down_ref[lines, lanes] = (h_right + h_left) + (h_down + h_up)
                up_ref[lines, lanes] = lam_sum
                g_ref[lines, lanes] = (
                    (lam_lr * h_right + lam_rl * h_left)
                    + (lam_down * h_down + lam_up * h_up)
                    - s * lam_sum
                )
        return carry

    lax.fori_loop(0, rows, descend, 0)
    decay_acc[...] = jnp.zeros_like(decay_acc)
    step_acc[...] = jnp.zeros_like(step_acc)
    gather_e, gather_b, gather_c = (spread_e[:part], spread_b[:PROJ], spread_c[:PROJ])

    def finish(tile, carry):
        lines = pl.ds(pl.multiple_of(tile * pos, pos), pos)
        delta, inner = (delta_keep[tile], got[tile, :part])
        of_source, of_mix, of_proj = (lhs_u[lines, :], lhs_m[lines, :], lhs_p[lines, :])
        delta_low = delta.astype(bf16)
        totals = None
        for k in range(width // span):
            lanes = slice(k * span, (k + 1) * span)
            h_sum, lam_sum = (down_ref[lines, lanes], up_ref[lines, lanes])
            scaled = (g_ref[lines, lanes] * rate_row[:, lanes]).astype(bf16)
            of_b = dot(of_proj, spread_b[:, lanes], (1, 0))
            of_c = dot(of_proj, spread_c[:, lanes], (1, 0))
            spread_u = dot(of_source, spread_e[:, lanes], (1, 0))
            spread_m = dot(of_mix, spread_e[:, lanes], (1, 0))
            decay_acc[:, lanes] += dot(delta_low, scaled, (1, 0))
            parts = (
                dot(gather_e[:, lanes], (h_sum * of_c).astype(bf16), (1, 1)),
                dot(gather_e[:, lanes], scaled, (1, 1)),
                dot(gather_e[:, lanes], (lam_sum * of_b).astype(bf16), (1, 1)),
                dot(gather_b[:, lanes], (lam_sum * spread_u).astype(bf16), (1, 1))
                + dot(gather_c[:, lanes], (h_sum * spread_m).astype(bf16), (1, 1)),
            )
            totals = parts if totals is None else [x + z for x, z in zip(totals, parts)]
        y, steps, sums, coefs = totals
        pre_grad = (steps + inner * sums) * sigmoid(step_keep[tile])
        send[tile, :part] = y
        send[tile, part : 2 * part] = delta * sums
        send[tile, 2 * part : 2 * part + 16] = coefs[:16] + fine_dot(step_own, pre_grad, (0, 0))
        send[tile, 2 * part + 16 :] = coefs[16:]
        step_acc[...] += fine_dot(pre_grad, got[tile, 2 * part : 2 * part + 16], (1, 1))
        return carry

    lax.fori_loop(0, devices, finish, 0)
    decay_grad = jnp.where(one_channel, decay_acc[...], 0.0)
    decay_high, decay_low = split(decay_grad)
    decay_grad = dot(decay_high, by_state, (1, 1)) + dot(decay_low, by_state, (1, 1))
    spot = (iota((part, small.shape[1]), 1) == iota((part, small.shape[1]), 0) + place[0] * part).astype(bf16)
    for at, value in ((0, step_acc[...]), (16, decay_grad)):
        high, low = split(value)
        small[at : at + 16] = dot(high, spot, (0, 0)) + dot(low, spot, (0, 0))


def mix_kernel(
    heights, place, core, got, small_in, tok, low, low_halo, cot, conv_own, conv_halo, pre, gate_in, grad_in,
    select_rows, table, in_w, out_t, conv_kernel, norm_gain, norm_bias,
    layer_out, act_out, up, down, gate_grad_out, keep, give,
    grads,
):
    devices, length, pos = got.shape
    model, inner_width = out_t.shape
    part = inner_width // devices
    lane = iota((1, pos), 1)
    y = jnp.concatenate([got[k, :part] for k in range(devices)], axis=0)
    inner_grad = jnp.concatenate([got[k, part : 2 * part] for k in range(devices)], axis=0)
    proj_grad = got[0, 2 * part :]
    for k in range(1, devices):
        proj_grad = proj_grad + got[k, 2 * part :]
    proj_grad = proj_grad.astype(bf16)
    pre_act, gate, gated_grad = (pre[...], gate_in[...], grad_in[...])
    skip = table[:, SKIP : SKIP + 1]
    sig_pre, sig_gate = (sigmoid(pre_act), sigmoid(gate))
    inner = (pre_act * sig_pre).astype(bf16)
    inner_f = inner.astype(f32)
    silu_gate = gate * sig_gate
    mix_grad = gated_grad * silu_gate
    inner_grad = inner_grad + mix_grad * skip + dot(select_rows[...], proj_grad, (1, 0))
    act_grad = inner_grad * (sig_pre * (1.0 + pre_act * (1.0 - sig_pre)))
    act_out[...] = act_grad
    half = inner_width // 2
    top, bottom = (act_grad[:half], act_grad[half:])
    up[...] = jnp.where(lane < 64, top, pltpu.roll(bottom, 64, 1))
    down[...] = jnp.where(lane < 64, pltpu.roll(top, 64, 1), bottom)

    y_all = y + skip * inner_f
    gated = (y_all * silu_gate).astype(bf16)
    gate_grad = (gated_grad * y_all * (sig_gate * (1.0 + gate * (1.0 - sig_gate)))).astype(bf16)
    gate_grad_out[...] = gate_grad
    natural = dot(gated, column_order(pos), (1, 0)).astype(bf16)
    layer = jnp.transpose(dot(out_t[...], natural, (1, 0)))
    layer_out[...] = (tok[...].astype(f32) + layer).astype(bf16)

    prev, following = row_masks(heights, place[0])
    low_in = low[...]
    upper, lower = rows_around(low_in.astype(f32), low_halo[...].astype(f32))
    which = iota((16, 1), 0)
    masks = jnp.where(which == 0, prev, jnp.where(which == 1, 1.0, following))
    left_hand = jnp.concatenate(
        [(upper * prev).astype(bf16), low_in, (lower * following).astype(bf16), masks.astype(bf16)], axis=0
    )
    field = conv_own[...]
    edge_upper, edge_lower = rows_around(field, conv_halo[...])
    fields = (edge_upper * prev, field, edge_lower * following)
    in_conv = conv_total = None
    tap_sums = [None] * 9
    for b, moved in enumerate((from_right(act_grad), act_grad, from_left(act_grad))):
        part_b = dot(left_hand, moved.astype(bf16), (1, 1))
        for a in range(3):
            tap = conv_kernel[a, b : b + 1, :]
            term = tap * part_b[a * model : (a + 1) * model]
            total = tap * part_b[3 * model + a : 3 * model + a + 1]
            in_conv = term if in_conv is None else in_conv + term
            conv_total = total if conv_total is None else conv_total + total
            tap_sums[3 * a + b] = patch_sums(moved * fields[a])
    in_gate = dot(low_in, gate_grad, (1, 1))
    put_blocks(grads, 0, in_conv)
    blocks = inner_width // 128
    put_blocks(grads, blocks * model, in_gate)
    put_blocks(grads, 2 * blocks * model, dot(cot[...], gated, (1, 1)))
    sums = jnp.broadcast_to(jnp.concatenate([conv_total, patch_sums(gate_grad.astype(f32))], axis=1), (8, 2 * inner_width))
    sums_high, sums_low = split(sums)
    shift_row = (dot(sums_high, in_w[...], (1, 1)) + dot(sums_low, in_w[...], (1, 1)))[0:1]
    weights = in_w[...].astype(f32)
    gain_row = patch_sums(weights[:, :inner_width] * in_conv + weights[:, inner_width:] * in_gate)
    gain_row = (gain_row - norm_bias[...].reshape(1, model) * shift_row) / norm_gain[...].reshape(1, model)
    smalls = jnp.concatenate(
        [dot(proj_grad, inner, (1, 1)), small_in[...]]
        + tap_sums
        + [patch_sums(act_grad), patch_sums(mix_grad * inner_f), jnp.zeros((4, inner_width), f32)]
        + [jnp.concatenate([gain_row, shift_row], axis=1)],
        axis=0,
    )
    start = 3 * blocks * model
    put_blocks(grads, start, smalls)
    start = start + blocks * SMALL
    grads[start:] = jnp.zeros((grads.shape[0] - start, 128), f32)
    first = core[0] == 0
    count = keep.shape[0]
    keep[...] = jnp.where(first, grads[:count], grads[count:])
    give[...] = jnp.where(first, grads[count:], grads[:count])


def exit_kernel(
    heights, place, act, from_above, from_below, gate_grad, tok, cot, in_w, conv_kernel, norm_gain,
    tokens_grad,
):
    inner_width, pos = act.shape
    model = in_w.shape[0]
    lane = iota((1, pos), 1)
    above, below = (from_above[...], from_below[...])
    halo_top = jnp.where(lane < 64, below, pltpu.roll(above, 64, 1))
    halo_bottom = jnp.where(lane < 64, pltpu.roll(below, 64, 1), above)
    act_grad = act[...]
    prev, following = row_masks(heights, place[0])
    upper, lower = rows_around(act_grad, jnp.concatenate([halo_top, halo_bottom], axis=0))
    taps = [[as_column(conv_kernel[2 - a, 2 - b, :]) for b in range(3)] for a in range(3)]
    conv_grad = conv_tile(upper * prev, act_grad, lower * following, taps).astype(bf16)
    halves = jnp.concatenate([conv_grad, gate_grad[...]], axis=0)
    halves = dot(halves, column_order(pos), (1, 0)).astype(bf16)
    normed_grad = dot(in_w[...], halves, (1, 0))
    xhat, inverse = normalized(jnp.transpose(tok[...].astype(f32)))
    scaled = normed_grad * as_column(norm_gain[...])
    x_grad = (
        scaled
        - jnp.mean(scaled, axis=0, keepdims=True)
        - xhat * jnp.mean(scaled * xhat, axis=0, keepdims=True)
    ) * inverse
    tokens_grad[...] = (jnp.transpose(x_grad) + cot[...].astype(f32)).astype(bf16)


def deal_kernel(
    core, mine, other, gain_grad, shift_grad, inproj, kernel_grad, offset, select, stepproj, stepbias,
    decay, skip, outproj,
):
    model, inner_width = outproj.shape
    blocks = inner_width // 128
    rank = stepproj.shape[0]
    states = decay.shape[0]
    own = core[0] == 0
    half = mine.shape[0]

    def rows(start, count):
        pieces = []
        while count:
            side, at = divmod(start, half)
            length = min(count, half - at)
            a, b = (mine[at : at + length], other[at : at + length])
            pieces.append(jnp.where(own, a, b) if side == 0 else jnp.where(own, b, a))
            start, count = (start + length, count - length)
        return pieces[0] if len(pieces) == 1 else jnp.concatenate(pieces, axis=0)

    for k in range(2 * blocks):
        inproj[:, k * 128 : (k + 1) * 128] = rows(k * model, model)
    start = 2 * blocks * model
    for k in range(blocks):
        outproj[:, k * 128 : (k + 1) * 128] = rows(start + k * model, model)
    start = start + blocks * model
    small = jnp.concatenate([rows(start + k * SMALL, SMALL) for k in range(blocks)], axis=1)
    select[:rank] = small[:rank]
    select[rank:] = small[IN:PROJ]
    stepproj[...] = small[STEP_AT : STEP_AT + rank]
    stepbias[...] = small[STEP_AT + ONE : STEP_AT + ONE + 1].reshape(stepbias.shape)
    decay[...] = small[DECAY_AT : DECAY_AT + states]
    for k in range(3):
        kernel_grad[k] = small[TAPS_AT + 3 * k : TAPS_AT + 3 * k + 3]
    offset[...] = small[OFFSET_AT : OFFSET_AT + 1].reshape(offset.shape)
    skip[...] = small[SKIP_AT : SKIP_AT + 1].reshape(skip.shape)
    norms = small[NORM_AT : NORM_AT + 1]
    gain_grad[...] = norms[:, :model].reshape(gain_grad.shape)
    shift_grad[...] = norms[:, model:].reshape(shift_grad.shape)


def vmem_call(kernel, out_shape, scalars, arrays, scratch=(), limit=60):
    return pl.pallas_call(
        kernel,
        out_shape=out_shape,
        in_specs=[pl.BlockSpec(memory_space=pltpu.SMEM)] * len(scalars)
        + [pl.BlockSpec(memory_space=pltpu.VMEM)] * len(arrays),
        out_specs=[pl.BlockSpec(memory_space=pltpu.VMEM)] * len(out_shape),
        scratch_shapes=list(scratch),
        compiler_params=pltpu.CompilerParams(vmem_limit_bytes=limit * 1024 * 1024),
    )(*scalars, *arrays)


def struct(*shape, dtype=f32):
    return jax.ShapeDtypeStruct(shape, dtype)


def scan_call(heights, place, got, table, states):
    devices, length, pos = got.shape
    inner_width = table.shape[0]
    part = inner_width // devices
    width = -(-part * states // 128) * 128
    total = devices * pos
    span = 256 if width % 256 == 0 else 128
    group = 384 if width % 384 == 0 else span
    big = pltpu.VMEM((total, width), f32)
    line = pltpu.VMEM((2 * devices * 8, width), f32)
    column = pltpu.VMEM((pos // 2, width), f32)
    own = pltpu.VMEM((devices, part, pos), f32)
    return vmem_call(
        functools.partial(scan_kernel, part=part, states=states, span=span, group=group),
        [struct(devices, length, pos), struct(32, inner_width)],
        [heights, place],
        [got, table],
        [big] * 5
        + [column] * 4
        + [line] * 9
        + [pltpu.VMEM((total, 2 * part), bf16)] * 2
        + [pltpu.VMEM((total, 2 * PROJ), bf16)]
        + [own] * 2
        + [pltpu.VMEM((part, width), f32), pltpu.VMEM((part, 16), f32)],
    )


def on_device(
    tokens, heights, cotangent, norm_gain, norm_bias, in_weight, conv_kernel, conv_bias, select_weight,
    step_weight, step_bias, decay_log, skip_gain, out_weight,
):
    _, tile_rows, grid_cols, model = tokens.shape
    inner_width = out_weight.shape[0]
    states = decay_log.shape[1]
    rank = step_weight.shape[0]
    devices = lax.axis_size("seq")
    groups = lax.axis_size("dp")
    place = lax.axis_index("seq").reshape(1)
    core = (lax.axis_index("dp") % 2).reshape(1)
    pos = tile_rows * grid_cols
    part = inner_width // devices
    length = 2 * part + PROJ
    up_pairs = [(i, i + 1) for i in range(devices - 1)]
    down_pairs = [(i + 1, i) for i in range(devices - 1)]

    tok, cot = (tokens.reshape(pos, model), cotangent.reshape(pos, model))
    wide = tok.astype(f32)
    above = lax.ppermute(wide, "seq", up_pairs)
    below = lax.ppermute(wide, "seq", down_pairs)
    out_t = out_weight.T
    channels = struct(inner_width, pos)
    narrow = struct(model, pos, dtype=bf16)
    sent, conv_own, conv_halo, pre_act, gate, gated_grad, low, low_halo, cot_in, select_rows, table = vmem_call(
        entry_kernel,
        [struct(devices, length, pos)]
        + [channels] * 5
        + [narrow] * 3
        + [struct(inner_width, PROJ, dtype=bf16), struct(inner_width, TABLE)],
        [heights, place],
        [
            tok, above, below, cot, in_weight, out_t, select_weight.T, conv_kernel, conv_bias, step_weight,
            step_bias, decay_log.T, skip_gain, norm_gain, norm_bias,
        ],
        [pltpu.VMEM((TABLE, inner_width), f32)],
    )
    got = lax.all_to_all(sent, "seq", 0, 0, tiled=True)
    sent, small = scan_call(heights, place, got, table, states)
    got = lax.all_to_all(sent, "seq", 0, 0, tiled=True)
    blocks = inner_width // 128
    whole = -(-blocks * (3 * model + SMALL) // 2048) * 2048
    half = whole // 2
    layer_out, act_grad, up, down, gate_grad, keep, give = vmem_call(
        mix_kernel,
        [struct(pos, model, dtype=bf16), channels]
        + [struct(inner_width // 2, pos)] * 2
        + [struct(inner_width, pos, dtype=bf16)]
        + [struct(half, 128)] * 2,
        [heights, place, core],
        [
            got, small, tok, low, low_halo, cot_in, conv_own, conv_halo, pre_act, gate, gated_grad, select_rows,
            table, in_weight, out_t, conv_kernel, norm_gain, norm_bias,
        ],
        [pltpu.VMEM((whole, 128), f32)],
    )
    from_above = lax.ppermute(down, "seq", up_pairs)
    from_below = lax.ppermute(up, "seq", down_pairs)
    swap = [(i, i ^ 1) for i in range(groups)]
    kept = keep + lax.ppermute(give, "dp", swap)
    kept, from_above, from_below = lax.optimization_barrier((kept, from_above, from_below))
    shares = lax.all_to_all(kept.reshape(devices, half // devices, 128), "seq", 0, 0, tiled=True)
    share = jnp.sum(shares, axis=0)
    total = share
    for k in range(2, groups, 2):
        total = total + lax.ppermute(share, "dp", [(i, (i + k) % groups) for i in range(groups)])
    (tokens_grad,) = vmem_call(
        exit_kernel,
        [struct(pos, model, dtype=bf16)],
        [heights, place],
        [act_grad, from_above, from_below, gate_grad, tok, cot, in_weight, conv_kernel, norm_gain],
    )
    total, tokens_grad = lax.optimization_barrier((total, tokens_grad))
    mine = lax.all_to_all(jnp.broadcast_to(total, shares.shape), "seq", 0, 0, tiled=True).reshape(half, 128)
    other = lax.ppermute(mine, "dp", swap)
    gain, shift, inproj, kernel, offset, select, stepproj, stepbias, decay, skip, outproj = vmem_call(
        deal_kernel,
        [
            struct(model), struct(model), struct(model, 2 * inner_width), struct(3, 3, inner_width),
            struct(inner_width), struct(rank + 2 * states, inner_width), struct(rank, inner_width),
            struct(inner_width), struct(states, inner_width), struct(inner_width), struct(model, inner_width),
        ],
        [core],
        [mine, other],
    )
    shape = tokens.shape
    return (
        layer_out.reshape(shape), tokens_grad.reshape(shape), gain, shift, inproj, kernel, offset, select.T,
        stepproj, stepbias, decay.T, skip, outproj.T,
    )


def solution(mesh):
    tile, whole = (P("dp", "seq", None, None), P())
    return jax.shard_map(
        on_device,
        mesh=mesh,
        in_specs=(tile, P("dp", None), tile) + (whole,) * 11,
        out_specs=(tile, tile) + (whole,) * 11,
        check_vma=False,
    )
```

```python
import functools

import jax
import jax.numpy as jnp
from jax import lax
from jax.experimental import pallas as pl
from jax.experimental.pallas import tpu as pltpu
from jax.sharding import PartitionSpec as P

epsilon = 1e-05
f32, bf16 = (jnp.float32, jnp.bfloat16)
ONE, IN, OUT, PROJ = (12, 16, 32, 48)
BIAS, SKIP, GAIN, SHIFT, STEP, DECAY, TABLE = (9, 10, 11, 12, 16, 32, 48)
STEP_AT, DECAY_AT, TAPS_AT, OFFSET_AT, SKIP_AT, NORM_AT, SMALL = (48, 64, 80, 89, 90, 95, 96)


def dot(a, b, over):
    return lax.dot_general(a, b, (((over[0],), (over[1],)), ((), ())), preferred_element_type=f32)


def split(value):
    high = value.astype(bf16)
    return (high, (value - high.astype(f32)).astype(bf16))


def fine_dot(a, b, over):
    (a_high, a_low), (b_high, b_low) = (split(a), split(b))
    return dot(a_high, b_high, over) + (dot(a_low, b_high, over) + dot(a_high, b_low, over))


def iota(shape, dim):
    return lax.broadcasted_iota(jnp.int32, shape, dim)


def sigmoid(v):
    return 1.0 / (1.0 + jnp.exp(-v))


def links_up(heights, row):
    end = jnp.int32(0)
    same = row > 0
    for k in range(heights.shape[1]):
        end = end + heights[0, k]
        same = same & (end != row)
    return jnp.where(same, 1.0, 0.0).astype(f32)


def row_masks(heights, place):
    lane = iota((1, 128), 1)
    flags = [links_up(heights, 2 * place + k) for k in range(3)]
    return (jnp.where(lane < 64, flags[0], flags[1]), jnp.where(lane < 64, flags[1], flags[2]))


def rows_around(own, halo):
    lane = iota((1, 128), 1)
    upper = pltpu.roll(jnp.where(lane < 64, own, halo), 64, 1)
    lower = pltpu.roll(jnp.where(lane < 64, halo, own), 64, 1)
    return (upper, lower)


def from_left(tile):
    place = iota((1, 128), 1) & 63
    wrapped = jnp.where(place == 0, 0.0, pltpu.roll(tile, 73, 1))
    return jnp.where(place < 8, wrapped, pltpu.roll(tile, 8, 1))


def from_right(tile):
    place = iota((1, 128), 1) & 63
    wrapped = jnp.where(place == 63, 0.0, pltpu.roll(tile, 55, 1))
    return jnp.where(place >= 56, wrapped, pltpu.roll(tile, 120, 1))


def conv_tile(upper, own, lower, taps):
    left, middle, right = [
        taps[0][b] * upper + taps[1][b] * own + taps[2][b] * lower for b in range(3)
    ]
    return middle + (from_left(left) + from_right(right))


def normalized(x):
    centred = x - jnp.mean(x, axis=0, keepdims=True)
    inverse = lax.rsqrt(jnp.mean(centred * centred, axis=0, keepdims=True) + epsilon)
    return (centred * inverse, inverse)


def eye(size):
    return (iota((size, size), 0) == iota((size, size), 1)).astype(bf16)


def flipped(value):
    pieces = [value[:, k : k + 128] for k in range(0, value.shape[1], 128)]
    return jnp.concatenate([dot(eye(piece.shape[1]), piece, (1, 1)) for piece in pieces], axis=0)


def flipped_fine(value):
    high, low = split(value)
    rest = (value - high.astype(f32) - low.astype(f32)).astype(bf16)
    return flipped(high) + (flipped(low) + flipped(rest))


def patch_sums(value):
    high, low = split(value)
    ones = jnp.ones((8, value.shape[1]), bf16)
    return (dot(ones, high, (1, 1)) + dot(ones, low, (1, 1)))[0:1]


def put_blocks(ref, start, value):
    for k in range(value.shape[1] // 128):
        ref[start + k * value.shape[0] : start + (k + 1) * value.shape[0]] = value[:, k * 128 : (k + 1) * 128]


def column_order(pos):
    new, old = (iota((pos, pos), 0), iota((pos, pos), 1))
    source = (new & ~63) | ((new & 7) << 3) | ((new >> 3) & 7)
    return (source == old).astype(bf16)


def lane_maps(part, states, width):
    lane = iota((1, width), 1)
    channel = jnp.floor((lane.astype(f32) + 0.5) * (1.0 / states)).astype(jnp.int32)
    return (channel, lane - channel * states, channel < part)


def entered(rows):
    return dot(flipped(rows).astype(bf16), column_order(rows.shape[0]), (1, 0))


def own_kernel(
    tok, cot, in_w, out_t, select_t, conv_kernel, conv_bias, step_weight, step_bias, decay_t, skip_gain,
    norm_gain, norm_bias,
    conv_out, gate_out, grad_out, mix_out, low_out, cot_out, conv_rows, select_rows, table,
    table_t,
):
    model, inner_width = out_t.shape
    states = decay_t.shape[0]
    rank = step_weight.shape[0]
    in_rows = flipped(in_w[...]).astype(bf16)
    conv_rows[...] = in_rows[:inner_width]
    out_rows = flipped(out_t[...]).astype(bf16)
    chosen = iota((PROJ, select_t.shape[0]), 0)
    chosen = jnp.where(chosen < rank, chosen, jnp.where(chosen < IN, -1, chosen - IN + rank))
    chosen = (chosen == iota((PROJ, select_t.shape[0]), 1)).astype(bf16)
    select_rows[...] = flipped(dot(chosen, select_t[...], (1, 0)).astype(bf16)).astype(bf16)
    table_t[...] = jnp.zeros_like(table_t)
    for k in range(3):
        table_t[3 * k : 3 * k + 3] = conv_kernel[k]
    table_t[BIAS : BIAS + 1] = conv_bias[...].reshape(1, inner_width)
    table_t[SKIP : SKIP + 1] = skip_gain[...].reshape(1, inner_width)
    table_t[GAIN : GAIN + 1, :model] = norm_gain[...].reshape(1, model)
    table_t[SHIFT : SHIFT + 1, :model] = norm_bias[...].reshape(1, model)
    table_t[STEP : STEP + rank] = step_weight[...]
    table_t[STEP + ONE : STEP + ONE + 1] = step_bias[...].reshape(1, inner_width)
    table_t[DECAY : DECAY + states] = decay_t[...]
    columns = flipped_fine(table_t[...])
    table[...] = columns
    gain, shift = (columns[:model, GAIN : GAIN + 1], columns[:model, SHIFT : SHIFT + 1])
    low = (normalized(entered(tok[...]))[0] * gain + shift).astype(bf16)
    cot_in = entered(cot[...]).astype(bf16)
    low_out[...] = low
    cot_out[...] = cot_in
    both = dot(in_rows, low, (1, 0))
    conv_out[...] = both[:inner_width]
    gate = both[inner_width:]
    gated_grad = dot(out_rows, cot_in, (1, 0))
    gate_out[...] = gate
    grad_out[...] = gated_grad
    mix_out[...] = gated_grad * (gate * sigmoid(gate))


def entry_kernel(
    heights, place, above, below, conv_own, mix, conv_rows, select_rows, table,
    send, halo_out, pre_out, low_halo_out,
):
    devices = send.shape[0]
    inner_width = conv_own.shape[0]
    model = conv_rows.shape[1]
    part = inner_width // devices
    columns = table[...]
    gain, shift = (columns[:model, GAIN : GAIN + 1], columns[:model, SHIFT : SHIFT + 1])
    halo = jnp.concatenate([below[:64], above[64:]], axis=0).astype(bf16)
    low_halo = (normalized(entered(halo))[0] * gain + shift).astype(bf16)
    low_halo_out[...] = low_halo
    around = dot(conv_rows[...], low_halo, (1, 0))
    halo_out[...] = around
    conv_in = conv_own[...]
    prev, following = row_masks(heights, place[0])
    upper, lower = rows_around(conv_in, around)
    taps = [[columns[:, 3 * a + b : 3 * a + b + 1] for b in range(3)] for a in range(3)]
    pre_act = columns[:, BIAS : BIAS + 1] + conv_tile(upper * prev, conv_in, lower * following, taps)
    inner = (pre_act * sigmoid(pre_act)).astype(bf16)
    proj = dot(flipped(select_rows[...]).astype(bf16), inner, (1, 0))
    proj = jnp.where(iota(proj.shape, 0) == ONE, 1.0, proj)
    pre_out[...] = pre_act
    inner = inner.astype(f32)
    for k in range(devices):
        send[k, :part] = inner[k * part : (k + 1) * part]
        send[k, part : 2 * part] = mix[k * part : (k + 1) * part]
        send[k, 2 * part :] = proj


def scan_kernel(
    heights, place, got, table,
    send, small,
    a_ref, s_ref, g_ref, down_ref, up_ref, col_h, col_m, row_h, row_m,
    prod, end_lr, end_rl, back_lr, back_rl, in_lr, in_rl, tail_lr, tail_rl,
    lhs_d, lhs_u, lhs_m, lhs_p, step_keep, delta_keep, y_keep, steps_keep, sums_keep, coefs_keep, decay_acc, *, part, states, span, group,
):
    devices, _, pos = got.shape
    rows = 2 * devices
    width = a_ref.shape[1]
    own_rows = table[pl.ds(pl.multiple_of(place[0] * part, 4), part), :]
    channel, state, live = lane_maps(part, states, width)
    twice = iota((2 * part, 1), 0)
    twice = jnp.where(twice >= part, twice - part, twice)
    spread_e = ((twice == channel) & live).astype(bf16)
    coef = iota((2 * PROJ, 1), 0)
    coef = jnp.where(coef >= PROJ, coef - PROJ, coef)
    near = state[:, :128]
    spread_bc = jnp.concatenate([coef - IN == near, coef - OUT == near], axis=1).astype(bf16)
    by_state = ((iota((states, 1), 0) == state) & live).astype(bf16)
    rate = -jnp.exp(own_rows[:, DECAY : DECAY + states])
    one_channel = (iota((part, 1), 0) == channel) & live
    rate_high, rate_low = split(rate)
    rate_rest = split(rate - rate_high.astype(f32) - rate_low.astype(f32))[0]
    rate_row = sum(dot(piece, by_state, (1, 0)) for piece in (rate_high, rate_low, rate_rest))
    rate_row = jnp.sum(jnp.where(one_channel, rate_row, 0.0), axis=0, keepdims=True)
    rate_two = rate_row * 1.4426950408889634
    step_own = own_rows[:, STEP : STEP + 16]
    step_high, step_low = split(step_own)
    step_three = jnp.concatenate([step_high, step_high, step_low], axis=1)
    one = eye(pos)

    def turned(value):
        return dot(one, jnp.concatenate(split(value), axis=0), (1, 1)).astype(bf16)

    for tile in range(devices):
        lines = slice(tile * pos, (tile + 1) * pos)
        inner_own = got[tile, :part]
        proj = got[tile, 2 * part :]
        high, low = split(proj[:16])
        pre_step = dot(step_three, jnp.concatenate([high, low, high], axis=0), (1, 0))
        tail = jnp.exp(-jnp.abs(pre_step))
        tail = jnp.where(tail < 1e-3, tail * (1.0 - 0.5 * tail), jnp.log(1.0 + tail))
        delta = jnp.maximum(pre_step, 0.0) + tail
        step_keep[tile] = sigmoid(pre_step)
        delta_keep[tile] = delta
        lhs_d[lines, :] = turned(delta)
        lhs_u[lines, :] = turned(delta * inner_own)
        lhs_m[lines, :] = turned(got[tile, part : 2 * part])
        lhs_p[lines, :] = turned(proj)

    def prepare(tile, carry):
        lines = pl.ds(pl.multiple_of(tile * pos, pos), pos)
        of_delta, of_source, of_mix, of_proj = (
            lhs_d[lines, :], lhs_u[lines, :], lhs_m[lines, :], lhs_p[lines, :]
        )
        of_bc = dot(of_proj, spread_bc, (1, 0))
        for k in range(width // span):
            lanes = slice(k * span, (k + 1) * span)
            a_ref[lines, lanes] = jnp.exp2(dot(of_delta, spread_e[:, lanes], (1, 0)) * rate_two[:, lanes])
            source = dot(of_source, spread_e[:, lanes], (1, 0))
            mix = dot(of_mix, spread_e[:, lanes], (1, 0))
            for j in range(span // 128):
                tile_lanes = slice(k * span + j * 128, k * span + (j + 1) * 128)
                piece = slice(j * 128, (j + 1) * 128)
                s_ref[lines, tile_lanes] = source[:, piece] * of_bc[:, :128]
                g_ref[lines, tile_lanes] = mix[:, piece] * of_bc[:, 128:]
        return carry

    lax.fori_loop(0, devices, prepare, 0)
    col_h[...] = jnp.zeros_like(col_h)
    col_m[...] = jnp.zeros_like(col_m)

    def packed(row, piece):
        return pl.ds(row * 64 + piece, 8, stride=8)

    def ascend(row, carry):
        keep = links_up(heights, row)
        for k in range(width // group):
            lanes = slice(k * group, (k + 1) * group)
            whole = lr = rl = mlr = mrl = None
            for c in range(8):
                lines = pl.ds(pl.multiple_of(row * 64 + c * 8, 8), 8)
                spot = slice(c * 8, c * 8 + 8)
                a, s, g = (a_ref[lines, lanes], s_ref[lines, lanes], g_ref[lines, lanes])
                state_h = a * (col_h[spot, lanes] * keep) + s
                col_h[spot, lanes] = state_h
                down_ref[lines, lanes] = state_h
                lam = g + col_m[spot, lanes] * keep
                col_m[spot, lanes] = a * lam
                up_ref[lines, lanes] = lam
                if c == 0:
                    whole, lr, rl, mlr, mrl = (a, s, s, a * g, a * g)
                else:
                    lr = a * lr + s
                    rl = rl + whole * s
                    whole = whole * a
                    mlr = mlr + whole * g
                    mrl = a * (mrl + g)
            for j in range(group // 128):
                spot = packed(row, k * (group // 128) + j)
                piece = slice(j * 128, (j + 1) * 128)
                prod[spot, :] = whole[:, piece]
                end_lr[spot, :] = lr[:, piece]
                end_rl[spot, :] = rl[:, piece]
                back_lr[spot, :] = mlr[:, piece]
                back_rl[spot, :] = mrl[:, piece]
        return carry

    lax.fori_loop(0, rows, ascend, 0)

    def chain(state_in, row, order, ends, starts):
        for c in order:
            line = pl.ds(pl.multiple_of(row * 64 + c * 8, 8), 8)
            starts[line, :] = state_in
            state_in = prod[line, :] * state_in + ends[line, :]
        return state_in

    def carries(pair, held):
        ahead, behind, back_ahead, back_behind = held
        right, left = (range(8), range(7, -1, -1))
        low = 2 * pair
        high = rows - 2 - low
        ahead = chain(ahead * links_up(heights, low), low, right, end_lr, in_lr)
        back_behind = chain(back_behind, low, right, back_rl, tail_rl)
        back_behind = back_behind * links_up(heights, low + 1)
        ahead = chain(ahead * links_up(heights, low + 1), low + 1, left, end_rl, in_rl)
        back_behind = chain(back_behind, low + 1, left, back_lr, tail_lr)
        back_behind = back_behind * links_up(heights, low + 2)
        behind = chain(behind * links_up(heights, high + 2), high + 1, right, end_lr, in_lr)
        back_ahead = chain(back_ahead, high + 1, right, back_rl, tail_rl)
        back_ahead = back_ahead * links_up(heights, high + 1)
        behind = chain(behind * links_up(heights, high + 1), high, left, end_rl, in_rl)
        back_ahead = chain(back_ahead, high, left, back_lr, tail_lr)
        back_ahead = back_ahead * links_up(heights, high)
        return (ahead, behind, back_ahead, back_behind)

    nothing = jnp.zeros((8, 128), f32)
    lax.fori_loop(0, devices, carries, (nothing,) * 4)
    col_h[...] = jnp.zeros_like(col_h)
    col_m[...] = jnp.zeros_like(col_m)

    def descend(step, carry):
        row = rows - 1 - step
        keep = links_up(heights, row + 1)

        def edge(ref, k):
            pieces = [ref[packed(row, k * (group // 128) + j), :] for j in range(group // 128)]
            return pieces[0] if len(pieces) == 1 else jnp.concatenate(pieces, axis=1)

        for k in range(width // group):
            lanes = slice(k * group, (k + 1) * group)
            h_right, m_left = (edge(in_lr, k), edge(tail_rl, k))
            for c in range(8):
                lines = pl.ds(pl.multiple_of(row * 64 + c * 8, 8), 8)
                spot = slice(c * 8, c * 8 + 8)
                a, s, g = (a_ref[lines, lanes], s_ref[lines, lanes], g_ref[lines, lanes])
                h_right = a * h_right + s
                lam = g + m_left
                m_left = a * lam
                row_h[spot, lanes] = h_right
                row_m[spot, lanes] = lam
            h_left, m_right = (edge(in_rl, k), edge(tail_lr, k))
            for c in range(7, -1, -1):
                lines = pl.ds(pl.multiple_of(row * 64 + c * 8, 8), 8)
                spot = slice(c * 8, c * 8 + 8)
                a, s, g = (a_ref[lines, lanes], s_ref[lines, lanes], g_ref[lines, lanes])
                h_left = a * h_left + s
                lam_lr = g + m_right
                m_right = a * lam_lr
                h_down, lam_up = (down_ref[lines, lanes], up_ref[lines, lanes])
                h_up = a * (col_h[spot, lanes] * keep) + s
                col_h[spot, lanes] = h_up
                lam_down = g + col_m[spot, lanes] * keep
                col_m[spot, lanes] = a * lam_down
                h_right, lam_rl = (row_h[spot, lanes], row_m[spot, lanes])
                lam_sum = (lam_lr + lam_rl) + (lam_down + lam_up)
                down_ref[lines, lanes] = (h_right + h_left) + (h_down + h_up)
                up_ref[lines, lanes] = lam_sum
                g_ref[lines, lanes] = (
                    (lam_lr * h_right + lam_rl * h_left)
                    + (lam_down * h_down + lam_up * h_up)
                    - s * lam_sum
                )
        return carry

    lax.fori_loop(0, rows, descend, 0)
    decay_acc[...] = jnp.zeros_like(decay_acc)
    gather_e, gather_b, gather_c = (spread_e[:part], spread_bc[:PROJ, :128], spread_bc[:PROJ, 128:])

    def finish(tile, carry):
        lines = pl.ds(pl.multiple_of(tile * pos, pos), pos)
        delta = delta_keep[tile]
        of_source, of_mix, of_proj = (lhs_u[lines, :], lhs_m[lines, :], lhs_p[lines, :])
        delta_low = delta.astype(bf16)
        of_bc = dot(of_proj, spread_bc, (1, 0))
        of_b, of_c = (of_bc[:, :128], of_bc[:, 128:])
        totals = grad_b = grad_c = None
        for k in range(width // span):
            lanes = slice(k * span, (k + 1) * span)
            scaled = (g_ref[lines, lanes] * rate_row[:, lanes]).astype(bf16)
            source = dot(of_source, spread_e[:, lanes], (1, 0))
            mix = dot(of_mix, spread_e[:, lanes], (1, 0))
            decay_acc[:, lanes] += dot(delta_low, scaled, (1, 0))
            of_y, of_sum = ([], [])
            for j in range(span // 128):
                tile_lanes = slice(k * span + j * 128, k * span + (j + 1) * 128)
                piece = slice(j * 128, (j + 1) * 128)
                h_sum, lam_sum = (down_ref[lines, tile_lanes], up_ref[lines, tile_lanes])
                of_y.append((h_sum * of_c).astype(bf16))
                of_sum.append((lam_sum * of_b).astype(bf16))
                term_b, term_c = (lam_sum * source[:, piece], h_sum * mix[:, piece])
                grad_b = term_b if grad_b is None else grad_b + term_b
                grad_c = term_c if grad_c is None else grad_c + term_c
            parts = (
                dot(gather_e[:, lanes], jnp.concatenate(of_y, axis=1), (1, 1)),
                dot(gather_e[:, lanes], scaled, (1, 1)),
                dot(gather_e[:, lanes], jnp.concatenate(of_sum, axis=1), (1, 1)),
            )
            totals = parts if totals is None else [x + z for x, z in zip(totals, parts)]
        y_keep[tile], steps_keep[tile], sums_keep[tile] = totals
        coefs_keep[tile] = dot(gather_b, grad_b.astype(bf16), (1, 1)) + dot(gather_c, grad_c.astype(bf16), (1, 1))
        return carry

    lax.fori_loop(0, devices, finish, 0)
    step_grad = jnp.zeros((part, 16), f32)
    for tile in range(devices):
        sums, coefs = (sums_keep[tile], coefs_keep[tile])
        pre_grad = (steps_keep[tile] + got[tile, :part] * sums) * step_keep[tile]
        send[tile, :part] = y_keep[tile]
        send[tile, part : 2 * part] = delta_keep[tile] * sums
        send[tile, 2 * part : 2 * part + 16] = coefs[:16] + fine_dot(step_own, pre_grad, (0, 0))
        send[tile, 2 * part + 16 :] = coefs[16:]
        step_grad = step_grad + fine_dot(pre_grad, got[tile, 2 * part : 2 * part + 16], (1, 1))
    decay_grad = jnp.where(one_channel, decay_acc[...], 0.0)
    decay_high, decay_low = split(decay_grad)
    decay_grad = dot(decay_high, by_state, (1, 1)) + dot(decay_low, by_state, (1, 1))
    spot = (iota((part, small.shape[1]), 1) == iota((part, small.shape[1]), 0) + place[0] * part).astype(bf16)
    for at, value in ((0, step_grad), (16, decay_grad)):
        high, low = split(value)
        small[at : at + 16] = dot(high, spot, (0, 0)) + dot(low, spot, (0, 0))


def mix_kernel(
    heights, place, group, got, small_in, tok, low, low_halo, cot, conv_own, conv_halo, pre, gate_in, grad_in,
    select_rows, table, in_w, out_t, conv_kernel, norm_gain, norm_bias,
    layer_out, act_out, up, down, gate_grad_out, keep, give,
    grads, *, pair,
):
    devices, length, pos = got.shape
    model, inner_width = out_t.shape
    part = inner_width // devices
    lane = iota((1, pos), 1)
    y = jnp.concatenate([got[k, :part] for k in range(devices)], axis=0)
    inner_grad = jnp.concatenate([got[k, part : 2 * part] for k in range(devices)], axis=0)
    proj_grad = got[0, 2 * part :]
    for k in range(1, devices):
        proj_grad = proj_grad + got[k, 2 * part :]
    proj_grad = proj_grad.astype(bf16)
    pre_act, gate, gated_grad = (pre[...], gate_in[...], grad_in[...])
    skip = table[:, SKIP : SKIP + 1]
    sig_pre, sig_gate = (sigmoid(pre_act), sigmoid(gate))
    inner = (pre_act * sig_pre).astype(bf16)
    inner_f = inner.astype(f32)
    silu_gate = gate * sig_gate
    mix_grad = gated_grad * silu_gate
    inner_grad = inner_grad + mix_grad * skip + dot(select_rows[...], proj_grad, (1, 0))
    act_grad = inner_grad * (sig_pre * (1.0 + pre_act * (1.0 - sig_pre)))
    act_out[...] = act_grad
    half = inner_width // 2
    top, bottom = (act_grad[:half], act_grad[half:])
    up[...] = jnp.where(lane < 64, top, pltpu.roll(bottom, 64, 1))
    down[...] = jnp.where(lane < 64, pltpu.roll(top, 64, 1), bottom)

    y_all = y + skip * inner_f
    gated = (y_all * silu_gate).astype(bf16)
    gate_grad = (gated_grad * y_all * (sig_gate * (1.0 + gate * (1.0 - sig_gate)))).astype(bf16)
    gate_grad_out[...] = gate_grad
    natural = dot(gated, column_order(pos), (1, 0)).astype(bf16)
    layer = jnp.transpose(dot(out_t[...], natural, (1, 0)))
    layer_out[...] = (tok[...].astype(f32) + layer).astype(bf16)

    prev, following = row_masks(heights, place[0])
    low_in = low[...]
    upper, lower = rows_around(low_in.astype(f32), low_halo[...].astype(f32))
    which = iota((16, 1), 0)
    masks = jnp.where(which == 0, prev, jnp.where(which == 1, 1.0, following))
    left_hand = jnp.concatenate(
        [(upper * prev).astype(bf16), low_in, (lower * following).astype(bf16), masks.astype(bf16)], axis=0
    )
    field = conv_own[...]
    edge_upper, edge_lower = rows_around(field, conv_halo[...])
    fields = (edge_upper * prev, field, edge_lower * following)
    in_conv = conv_total = None
    tap_sums = [None] * 9
    for b, moved in enumerate((from_right(act_grad), act_grad, from_left(act_grad))):
        part_b = dot(left_hand, moved.astype(bf16), (1, 1))
        for a in range(3):
            tap = conv_kernel[a, b : b + 1, :]
            term = tap * part_b[a * model : (a + 1) * model]
            total = tap * part_b[3 * model + a : 3 * model + a + 1]
            in_conv = term if in_conv is None else in_conv + term
            conv_total = total if conv_total is None else conv_total + total
            tap_sums[3 * a + b] = patch_sums(moved * fields[a])
    in_gate = dot(low_in, gate_grad, (1, 1))
    put_blocks(grads, 0, in_conv)
    blocks = inner_width // 128
    put_blocks(grads, blocks * model, in_gate)
    put_blocks(grads, 2 * blocks * model, dot(cot[...], gated, (1, 1)))
    sums = jnp.broadcast_to(jnp.concatenate([conv_total, patch_sums(gate_grad.astype(f32))], axis=1), (8, 2 * inner_width))
    sums_high, sums_low = split(sums)
    shift_row = (dot(sums_high, in_w[...], (1, 1)) + dot(sums_low, in_w[...], (1, 1)))[0:1]
    weights = in_w[...].astype(f32)
    gain_row = patch_sums(weights[:, :inner_width] * in_conv + weights[:, inner_width:] * in_gate)
    gain_row = (gain_row - norm_bias[...].reshape(1, model) * shift_row) / norm_gain[...].reshape(1, model)
    smalls = jnp.concatenate(
        [dot(proj_grad, inner, (1, 1)), small_in[...]]
        + tap_sums
        + [patch_sums(act_grad), patch_sums(mix_grad * inner_f), jnp.zeros((4, inner_width), f32)]
        + [jnp.concatenate([gain_row, shift_row], axis=1)],
        axis=0,
    )
    start = 3 * blocks * model
    put_blocks(grads, start, smalls)
    start = start + blocks * SMALL
    grads[start:] = jnp.zeros((grads.shape[0] - start, 128), f32)
    own = group[0] % 2
    if pair:
        count = keep.shape[0] // 2
        height = group[0] // 2
        for ref, side in ((keep, own), (give, 1 - own)):
            for k, at in enumerate((height, 1 - height)):
                ref[k * count : (k + 1) * count] = grads[pl.ds(pl.multiple_of((2 * side + at) * count, count), count)]
    else:
        count = keep.shape[0]
        keep[...] = grads[pl.ds(pl.multiple_of(own * count, count), count)]
        give[...] = grads[pl.ds(pl.multiple_of((1 - own) * count, count), count)]


def exit_kernel(
    heights, place, act, from_above, from_below, gate_grad, tok, cot, in_w, table,
    tokens_grad,
):
    inner_width, pos = act.shape
    model = in_w.shape[0]
    lane = iota((1, pos), 1)
    above, below = (from_above[...], from_below[...])
    halo_top = jnp.where(lane < 64, below, pltpu.roll(above, 64, 1))
    halo_bottom = jnp.where(lane < 64, pltpu.roll(below, 64, 1), above)
    act_grad = act[...]
    prev, following = row_masks(heights, place[0])
    upper, lower = rows_around(act_grad, jnp.concatenate([halo_top, halo_bottom], axis=0))
    columns = table[...]
    taps = [[columns[:, 8 - 3 * a - b : 9 - 3 * a - b] for b in range(3)] for a in range(3)]
    conv_grad = conv_tile(upper * prev, act_grad, lower * following, taps).astype(bf16)
    halves = jnp.concatenate([conv_grad, gate_grad[...]], axis=0)
    halves = dot(halves, column_order(pos), (1, 0)).astype(bf16)
    normed_grad = dot(in_w[...], halves, (1, 0))
    xhat, inverse = normalized(flipped(tok[...]))
    scaled = normed_grad * columns[:model, GAIN : GAIN + 1]
    x_grad = (
        scaled
        - jnp.mean(scaled, axis=0, keepdims=True)
        - xhat * jnp.mean(scaled * xhat, axis=0, keepdims=True)
    ) * inverse
    x_grad = jnp.transpose(x_grad)
    tokens_grad[...] = (x_grad + cot[...].astype(f32)).astype(bf16)


def deal_kernel(group, *refs, members, pair):
    pieces, ordered = (refs[:members], refs[-1])
    (
        gain_grad, shift_grad, inproj, kernel_grad, offset, select, stepproj, stepbias, decay, skip, outproj,
    ) = refs[members:-1]
    model, inner_width = outproj.shape
    blocks = inner_width // 128
    rank = stepproj.shape[0]
    states = decay.shape[0]
    count = pieces[0].shape[0]
    for k, piece in enumerate(pieces):
        if pair:
            core, height = (group[0] % 2, group[0] // 2)
            core = 1 - core if k // 2 else core
            height = 1 - height if k % 2 else height
            slot = core * 2 + height
        else:
            slot = k % 2 * (members // 2) + k // 2
        ordered[pl.ds(pl.multiple_of(slot * count, count), count)] = piece[...]

    def rows(start, count):
        return ordered[start : start + count]

    for k in range(2 * blocks):
        inproj[:, k * 128 : (k + 1) * 128] = rows(k * model, model)
    start = 2 * blocks * model
    for k in range(blocks):
        outproj[:, k * 128 : (k + 1) * 128] = rows(start + k * model, model)
    start = start + blocks * model
    small = jnp.concatenate([rows(start + k * SMALL, SMALL) for k in range(blocks)], axis=1)
    select[:rank] = small[:rank]
    select[rank:] = small[IN:PROJ]
    stepproj[...] = small[STEP_AT : STEP_AT + rank]
    stepbias[...] = small[STEP_AT + ONE : STEP_AT + ONE + 1].reshape(stepbias.shape)
    decay[...] = small[DECAY_AT : DECAY_AT + states]
    for k in range(3):
        kernel_grad[k] = small[TAPS_AT + 3 * k : TAPS_AT + 3 * k + 3]
    offset[...] = small[OFFSET_AT : OFFSET_AT + 1].reshape(offset.shape)
    skip[...] = small[SKIP_AT : SKIP_AT + 1].reshape(skip.shape)
    norms = small[NORM_AT : NORM_AT + 1]
    gain_grad[...] = norms[:, :model].reshape(gain_grad.shape)
    shift_grad[...] = norms[:, model:].reshape(shift_grad.shape)


def vmem_call(kernel, out_shape, scalars, arrays, scratch=(), limit=60):
    return pl.pallas_call(
        kernel,
        out_shape=out_shape,
        in_specs=[pl.BlockSpec(memory_space=pltpu.SMEM)] * len(scalars)
        + [pl.BlockSpec(memory_space=pltpu.VMEM)] * len(arrays),
        out_specs=[pl.BlockSpec(memory_space=pltpu.VMEM)] * len(out_shape),
        scratch_shapes=list(scratch),
        compiler_params=pltpu.CompilerParams(vmem_limit_bytes=limit * 1024 * 1024),
    )(*scalars, *arrays)


def struct(*shape, dtype=f32):
    return jax.ShapeDtypeStruct(shape, dtype)


def scan_call(heights, place, got, table, states):
    devices, length, pos = got.shape
    inner_width = table.shape[0]
    part = inner_width // devices
    width = -(-part * states // 128) * 128
    total = devices * pos
    span = 256 if width % 256 == 0 else 128
    group = 384 if width % 384 == 0 else span
    big = pltpu.VMEM((total, width), f32)
    line = pltpu.VMEM((2 * devices * 64, 128), f32)
    column = pltpu.VMEM((pos // 2, width), f32)
    own = pltpu.VMEM((devices, part, pos), f32)
    return vmem_call(
        functools.partial(scan_kernel, part=part, states=states, span=span, group=group),
        [struct(devices, length, pos), struct(32, inner_width)],
        [heights, place],
        [got, table],
        [big] * 5
        + [column] * 4
        + [line] * 9
        + [pltpu.VMEM((total, 2 * part), bf16)] * 3
        + [pltpu.VMEM((total, 2 * PROJ), bf16)]
        + [own] * 5
        + [pltpu.VMEM((devices, PROJ, pos), f32), pltpu.VMEM((part, width), f32)],
    )


def on_device(
    tokens, heights, cotangent, norm_gain, norm_bias, in_weight, conv_kernel, conv_bias, select_weight,
    step_weight, step_bias, decay_log, skip_gain, out_weight,
):
    _, tile_rows, grid_cols, model = tokens.shape
    inner_width = out_weight.shape[0]
    states = decay_log.shape[1]
    rank = step_weight.shape[0]
    devices = lax.axis_size("seq")
    groups = lax.axis_size("dp")
    place = lax.axis_index("seq").reshape(1)
    group = lax.axis_index("dp").reshape(1)
    pair = groups == 4
    pos = tile_rows * grid_cols
    part = inner_width // devices
    length = 2 * part + PROJ
    up_pairs = [(i, (i + 1) % devices) for i in range(devices)]
    down_pairs = [(j, i) for i, j in up_pairs]

    tok, cot = (tokens.reshape(pos, model), cotangent.reshape(pos, model))
    wide = tok.astype(f32)
    above = lax.ppermute(wide, "seq", up_pairs)
    below = lax.ppermute(wide, "seq", down_pairs)
    out_t = out_weight.T
    channels = struct(inner_width, pos)
    narrow = struct(model, pos, dtype=bf16)
    conv_own, gate, gated_grad, mix, low, cot_in, conv_rows, select_rows, table = vmem_call(
        own_kernel,
        [channels] * 4
        + [narrow] * 2
        + [struct(inner_width, model, dtype=bf16), struct(inner_width, PROJ, dtype=bf16), struct(inner_width, TABLE)],
        [],
        [
            tok, cot, in_weight, out_t, select_weight.T, conv_kernel, conv_bias, step_weight, step_bias,
            decay_log.T, skip_gain, norm_gain, norm_bias,
        ],
        [pltpu.VMEM((TABLE, inner_width), f32)],
    )
    sent, conv_halo, pre_act, low_halo = vmem_call(
        entry_kernel,
        [struct(devices, length, pos), channels, channels, narrow],
        [heights, place],
        [above, below, conv_own, mix, conv_rows, select_rows, table],
    )
    got = lax.all_to_all(sent, "seq", 0, 0, tiled=True)
    sent, small = scan_call(heights, place, got, table, states)
    got = lax.all_to_all(sent, "seq", 0, 0, tiled=True)
    blocks = inner_width // 128
    whole = -(-blocks * (3 * model + SMALL) // 2048) * 2048
    half = whole // 2
    layer_out, act_grad, up, down, gate_grad, keep, give = vmem_call(
        functools.partial(mix_kernel, pair=pair),
        [struct(pos, model, dtype=bf16), channels]
        + [struct(inner_width // 2, pos)] * 2
        + [struct(inner_width, pos, dtype=bf16)]
        + [struct(half, 128)] * 2,
        [heights, place, group],
        [
            got, small, tok, low, low_halo, cot_in, conv_own, conv_halo, pre_act, gate, gated_grad, select_rows,
            table, in_weight, out_t, conv_kernel, norm_gain, norm_bias,
        ],
        [pltpu.VMEM((whole, 128), f32)],
    )
    from_above = lax.ppermute(down, "seq", up_pairs)
    from_below = lax.ppermute(up, "seq", down_pairs)
    swap = [(i, i ^ 1) for i in range(groups)]
    taken = lax.ppermute(give, "dp", swap)
    count = half // (groups // 2)
    if pair:
        across = [(i, i ^ 2) for i in range(groups)]
        other = lax.ppermute(keep[count:] + taken[count:], "dp", across)
        piece = keep[:count] + taken[:count]
    else:
        same_core = [list(range(c, groups, 2)) for c in range(2)]
        pieces = (keep + taken).reshape(groups // 2, count, 128)
        pieces = lax.all_to_all(pieces, "dp", 0, 0, tiled=True, axis_index_groups=same_core)
        piece, other = (pieces[0], jnp.sum(pieces[1:], axis=0))
    other, from_above, from_below = lax.optimization_barrier((other, from_above, from_below))
    shares = (piece + other).reshape(devices, count // devices, 128)
    shares = lax.all_to_all(shares, "seq", 0, 0, tiled=True)
    share = jnp.broadcast_to(jnp.sum(shares, axis=0), shares.shape)
    mine = lax.all_to_all(share, "seq", 0, 0, tiled=True).reshape(count, 128)
    mine, from_above, from_below = lax.optimization_barrier((mine, from_above, from_below))
    (tokens_grad,) = vmem_call(
        exit_kernel,
        [struct(pos, model, dtype=bf16)],
        [heights, place],
        [act_grad, from_above, from_below, gate_grad, tok, cot, in_weight, table],
    )
    if pair:
        from_y = lax.ppermute(mine, "dp", across)
        from_y, tokens_grad = lax.optimization_barrier((from_y, tokens_grad))
        pieces = [mine, from_y, lax.ppermute(mine, "dp", swap), lax.ppermute(from_y, "dp", swap)]
    else:
        pieces = list(lax.all_gather(mine, "dp"))
    gain, shift, inproj, kernel, offset, select, stepproj, stepbias, decay, skip, outproj = vmem_call(
        functools.partial(deal_kernel, members=len(pieces), pair=pair),
        [
            struct(model), struct(model), struct(model, 2 * inner_width), struct(3, 3, inner_width),
            struct(inner_width), struct(rank + 2 * states, inner_width), struct(rank, inner_width),
            struct(inner_width), struct(states, inner_width), struct(inner_width), struct(model, inner_width),
        ],
        [group],
        pieces,
        [pltpu.VMEM((whole, 128), f32)],
    )
    shape = tokens.shape
    return (
        layer_out.reshape(shape), tokens_grad.reshape(shape), gain, shift, inproj, kernel, offset, select.T,
        stepproj, stepbias, decay.T, skip, outproj.T,
    )


def solution(mesh):
    tile, whole = (P("dp", "seq", None, None), P())
    return jax.shard_map(
        on_device,
        mesh=mesh,
        in_specs=(tile, P("dp", None), tile) + (whole,) * 11,
        out_specs=(tile, tile) + (whole,) * 11,
        check_vma=False,
    )
```

```python
import functools

import jax
import jax.numpy as jnp
from jax import lax
from jax.experimental import pallas as pl
from jax.experimental.pallas import tpu as pltpu
from jax.sharding import PartitionSpec as P

epsilon = 1e-05
f32, bf16 = (jnp.float32, jnp.bfloat16)
ONE, IN, OUT, PROJ = (12, 16, 32, 48)
BIAS, SKIP, GAIN, SHIFT, STEP, DECAY, TABLE = (9, 10, 11, 12, 16, 32, 48)
STEP_AT, DECAY_AT, TAPS_AT, OFFSET_AT, SKIP_AT, NORM_AT, SMALL = (48, 64, 80, 89, 90, 95, 96)


def dot(a, b, over):
    return lax.dot_general(a, b, (((over[0],), (over[1],)), ((), ())), preferred_element_type=f32)


def split(value):
    high = value.astype(bf16)
    return (high, (value - high.astype(f32)).astype(bf16))


def fine_dot(a, b, over):
    (a_high, a_low), (b_high, b_low) = (split(a), split(b))
    return dot(a_high, b_high, over) + (dot(a_low, b_high, over) + dot(a_high, b_low, over))


def iota(shape, dim):
    return lax.broadcasted_iota(jnp.int32, shape, dim)


def sigmoid(v):
    return 1.0 / (1.0 + jnp.exp(-v))


def links_up(heights, row):
    end = jnp.int32(0)
    same = row > 0
    for k in range(heights.shape[1]):
        end = end + heights[0, k]
        same = same & (end != row)
    return jnp.where(same, 1.0, 0.0).astype(f32)


def row_masks(heights, place):
    lane = iota((1, 128), 1)
    flags = [links_up(heights, 2 * place + k) for k in range(3)]
    return (jnp.where(lane < 64, flags[0], flags[1]), jnp.where(lane < 64, flags[1], flags[2]))


def rows_around(own, halo):
    lane = iota((1, 128), 1)
    upper = pltpu.roll(jnp.where(lane < 64, own, halo), 64, 1)
    lower = pltpu.roll(jnp.where(lane < 64, halo, own), 64, 1)
    return (upper, lower)


def from_left(tile):
    place = iota((1, 128), 1) & 63
    wrapped = jnp.where(place == 0, 0.0, pltpu.roll(tile, 73, 1))
    return jnp.where(place < 8, wrapped, pltpu.roll(tile, 8, 1))


def from_right(tile):
    place = iota((1, 128), 1) & 63
    wrapped = jnp.where(place == 63, 0.0, pltpu.roll(tile, 55, 1))
    return jnp.where(place >= 56, wrapped, pltpu.roll(tile, 120, 1))


def conv_tile(upper, own, lower, taps):
    left, middle, right = [
        taps[0][b] * upper + taps[1][b] * own + taps[2][b] * lower for b in range(3)
    ]
    return middle + (from_left(left) + from_right(right))


def normalized(x):
    centred = x - jnp.mean(x, axis=0, keepdims=True)
    inverse = lax.rsqrt(jnp.mean(centred * centred, axis=0, keepdims=True) + epsilon)
    return (centred * inverse, inverse)


def eye(size):
    return (iota((size, size), 0) == iota((size, size), 1)).astype(bf16)


def flipped(value):
    pieces = [value[:, k : k + 128] for k in range(0, value.shape[1], 128)]
    return jnp.concatenate([dot(eye(piece.shape[1]), piece, (1, 1)) for piece in pieces], axis=0)


def flipped_fine(value):
    high, low = split(value)
    rest = (value - high.astype(f32) - low.astype(f32)).astype(bf16)
    return flipped(high) + (flipped(low) + flipped(rest))


def patch_sums(value):
    high, low = split(value)
    ones = jnp.ones((8, value.shape[1]), bf16)
    return (dot(ones, high, (1, 1)) + dot(ones, low, (1, 1)))[0:1]


def put_blocks(ref, start, value):
    for k in range(value.shape[1] // 128):
        ref[start + k * value.shape[0] : start + (k + 1) * value.shape[0]] = value[:, k * 128 : (k + 1) * 128]


def column_order(pos):
    new, old = (iota((pos, pos), 0), iota((pos, pos), 1))
    source = (new & ~63) | ((new & 7) << 3) | ((new >> 3) & 7)
    return (source == old).astype(bf16)


def lane_maps(part, states, width):
    lane = iota((1, width), 1)
    channel = jnp.floor((lane.astype(f32) + 0.5) * (1.0 / states)).astype(jnp.int32)
    return (channel, lane - channel * states, channel < part)


def entered(rows):
    return dot(flipped(rows).astype(bf16), column_order(rows.shape[0]), (1, 0))


def own_kernel(
    tok, cot, in_w, out_t, select_t, conv_kernel, conv_bias, step_weight, step_bias, decay_t, skip_gain,
    norm_gain, norm_bias,
    conv_out, gate_out, grad_out, mix_out, low_out, cot_out, conv_rows, select_rows, table,
    table_t,
):
    model, inner_width = out_t.shape
    states = decay_t.shape[0]
    rank = step_weight.shape[0]
    in_rows = flipped(in_w[...]).astype(bf16)
    conv_rows[...] = in_rows[:inner_width]
    out_rows = flipped(out_t[...]).astype(bf16)
    chosen = iota((PROJ, select_t.shape[0]), 0)
    chosen = jnp.where(chosen < rank, chosen, jnp.where(chosen < IN, -1, chosen - IN + rank))
    chosen = (chosen == iota((PROJ, select_t.shape[0]), 1)).astype(bf16)
    select_rows[...] = flipped(dot(chosen, select_t[...], (1, 0)).astype(bf16)).astype(bf16)
    table_t[...] = jnp.zeros_like(table_t)
    for k in range(3):
        table_t[3 * k : 3 * k + 3] = conv_kernel[k]
    table_t[BIAS : BIAS + 1] = conv_bias[...].reshape(1, inner_width)
    table_t[SKIP : SKIP + 1] = skip_gain[...].reshape(1, inner_width)
    table_t[GAIN : GAIN + 1, :model] = norm_gain[...].reshape(1, model)
    table_t[SHIFT : SHIFT + 1, :model] = norm_bias[...].reshape(1, model)
    table_t[STEP : STEP + rank] = step_weight[...]
    table_t[STEP + ONE : STEP + ONE + 1] = step_bias[...].reshape(1, inner_width)
    table_t[DECAY : DECAY + states] = decay_t[...]
    columns = flipped_fine(table_t[...])
    table[...] = columns
    gain, shift = (columns[:model, GAIN : GAIN + 1], columns[:model, SHIFT : SHIFT + 1])
    low = (normalized(entered(tok[...]))[0] * gain + shift).astype(bf16)
    cot_in = entered(cot[...]).astype(bf16)
    low_out[...] = low
    cot_out[...] = cot_in
    both = dot(in_rows, low, (1, 0))
    conv_out[...] = both[:inner_width]
    gate = both[inner_width:]
    gated_grad = dot(out_rows, cot_in, (1, 0))
    gate_out[...] = gate
    grad_out[...] = gated_grad
    mix_out[...] = gated_grad * (gate * sigmoid(gate))


def entry_kernel(
    heights, place, above, below, conv_own, mix, conv_rows, select_rows, table,
    send, halo_out, pre_out, low_halo_out,
):
    devices = send.shape[0]
    inner_width = conv_own.shape[0]
    model = conv_rows.shape[1]
    part = inner_width // devices
    columns = table[...]
    gain, shift = (columns[:model, GAIN : GAIN + 1], columns[:model, SHIFT : SHIFT + 1])
    halo = jnp.concatenate([below[:64], above[64:]], axis=0).astype(bf16)
    low_halo = (normalized(entered(halo))[0] * gain + shift).astype(bf16)
    low_halo_out[...] = low_halo
    around = dot(conv_rows[...], low_halo, (1, 0))
    halo_out[...] = around
    conv_in = conv_own[...]
    prev, following = row_masks(heights, place[0])
    upper, lower = rows_around(conv_in, around)
    taps = [[columns[:, 3 * a + b : 3 * a + b + 1] for b in range(3)] for a in range(3)]
    pre_act = columns[:, BIAS : BIAS + 1] + conv_tile(upper * prev, conv_in, lower * following, taps)
    inner = (pre_act * sigmoid(pre_act)).astype(bf16)
    proj = dot(flipped(select_rows[...]).astype(bf16), inner, (1, 0))
    proj = jnp.where(iota(proj.shape, 0) == ONE, 1.0, proj)
    pre_out[...] = pre_act
    inner = inner.astype(f32)
    for k in range(devices):
        send[k, :part] = inner[k * part : (k + 1) * part]
        send[k, part : 2 * part] = mix[k * part : (k + 1) * part]
        send[k, 2 * part :] = proj


def scan_kernel(
    heights, place, got, table,
    send, small,
    a_ref, s_ref, g_ref, down_ref, up_ref, col_h, col_m, row_h, row_m,
    prod, end_lr, end_rl, back_lr, back_rl, in_lr, in_rl, tail_lr, tail_rl,
    lhs_d, lhs_u, lhs_m, lhs_p, step_keep, delta_keep, y_keep, steps_keep, sums_keep, coefs_keep, decay_acc, *, part, states, span, group,
):
    devices, _, pos = got.shape
    rows = 2 * devices
    width = a_ref.shape[1]
    own_rows = table[pl.ds(pl.multiple_of(place[0] * part, 4), part), :]
    channel, state, live = lane_maps(part, states, width)
    twice = iota((2 * part, 1), 0)
    twice = jnp.where(twice >= part, twice - part, twice)
    spread_e = ((twice == channel) & live).astype(bf16)
    coef = iota((2 * PROJ, 1), 0)
    coef = jnp.where(coef >= PROJ, coef - PROJ, coef)
    near = state[:, :128]
    spread_bc = jnp.concatenate([coef - IN == near, coef - OUT == near], axis=1).astype(bf16)
    by_state = ((iota((states, 1), 0) == state) & live).astype(bf16)
    rate = -jnp.exp(own_rows[:, DECAY : DECAY + states])
    one_channel = (iota((part, 1), 0) == channel) & live
    rate_high, rate_low = split(rate)
    rate_rest = split(rate - rate_high.astype(f32) - rate_low.astype(f32))[0]
    rate_row = sum(dot(piece, by_state, (1, 0)) for piece in (rate_high, rate_low, rate_rest))
    rate_row = jnp.sum(jnp.where(one_channel, rate_row, 0.0), axis=0, keepdims=True)
    rate_two = rate_row * 1.4426950408889634
    step_own = own_rows[:, STEP : STEP + 16]
    step_high, step_low = split(step_own)
    step_three = jnp.concatenate([step_high, step_high, step_low], axis=1)
    one = eye(pos)

    def turned(value):
        return dot(one, jnp.concatenate(split(value), axis=0), (1, 1)).astype(bf16)

    for tile in range(devices):
        lines = slice(tile * pos, (tile + 1) * pos)
        inner_own = got[tile, :part]
        proj = got[tile, 2 * part :]
        high, low = split(proj[:16])
        pre_step = dot(step_three, jnp.concatenate([high, low, high], axis=0), (1, 0))
        tail = jnp.exp(-jnp.abs(pre_step))
        tail = jnp.where(tail < 1e-3, tail * (1.0 - 0.5 * tail), jnp.log(1.0 + tail))
        delta = jnp.maximum(pre_step, 0.0) + tail
        step_keep[tile] = sigmoid(pre_step)
        delta_keep[tile] = delta
        lhs_d[lines, :] = turned(delta)
        lhs_u[lines, :] = turned(delta * inner_own)
        lhs_m[lines, :] = turned(got[tile, part : 2 * part])
        lhs_p[lines, :] = turned(proj)

    def prepare(tile, carry):
        lines = pl.ds(pl.multiple_of(tile * pos, pos), pos)
        of_delta, of_source, of_mix, of_proj = (
            lhs_d[lines, :], lhs_u[lines, :], lhs_m[lines, :], lhs_p[lines, :]
        )
        of_bc = dot(of_proj, spread_bc, (1, 0))
        for k in range(width // span):
            lanes = slice(k * span, (k + 1) * span)
            a_ref[lines, lanes] = jnp.exp2(dot(of_delta, spread_e[:, lanes], (1, 0)) * rate_two[:, lanes])
            source = dot(of_source, spread_e[:, lanes], (1, 0))
            mix = dot(of_mix, spread_e[:, lanes], (1, 0))
            for j in range(span // 128):
                tile_lanes = slice(k * span + j * 128, k * span + (j + 1) * 128)
                piece = slice(j * 128, (j + 1) * 128)
                s_ref[lines, tile_lanes] = source[:, piece] * of_bc[:, :128]
                g_ref[lines, tile_lanes] = mix[:, piece] * of_bc[:, 128:]
        return carry

    lax.fori_loop(0, devices, prepare, 0)
    col_h[...] = jnp.zeros_like(col_h)
    col_m[...] = jnp.zeros_like(col_m)

    def packed(row, piece):
        return pl.ds(row * 64 + piece, 8, stride=8)

    def ascend(row, carry):
        keep = links_up(heights, row)
        for k in range(width // group):
            lanes = slice(k * group, (k + 1) * group)
            whole = lr = rl = mlr = mrl = None
            for c in range(8):
                lines = pl.ds(pl.multiple_of(row * 64 + c * 8, 8), 8)
                spot = slice(c * 8, c * 8 + 8)
                a, s, g = (a_ref[lines, lanes], s_ref[lines, lanes], g_ref[lines, lanes])
                state_h = a * (col_h[spot, lanes] * keep) + s
                col_h[spot, lanes] = state_h
                down_ref[lines, lanes] = state_h
                lam = g + col_m[spot, lanes] * keep
                col_m[spot, lanes] = a * lam
                up_ref[lines, lanes] = lam
                if c == 0:
                    whole, lr, rl, mlr, mrl = (a, s, s, a * g, a * g)
                else:
                    lr = a * lr + s
                    rl = rl + whole * s
                    whole = whole * a
                    mlr = mlr + whole * g
                    mrl = a * (mrl + g)
            for j in range(group // 128):
                spot = packed(row, k * (group // 128) + j)
                piece = slice(j * 128, (j + 1) * 128)
                prod[spot, :] = whole[:, piece]
                end_lr[spot, :] = lr[:, piece]
                end_rl[spot, :] = rl[:, piece]
                back_lr[spot, :] = mlr[:, piece]
                back_rl[spot, :] = mrl[:, piece]
        return carry

    lax.fori_loop(0, rows, ascend, 0)

    def chain(state_in, row, order, ends, starts):
        for c in order:
            line = pl.ds(pl.multiple_of(row * 64 + c * 8, 8), 8)
            starts[line, :] = state_in
            state_in = prod[line, :] * state_in + ends[line, :]
        return state_in

    def carries(pair, held):
        ahead, behind, back_ahead, back_behind = held
        right, left = (range(8), range(7, -1, -1))
        low = 2 * pair
        high = rows - 2 - low
        ahead = chain(ahead * links_up(heights, low), low, right, end_lr, in_lr)
        back_behind = chain(back_behind, low, right, back_rl, tail_rl)
        back_behind = back_behind * links_up(heights, low + 1)
        ahead = chain(ahead * links_up(heights, low + 1), low + 1, left, end_rl, in_rl)
        back_behind = chain(back_behind, low + 1, left, back_lr, tail_lr)
        back_behind = back_behind * links_up(heights, low + 2)
        behind = chain(behind * links_up(heights, high + 2), high + 1, right, end_lr, in_lr)
        back_ahead = chain(back_ahead, high + 1, right, back_rl, tail_rl)
        back_ahead = back_ahead * links_up(heights, high + 1)
        behind = chain(behind * links_up(heights, high + 1), high, left, end_rl, in_rl)
        back_ahead = chain(back_ahead, high, left, back_lr, tail_lr)
        back_ahead = back_ahead * links_up(heights, high)
        return (ahead, behind, back_ahead, back_behind)

    nothing = jnp.zeros((8, 128), f32)
    lax.fori_loop(0, devices, carries, (nothing,) * 4)
    col_h[...] = jnp.zeros_like(col_h)
    col_m[...] = jnp.zeros_like(col_m)

    def descend(step, carry):
        row = rows - 1 - step
        keep = links_up(heights, row + 1)

        def edge(ref, k):
            pieces = [ref[packed(row, k * (group // 128) + j), :] for j in range(group // 128)]
            return pieces[0] if len(pieces) == 1 else jnp.concatenate(pieces, axis=1)

        for k in range(width // group):
            lanes = slice(k * group, (k + 1) * group)
            h_right, m_left = (edge(in_lr, k), edge(tail_rl, k))
            for c in range(8):
                lines = pl.ds(pl.multiple_of(row * 64 + c * 8, 8), 8)
                spot = slice(c * 8, c * 8 + 8)
                a, s, g = (a_ref[lines, lanes], s_ref[lines, lanes], g_ref[lines, lanes])
                h_right = a * h_right + s
                lam = g + m_left
                m_left = a * lam
                row_h[spot, lanes] = h_right
                row_m[spot, lanes] = lam
            h_left, m_right = (edge(in_rl, k), edge(tail_lr, k))
            for c in range(7, -1, -1):
                lines = pl.ds(pl.multiple_of(row * 64 + c * 8, 8), 8)
                spot = slice(c * 8, c * 8 + 8)
                a, s, g = (a_ref[lines, lanes], s_ref[lines, lanes], g_ref[lines, lanes])
                h_left = a * h_left + s
                lam_lr = g + m_right
                m_right = a * lam_lr
                h_down, lam_up = (down_ref[lines, lanes], up_ref[lines, lanes])
                h_up = a * (col_h[spot, lanes] * keep) + s
                col_h[spot, lanes] = h_up
                lam_down = g + col_m[spot, lanes] * keep
                col_m[spot, lanes] = a * lam_down
                h_right, lam_rl = (row_h[spot, lanes], row_m[spot, lanes])
                lam_sum = (lam_lr + lam_rl) + (lam_down + lam_up)
                down_ref[lines, lanes] = (h_right + h_left) + (h_down + h_up)
                up_ref[lines, lanes] = lam_sum
                g_ref[lines, lanes] = (
                    (lam_lr * h_right + lam_rl * h_left)
                    + (lam_down * h_down + lam_up * h_up)
                    - s * lam_sum
                )
        return carry

    lax.fori_loop(0, rows, descend, 0)
    decay_acc[...] = jnp.zeros_like(decay_acc)
    gather_e, gather_b, gather_c = (spread_e[:part], spread_bc[:PROJ, :128], spread_bc[:PROJ, 128:])

    def finish(tile, carry):
        lines = pl.ds(pl.multiple_of(tile * pos, pos), pos)
        delta = delta_keep[tile]
        of_source, of_mix, of_proj = (lhs_u[lines, :], lhs_m[lines, :], lhs_p[lines, :])
        delta_low = delta.astype(bf16)
        of_bc = dot(of_proj, spread_bc, (1, 0))
        of_b, of_c = (of_bc[:, :128], of_bc[:, 128:])
        totals = grad_b = grad_c = None
        for k in range(width // span):
            lanes = slice(k * span, (k + 1) * span)
            scaled = (g_ref[lines, lanes] * rate_row[:, lanes]).astype(bf16)
            source = dot(of_source, spread_e[:, lanes], (1, 0))
            mix = dot(of_mix, spread_e[:, lanes], (1, 0))
            decay_acc[:, lanes] += dot(delta_low, scaled, (1, 0))
            of_y, of_sum = ([], [])
            for j in range(span // 128):
                tile_lanes = slice(k * span + j * 128, k * span + (j + 1) * 128)
                piece = slice(j * 128, (j + 1) * 128)
                h_sum, lam_sum = (down_ref[lines, tile_lanes], up_ref[lines, tile_lanes])
                of_y.append((h_sum * of_c).astype(bf16))
                of_sum.append((lam_sum * of_b).astype(bf16))
                term_b, term_c = (lam_sum * source[:, piece], h_sum * mix[:, piece])
                grad_b = term_b if grad_b is None else grad_b + term_b
                grad_c = term_c if grad_c is None else grad_c + term_c
            parts = (
                dot(gather_e[:, lanes], jnp.concatenate(of_y, axis=1), (1, 1)),
                dot(gather_e[:, lanes], scaled, (1, 1)),
                dot(gather_e[:, lanes], jnp.concatenate(of_sum, axis=1), (1, 1)),
            )
            totals = parts if totals is None else [x + z for x, z in zip(totals, parts)]
        y_keep[tile], steps_keep[tile], sums_keep[tile] = totals
        coefs_keep[tile] = dot(gather_b, grad_b.astype(bf16), (1, 1)) + dot(gather_c, grad_c.astype(bf16), (1, 1))
        return carry

    lax.fori_loop(0, devices, finish, 0)
    step_grad = jnp.zeros((part, 16), f32)
    for tile in range(devices):
        sums, coefs = (sums_keep[tile], coefs_keep[tile])
        pre_grad = (steps_keep[tile] + got[tile, :part] * sums) * step_keep[tile]
        send[tile, :part] = y_keep[tile]
        send[tile, part : 2 * part] = delta_keep[tile] * sums
        send[tile, 2 * part : 2 * part + 16] = coefs[:16] + fine_dot(step_own, pre_grad, (0, 0))
        send[tile, 2 * part + 16 :] = coefs[16:]
        step_grad = step_grad + fine_dot(pre_grad, got[tile, 2 * part : 2 * part + 16], (1, 1))
    decay_grad = jnp.where(one_channel, decay_acc[...], 0.0)
    decay_high, decay_low = split(decay_grad)
    decay_grad = dot(decay_high, by_state, (1, 1)) + dot(decay_low, by_state, (1, 1))
    spot = (iota((part, small.shape[1]), 1) == iota((part, small.shape[1]), 0) + place[0] * part).astype(bf16)
    for at, value in ((0, step_grad), (16, decay_grad)):
        high, low = split(value)
        small[at : at + 16] = dot(high, spot, (0, 0)) + dot(low, spot, (0, 0))


def mix_kernel(
    heights, place, group, got, small_in, low, low_halo, cot, conv_own, conv_halo, pre, gate_in, grad_in,
    select_rows, table, tok, in_w, out_t, conv_kernel, norm_gain, norm_bias,
    layer_out, act_out, up, down, gate_grad_out, keep, give,
    grads, *, pair,
):
    devices, length, pos = got.shape
    model, inner_width = out_t.shape
    part = inner_width // devices
    lane = iota((1, pos), 1)
    y = jnp.concatenate([got[k, :part] for k in range(devices)], axis=0)
    inner_grad = jnp.concatenate([got[k, part : 2 * part] for k in range(devices)], axis=0)
    proj_grad = got[0, 2 * part :]
    for k in range(1, devices):
        proj_grad = proj_grad + got[k, 2 * part :]
    proj_grad = proj_grad.astype(bf16)
    pre_act, gate, gated_grad = (pre[...], gate_in[...], grad_in[...])
    skip = table[:, SKIP : SKIP + 1]
    sig_pre, sig_gate = (sigmoid(pre_act), sigmoid(gate))
    inner = (pre_act * sig_pre).astype(bf16)
    inner_f = inner.astype(f32)
    silu_gate = gate * sig_gate
    mix_grad = gated_grad * silu_gate
    inner_grad = inner_grad + mix_grad * skip + dot(select_rows[...], proj_grad, (1, 0))
    act_grad = inner_grad * (sig_pre * (1.0 + pre_act * (1.0 - sig_pre)))
    act_out[...] = act_grad
    half = inner_width // 2
    top, bottom = (act_grad[:half], act_grad[half:])
    up[...] = jnp.where(lane < 64, top, pltpu.roll(bottom, 64, 1))
    down[...] = jnp.where(lane < 64, pltpu.roll(top, 64, 1), bottom)

    y_all = y + skip * inner_f
    gated = (y_all * silu_gate).astype(bf16)
    gate_grad = (gated_grad * y_all * (sig_gate * (1.0 + gate * (1.0 - sig_gate)))).astype(bf16)
    gate_grad_out[...] = gate_grad
    natural = dot(gated, column_order(pos), (1, 0)).astype(bf16)
    layer = jnp.transpose(dot(out_t[...], natural, (1, 0)))
    layer_out[...] = (tok[...].astype(f32) + layer).astype(bf16)

    prev, following = row_masks(heights, place[0])
    low_in = low[...]
    upper, lower = rows_around(low_in.astype(f32), low_halo[...].astype(f32))
    which = iota((16, 1), 0)
    masks = jnp.where(which == 0, prev, jnp.where(which == 1, 1.0, following))
    left_hand = jnp.concatenate(
        [(upper * prev).astype(bf16), low_in, (lower * following).astype(bf16), masks.astype(bf16)], axis=0
    )
    field = conv_own[...]
    edge_upper, edge_lower = rows_around(field, conv_halo[...])
    fields = (edge_upper * prev, field, edge_lower * following)
    in_conv = conv_total = None
    tap_sums = [None] * 9
    for b, moved in enumerate((from_right(act_grad), act_grad, from_left(act_grad))):
        part_b = dot(left_hand, moved.astype(bf16), (1, 1))
        for a in range(3):
            tap = conv_kernel[a, b : b + 1, :]
            term = tap * part_b[a * model : (a + 1) * model]
            total = tap * part_b[3 * model + a : 3 * model + a + 1]
            in_conv = term if in_conv is None else in_conv + term
            conv_total = total if conv_total is None else conv_total + total
            tap_sums[3 * a + b] = patch_sums(moved * fields[a])
    in_gate = dot(low_in, gate_grad, (1, 1))
    put_blocks(grads, 0, in_conv)
    blocks = inner_width // 128
    put_blocks(grads, blocks * model, in_gate)
    put_blocks(grads, 2 * blocks * model, dot(cot[...], gated, (1, 1)))
    sums = jnp.broadcast_to(jnp.concatenate([conv_total, patch_sums(gate_grad.astype(f32))], axis=1), (8, 2 * inner_width))
    sums_high, sums_low = split(sums)
    shift_row = (dot(sums_high, in_w[...], (1, 1)) + dot(sums_low, in_w[...], (1, 1)))[0:1]
    weights = in_w[...].astype(f32)
    gain_row = patch_sums(weights[:, :inner_width] * in_conv + weights[:, inner_width:] * in_gate)
    gain_row = (gain_row - norm_bias[...].reshape(1, model) * shift_row) / norm_gain[...].reshape(1, model)
    smalls = jnp.concatenate(
        [dot(proj_grad, inner, (1, 1)), small_in[...]]
        + tap_sums
        + [patch_sums(act_grad), patch_sums(mix_grad * inner_f), jnp.zeros((4, inner_width), f32)]
        + [jnp.concatenate([gain_row, shift_row], axis=1)],
        axis=0,
    )
    start = 3 * blocks * model
    put_blocks(grads, start, smalls)
    start = start + blocks * SMALL
    grads[start:] = jnp.zeros((grads.shape[0] - start, 128), f32)
    own = group[0] % 2
    if pair:
        count = keep.shape[0] // 2
        height = group[0] // 2
        for ref, side in ((keep, own), (give, 1 - own)):
            for k, at in enumerate((height, 1 - height)):
                ref[k * count : (k + 1) * count] = grads[pl.ds(pl.multiple_of((2 * side + at) * count, count), count)]
    else:
        count = keep.shape[0]
        keep[...] = grads[pl.ds(pl.multiple_of(own * count, count), count)]
        give[...] = grads[pl.ds(pl.multiple_of((1 - own) * count, count), count)]


def exit_kernel(
    heights, place, act, from_above, from_below, gate_grad, table, tok, cot, in_w,
    tokens_grad,
):
    inner_width, pos = act.shape
    model = in_w.shape[0]
    lane = iota((1, pos), 1)
    above, below = (from_above[...], from_below[...])
    halo_top = jnp.where(lane < 64, below, pltpu.roll(above, 64, 1))
    halo_bottom = jnp.where(lane < 64, pltpu.roll(below, 64, 1), above)
    act_grad = act[...]
    prev, following = row_masks(heights, place[0])
    upper, lower = rows_around(act_grad, jnp.concatenate([halo_top, halo_bottom], axis=0))
    columns = table[...]
    taps = [[columns[:, 8 - 3 * a - b : 9 - 3 * a - b] for b in range(3)] for a in range(3)]
    conv_grad = conv_tile(upper * prev, act_grad, lower * following, taps).astype(bf16)
    halves = jnp.concatenate([conv_grad, gate_grad[...]], axis=0)
    halves = dot(halves, column_order(pos), (1, 0)).astype(bf16)
    normed_grad = dot(in_w[...], halves, (1, 0))
    xhat, inverse = normalized(flipped(tok[...]))
    scaled = normed_grad * columns[:model, GAIN : GAIN + 1]
    x_grad = (
        scaled
        - jnp.mean(scaled, axis=0, keepdims=True)
        - xhat * jnp.mean(scaled * xhat, axis=0, keepdims=True)
    ) * inverse
    x_grad = jnp.transpose(x_grad)
    tokens_grad[...] = (x_grad + cot[...].astype(f32)).astype(bf16)


def deal_kernel(group, *refs, members, pair):
    pieces, ordered = (refs[:members], refs[-1])
    (
        gain_grad, shift_grad, inproj, kernel_grad, offset, select, stepproj, stepbias, decay, skip, outproj,
    ) = refs[members:-1]
    model, inner_width = outproj.shape
    blocks = inner_width // 128
    rank = stepproj.shape[0]
    states = decay.shape[0]
    count = pieces[0].shape[0]
    for k, piece in enumerate(pieces):
        if pair:
            core, height = (group[0] % 2, group[0] // 2)
            core = 1 - core if k // 2 else core
            height = 1 - height if k % 2 else height
            slot = core * 2 + height
        else:
            slot = k % 2 * (members // 2) + k // 2
        ordered[pl.ds(pl.multiple_of(slot * count, count), count)] = piece[...]

    def rows(start, count):
        return ordered[start : start + count]

    for k in range(2 * blocks):
        inproj[:, k * 128 : (k + 1) * 128] = rows(k * model, model)
    start = 2 * blocks * model
    for k in range(blocks):
        outproj[:, k * 128 : (k + 1) * 128] = rows(start + k * model, model)
    start = start + blocks * model
    small = jnp.concatenate([rows(start + k * SMALL, SMALL) for k in range(blocks)], axis=1)
    select[:rank] = small[:rank]
    select[rank:] = small[IN:PROJ]
    stepproj[...] = small[STEP_AT : STEP_AT + rank]
    stepbias[...] = small[STEP_AT + ONE : STEP_AT + ONE + 1].reshape(stepbias.shape)
    decay[...] = small[DECAY_AT : DECAY_AT + states]
    for k in range(3):
        kernel_grad[k] = small[TAPS_AT + 3 * k : TAPS_AT + 3 * k + 3]
    offset[...] = small[OFFSET_AT : OFFSET_AT + 1].reshape(offset.shape)
    skip[...] = small[SKIP_AT : SKIP_AT + 1].reshape(skip.shape)
    norms = small[NORM_AT : NORM_AT + 1]
    gain_grad[...] = norms[:, :model].reshape(gain_grad.shape)
    shift_grad[...] = norms[:, model:].reshape(shift_grad.shape)


def vmem_call(kernel, out_shape, scalars, arrays, weights=(), scratch=(), limit=16):
    arrays = [pltpu.with_memory_space_constraint(x, pltpu.VMEM) for x in arrays]
    arrays += [pltpu.with_memory_space_constraint(x, pltpu.HBM) for x in weights]
    return pl.pallas_call(
        kernel,
        out_shape=out_shape,
        in_specs=[pl.BlockSpec(memory_space=pltpu.SMEM)] * len(scalars)
        + [pl.BlockSpec(memory_space=pltpu.VMEM)] * len(arrays),
        out_specs=[pl.BlockSpec(memory_space=pltpu.VMEM)] * len(out_shape),
        scratch_shapes=list(scratch),
        compiler_params=pltpu.CompilerParams(vmem_limit_bytes=limit * 1024 * 1024),
    )(*scalars, *arrays)


def struct(*shape, dtype=f32):
    return jax.ShapeDtypeStruct(shape, dtype)


def scan_call(heights, place, got, table, states):
    devices, length, pos = got.shape
    inner_width = table.shape[0]
    part = inner_width // devices
    width = -(-part * states // 128) * 128
    total = devices * pos
    span = 256 if width % 256 == 0 else 128
    group = 384 if width % 384 == 0 else span
    big = pltpu.VMEM((total, width), f32)
    line = pltpu.VMEM((2 * devices * 64, 128), f32)
    column = pltpu.VMEM((pos // 2, width), f32)
    own = pltpu.VMEM((devices, part, pos), f32)
    return vmem_call(
        functools.partial(scan_kernel, part=part, states=states, span=span, group=group),
        [struct(devices, length, pos), struct(32, inner_width)],
        [heights, place],
        [got, table],
        (),
        [big] * 5
        + [column] * 4
        + [line] * 9
        + [pltpu.VMEM((total, 2 * part), bf16)] * 3
        + [pltpu.VMEM((total, 2 * PROJ), bf16)]
        + [own] * 5
        + [pltpu.VMEM((devices, PROJ, pos), f32), pltpu.VMEM((part, width), f32)],
        limit=32 if total <= 1024 else 52,
    )


def on_device(
    tokens, heights, cotangent, norm_gain, norm_bias, in_weight, conv_kernel, conv_bias, select_weight,
    step_weight, step_bias, decay_log, skip_gain, out_weight,
):
    _, tile_rows, grid_cols, model = tokens.shape
    inner_width = out_weight.shape[0]
    states = decay_log.shape[1]
    rank = step_weight.shape[0]
    devices = lax.axis_size("seq")
    groups = lax.axis_size("dp")
    place = lax.axis_index("seq").reshape(1)
    group = lax.axis_index("dp").reshape(1)
    pair = groups == 4
    pos = tile_rows * grid_cols
    part = inner_width // devices
    length = 2 * part + PROJ
    up_pairs = [(i, (i + 1) % devices) for i in range(devices)]
    down_pairs = [(j, i) for i, j in up_pairs]

    tok, cot = (tokens.reshape(pos, model), cotangent.reshape(pos, model))
    wide = tok.astype(f32)
    above = lax.ppermute(wide, "seq", up_pairs)
    below = lax.ppermute(wide, "seq", down_pairs)
    out_t = out_weight.T
    channels = struct(inner_width, pos)
    narrow = struct(model, pos, dtype=bf16)
    conv_own, gate, gated_grad, mix, low, cot_in, conv_rows, select_rows, table = vmem_call(
        own_kernel,
        [channels] * 4
        + [narrow] * 2
        + [struct(inner_width, model, dtype=bf16), struct(inner_width, PROJ, dtype=bf16), struct(inner_width, TABLE)],
        [],
        [],
        [
            tok, cot, in_weight, out_t, select_weight.T, conv_kernel, conv_bias, step_weight, step_bias,
            decay_log.T, skip_gain, norm_gain, norm_bias,
        ],
        [pltpu.VMEM((TABLE, inner_width), f32)],
    )
    sent, conv_halo, pre_act, low_halo = vmem_call(
        entry_kernel,
        [struct(devices, length, pos), channels, channels, narrow],
        [heights, place],
        [above, below, conv_own, mix, conv_rows, select_rows, table],
    )
    got = lax.all_to_all(sent, "seq", 0, 0, tiled=True)
    sent, small = scan_call(heights, place, got, table, states)
    got = lax.all_to_all(sent, "seq", 0, 0, tiled=True)
    blocks = inner_width // 128
    whole = -(-blocks * (3 * model + SMALL) // 2048) * 2048
    half = whole // 2
    layer_out, act_grad, up, down, gate_grad, keep, give = vmem_call(
        functools.partial(mix_kernel, pair=pair),
        [struct(pos, model, dtype=bf16), channels]
        + [struct(inner_width // 2, pos)] * 2
        + [struct(inner_width, pos, dtype=bf16)]
        + [struct(half, 128)] * 2,
        [heights, place, group],
        [
            got, small, low, low_halo, cot_in, conv_own, conv_halo, pre_act, gate, gated_grad, select_rows, table,
        ],
        [tok, in_weight, out_t, conv_kernel, norm_gain, norm_bias],
        [pltpu.VMEM((whole, 128), f32)],
    )
    from_above = lax.ppermute(down, "seq", up_pairs)
    from_below = lax.ppermute(up, "seq", down_pairs)
    swap = [(i, i ^ 1) for i in range(groups)]
    taken = lax.ppermute(give, "dp", swap)
    count = half // (groups // 2)
    if pair:
        across = [(i, i ^ 2) for i in range(groups)]
        other = lax.ppermute(keep[count:] + taken[count:], "dp", across)
        piece = keep[:count] + taken[:count]
    else:
        same_core = [list(range(c, groups, 2)) for c in range(2)]
        pieces = (keep + taken).reshape(groups // 2, count, 128)
        pieces = lax.all_to_all(pieces, "dp", 0, 0, tiled=True, axis_index_groups=same_core)
        piece, other = (pieces[0], jnp.sum(pieces[1:], axis=0))
    other, from_above, from_below = lax.optimization_barrier((other, from_above, from_below))
    shares = (piece + other).reshape(devices, count // devices, 128)
    shares = lax.all_to_all(shares, "seq", 0, 0, tiled=True)
    share = jnp.broadcast_to(jnp.sum(shares, axis=0), shares.shape)
    mine = lax.all_to_all(share, "seq", 0, 0, tiled=True).reshape(count, 128)
    mine, from_above, from_below = lax.optimization_barrier((mine, from_above, from_below))
    (tokens_grad,) = vmem_call(
        exit_kernel,
        [struct(pos, model, dtype=bf16)],
        [heights, place],
        [act_grad, from_above, from_below, gate_grad, table],
        [tok, cot, in_weight],
    )
    if pair:
        from_y = lax.ppermute(mine, "dp", across)
        from_y, tokens_grad = lax.optimization_barrier((from_y, tokens_grad))
        pieces = [mine, from_y, lax.ppermute(mine, "dp", swap), lax.ppermute(from_y, "dp", swap)]
    else:
        pieces = list(lax.all_gather(mine, "dp"))
    gain, shift, inproj, kernel, offset, select, stepproj, stepbias, decay, skip, outproj = vmem_call(
        functools.partial(deal_kernel, members=len(pieces), pair=pair),
        [
            struct(model), struct(model), struct(model, 2 * inner_width), struct(3, 3, inner_width),
            struct(inner_width), struct(rank + 2 * states, inner_width), struct(rank, inner_width),
            struct(inner_width), struct(states, inner_width), struct(inner_width), struct(model, inner_width),
        ],
        [group],
        pieces,
        (),
        [pltpu.VMEM((whole, 128), f32)],
    )
    shape = tokens.shape
    return (
        layer_out.reshape(shape), tokens_grad.reshape(shape), gain, shift, inproj, kernel, offset, select.T,
        stepproj, stepbias, decay.T, skip, outproj.T,
    )


def solution(mesh):
    tile, whole = (P("dp", "seq", None, None), P())
    return jax.shard_map(
        on_device,
        mesh=mesh,
        in_specs=(tile, P("dp", None), tile) + (whole,) * 11,
        out_specs=(tile, tile) + (whole,) * 11,
        check_vma=False,
    )
```

```python
import functools

import jax
import jax.numpy as jnp
from jax import lax
from jax.experimental import pallas as pl
from jax.experimental.pallas import tpu as pltpu
from jax.sharding import PartitionSpec as P

epsilon = 1e-05
f32, bf16 = (jnp.float32, jnp.bfloat16)
ONE, IN, OUT, PROJ = (12, 16, 32, 48)
BIAS, SKIP, GAIN, SHIFT, STEP, DECAY, TABLE = (9, 10, 11, 12, 16, 32, 48)
STEP_AT, DECAY_AT, TAPS_AT, OFFSET_AT, SKIP_AT, NORM_AT, SMALL = (48, 64, 80, 89, 90, 95, 96)


def dot(a, b, over):
    return lax.dot_general(a, b, (((over[0],), (over[1],)), ((), ())), preferred_element_type=f32)


def split(value):
    high = value.astype(bf16)
    return (high, (value - high.astype(f32)).astype(bf16))


def fine_dot(a, b, over):
    (a_high, a_low), (b_high, b_low) = (split(a), split(b))
    return dot(a_high, b_high, over) + (dot(a_low, b_high, over) + dot(a_high, b_low, over))


def iota(shape, dim):
    return lax.broadcasted_iota(jnp.int32, shape, dim)


def sigmoid(v):
    return 1.0 / (1.0 + jnp.exp(-v))


def links_up(heights, row):
    end = jnp.int32(0)
    same = row > 0
    for k in range(heights.shape[1]):
        end = end + heights[0, k]
        same = same & (end != row)
    return jnp.where(same, 1.0, 0.0).astype(f32)


def row_masks(heights, place):
    lane = iota((1, 128), 1)
    flags = [links_up(heights, 2 * place + k) for k in range(3)]
    return (jnp.where(lane < 64, flags[0], flags[1]), jnp.where(lane < 64, flags[1], flags[2]))


def rows_around(own, halo):
    lane = iota((1, 128), 1)
    upper = pltpu.roll(jnp.where(lane < 64, own, halo), 64, 1)
    lower = pltpu.roll(jnp.where(lane < 64, halo, own), 64, 1)
    return (upper, lower)


def from_left(tile):
    place = iota((1, 128), 1) & 63
    wrapped = jnp.where(place == 0, 0.0, pltpu.roll(tile, 73, 1))
    return jnp.where(place < 8, wrapped, pltpu.roll(tile, 8, 1))


def from_right(tile):
    place = iota((1, 128), 1) & 63
    wrapped = jnp.where(place == 63, 0.0, pltpu.roll(tile, 55, 1))
    return jnp.where(place >= 56, wrapped, pltpu.roll(tile, 120, 1))


def conv_tile(upper, own, lower, taps):
    left, middle, right = [
        taps[0][b] * upper + taps[1][b] * own + taps[2][b] * lower for b in range(3)
    ]
    return middle + (from_left(left) + from_right(right))


def normalized(x):
    centred = x - jnp.mean(x, axis=0, keepdims=True)
    inverse = lax.rsqrt(jnp.mean(centred * centred, axis=0, keepdims=True) + epsilon)
    return (centred * inverse, inverse)


def eye(size):
    return (iota((size, size), 0) == iota((size, size), 1)).astype(bf16)


def flipped(value):
    pieces = [value[:, k : k + 128] for k in range(0, value.shape[1], 128)]
    return jnp.concatenate([dot(eye(piece.shape[1]), piece, (1, 1)) for piece in pieces], axis=0)


def flipped_fine(value):
    high, low = split(value)
    rest = (value - high.astype(f32) - low.astype(f32)).astype(bf16)
    return flipped(high) + (flipped(low) + flipped(rest))


def patch_sums(value):
    high, low = split(value)
    ones = jnp.ones((8, value.shape[1]), bf16)
    return (dot(ones, high, (1, 1)) + dot(ones, low, (1, 1)))[0:1]


def put_blocks(ref, start, value):
    for k in range(value.shape[1] // 128):
        ref[start + k * value.shape[0] : start + (k + 1) * value.shape[0]] = value[:, k * 128 : (k + 1) * 128]


def column_order(pos):
    new, old = (iota((pos, pos), 0), iota((pos, pos), 1))
    source = (new & ~63) | ((new & 7) << 3) | ((new >> 3) & 7)
    return (source == old).astype(bf16)


def lane_maps(part, states, width):
    lane = iota((1, width), 1)
    channel = jnp.floor((lane.astype(f32) + 0.5) * (1.0 / states)).astype(jnp.int32)
    return (channel, lane - channel * states, channel < part)


def entered(rows):
    return dot(flipped(rows).astype(bf16), column_order(rows.shape[0]), (1, 0))


def own_kernel(
    tok, cot, in_w, out_t, select_t, conv_kernel, conv_bias, step_weight, step_bias, decay_t, skip_gain,
    norm_gain, norm_bias,
    conv_out, gate_out, grad_out, mix_out, low_out, cot_out, conv_rows, select_rows, table,
    table_t,
):
    model, inner_width = out_t.shape
    states = decay_t.shape[0]
    rank = step_weight.shape[0]
    in_rows = flipped(in_w[...]).astype(bf16)
    conv_rows[...] = in_rows[:inner_width]
    out_rows = flipped(out_t[...]).astype(bf16)
    chosen = iota((PROJ, select_t.shape[0]), 0)
    chosen = jnp.where(chosen < rank, chosen, jnp.where(chosen < IN, -1, chosen - IN + rank))
    chosen = (chosen == iota((PROJ, select_t.shape[0]), 1)).astype(bf16)
    select_rows[...] = flipped(dot(chosen, select_t[...], (1, 0)).astype(bf16)).astype(bf16)
    table_t[...] = jnp.zeros_like(table_t)
    for k in range(3):
        table_t[3 * k : 3 * k + 3] = conv_kernel[k]
    table_t[BIAS : BIAS + 1] = conv_bias[...].reshape(1, inner_width)
    table_t[SKIP : SKIP + 1] = skip_gain[...].reshape(1, inner_width)
    table_t[GAIN : GAIN + 1, :model] = norm_gain[...].reshape(1, model)
    table_t[SHIFT : SHIFT + 1, :model] = norm_bias[...].reshape(1, model)
    table_t[STEP : STEP + rank] = step_weight[...]
    table_t[STEP + ONE : STEP + ONE + 1] = step_bias[...].reshape(1, inner_width)
    table_t[DECAY : DECAY + states] = decay_t[...]
    columns = flipped_fine(table_t[...])
    table[...] = columns
    gain, shift = (columns[:model, GAIN : GAIN + 1], columns[:model, SHIFT : SHIFT + 1])
    low = (normalized(entered(tok[...]))[0] * gain + shift).astype(bf16)
    cot_in = entered(cot[...]).astype(bf16)
    low_out[...] = low
    cot_out[...] = cot_in
    both = dot(in_rows, low, (1, 0))
    conv_out[...] = both[:inner_width]
    gate = both[inner_width:]
    gated_grad = dot(out_rows, cot_in, (1, 0))
    gate_out[...] = gate
    grad_out[...] = gated_grad
    mix_out[...] = gated_grad * (gate * sigmoid(gate))


def entry_kernel(
    heights, place, above, below, conv_own, mix, conv_rows, select_rows, table,
    send, halo_out, pre_out, low_halo_out,
):
    devices = send.shape[0]
    inner_width = conv_own.shape[0]
    model = conv_rows.shape[1]
    part = inner_width // devices
    columns = table[...]
    gain, shift = (columns[:model, GAIN : GAIN + 1], columns[:model, SHIFT : SHIFT + 1])
    halo = jnp.concatenate([below[...], above[...]], axis=0).astype(bf16)
    low_halo = (normalized(entered(halo))[0] * gain + shift).astype(bf16)
    low_halo_out[...] = low_halo
    around = dot(conv_rows[...], low_halo, (1, 0))
    halo_out[...] = around
    conv_in = conv_own[...]
    prev, following = row_masks(heights, place[0])
    upper, lower = rows_around(conv_in, around)
    taps = [[columns[:, 3 * a + b : 3 * a + b + 1] for b in range(3)] for a in range(3)]
    pre_act = columns[:, BIAS : BIAS + 1] + conv_tile(upper * prev, conv_in, lower * following, taps)
    inner = (pre_act * sigmoid(pre_act)).astype(bf16)
    proj = dot(flipped(select_rows[...]).astype(bf16), inner, (1, 0))
    proj = jnp.where(iota(proj.shape, 0) == ONE, 1.0, proj)
    pre_out[...] = pre_act
    inner = inner.astype(f32)
    for k in range(devices):
        send[k, :part] = inner[k * part : (k + 1) * part]
        send[k, part : 2 * part] = mix[k * part : (k + 1) * part]
        send[k, 2 * part :] = proj


def scan_kernel(
    heights, place, got, table,
    send, small,
    a_ref, s_ref, g_ref, down_ref, up_ref, col_h, col_m, row_h, row_m,
    prod, end_lr, end_rl, back_lr, back_rl, in_lr, in_rl, tail_lr, tail_rl,
    lhs_d, lhs_u, lhs_m, lhs_p, step_keep, delta_keep, y_keep, steps_keep, sums_keep, coefs_keep, decay_acc, *, part, states, span, group,
):
    devices, _, pos = got.shape
    rows = 2 * devices
    width = a_ref.shape[1]
    own_rows = table[pl.ds(pl.multiple_of(place[0] * part, 4), part), :]
    channel, state, live = lane_maps(part, states, width)
    twice = iota((2 * part, 1), 0)
    twice = jnp.where(twice >= part, twice - part, twice)
    spread_e = ((twice == channel) & live).astype(bf16)
    coef = iota((2 * PROJ, 1), 0)
    coef = jnp.where(coef >= PROJ, coef - PROJ, coef)
    near = state[:, :128]
    spread_bc = jnp.concatenate([coef - IN == near, coef - OUT == near], axis=1).astype(bf16)
    by_state = ((iota((states, 1), 0) == state) & live).astype(bf16)
    rate = -jnp.exp(own_rows[:, DECAY : DECAY + states])
    one_channel = (iota((part, 1), 0) == channel) & live
    rate_high, rate_low = split(rate)
    rate_rest = split(rate - rate_high.astype(f32) - rate_low.astype(f32))[0]
    rate_row = sum(dot(piece, by_state, (1, 0)) for piece in (rate_high, rate_low, rate_rest))
    rate_row = jnp.sum(jnp.where(one_channel, rate_row, 0.0), axis=0, keepdims=True)
    rate_two = rate_row * 1.4426950408889634
    step_own = own_rows[:, STEP : STEP + 16]
    step_high, step_low = split(step_own)
    step_three = jnp.concatenate([step_high, step_high, step_low], axis=1)
    one = eye(pos)

    def turned(value):
        return dot(one, jnp.concatenate(split(value), axis=0), (1, 1)).astype(bf16)

    for tile in range(devices):
        lines = slice(tile * pos, (tile + 1) * pos)
        inner_own = got[tile, :part]
        proj = got[tile, 2 * part :]
        high, low = split(proj[:16])
        pre_step = dot(step_three, jnp.concatenate([high, low, high], axis=0), (1, 0))
        tail = jnp.exp(-jnp.abs(pre_step))
        tail = jnp.where(tail < 1e-3, tail * (1.0 - 0.5 * tail), jnp.log(1.0 + tail))
        delta = jnp.maximum(pre_step, 0.0) + tail
        step_keep[tile] = sigmoid(pre_step)
        delta_keep[tile] = delta
        lhs_d[lines, :] = turned(delta)
        lhs_u[lines, :] = turned(delta * inner_own)
        lhs_m[lines, :] = turned(got[tile, part : 2 * part])
        lhs_p[lines, :] = turned(proj)

    def prepare(tile, carry):
        lines = pl.ds(pl.multiple_of(tile * pos, pos), pos)
        of_delta, of_source, of_mix, of_proj = (
            lhs_d[lines, :], lhs_u[lines, :], lhs_m[lines, :], lhs_p[lines, :]
        )
        of_bc = dot(of_proj, spread_bc, (1, 0))
        for k in range(width // span):
            lanes = slice(k * span, (k + 1) * span)
            a_ref[lines, lanes] = jnp.exp2(dot(of_delta, spread_e[:, lanes], (1, 0)) * rate_two[:, lanes])
            source = dot(of_source, spread_e[:, lanes], (1, 0))
            mix = dot(of_mix, spread_e[:, lanes], (1, 0))
            for j in range(span // 128):
                tile_lanes = slice(k * span + j * 128, k * span + (j + 1) * 128)
                piece = slice(j * 128, (j + 1) * 128)
                s_ref[lines, tile_lanes] = source[:, piece] * of_bc[:, :128]
                g_ref[lines, tile_lanes] = mix[:, piece] * of_bc[:, 128:]
        return carry

    lax.fori_loop(0, devices, prepare, 0, unroll=8)
    col_h[...] = jnp.zeros_like(col_h)
    col_m[...] = jnp.zeros_like(col_m)

    def packed(row, piece):
        return pl.ds(row * 64 + piece, 8, stride=8)

    def ascend(row, carry):
        keep = links_up(heights, row)
        for k in range(width // group):
            lanes = slice(k * group, (k + 1) * group)
            whole = lr = rl = mlr = mrl = None
            for c in range(8):
                lines = pl.ds(pl.multiple_of(row * 64 + c * 8, 8), 8)
                spot = slice(c * 8, c * 8 + 8)
                a, s, g = (a_ref[lines, lanes], s_ref[lines, lanes], g_ref[lines, lanes])
                state_h = a * (col_h[spot, lanes] * keep) + s
                col_h[spot, lanes] = state_h
                down_ref[lines, lanes] = state_h
                lam = g + col_m[spot, lanes] * keep
                col_m[spot, lanes] = a * lam
                up_ref[lines, lanes] = lam
                if c == 0:
                    whole, lr, rl, mlr, mrl = (a, s, s, a * g, a * g)
                else:
                    lr = a * lr + s
                    rl = rl + whole * s
                    whole = whole * a
                    mlr = mlr + whole * g
                    mrl = a * (mrl + g)
            for j in range(group // 128):
                spot = packed(row, k * (group // 128) + j)
                piece = slice(j * 128, (j + 1) * 128)
                prod[spot, :] = whole[:, piece]
                end_lr[spot, :] = lr[:, piece]
                end_rl[spot, :] = rl[:, piece]
                back_lr[spot, :] = mlr[:, piece]
                back_rl[spot, :] = mrl[:, piece]
        return carry

    lax.fori_loop(0, rows, ascend, 0)

    def chain(state_in, row, order, ends, starts):
        for c in order:
            line = pl.ds(pl.multiple_of(row * 64 + c * 8, 8), 8)
            starts[line, :] = state_in
            state_in = prod[line, :] * state_in + ends[line, :]
        return state_in

    def carries(pair, held):
        ahead, behind, back_ahead, back_behind = held
        right, left = (range(8), range(7, -1, -1))
        low = 2 * pair
        high = rows - 2 - low
        ahead = chain(ahead * links_up(heights, low), low, right, end_lr, in_lr)
        back_behind = chain(back_behind, low, right, back_rl, tail_rl)
        back_behind = back_behind * links_up(heights, low + 1)
        ahead = chain(ahead * links_up(heights, low + 1), low + 1, left, end_rl, in_rl)
        back_behind = chain(back_behind, low + 1, left, back_lr, tail_lr)
        back_behind = back_behind * links_up(heights, low + 2)
        behind = chain(behind * links_up(heights, high + 2), high + 1, right, end_lr, in_lr)
        back_ahead = chain(back_ahead, high + 1, right, back_rl, tail_rl)
        back_ahead = back_ahead * links_up(heights, high + 1)
        behind = chain(behind * links_up(heights, high + 1), high, left, end_rl, in_rl)
        back_ahead = chain(back_ahead, high, left, back_lr, tail_lr)
        back_ahead = back_ahead * links_up(heights, high)
        return (ahead, behind, back_ahead, back_behind)

    nothing = jnp.zeros((8, 128), f32)
    lax.fori_loop(0, devices, carries, (nothing,) * 4)
    col_h[...] = jnp.zeros_like(col_h)
    col_m[...] = jnp.zeros_like(col_m)

    def descend(step, carry):
        row = rows - 1 - step
        keep = links_up(heights, row + 1)

        def edge(ref, k):
            pieces = [ref[packed(row, k * (group // 128) + j), :] for j in range(group // 128)]
            return pieces[0] if len(pieces) == 1 else jnp.concatenate(pieces, axis=1)

        for k in range(width // group):
            lanes = slice(k * group, (k + 1) * group)
            h_right, m_left = (edge(in_lr, k), edge(tail_rl, k))
            for c in range(8):
                lines = pl.ds(pl.multiple_of(row * 64 + c * 8, 8), 8)
                spot = slice(c * 8, c * 8 + 8)
                a, s, g = (a_ref[lines, lanes], s_ref[lines, lanes], g_ref[lines, lanes])
                h_right = a * h_right + s
                lam = g + m_left
                m_left = a * lam
                row_h[spot, lanes] = h_right
                row_m[spot, lanes] = lam
            h_left, m_right = (edge(in_rl, k), edge(tail_lr, k))
            for c in range(7, -1, -1):
                lines = pl.ds(pl.multiple_of(row * 64 + c * 8, 8), 8)
                spot = slice(c * 8, c * 8 + 8)
                a, s, g = (a_ref[lines, lanes], s_ref[lines, lanes], g_ref[lines, lanes])
                h_left = a * h_left + s
                lam_lr = g + m_right
                m_right = a * lam_lr
                h_down, lam_up = (down_ref[lines, lanes], up_ref[lines, lanes])
                h_up = a * (col_h[spot, lanes] * keep) + s
                col_h[spot, lanes] = h_up
                lam_down = g + col_m[spot, lanes] * keep
                col_m[spot, lanes] = a * lam_down
                h_right, lam_rl = (row_h[spot, lanes], row_m[spot, lanes])
                lam_sum = (lam_lr + lam_rl) + (lam_down + lam_up)
                down_ref[lines, lanes] = (h_right + h_left) + (h_down + h_up)
                up_ref[lines, lanes] = lam_sum
                g_ref[lines, lanes] = (
                    (lam_lr * h_right + lam_rl * h_left)
                    + (lam_down * h_down + lam_up * h_up)
                    - s * lam_sum
                )
        return carry

    lax.fori_loop(0, rows, descend, 0)
    decay_acc[...] = jnp.zeros_like(decay_acc)
    gather_e, gather_b, gather_c = (spread_e[:part], spread_bc[:PROJ, :128], spread_bc[:PROJ, 128:])

    def finish(tile, carry):
        lines = pl.ds(pl.multiple_of(tile * pos, pos), pos)
        delta = delta_keep[tile]
        of_source, of_mix, of_proj = (lhs_u[lines, :], lhs_m[lines, :], lhs_p[lines, :])
        delta_low = delta.astype(bf16)
        of_bc = dot(of_proj, spread_bc, (1, 0))
        of_b, of_c = (of_bc[:, :128], of_bc[:, 128:])
        totals = grad_b = grad_c = None
        for k in range(width // span):
            lanes = slice(k * span, (k + 1) * span)
            scaled = (g_ref[lines, lanes] * rate_row[:, lanes]).astype(bf16)
            source = dot(of_source, spread_e[:, lanes], (1, 0))
            mix = dot(of_mix, spread_e[:, lanes], (1, 0))
            decay_acc[:, lanes] += dot(delta_low, scaled, (1, 0))
            of_y, of_sum = ([], [])
            for j in range(span // 128):
                tile_lanes = slice(k * span + j * 128, k * span + (j + 1) * 128)
                piece = slice(j * 128, (j + 1) * 128)
                h_sum, lam_sum = (down_ref[lines, tile_lanes], up_ref[lines, tile_lanes])
                of_y.append((h_sum * of_c).astype(bf16))
                of_sum.append((lam_sum * of_b).astype(bf16))
                term_b, term_c = (lam_sum * source[:, piece], h_sum * mix[:, piece])
                grad_b = term_b if grad_b is None else grad_b + term_b
                grad_c = term_c if grad_c is None else grad_c + term_c
            parts = (
                dot(gather_e[:, lanes], jnp.concatenate(of_y, axis=1), (1, 1)),
                dot(gather_e[:, lanes], scaled, (1, 1)),
                dot(gather_e[:, lanes], jnp.concatenate(of_sum, axis=1), (1, 1)),
            )
            totals = parts if totals is None else [x + z for x, z in zip(totals, parts)]
        y_keep[tile], steps_keep[tile], sums_keep[tile] = totals
        coefs_keep[tile] = dot(gather_b, grad_b.astype(bf16), (1, 1)) + dot(gather_c, grad_c.astype(bf16), (1, 1))
        return carry

    lax.fori_loop(0, devices, finish, 0, unroll=8)
    step_grad = jnp.zeros((part, 16), f32)
    for tile in range(devices):
        sums, coefs = (sums_keep[tile], coefs_keep[tile])
        pre_grad = (steps_keep[tile] + got[tile, :part] * sums) * step_keep[tile]
        send[tile, :part] = y_keep[tile]
        send[tile, part : 2 * part] = delta_keep[tile] * sums
        send[tile, 2 * part : 2 * part + 16] = coefs[:16] + fine_dot(step_own, pre_grad, (0, 0))
        send[tile, 2 * part + 16 :] = coefs[16:]
        step_grad = step_grad + fine_dot(pre_grad, got[tile, 2 * part : 2 * part + 16], (1, 1))
    decay_grad = jnp.where(one_channel, decay_acc[...], 0.0)
    decay_high, decay_low = split(decay_grad)
    decay_grad = dot(decay_high, by_state, (1, 1)) + dot(decay_low, by_state, (1, 1))
    spot = (iota((part, small.shape[1]), 1) == iota((part, small.shape[1]), 0) + place[0] * part).astype(bf16)
    for at, value in ((0, step_grad), (16, decay_grad)):
        high, low = split(value)
        small[at : at + 16] = dot(high, spot, (0, 0)) + dot(low, spot, (0, 0))


def mix_kernel(
    heights, place, group, got, small_in, low, low_halo, cot, conv_own, conv_halo, pre, gate_in, grad_in,
    select_rows, table, tok, in_w, out_t, conv_kernel, norm_gain, norm_bias,
    layer_out, act_out, up, down, gate_grad_out, keep, give,
    grads, *, pair,
):
    devices, length, pos = got.shape
    model, inner_width = out_t.shape
    part = inner_width // devices
    lane = iota((1, pos), 1)
    y = jnp.concatenate([got[k, :part] for k in range(devices)], axis=0)
    inner_grad = jnp.concatenate([got[k, part : 2 * part] for k in range(devices)], axis=0)
    proj_grad = got[0, 2 * part :]
    for k in range(1, devices):
        proj_grad = proj_grad + got[k, 2 * part :]
    proj_grad = proj_grad.astype(bf16)
    pre_act, gate, gated_grad = (pre[...], gate_in[...], grad_in[...])
    skip = table[:, SKIP : SKIP + 1]
    sig_pre, sig_gate = (sigmoid(pre_act), sigmoid(gate))
    inner = (pre_act * sig_pre).astype(bf16)
    inner_f = inner.astype(f32)
    silu_gate = gate * sig_gate
    mix_grad = gated_grad * silu_gate
    inner_grad = inner_grad + mix_grad * skip + dot(select_rows[...], proj_grad, (1, 0))
    act_grad = inner_grad * (sig_pre * (1.0 + pre_act * (1.0 - sig_pre)))
    act_out[...] = act_grad
    half = inner_width // 2
    top, bottom = (act_grad[:half], act_grad[half:])
    up[...] = jnp.where(lane < 64, top, pltpu.roll(bottom, 64, 1))
    down[...] = jnp.where(lane < 64, pltpu.roll(top, 64, 1), bottom)

    y_all = y + skip * inner_f
    gated = (y_all * silu_gate).astype(bf16)
    gate_grad = (gated_grad * y_all * (sig_gate * (1.0 + gate * (1.0 - sig_gate)))).astype(bf16)
    gate_grad_out[...] = gate_grad
    natural = dot(gated, column_order(pos), (1, 0)).astype(bf16)
    layer = jnp.transpose(dot(out_t[...], natural, (1, 0)))
    layer_out[...] = (tok[...].astype(f32) + layer).astype(bf16)

    prev, following = row_masks(heights, place[0])
    low_in = low[...]
    upper, lower = rows_around(low_in.astype(f32), low_halo[...].astype(f32))
    which = iota((16, 1), 0)
    masks = jnp.where(which == 0, prev, jnp.where(which == 1, 1.0, following))
    left_hand = jnp.concatenate(
        [(upper * prev).astype(bf16), low_in, (lower * following).astype(bf16), masks.astype(bf16)], axis=0
    )
    field = conv_own[...]
    edge_upper, edge_lower = rows_around(field, conv_halo[...])
    fields = (edge_upper * prev, field, edge_lower * following)
    in_conv = conv_total = None
    tap_sums = [None] * 9
    for b, moved in enumerate((from_right(act_grad), act_grad, from_left(act_grad))):
        part_b = dot(left_hand, moved.astype(bf16), (1, 1))
        for a in range(3):
            tap = conv_kernel[a, b : b + 1, :]
            term = tap * part_b[a * model : (a + 1) * model]
            total = tap * part_b[3 * model + a : 3 * model + a + 1]
            in_conv = term if in_conv is None else in_conv + term
            conv_total = total if conv_total is None else conv_total + total
            tap_sums[3 * a + b] = patch_sums(moved * fields[a])
    in_gate = dot(low_in, gate_grad, (1, 1))
    put_blocks(grads, 0, in_conv)
    blocks = inner_width // 128
    put_blocks(grads, blocks * model, in_gate)
    put_blocks(grads, 2 * blocks * model, dot(cot[...], gated, (1, 1)))
    sums = jnp.broadcast_to(jnp.concatenate([conv_total, patch_sums(gate_grad.astype(f32))], axis=1), (8, 2 * inner_width))
    sums_high, sums_low = split(sums)
    shift_row = (dot(sums_high, in_w[...], (1, 1)) + dot(sums_low, in_w[...], (1, 1)))[0:1]
    weights = in_w[...].astype(f32)
    gain_row = patch_sums(weights[:, :inner_width] * in_conv + weights[:, inner_width:] * in_gate)
    gain_row = (gain_row - norm_bias[...].reshape(1, model) * shift_row) / norm_gain[...].reshape(1, model)
    smalls = jnp.concatenate(
        [dot(proj_grad, inner, (1, 1)), small_in[...]]
        + tap_sums
        + [patch_sums(act_grad), patch_sums(mix_grad * inner_f), jnp.zeros((4, inner_width), f32)]
        + [jnp.concatenate([gain_row, shift_row], axis=1)],
        axis=0,
    )
    start = 3 * blocks * model
    put_blocks(grads, start, smalls)
    start = start + blocks * SMALL
    grads[start:] = jnp.zeros((grads.shape[0] - start, 128), f32)
    own = group[0] % 2
    if pair:
        count = keep.shape[0] // 2
        height = group[0] // 2
        for ref, side in ((keep, own), (give, 1 - own)):
            for k, at in enumerate((height, 1 - height)):
                ref[k * count : (k + 1) * count] = grads[pl.ds(pl.multiple_of((2 * side + at) * count, count), count)]
    else:
        count = keep.shape[0]
        keep[...] = grads[pl.ds(pl.multiple_of(own * count, count), count)]
        give[...] = grads[pl.ds(pl.multiple_of((1 - own) * count, count), count)]


def exit_kernel(
    heights, place, act, from_above, from_below, gate_grad, table, tok, cot, in_w,
    tokens_grad,
):
    inner_width, pos = act.shape
    model = in_w.shape[0]
    lane = iota((1, pos), 1)
    above, below = (from_above[...], from_below[...])
    halo_top = jnp.where(lane < 64, below, pltpu.roll(above, 64, 1))
    halo_bottom = jnp.where(lane < 64, pltpu.roll(below, 64, 1), above)
    act_grad = act[...]
    prev, following = row_masks(heights, place[0])
    upper, lower = rows_around(act_grad, jnp.concatenate([halo_top, halo_bottom], axis=0))
    columns = table[...]
    taps = [[columns[:, 8 - 3 * a - b : 9 - 3 * a - b] for b in range(3)] for a in range(3)]
    conv_grad = conv_tile(upper * prev, act_grad, lower * following, taps).astype(bf16)
    halves = jnp.concatenate([conv_grad, gate_grad[...]], axis=0)
    halves = dot(halves, column_order(pos), (1, 0)).astype(bf16)
    normed_grad = dot(in_w[...], halves, (1, 0))
    xhat, inverse = normalized(flipped(tok[...]))
    scaled = normed_grad * columns[:model, GAIN : GAIN + 1]
    x_grad = (
        scaled
        - jnp.mean(scaled, axis=0, keepdims=True)
        - xhat * jnp.mean(scaled * xhat, axis=0, keepdims=True)
    ) * inverse
    x_grad = jnp.transpose(x_grad)
    tokens_grad[...] = (x_grad + cot[...].astype(f32)).astype(bf16)


def deal_kernel(group, *refs, members, pair):
    pieces, ordered = (refs[:members], refs[-1])
    (
        gain_grad, shift_grad, inproj, kernel_grad, offset, select, stepproj, stepbias, decay, skip, outproj,
    ) = refs[members:-1]
    model, inner_width = outproj.shape
    blocks = inner_width // 128
    rank = stepproj.shape[0]
    states = decay.shape[0]
    count = pieces[0].shape[0]
    for k, piece in enumerate(pieces):
        if pair:
            core, height = (group[0] % 2, group[0] // 2)
            core = 1 - core if k // 2 else core
            height = 1 - height if k % 2 else height
            slot = core * 2 + height
        else:
            slot = k % 2 * (members // 2) + k // 2
        ordered[pl.ds(pl.multiple_of(slot * count, count), count)] = piece[...]

    def rows(start, count):
        return ordered[start : start + count]

    for k in range(2 * blocks):
        inproj[:, k * 128 : (k + 1) * 128] = rows(k * model, model)
    start = 2 * blocks * model
    for k in range(blocks):
        outproj[:, k * 128 : (k + 1) * 128] = rows(start + k * model, model)
    start = start + blocks * model
    small = jnp.concatenate([rows(start + k * SMALL, SMALL) for k in range(blocks)], axis=1)
    select[:rank] = small[:rank]
    select[rank:] = small[IN:PROJ]
    stepproj[...] = small[STEP_AT : STEP_AT + rank]
    stepbias[...] = small[STEP_AT + ONE : STEP_AT + ONE + 1].reshape(stepbias.shape)
    decay[...] = small[DECAY_AT : DECAY_AT + states]
    for k in range(3):
        kernel_grad[k] = small[TAPS_AT + 3 * k : TAPS_AT + 3 * k + 3]
    offset[...] = small[OFFSET_AT : OFFSET_AT + 1].reshape(offset.shape)
    skip[...] = small[SKIP_AT : SKIP_AT + 1].reshape(skip.shape)
    norms = small[NORM_AT : NORM_AT + 1]
    gain_grad[...] = norms[:, :model].reshape(gain_grad.shape)
    shift_grad[...] = norms[:, model:].reshape(shift_grad.shape)


def vmem_call(kernel, out_shape, scalars, arrays, weights=(), scratch=(), limit=16):
    scalars = [pltpu.with_memory_space_constraint(x, pltpu.HBM) if x.ndim == 2 else x for x in scalars]
    arrays = [pltpu.with_memory_space_constraint(x, pltpu.VMEM) for x in arrays]
    arrays += [pltpu.with_memory_space_constraint(x, pltpu.HBM) for x in weights]
    return pl.pallas_call(
        kernel,
        out_shape=out_shape,
        in_specs=[pl.BlockSpec(memory_space=pltpu.SMEM)] * len(scalars)
        + [pl.BlockSpec(memory_space=pltpu.VMEM)] * len(arrays),
        out_specs=[pl.BlockSpec(memory_space=pltpu.VMEM)] * len(out_shape),
        scratch_shapes=list(scratch),
        compiler_params=pltpu.CompilerParams(vmem_limit_bytes=limit * 1024 * 1024),
    )(*scalars, *arrays)


def struct(*shape, dtype=f32):
    return jax.ShapeDtypeStruct(shape, dtype)


def inside(*shape, dtype=f32):
    return pltpu.VMEM(shape, dtype)


def scan_call(heights, place, got, table, states):
    devices, length, pos = got.shape
    inner_width = table.shape[0]
    part = inner_width // devices
    width = -(-part * states // 128) * 128
    total = devices * pos
    span = 256 if width % 256 == 0 else 128
    group = 768 if width % 768 == 0 else span
    big = pltpu.VMEM((total, width), f32)
    line = pltpu.VMEM((2 * devices * 64, 128), f32)
    column = pltpu.VMEM((pos // 2, width), f32)
    own = pltpu.VMEM((devices, part, pos), f32)
    return vmem_call(
        functools.partial(scan_kernel, part=part, states=states, span=span, group=group),
        [inside(devices, length, pos), inside(32, inner_width)],
        [heights, place],
        [got, table],
        (),
        [big] * 5
        + [column] * 4
        + [line] * 9
        + [pltpu.VMEM((total, 2 * part), bf16)] * 3
        + [pltpu.VMEM((total, 2 * PROJ), bf16)]
        + [own] * 5
        + [pltpu.VMEM((devices, PROJ, pos), f32), pltpu.VMEM((part, width), f32)],
        limit=32 if total <= 1024 else 52,
    )


def on_device(
    tokens, heights, cotangent, norm_gain, norm_bias, in_weight, conv_kernel, conv_bias, select_weight,
    step_weight, step_bias, decay_log, skip_gain, out_weight,
):
    _, tile_rows, grid_cols, model = tokens.shape
    inner_width = out_weight.shape[0]
    states = decay_log.shape[1]
    rank = step_weight.shape[0]
    devices = lax.axis_size("seq")
    groups = lax.axis_size("dp")
    place = lax.axis_index("seq").reshape(1)
    group = lax.axis_index("dp").reshape(1)
    pair = groups == 4
    pos = tile_rows * grid_cols
    part = inner_width // devices
    length = 2 * part + PROJ
    up_pairs = [(i, (i + 1) % devices) for i in range(devices)]
    down_pairs = [(j, i) for i, j in up_pairs]

    tok, cot = (tokens.reshape(pos, model), cotangent.reshape(pos, model))
    above = lax.ppermute(tok[grid_cols:].astype(f32), "seq", up_pairs)
    below = lax.ppermute(tok[:grid_cols].astype(f32), "seq", down_pairs)
    out_t = out_weight.T
    channels = inside(inner_width, pos)
    narrow = inside(model, pos, dtype=bf16)
    conv_own, gate, gated_grad, mix, low, cot_in, conv_rows, select_rows, table = vmem_call(
        own_kernel,
        [channels] * 4
        + [narrow] * 2
        + [inside(inner_width, model, dtype=bf16), inside(inner_width, PROJ, dtype=bf16), inside(inner_width, TABLE)],
        [],
        [],
        [
            tok, cot, in_weight, out_t, select_weight.T, conv_kernel, conv_bias, step_weight, step_bias,
            decay_log.T, skip_gain, norm_gain, norm_bias,
        ],
        [pltpu.VMEM((TABLE, inner_width), f32)],
    )
    sent, conv_halo, pre_act, low_halo = vmem_call(
        entry_kernel,
        [inside(devices, length, pos), channels, channels, narrow],
        [heights, place],
        [above, below, conv_own, mix, conv_rows, select_rows, table],
    )
    got = lax.all_to_all(sent, "seq", 0, 0, tiled=True)
    sent, small = scan_call(heights, place, got, table, states)
    got = lax.all_to_all(sent, "seq", 0, 0, tiled=True)
    blocks = inner_width // 128
    whole = -(-blocks * (3 * model + SMALL) // 2048) * 2048
    half = whole // 2
    layer_out, act_grad, up, down, gate_grad, keep, give = vmem_call(
        functools.partial(mix_kernel, pair=pair),
        [struct(pos, model, dtype=bf16), channels]
        + [inside(inner_width // 2, pos)] * 2
        + [inside(inner_width, pos, dtype=bf16)]
        + [inside(half, 128)] * 2,
        [heights, place, group],
        [
            got, small, low, low_halo, cot_in, conv_own, conv_halo, pre_act, gate, gated_grad, select_rows, table,
        ],
        [tok, in_weight, out_t, conv_kernel, norm_gain, norm_bias],
        [pltpu.VMEM((whole, 128), f32)],
    )
    from_above = lax.ppermute(down, "seq", up_pairs)
    from_below = lax.ppermute(up, "seq", down_pairs)
    swap = [(i, i ^ 1) for i in range(groups)]
    taken = lax.ppermute(give, "dp", swap)
    count = half // (groups // 2)
    if pair:
        across = [(i, i ^ 2) for i in range(groups)]
        other = lax.ppermute(keep[count:] + taken[count:], "dp", across)
        piece = keep[:count] + taken[:count]
    else:
        same_core = [list(range(c, groups, 2)) for c in range(2)]
        pieces = (keep + taken).reshape(groups // 2, count, 128)
        pieces = lax.all_to_all(pieces, "dp", 0, 0, tiled=True, axis_index_groups=same_core)
        piece, other = (pieces[0], jnp.sum(pieces[1:], axis=0))
    other, from_above, from_below = lax.optimization_barrier((other, from_above, from_below))
    shares = (piece + other).reshape(devices, count // devices, 128)
    shares = lax.all_to_all(shares, "seq", 0, 0, tiled=True)
    share = jnp.broadcast_to(jnp.sum(shares, axis=0), shares.shape)
    mine = lax.all_to_all(share, "seq", 0, 0, tiled=True).reshape(count, 128)
    mine, from_above, from_below = lax.optimization_barrier((mine, from_above, from_below))
    (tokens_grad,) = vmem_call(
        exit_kernel,
        [struct(pos, model, dtype=bf16)],
        [heights, place],
        [act_grad, from_above, from_below, gate_grad, table],
        [tok, cot, in_weight],
    )
    if pair:
        from_y = lax.ppermute(mine, "dp", across)
        from_y, tokens_grad = lax.optimization_barrier((from_y, tokens_grad))
        pieces = [mine, from_y, lax.ppermute(mine, "dp", swap), lax.ppermute(from_y, "dp", swap)]
    else:
        pieces = list(lax.all_gather(mine, "dp"))
    gain, shift, inproj, kernel, offset, select, stepproj, stepbias, decay, skip, outproj = vmem_call(
        functools.partial(deal_kernel, members=len(pieces), pair=pair),
        [
            struct(model), struct(model), struct(model, 2 * inner_width), struct(3, 3, inner_width),
            struct(inner_width), struct(rank + 2 * states, inner_width), struct(rank, inner_width),
            struct(inner_width), struct(states, inner_width), struct(inner_width), struct(model, inner_width),
        ],
        [group],
        pieces,
        (),
        [pltpu.VMEM((whole, 128), f32)],
    )
    shape = tokens.shape
    return (
        layer_out.reshape(shape), tokens_grad.reshape(shape), gain, shift, inproj, kernel, offset, select.T,
        stepproj, stepbias, decay.T, skip, outproj.T,
    )


def solution(mesh):
    tile, whole = (P("dp", "seq", None, None), P())
    return jax.shard_map(
        on_device,
        mesh=mesh,
        in_specs=(tile, P("dp", None), tile) + (whole,) * 11,
        out_specs=(tile, tile) + (whole,) * 11,
        check_vma=False,
    )
```

```python
import functools

import jax
import jax.numpy as jnp
from jax import lax
from jax.experimental import pallas as pl
from jax.experimental.pallas import tpu as pltpu
from jax.sharding import PartitionSpec as P

epsilon = 1e-05
f32, bf16 = (jnp.float32, jnp.bfloat16)
ONE, IN, OUT, PROJ = (12, 16, 32, 48)
BIAS, SKIP, GAIN, SHIFT, STEP, DECAY, TABLE = (9, 10, 11, 12, 16, 32, 48)
STEP_AT, DECAY_AT, TAPS_AT, OFFSET_AT, SKIP_AT, NORM_AT, SMALL = (48, 64, 80, 89, 90, 95, 96)


def dot(a, b, over):
    return lax.dot_general(a, b, (((over[0],), (over[1],)), ((), ())), preferred_element_type=f32)


def split(value):
    high = value.astype(bf16)
    return (high, (value - high.astype(f32)).astype(bf16))


def fine_dot(a, b, over):
    (a_high, a_low), (b_high, b_low) = (split(a), split(b))
    return dot(a_high, b_high, over) + (dot(a_low, b_high, over) + dot(a_high, b_low, over))


def iota(shape, dim):
    return lax.broadcasted_iota(jnp.int32, shape, dim)


def sigmoid(v):
    return 1.0 / (1.0 + jnp.exp(-v))


def links_up(heights, row):
    end = jnp.int32(0)
    same = row > 0
    for k in range(heights.shape[1]):
        end = end + heights[0, k]
        same = same & (end != row)
    return jnp.where(same, 1.0, 0.0).astype(f32)


def row_masks(heights, place):
    lane = iota((1, 128), 1)
    flags = [links_up(heights, 2 * place + k) for k in range(3)]
    return (jnp.where(lane < 64, flags[0], flags[1]), jnp.where(lane < 64, flags[1], flags[2]))


def rows_around(own, halo):
    lane = iota((1, 128), 1)
    upper = pltpu.roll(jnp.where(lane < 64, own, halo), 64, 1)
    lower = pltpu.roll(jnp.where(lane < 64, halo, own), 64, 1)
    return (upper, lower)


def from_left(tile):
    place = iota((1, 128), 1) & 63
    wrapped = jnp.where(place == 0, 0.0, pltpu.roll(tile, 73, 1))
    return jnp.where(place < 8, wrapped, pltpu.roll(tile, 8, 1))


def from_right(tile):
    place = iota((1, 128), 1) & 63
    wrapped = jnp.where(place == 63, 0.0, pltpu.roll(tile, 55, 1))
    return jnp.where(place >= 56, wrapped, pltpu.roll(tile, 120, 1))


def conv_tile(upper, own, lower, taps):
    left, middle, right = [
        taps[0][b] * upper + taps[1][b] * own + taps[2][b] * lower for b in range(3)
    ]
    return middle + (from_left(left) + from_right(right))


def normalized(x):
    centred = x - jnp.mean(x, axis=0, keepdims=True)
    inverse = lax.rsqrt(jnp.mean(centred * centred, axis=0, keepdims=True) + epsilon)
    return (centred * inverse, inverse)


def eye(size):
    return (iota((size, size), 0) == iota((size, size), 1)).astype(bf16)


def flipped(value):
    pieces = [value[:, k : k + 128] for k in range(0, value.shape[1], 128)]
    return jnp.concatenate([dot(eye(piece.shape[1]), piece, (1, 1)) for piece in pieces], axis=0)


def flipped_fine(value):
    high, low = split(value)
    rest = (value - high.astype(f32) - low.astype(f32)).astype(bf16)
    return flipped(high) + (flipped(low) + flipped(rest))


def patch_sums(value):
    high, low = split(value)
    ones = jnp.ones((8, value.shape[1]), bf16)
    return (dot(ones, high, (1, 1)) + dot(ones, low, (1, 1)))[0:1]


def put_blocks(ref, start, value):
    for k in range(value.shape[1] // 128):
        ref[start + k * value.shape[0] : start + (k + 1) * value.shape[0]] = value[:, k * 128 : (k + 1) * 128]


def column_order(pos):
    new, old = (iota((pos, pos), 0), iota((pos, pos), 1))
    source = (new & ~63) | ((new & 7) << 3) | ((new >> 3) & 7)
    return (source == old).astype(bf16)


def lane_maps(part, states, width):
    lane = iota((1, width), 1)
    channel = jnp.floor((lane.astype(f32) + 0.5) * (1.0 / states)).astype(jnp.int32)
    return (channel, lane - channel * states, channel < part)


def entered(rows):
    return dot(flipped(rows).astype(bf16), column_order(rows.shape[0]), (1, 0))


def own_kernel(
    tok, cot, in_w, out_t, select_t, conv_kernel, conv_bias, step_weight, step_bias, decay_t, skip_gain,
    norm_gain, norm_bias,
    conv_out, gate_out, grad_out, mix_out, low_out, cot_out, conv_rows, select_rows, table,
    table_t,
):
    model, inner_width = out_t.shape
    states = decay_t.shape[0]
    rank = step_weight.shape[0]
    in_rows = flipped(in_w[...]).astype(bf16)
    conv_rows[...] = in_rows[:inner_width]
    out_rows = flipped(out_t[...]).astype(bf16)
    chosen = iota((PROJ, select_t.shape[0]), 0)
    chosen = jnp.where(chosen < rank, chosen, jnp.where(chosen < IN, -1, chosen - IN + rank))
    chosen = (chosen == iota((PROJ, select_t.shape[0]), 1)).astype(bf16)
    select_rows[...] = flipped(dot(chosen, select_t[...], (1, 0)).astype(bf16)).astype(bf16)
    table_t[...] = jnp.zeros_like(table_t)
    for k in range(3):
        table_t[3 * k : 3 * k + 3] = conv_kernel[k]
    table_t[BIAS : BIAS + 1] = conv_bias[...].reshape(1, inner_width)
    table_t[SKIP : SKIP + 1] = skip_gain[...].reshape(1, inner_width)
    table_t[GAIN : GAIN + 1, :model] = norm_gain[...].reshape(1, model)
    table_t[SHIFT : SHIFT + 1, :model] = norm_bias[...].reshape(1, model)
    table_t[STEP : STEP + rank] = step_weight[...]
    table_t[STEP + ONE : STEP + ONE + 1] = step_bias[...].reshape(1, inner_width)
    table_t[DECAY : DECAY + states] = decay_t[...]
    columns = flipped_fine(table_t[...])
    table[...] = columns
    gain, shift = (columns[:model, GAIN : GAIN + 1], columns[:model, SHIFT : SHIFT + 1])
    low = (normalized(entered(tok[...]))[0] * gain + shift).astype(bf16)
    cot_in = entered(cot[...]).astype(bf16)
    low_out[...] = low
    cot_out[...] = cot_in
    both = dot(in_rows, low, (1, 0))
    conv_out[...] = both[:inner_width]
    gate = both[inner_width:]
    gated_grad = dot(out_rows, cot_in, (1, 0))
    gate_out[...] = gate
    grad_out[...] = gated_grad
    mix_out[...] = gated_grad * (gate * sigmoid(gate))


def entry_kernel(
    heights, place, above, below, conv_own, mix, conv_rows, select_rows, table,
    send, halo_out, pre_out, low_halo_out,
):
    devices = send.shape[0]
    inner_width = conv_own.shape[0]
    model = conv_rows.shape[1]
    part = inner_width // devices
    columns = table[...]
    gain, shift = (columns[:model, GAIN : GAIN + 1], columns[:model, SHIFT : SHIFT + 1])
    even = place[0] % 2 == 0
    halo = jnp.concatenate(
        [jnp.where(even, below[...], above[...]), jnp.where(even, above[...], below[...])], axis=0
    ).astype(bf16)
    low_halo = (normalized(entered(halo))[0] * gain + shift).astype(bf16)
    low_halo_out[...] = low_halo
    around = dot(conv_rows[...], low_halo, (1, 0))
    halo_out[...] = around
    conv_in = conv_own[...]
    prev, following = row_masks(heights, place[0])
    upper, lower = rows_around(conv_in, around)
    taps = [[columns[:, 3 * a + b : 3 * a + b + 1] for b in range(3)] for a in range(3)]
    pre_act = columns[:, BIAS : BIAS + 1] + conv_tile(upper * prev, conv_in, lower * following, taps)
    inner = (pre_act * sigmoid(pre_act)).astype(bf16)
    proj = dot(flipped(select_rows[...]).astype(bf16), inner, (1, 0))
    proj = jnp.where(iota(proj.shape, 0) == ONE, 1.0, proj)
    pre_out[...] = pre_act
    inner = inner.astype(f32)
    for k in range(devices):
        send[k, :part] = inner[k * part : (k + 1) * part]
        send[k, part : 2 * part] = mix[k * part : (k + 1) * part]
        send[k, 2 * part :] = proj


def scan_kernel(
    heights, place, got, table,
    send, small,
    a_ref, s_ref, g_ref, down_ref, up_ref, col_h, col_m, row_h, row_m,
    prod, end_lr, end_rl, back_lr, back_rl, in_lr, in_rl, tail_lr, tail_rl,
    lhs_d, lhs_u, lhs_m, lhs_p, step_keep, delta_keep, y_keep, steps_keep, sums_keep, coefs_keep, decay_acc, *, part, states, span, group,
):
    devices, _, pos = got.shape
    rows = 2 * devices
    width = a_ref.shape[1]
    own_rows = table[pl.ds(pl.multiple_of(place[0] * part, 4), part), :]
    channel, state, live = lane_maps(part, states, width)
    twice = iota((2 * part, 1), 0)
    twice = jnp.where(twice >= part, twice - part, twice)
    spread_e = ((twice == channel) & live).astype(bf16)
    coef = iota((2 * PROJ, 1), 0)
    coef = jnp.where(coef >= PROJ, coef - PROJ, coef)
    near = state[:, :128]
    spread_bc = jnp.concatenate([coef - IN == near, coef - OUT == near], axis=1).astype(bf16)
    by_state = ((iota((states, 1), 0) == state) & live).astype(bf16)
    rate = -jnp.exp(own_rows[:, DECAY : DECAY + states])
    one_channel = (iota((part, 1), 0) == channel) & live
    rate_high, rate_low = split(rate)
    rate_rest = split(rate - rate_high.astype(f32) - rate_low.astype(f32))[0]
    rate_row = sum(dot(piece, by_state, (1, 0)) for piece in (rate_high, rate_low, rate_rest))
    rate_row = jnp.sum(jnp.where(one_channel, rate_row, 0.0), axis=0, keepdims=True)
    rate_two = rate_row * 1.4426950408889634
    step_own = own_rows[:, STEP : STEP + 16]
    step_high, step_low = split(step_own)
    step_three = jnp.concatenate([step_high, step_high, step_low], axis=1)
    one = eye(pos)

    def turned(value):
        return dot(one, jnp.concatenate(split(value), axis=0), (1, 1)).astype(bf16)

    for tile in range(devices):
        lines = slice(tile * pos, (tile + 1) * pos)
        inner_own = got[tile, :part]
        proj = got[tile, 2 * part :]
        high, low = split(proj[:16])
        pre_step = dot(step_three, jnp.concatenate([high, low, high], axis=0), (1, 0))
        tail = jnp.exp(-jnp.abs(pre_step))
        tail = jnp.where(tail < 1e-3, tail * (1.0 - 0.5 * tail), jnp.log(1.0 + tail))
        delta = jnp.maximum(pre_step, 0.0) + tail
        step_keep[tile] = sigmoid(pre_step)
        delta_keep[tile] = delta
        lhs_d[lines, :] = turned(delta)
        lhs_u[lines, :] = turned(delta * inner_own)
        lhs_m[lines, :] = turned(got[tile, part : 2 * part])
        lhs_p[lines, :] = turned(proj)

    def prepare(tile, carry):
        lines = pl.ds(pl.multiple_of(tile * pos, pos), pos)
        of_delta, of_source, of_mix, of_proj = (
            lhs_d[lines, :], lhs_u[lines, :], lhs_m[lines, :], lhs_p[lines, :]
        )
        of_bc = dot(of_proj, spread_bc, (1, 0))
        for k in range(width // span):
            lanes = slice(k * span, (k + 1) * span)
            a_ref[lines, lanes] = jnp.exp2(dot(of_delta, spread_e[:, lanes], (1, 0)) * rate_two[:, lanes])
            source = dot(of_source, spread_e[:, lanes], (1, 0))
            mix = dot(of_mix, spread_e[:, lanes], (1, 0))
            for j in range(span // 128):
                tile_lanes = slice(k * span + j * 128, k * span + (j + 1) * 128)
                piece = slice(j * 128, (j + 1) * 128)
                s_ref[lines, tile_lanes] = source[:, piece] * of_bc[:, :128]
                g_ref[lines, tile_lanes] = mix[:, piece] * of_bc[:, 128:]
        return carry

    lax.fori_loop(0, devices, prepare, 0, unroll=8)
    col_h[...] = jnp.zeros_like(col_h)
    col_m[...] = jnp.zeros_like(col_m)
    right, left = (range(8), range(7, -1, -1))
    nothing = jnp.zeros((8, 128), f32)

    def packed(row, piece):
        return pl.ds(row * 64 + piece, 8, stride=8)

    def chain(state, row, order, ends, starts):
        for c in order:
            line = pl.ds(pl.multiple_of(row * 64 + c * 8, 8), 8)
            starts[line, :] = state
            state = prod[line, :] * state + ends[line, :]
        return state

    def carry_on(held, row, odd):
        ahead, behind = held
        ahead = ahead * links_up(heights, row)
        if odd:
            ahead = chain(ahead, row, left, end_rl, in_rl)
            behind = chain(behind, row, left, back_lr, tail_lr)
        else:
            ahead = chain(ahead, row, right, end_lr, in_lr)
            behind = chain(behind, row, right, back_rl, tail_rl)
        return (ahead, behind * links_up(heights, row + 1))

    def carry_back(held, row, odd):
        behind, ahead = held
        behind = behind * links_up(heights, row + 1)
        if odd:
            behind = chain(behind, row, right, end_lr, in_lr)
            ahead = chain(ahead, row, right, back_rl, tail_rl)
        else:
            behind = chain(behind, row, left, end_rl, in_rl)
            ahead = chain(ahead, row, left, back_lr, tail_lr)
        return (behind, ahead * links_up(heights, row))

    def ascend(row):
        keep = links_up(heights, row)
        for k in range(width // group):
            lanes = slice(k * group, (k + 1) * group)
            whole = lr = rl = mlr = mrl = None
            for c in range(8):
                lines = pl.ds(pl.multiple_of(row * 64 + c * 8, 8), 8)
                spot = slice(c * 8, c * 8 + 8)
                a, s, g = (a_ref[lines, lanes], s_ref[lines, lanes], g_ref[lines, lanes])
                state_h = a * (col_h[spot, lanes] * keep) + s
                col_h[spot, lanes] = state_h
                down_ref[lines, lanes] = state_h
                lam = g + col_m[spot, lanes] * keep
                col_m[spot, lanes] = a * lam
                up_ref[lines, lanes] = lam
                if c == 0:
                    whole, lr, rl, mlr, mrl = (a, s, s, a * g, a * g)
                else:
                    lr = a * lr + s
                    rl = rl + whole * s
                    whole = whole * a
                    mlr = mlr + whole * g
                    mrl = a * (mrl + g)
            for j in range(group // 128):
                spot = packed(row, k * (group // 128) + j)
                piece = slice(j * 128, (j + 1) * 128)
                prod[spot, :] = whole[:, piece]
                end_lr[spot, :] = lr[:, piece]
                end_rl[spot, :] = rl[:, piece]
                back_lr[spot, :] = mlr[:, piece]
                back_rl[spot, :] = mrl[:, piece]

    def ascend_two(step, held):
        row = 2 * step + 1
        held = carry_on(held, row - 1, False)
        ascend(row)
        held = carry_on(held, row, True)
        ascend(row + 1)
        return held

    ascend(0)
    held = lax.fori_loop(0, devices - 1, ascend_two, (nothing,) * 2)
    held = carry_on(held, rows - 2, False)
    ascend(rows - 1)
    carry_on(held, rows - 1, True)
    col_h[...] = jnp.zeros_like(col_h)
    col_m[...] = jnp.zeros_like(col_m)

    def descend(row):
        keep = links_up(heights, row + 1)

        def edge(ref, k):
            pieces = [ref[packed(row, k * (group // 128) + j), :] for j in range(group // 128)]
            return pieces[0] if len(pieces) == 1 else jnp.concatenate(pieces, axis=1)

        for k in range(width // group):
            lanes = slice(k * group, (k + 1) * group)
            h_right, m_left = (edge(in_lr, k), edge(tail_rl, k))
            for c in range(8):
                lines = pl.ds(pl.multiple_of(row * 64 + c * 8, 8), 8)
                spot = slice(c * 8, c * 8 + 8)
                a, s, g = (a_ref[lines, lanes], s_ref[lines, lanes], g_ref[lines, lanes])
                h_right = a * h_right + s
                lam = g + m_left
                m_left = a * lam
                row_h[spot, lanes] = h_right
                row_m[spot, lanes] = lam
            h_left, m_right = (edge(in_rl, k), edge(tail_lr, k))
            for c in range(7, -1, -1):
                lines = pl.ds(pl.multiple_of(row * 64 + c * 8, 8), 8)
                spot = slice(c * 8, c * 8 + 8)
                a, s, g = (a_ref[lines, lanes], s_ref[lines, lanes], g_ref[lines, lanes])
                h_left = a * h_left + s
                lam_lr = g + m_right
                m_right = a * lam_lr
                h_down, lam_up = (down_ref[lines, lanes], up_ref[lines, lanes])
                h_up = a * (col_h[spot, lanes] * keep) + s
                col_h[spot, lanes] = h_up
                lam_down = g + col_m[spot, lanes] * keep
                col_m[spot, lanes] = a * lam_down
                h_right, lam_rl = (row_h[spot, lanes], row_m[spot, lanes])
                lam_sum = (lam_lr + lam_rl) + (lam_down + lam_up)
                down_ref[lines, lanes] = (h_right + h_left) + (h_down + h_up)
                up_ref[lines, lanes] = lam_sum
                g_ref[lines, lanes] = (
                    (lam_lr * h_right + lam_rl * h_left)
                    + (lam_down * h_down + lam_up * h_up)
                    - s * lam_sum
                )

    def descend_two(step, held):
        row = rows - 1 - 2 * step
        held = carry_back(held, row - 1, False)
        descend(row)
        held = carry_back(held, row - 2, True)
        descend(row - 1)
        return held

    held = carry_back((nothing,) * 2, rows - 1, True)
    held = lax.fori_loop(0, devices - 1, descend_two, held)
    carry_back(held, 0, False)
    descend(1)
    descend(0)
    decay_acc[...] = jnp.zeros_like(decay_acc)
    gather_e, gather_b, gather_c = (spread_e[:part], spread_bc[:PROJ, :128], spread_bc[:PROJ, 128:])

    def finish(tile, carry):
        lines = pl.ds(pl.multiple_of(tile * pos, pos), pos)
        delta = delta_keep[tile]
        of_source, of_mix, of_proj = (lhs_u[lines, :], lhs_m[lines, :], lhs_p[lines, :])
        delta_low = delta.astype(bf16)
        of_bc = dot(of_proj, spread_bc, (1, 0))
        of_b, of_c = (of_bc[:, :128], of_bc[:, 128:])
        totals = grad_b = grad_c = None
        for k in range(width // span):
            lanes = slice(k * span, (k + 1) * span)
            scaled = (g_ref[lines, lanes] * rate_row[:, lanes]).astype(bf16)
            source = dot(of_source, spread_e[:, lanes], (1, 0))
            mix = dot(of_mix, spread_e[:, lanes], (1, 0))
            decay_acc[:, lanes] += dot(delta_low, scaled, (1, 0))
            of_y, of_sum = ([], [])
            for j in range(span // 128):
                tile_lanes = slice(k * span + j * 128, k * span + (j + 1) * 128)
                piece = slice(j * 128, (j + 1) * 128)
                h_sum, lam_sum = (down_ref[lines, tile_lanes], up_ref[lines, tile_lanes])
                of_y.append((h_sum * of_c).astype(bf16))
                of_sum.append((lam_sum * of_b).astype(bf16))
                term_b, term_c = (lam_sum * source[:, piece], h_sum * mix[:, piece])
                grad_b = term_b if grad_b is None else grad_b + term_b
                grad_c = term_c if grad_c is None else grad_c + term_c
            parts = (
                dot(gather_e[:, lanes], jnp.concatenate(of_y, axis=1), (1, 1)),
                dot(gather_e[:, lanes], scaled, (1, 1)),
                dot(gather_e[:, lanes], jnp.concatenate(of_sum, axis=1), (1, 1)),
            )
            totals = parts if totals is None else [x + z for x, z in zip(totals, parts)]
        y_keep[tile], steps_keep[tile], sums_keep[tile] = totals
        coefs_keep[tile] = dot(gather_b, grad_b.astype(bf16), (1, 1)) + dot(gather_c, grad_c.astype(bf16), (1, 1))
        return carry

    lax.fori_loop(0, devices, finish, 0, unroll=8)
    step_grad = jnp.zeros((part, 16), f32)
    for tile in range(devices):
        sums, coefs = (sums_keep[tile], coefs_keep[tile])
        pre_grad = (steps_keep[tile] + got[tile, :part] * sums) * step_keep[tile]
        send[tile, :part] = y_keep[tile]
        send[tile, part : 2 * part] = delta_keep[tile] * sums
        send[tile, 2 * part : 2 * part + 16] = coefs[:16] + fine_dot(step_own, pre_grad, (0, 0))
        send[tile, 2 * part + 16 :] = coefs[16:]
        step_grad = step_grad + fine_dot(pre_grad, got[tile, 2 * part : 2 * part + 16], (1, 1))
    decay_grad = jnp.where(one_channel, decay_acc[...], 0.0)
    decay_high, decay_low = split(decay_grad)
    decay_grad = dot(decay_high, by_state, (1, 1)) + dot(decay_low, by_state, (1, 1))
    spot = (iota((part, small.shape[1]), 1) == iota((part, small.shape[1]), 0) + place[0] * part).astype(bf16)
    for at, value in ((0, step_grad), (16, decay_grad)):
        high, low = split(value)
        small[at : at + 16] = dot(high, spot, (0, 0)) + dot(low, spot, (0, 0))


def mix_kernel(
    heights, place, group, got, small_in, low, low_halo, cot, conv_own, conv_halo, pre, gate_in, grad_in,
    select_rows, table, tok, in_w, out_t, conv_kernel, norm_gain, norm_bias,
    layer_out, act_out, near, far, gate_grad_out, keep, give,
    grads, gated_ref, inner_ref, moved_ref, sums_ref, *, pair,
):
    devices, length, pos = got.shape
    model, inner_width = out_t.shape
    part = inner_width // devices
    lane = iota((1, pos), 1)
    prev, following = row_masks(heights, place[0])
    proj_grad = got[0, 2 * part :]
    for k in range(1, devices):
        proj_grad = proj_grad + got[k, 2 * part :]
    proj_grad = proj_grad.astype(bf16)
    together = max(1, 48 // part)
    for first in range(0, devices, together):
        members = range(first, first + together)
        rows = slice(first * part, (first + together) * part)
        y = jnp.concatenate([got[k, :part] for k in members], axis=0)
        inner_grad = jnp.concatenate([got[k, part : 2 * part] for k in members], axis=0)
        pre_act, gate, gated_grad = (pre[rows], gate_in[rows], grad_in[rows])
        skip = table[rows, SKIP : SKIP + 1]
        sig_pre, sig_gate = (sigmoid(pre_act), sigmoid(gate))
        inner = (pre_act * sig_pre).astype(bf16)
        inner_ref[rows] = inner
        inner = inner.astype(f32)
        silu_gate = gate * sig_gate
        mix_grad = gated_grad * silu_gate
        inner_grad = inner_grad + mix_grad * skip + dot(select_rows[rows], proj_grad, (1, 0))
        act_grad = inner_grad * (sig_pre * (1.0 + pre_act * (1.0 - sig_pre)))
        act_out[rows] = act_grad
        y_all = y + skip * inner
        gated_ref[rows] = (y_all * silu_gate).astype(bf16)
        gate_grad_out[rows] = (gated_grad * y_all * (sig_gate * (1.0 + gate * (1.0 - sig_gate)))).astype(bf16)
        field = conv_own[rows]
        upper, lower = rows_around(field, conv_halo[rows])
        fields = (upper * prev, field, lower * following)
        sums = jnp.where(lane == 9, jnp.sum(act_grad, axis=1, keepdims=True), 0.0)
        sums = jnp.where(lane == 10, jnp.sum(mix_grad * inner, axis=1, keepdims=True), sums)
        for b, moved in enumerate((from_right(act_grad), act_grad, from_left(act_grad))):
            moved_ref[b, rows] = moved.astype(bf16)
            for a in range(3):
                sums = jnp.where(lane == 3 * a + b, jnp.sum(moved * fields[a], axis=1, keepdims=True), sums)
        sums_ref[rows] = sums
    half = inner_width // 2
    top, bottom = (act_out[:half], act_out[half:])
    up = jnp.where(lane < 64, top, pltpu.roll(bottom, 64, 1))
    down = jnp.where(lane < 64, pltpu.roll(top, 64, 1), bottom)
    even = place[0] % 2 == 0
    near[...] = jnp.where(even, down, up)
    far[...] = jnp.where(even, up, down)
    gated, gate_grad = (gated_ref[...], gate_grad_out[...])
    natural = dot(gated, column_order(pos), (1, 0)).astype(bf16)
    layer = jnp.transpose(dot(out_t[...], natural, (1, 0)))
    layer_out[...] = (tok[...].astype(f32) + layer).astype(bf16)

    low_in = low[...]
    upper, lower = rows_around(low_in.astype(f32), low_halo[...].astype(f32))
    which = iota((16, 1), 0)
    masks = jnp.where(which == 0, prev, jnp.where(which == 1, 1.0, following))
    left_hand = jnp.concatenate(
        [(upper * prev).astype(bf16), low_in, (lower * following).astype(bf16), masks.astype(bf16)], axis=0
    )
    blocks = inner_width // 128
    gate_at, out_at, small_at = [k * blocks * model for k in (1, 2, 3)]
    ones = jnp.ones((16, pos), bf16)
    totals = [[], []]
    gain_sum = jnp.zeros((model, 128), f32)
    for n in range(blocks):
        columns = slice(n * 128, (n + 1) * 128)
        in_conv = conv_total = None
        for b in range(3):
            part_b = dot(left_hand, moved_ref[b, columns], (1, 1))
            for a in range(3):
                tap = conv_kernel[a, b : b + 1, columns]
                term = tap * part_b[a * model : (a + 1) * model]
                total = tap * part_b[3 * model + a : 3 * model + a + 1]
                in_conv = term if in_conv is None else in_conv + term
                conv_total = total if conv_total is None else conv_total + total
        in_gate = dot(low_in, gate_grad[columns], (1, 1))
        grads[n * model : (n + 1) * model] = in_conv
        grads[gate_at + n * model : gate_at + (n + 1) * model] = in_gate
        grads[out_at + n * model : out_at + (n + 1) * model] = dot(cot[...], gated[columns], (1, 1))
        totals[0].append(conv_total)
        totals[1].append(dot(ones, gate_grad[columns], (1, 1))[0:1])
        conv_w = in_w[:, columns].astype(f32)
        gate_w = in_w[:, inner_width + n * 128 : inner_width + (n + 1) * 128].astype(f32)
        gain_sum = gain_sum + (conv_w * in_conv + gate_w * in_gate)
    sums = jnp.broadcast_to(jnp.concatenate(totals[0] + totals[1], axis=1), (16, 2 * inner_width))
    sums_high, sums_low = split(sums)
    shift_row = (dot(sums_high, in_w[...], (1, 1)) + dot(sums_low, in_w[...], (1, 1)))[0:1]
    gain_row = patch_sums(gain_sum)
    gain_row = (gain_row - norm_bias[...].reshape(1, model) * shift_row) / norm_gain[...].reshape(1, model)
    high, mid = split(sums_ref[...])
    rest = (sums_ref[...] - high.astype(f32) - mid.astype(f32)).astype(bf16)
    chosen = (iota((16, pos), 0) == iota((16, pos), 1)).astype(bf16)
    sums = dot(chosen, high, (1, 1)) + (dot(chosen, mid, (1, 1)) + dot(chosen, rest, (1, 1)))
    norms = jnp.concatenate([gain_row, shift_row], axis=1)
    sums = jnp.where(iota((16, 1), 0) == NORM_AT - TAPS_AT, norms, sums)
    smalls = jnp.concatenate([dot(proj_grad, inner_ref[...], (1, 1)), small_in[...], sums], axis=0)
    put_blocks(grads, small_at, smalls)
    small_at = small_at + blocks * SMALL
    grads[small_at:] = jnp.zeros((grads.shape[0] - small_at, 128), f32)
    own = group[0] % 2
    if pair:
        count = keep.shape[0] // 2
        height = group[0] // 2
        for ref, side in ((keep, own), (give, 1 - own)):
            for k, at in enumerate((height, 1 - height)):
                ref[k * count : (k + 1) * count] = grads[pl.ds(pl.multiple_of((2 * side + at) * count, count), count)]
    else:
        count = keep.shape[0]
        keep[...] = grads[pl.ds(pl.multiple_of(own * count, count), count)]
        give[...] = grads[pl.ds(pl.multiple_of((1 - own) * count, count), count)]


def exit_kernel(
    heights, place, act, from_above, from_below, gate_grad, table, tok, cot, in_w,
    tokens_grad,
):
    inner_width, pos = act.shape
    model = in_w.shape[0]
    lane = iota((1, pos), 1)
    even = place[0] % 2 == 0
    above, below = (
        jnp.where(even, from_above[...], from_below[...]), jnp.where(even, from_below[...], from_above[...])
    )
    halo_top = jnp.where(lane < 64, below, pltpu.roll(above, 64, 1))
    halo_bottom = jnp.where(lane < 64, pltpu.roll(below, 64, 1), above)
    act_grad = act[...]
    prev, following = row_masks(heights, place[0])
    upper, lower = rows_around(act_grad, jnp.concatenate([halo_top, halo_bottom], axis=0))
    columns = table[...]
    taps = [[columns[:, 8 - 3 * a - b : 9 - 3 * a - b] for b in range(3)] for a in range(3)]
    conv_grad = conv_tile(upper * prev, act_grad, lower * following, taps).astype(bf16)
    halves = jnp.concatenate([conv_grad, gate_grad[...]], axis=0)
    halves = dot(halves, column_order(pos), (1, 0)).astype(bf16)
    normed_grad = dot(in_w[...], halves, (1, 0))
    xhat, inverse = normalized(flipped(tok[...]))
    scaled = normed_grad * columns[:model, GAIN : GAIN + 1]
    x_grad = (
        scaled
        - jnp.mean(scaled, axis=0, keepdims=True)
        - xhat * jnp.mean(scaled * xhat, axis=0, keepdims=True)
    ) * inverse
    x_grad = jnp.transpose(x_grad)
    tokens_grad[...] = (x_grad + cot[...].astype(f32)).astype(bf16)


def deal_kernel(group, *refs, members, pair):
    pieces, ordered = (refs[:members], refs[-1])
    (
        gain_grad, shift_grad, inproj, kernel_grad, offset, select, stepproj, stepbias, decay, skip, outproj,
    ) = refs[members:-1]
    model, inner_width = outproj.shape
    blocks = inner_width // 128
    rank = stepproj.shape[0]
    states = decay.shape[0]
    count = pieces[0].shape[0]
    for k, piece in enumerate(pieces):
        if pair:
            core, height = (group[0] % 2, group[0] // 2)
            core = 1 - core if k // 2 else core
            height = 1 - height if k % 2 else height
            slot = core * 2 + height
        else:
            slot = k % 2 * (members // 2) + k // 2
        ordered[pl.ds(pl.multiple_of(slot * count, count), count)] = piece[...]

    def rows(start, count):
        return ordered[start : start + count]

    for k in range(2 * blocks):
        inproj[:, k * 128 : (k + 1) * 128] = rows(k * model, model)
    start = 2 * blocks * model
    for k in range(blocks):
        outproj[:, k * 128 : (k + 1) * 128] = rows(start + k * model, model)
    start = start + blocks * model
    small = jnp.concatenate([rows(start + k * SMALL, SMALL) for k in range(blocks)], axis=1)
    select[:rank] = small[:rank]
    select[rank:] = small[IN:PROJ]
    stepproj[...] = small[STEP_AT : STEP_AT + rank]
    stepbias[...] = small[STEP_AT + ONE : STEP_AT + ONE + 1].reshape(stepbias.shape)
    decay[...] = small[DECAY_AT : DECAY_AT + states]
    for k in range(3):
        kernel_grad[k] = small[TAPS_AT + 3 * k : TAPS_AT + 3 * k + 3]
    offset[...] = small[OFFSET_AT : OFFSET_AT + 1].reshape(offset.shape)
    skip[...] = small[SKIP_AT : SKIP_AT + 1].reshape(skip.shape)
    norms = small[NORM_AT : NORM_AT + 1]
    gain_grad[...] = norms[:, :model].reshape(gain_grad.shape)
    shift_grad[...] = norms[:, model:].reshape(shift_grad.shape)


def vmem_call(kernel, out_shape, scalars, arrays, weights=(), scratch=(), limit=16):
    scalars = [pltpu.with_memory_space_constraint(x, pltpu.HBM) if x.ndim == 2 else x for x in scalars]
    arrays = [pltpu.with_memory_space_constraint(x, pltpu.VMEM) for x in arrays]
    arrays += [pltpu.with_memory_space_constraint(x, pltpu.HBM) for x in weights]
    return pl.pallas_call(
        kernel,
        out_shape=out_shape,
        in_specs=[pl.BlockSpec(memory_space=pltpu.SMEM)] * len(scalars)
        + [pl.BlockSpec(memory_space=pltpu.VMEM)] * len(arrays),
        out_specs=[pl.BlockSpec(memory_space=pltpu.VMEM)] * len(out_shape),
        scratch_shapes=list(scratch),
        compiler_params=pltpu.CompilerParams(vmem_limit_bytes=limit * 1024 * 1024),
    )(*scalars, *arrays)


def struct(*shape, dtype=f32):
    return jax.ShapeDtypeStruct(shape, dtype)


def inside(*shape, dtype=f32):
    return pltpu.VMEM(shape, dtype)


def scan_call(heights, place, got, table, states):
    devices, length, pos = got.shape
    inner_width = table.shape[0]
    part = inner_width // devices
    width = -(-part * states // 128) * 128
    total = devices * pos
    span = 256 if width % 256 == 0 else 128
    group = 768 if width % 768 == 0 else span
    big = pltpu.VMEM((total, width), f32)
    line = pltpu.VMEM((2 * devices * 64, 128), f32)
    column = pltpu.VMEM((pos // 2, width), f32)
    own = pltpu.VMEM((devices, part, pos), f32)
    return vmem_call(
        functools.partial(scan_kernel, part=part, states=states, span=span, group=group),
        [inside(devices, length, pos), inside(32, inner_width)],
        [heights, place],
        [got, table],
        (),
        [big] * 5
        + [column] * 4
        + [line] * 9
        + [pltpu.VMEM((total, 2 * part), bf16)] * 3
        + [pltpu.VMEM((total, 2 * PROJ), bf16)]
        + [own] * 5
        + [pltpu.VMEM((devices, PROJ, pos), f32), pltpu.VMEM((part, width), f32)],
        limit=32 if total <= 1024 else 52,
    )


def on_device(
    tokens, heights, cotangent, norm_gain, norm_bias, in_weight, conv_kernel, conv_bias, select_weight,
    step_weight, step_bias, decay_log, skip_gain, out_weight,
):
    _, tile_rows, grid_cols, model = tokens.shape
    inner_width = out_weight.shape[0]
    states = decay_log.shape[1]
    rank = step_weight.shape[0]
    devices = lax.axis_size("seq")
    groups = lax.axis_size("dp")
    place = lax.axis_index("seq").reshape(1)
    group = lax.axis_index("dp").reshape(1)
    pair = groups == 4
    pos = tile_rows * grid_cols
    part = inner_width // devices
    length = 2 * part + PROJ
    near_pairs = [(i, i ^ 1) for i in range(devices)]
    far_pairs = [(i, (i - 1 + 2 * (i % 2)) % devices) for i in range(devices)]

    tok, cot = (tokens.reshape(pos, model), cotangent.reshape(pos, model))
    even = place[0] % 2 == 0
    upper, lower = (tok[:grid_cols].astype(f32), tok[grid_cols:].astype(f32))
    above = lax.ppermute(jnp.where(even, upper, lower), "seq", far_pairs)
    below = lax.ppermute(jnp.where(even, lower, upper), "seq", near_pairs)
    out_t = out_weight.T
    channels = inside(inner_width, pos)
    narrow = inside(model, pos, dtype=bf16)
    conv_own, gate, gated_grad, mix, low, cot_in, conv_rows, select_rows, table = vmem_call(
        own_kernel,
        [channels] * 4
        + [narrow] * 2
        + [inside(inner_width, model, dtype=bf16), inside(inner_width, PROJ, dtype=bf16), inside(inner_width, TABLE)],
        [],
        [],
        [
            tok, cot, in_weight, out_t, select_weight.T, conv_kernel, conv_bias, step_weight, step_bias,
            decay_log.T, skip_gain, norm_gain, norm_bias,
        ],
        [pltpu.VMEM((TABLE, inner_width), f32)],
    )
    sent, conv_halo, pre_act, low_halo = vmem_call(
        entry_kernel,
        [inside(devices, length, pos), channels, channels, narrow],
        [heights, place],
        [above, below, conv_own, mix, conv_rows, select_rows, table],
    )
    got = lax.all_to_all(sent, "seq", 0, 0, tiled=True)
    sent, small = scan_call(heights, place, got, table, states)
    got = lax.all_to_all(sent, "seq", 0, 0, tiled=True)
    blocks = inner_width // 128
    whole = -(-blocks * (3 * model + SMALL) // 2048) * 2048
    half = whole // 2
    layer_out, act_grad, near, far, gate_grad, keep, give = vmem_call(
        functools.partial(mix_kernel, pair=pair),
        [struct(pos, model, dtype=bf16), channels]
        + [inside(inner_width // 2, pos)] * 2
        + [inside(inner_width, pos, dtype=bf16)]
        + [inside(half, 128)] * 2,
        [heights, place, group],
        [
            got, small, low, low_halo, cot_in, conv_own, conv_halo, pre_act, gate, gated_grad, select_rows, table,
        ],
        [tok, in_weight, out_t, conv_kernel, norm_gain, norm_bias],
        [
            pltpu.VMEM((whole, 128), f32), pltpu.VMEM((inner_width, pos), bf16), pltpu.VMEM((inner_width, pos), bf16),
            pltpu.VMEM((3, inner_width, pos), bf16), pltpu.VMEM((inner_width, pos), f32),
        ],
    )
    from_above = lax.ppermute(far, "seq", far_pairs)
    from_below = lax.ppermute(near, "seq", near_pairs)
    swap = [(i, i ^ 1) for i in range(groups)]
    taken = lax.ppermute(give, "dp", swap)
    count = half // (groups // 2)
    if pair:
        across = [(i, i ^ 2) for i in range(groups)]
        other = lax.ppermute(keep[count:] + taken[count:], "dp", across)
        piece = keep[:count] + taken[:count]
    else:
        same_core = [list(range(c, groups, 2)) for c in range(2)]
        pieces = (keep + taken).reshape(groups // 2, count, 128)
        pieces = lax.all_to_all(pieces, "dp", 0, 0, tiled=True, axis_index_groups=same_core)
        piece, other = (pieces[0], jnp.sum(pieces[1:], axis=0))
    other, from_above, from_below = lax.optimization_barrier((other, from_above, from_below))
    shares = (piece + other).reshape(devices, count // devices, 128)
    shares = lax.all_to_all(shares, "seq", 0, 0, tiled=True)
    share = jnp.broadcast_to(jnp.sum(shares, axis=0), shares.shape)
    mine = lax.all_to_all(share, "seq", 0, 0, tiled=True).reshape(count, 128)
    mine, from_above, from_below = lax.optimization_barrier((mine, from_above, from_below))
    (tokens_grad,) = vmem_call(
        exit_kernel,
        [struct(pos, model, dtype=bf16)],
        [heights, place],
        [act_grad, from_above, from_below, gate_grad, table],
        [tok, cot, in_weight],
    )
    if pair:
        from_y = lax.ppermute(mine, "dp", across)
        from_y, tokens_grad = lax.optimization_barrier((from_y, tokens_grad))
        pieces = [mine, from_y, lax.ppermute(mine, "dp", swap), lax.ppermute(from_y, "dp", swap)]
    else:
        pieces = list(lax.all_gather(mine, "dp"))
    gain, shift, inproj, kernel, offset, select, stepproj, stepbias, decay, skip, outproj = vmem_call(
        functools.partial(deal_kernel, members=len(pieces), pair=pair),
        [
            struct(model), struct(model), struct(model, 2 * inner_width), struct(3, 3, inner_width),
            struct(inner_width), struct(rank + 2 * states, inner_width), struct(rank, inner_width),
            struct(inner_width), struct(states, inner_width), struct(inner_width), struct(model, inner_width),
        ],
        [group],
        pieces,
        (),
        [pltpu.VMEM((whole, 128), f32)],
    )
    shape = tokens.shape
    return (
        layer_out.reshape(shape), tokens_grad.reshape(shape), gain, shift, inproj, kernel, offset, select.T,
        stepproj, stepbias, decay.T, skip, outproj.T,
    )


def solution(mesh):
    tile, whole = (P("dp", "seq", None, None), P())
    return jax.shard_map(
        on_device,
        mesh=mesh,
        in_specs=(tile, P("dp", None), tile) + (whole,) * 11,
        out_specs=(tile, tile) + (whole,) * 11,
        check_vma=False,
    )
```

```python
import functools

import jax
import jax.numpy as jnp
from jax import lax
from jax.experimental import pallas as pl
from jax.experimental.pallas import tpu as pltpu
from jax.sharding import PartitionSpec as P

epsilon = 1e-05
f32, bf16 = (jnp.float32, jnp.bfloat16)
ONE, IN, OUT, PROJ = (12, 16, 32, 48)
BIAS, SKIP, GAIN, SHIFT, STEP, DECAY, TABLE = (9, 10, 11, 12, 16, 32, 48)
STEP_AT, DECAY_AT, TAPS_AT, OFFSET_AT, SKIP_AT, NORM_AT, SMALL = (48, 64, 80, 89, 90, 95, 96)


def dot(a, b, over):
    return lax.dot_general(a, b, (((over[0],), (over[1],)), ((), ())), preferred_element_type=f32)


def split(value):
    high = value.astype(bf16)
    return (high, (value - high.astype(f32)).astype(bf16))


def fine_dot(a, b, over):
    (a_high, a_low), (b_high, b_low) = (split(a), split(b))
    return dot(a_high, b_high, over) + (dot(a_low, b_high, over) + dot(a_high, b_low, over))


def iota(shape, dim):
    return lax.broadcasted_iota(jnp.int32, shape, dim)


def sigmoid(v):
    return 1.0 / (1.0 + jnp.exp(-v))


def links_up(heights, row):
    end = jnp.int32(0)
    same = row > 0
    for k in range(heights.shape[1]):
        end = end + heights[0, k]
        same = same & (end != row)
    return jnp.where(same, 1.0, 0.0).astype(f32)


def row_masks(heights, place):
    lane = iota((1, 128), 1)
    flags = [links_up(heights, 2 * place + k) for k in range(3)]
    return (jnp.where(lane < 64, flags[0], flags[1]), jnp.where(lane < 64, flags[1], flags[2]))


def rows_around(own, halo):
    lane = iota((1, 128), 1)
    upper = pltpu.roll(jnp.where(lane < 64, own, halo), 64, 1)
    lower = pltpu.roll(jnp.where(lane < 64, halo, own), 64, 1)
    return (upper, lower)


def from_left(tile):
    place = iota((1, 128), 1) & 63
    wrapped = jnp.where(place == 0, 0.0, pltpu.roll(tile, 73, 1))
    return jnp.where(place < 8, wrapped, pltpu.roll(tile, 8, 1))


def from_right(tile):
    place = iota((1, 128), 1) & 63
    wrapped = jnp.where(place == 63, 0.0, pltpu.roll(tile, 55, 1))
    return jnp.where(place >= 56, wrapped, pltpu.roll(tile, 120, 1))


def conv_tile(upper, own, lower, taps):
    left, middle, right = [
        taps[0][b] * upper + taps[1][b] * own + taps[2][b] * lower for b in range(3)
    ]
    return middle + (from_left(left) + from_right(right))


def normalized(x):
    centred = x - jnp.mean(x, axis=0, keepdims=True)
    inverse = lax.rsqrt(jnp.mean(centred * centred, axis=0, keepdims=True) + epsilon)
    return (centred * inverse, inverse)


def eye(size):
    return (iota((size, size), 0) == iota((size, size), 1)).astype(bf16)


def flipped(value):
    pieces = [value[:, k : k + 128] for k in range(0, value.shape[1], 128)]
    return jnp.concatenate([dot(eye(piece.shape[1]), piece, (1, 1)) for piece in pieces], axis=0)


def flipped_fine(value):
    high, low = split(value)
    rest = (value - high.astype(f32) - low.astype(f32)).astype(bf16)
    return flipped(high) + (flipped(low) + flipped(rest))


def patch_sums(value):
    high, low = split(value)
    ones = jnp.ones((8, value.shape[1]), bf16)
    return (dot(ones, high, (1, 1)) + dot(ones, low, (1, 1)))[0:1]


def put_blocks(ref, start, value):
    for k in range(value.shape[1] // 128):
        ref[start + k * value.shape[0] : start + (k + 1) * value.shape[0]] = value[:, k * 128 : (k + 1) * 128]


def column_order(pos):
    new, old = (iota((pos, pos), 0), iota((pos, pos), 1))
    source = (new & ~63) | ((new & 7) << 3) | ((new >> 3) & 7)
    return (source == old).astype(bf16)


def lane_maps(part, states, width):
    lane = iota((1, width), 1)
    channel = jnp.floor((lane.astype(f32) + 0.5) * (1.0 / states)).astype(jnp.int32)
    return (channel, lane - channel * states, channel < part)


def entered(rows):
    return dot(flipped(rows).astype(bf16), column_order(rows.shape[0]), (1, 0))


def own_kernel(
    tok, cot, in_w, out_t, select_t, conv_kernel, conv_bias, step_weight, step_bias, decay_t, skip_gain,
    norm_gain, norm_bias,
    conv_out, gate_out, grad_out, mix_out, low_out, cot_out, conv_rows, select_rows, table,
    table_t,
):
    model, inner_width = out_t.shape
    states = decay_t.shape[0]
    rank = step_weight.shape[0]
    in_rows = flipped(in_w[...]).astype(bf16)
    conv_rows[...] = in_rows[:inner_width]
    out_rows = flipped(out_t[...]).astype(bf16)
    chosen = iota((PROJ, select_t.shape[0]), 0)
    chosen = jnp.where(chosen < rank, chosen, jnp.where(chosen < IN, -1, chosen - IN + rank))
    chosen = (chosen == iota((PROJ, select_t.shape[0]), 1)).astype(bf16)
    select_rows[...] = flipped(dot(chosen, select_t[...], (1, 0)).astype(bf16)).astype(bf16)
    table_t[...] = jnp.zeros_like(table_t)
    for k in range(3):
        table_t[3 * k : 3 * k + 3] = conv_kernel[k]
    table_t[BIAS : BIAS + 1] = conv_bias[...].reshape(1, inner_width)
    table_t[SKIP : SKIP + 1] = skip_gain[...].reshape(1, inner_width)
    table_t[GAIN : GAIN + 1, :model] = norm_gain[...].reshape(1, model)
    table_t[SHIFT : SHIFT + 1, :model] = norm_bias[...].reshape(1, model)
    table_t[STEP : STEP + rank] = step_weight[...]
    table_t[STEP + ONE : STEP + ONE + 1] = step_bias[...].reshape(1, inner_width)
    table_t[DECAY : DECAY + states] = decay_t[...]
    columns = flipped_fine(table_t[...])
    table[...] = columns
    gain, shift = (columns[:model, GAIN : GAIN + 1], columns[:model, SHIFT : SHIFT + 1])
    low = (normalized(entered(tok[...]))[0] * gain + shift).astype(bf16)
    cot_in = entered(cot[...]).astype(bf16)
    low_out[...] = low
    cot_out[...] = cot_in
    both = dot(in_rows, low, (1, 0))
    conv_out[...] = both[:inner_width]
    gate = both[inner_width:]
    gated_grad = dot(out_rows, cot_in, (1, 0))
    gate_out[...] = gate
    grad_out[...] = gated_grad
    mix_out[...] = gated_grad * (gate * sigmoid(gate))


def entry_kernel(
    heights, place, above, below, conv_own, mix, conv_rows, select_rows, table,
    send, halo_out, pre_out, low_halo_out,
):
    devices = send.shape[0]
    inner_width = conv_own.shape[0]
    model = conv_rows.shape[1]
    part = inner_width // devices
    columns = table[...]
    gain, shift = (columns[:model, GAIN : GAIN + 1], columns[:model, SHIFT : SHIFT + 1])
    even = place[0] % 2 == 0
    halo = jnp.concatenate(
        [jnp.where(even, below[...], above[...]), jnp.where(even, above[...], below[...])], axis=0
    ).astype(bf16)
    low_halo = (normalized(entered(halo))[0] * gain + shift).astype(bf16)
    low_halo_out[...] = low_halo
    around = dot(conv_rows[...], low_halo, (1, 0))
    halo_out[...] = around
    conv_in = conv_own[...]
    prev, following = row_masks(heights, place[0])
    upper, lower = rows_around(conv_in, around)
    taps = [[columns[:, 3 * a + b : 3 * a + b + 1] for b in range(3)] for a in range(3)]
    pre_act = columns[:, BIAS : BIAS + 1] + conv_tile(upper * prev, conv_in, lower * following, taps)
    inner = (pre_act * sigmoid(pre_act)).astype(bf16)
    proj = dot(flipped(select_rows[...]).astype(bf16), inner, (1, 0))
    proj = jnp.where(iota(proj.shape, 0) == ONE, 1.0, proj)
    pre_out[...] = pre_act
    inner = inner.astype(f32)
    for k in range(devices):
        send[k, :part] = inner[k * part : (k + 1) * part]
        send[k, part : 2 * part] = mix[k * part : (k + 1) * part]
        send[k, 2 * part :] = proj


def scan_kernel(
    heights, place, got, table,
    send, small,
    a_ref, s_ref, g_ref, down_ref, up_ref, source_ref, mix_ref, col_h, col_m, row_h, row_m,
    prod, end_lr, end_rl, back_lr, back_rl, in_lr, in_rl, tail_lr, tail_rl,
    lhs_d, lhs_u, lhs_m, coef_keep, step_keep, delta_keep, y_keep, steps_keep, sums_keep, coefs_keep, decay_acc, *, part, states, span, group,
):
    devices, _, pos = got.shape
    rows = 2 * devices
    width = a_ref.shape[1]
    own_rows = table[pl.ds(pl.multiple_of(place[0] * part, 4), part), :]
    channel, state, live = lane_maps(part, states, width)
    twice = iota((2 * part, 1), 0)
    twice = jnp.where(twice >= part, twice - part, twice)
    spread_e = ((twice == channel) & live).astype(bf16)
    coef = iota((2 * PROJ, 1), 0)
    coef = jnp.where(coef >= PROJ, coef - PROJ, coef)
    near = state[:, :128]
    spread_bc = jnp.concatenate([coef - IN == near, coef - OUT == near], axis=1).astype(bf16)
    by_state = ((iota((states, 1), 0) == state) & live).astype(bf16)
    rate = -jnp.exp(own_rows[:, DECAY : DECAY + states])
    one_channel = (iota((part, 1), 0) == channel) & live
    rate_high, rate_low = split(rate)
    rate_rest = split(rate - rate_high.astype(f32) - rate_low.astype(f32))[0]
    rate_row = sum(dot(piece, by_state, (1, 0)) for piece in (rate_high, rate_low, rate_rest))
    rate_row = jnp.sum(jnp.where(one_channel, rate_row, 0.0), axis=0, keepdims=True)
    rate_two = rate_row * 1.4426950408889634
    step_own = own_rows[:, STEP : STEP + 16]
    step_high, step_low = split(step_own)
    step_three = jnp.concatenate([step_high, step_high, step_low], axis=1)

    def turned(value):
        return jnp.transpose(jnp.concatenate(split(value), axis=0))

    for tile in range(devices):
        lines = slice(tile * pos, (tile + 1) * pos)
        inner_own = got[tile, :part]
        proj = got[tile, 2 * part :]
        high, low = split(proj[:16])
        pre_step = dot(step_three, jnp.concatenate([high, low, high], axis=0), (1, 0))
        tail = jnp.exp(-jnp.abs(pre_step))
        tail = jnp.where(tail < 1e-3, tail * (1.0 - 0.5 * tail), jnp.log(1.0 + tail))
        delta = jnp.maximum(pre_step, 0.0) + tail
        step_keep[tile] = sigmoid(pre_step)
        delta_keep[tile] = delta
        lhs_d[lines, :] = turned(delta)
        lhs_u[lines, :] = turned(delta * inner_own)
        lhs_m[lines, :] = turned(got[tile, part : 2 * part])
        coef_keep[lines, :] = dot(turned(proj), spread_bc, (1, 0))

    for k in range(width // span):
        lanes = slice(k * span, (k + 1) * span)

        def prepare(tile, carry):
            lines = pl.ds(pl.multiple_of(tile * pos, pos), pos)
            of_delta, of_source, of_mix = (lhs_d[lines, :], lhs_u[lines, :], lhs_m[lines, :])
            a_ref[lines, lanes] = jnp.exp2(dot(of_delta, spread_e[:, lanes], (1, 0)) * rate_two[:, lanes])
            source = dot(of_source, spread_e[:, lanes], (1, 0))
            mix = dot(of_mix, spread_e[:, lanes], (1, 0))
            source_ref[lines, lanes] = source
            mix_ref[lines, lanes] = mix
            for j in range(span // 128):
                tile_lanes = slice(k * span + j * 128, k * span + (j + 1) * 128)
                piece = slice(j * 128, (j + 1) * 128)
                s_ref[lines, tile_lanes] = source[:, piece] * coef_keep[lines, :128]
                g_ref[lines, tile_lanes] = mix[:, piece] * coef_keep[lines, 128:]
            return carry

        lax.fori_loop(0, devices, prepare, 0, unroll=8)
    down_ref[:64] = jnp.zeros((64, width), f32)
    col_m[...] = jnp.zeros_like(col_m)
    right, left = (range(8), range(7, -1, -1))
    nothing = jnp.zeros((8, 128), f32)

    def packed(row, piece):
        return pl.ds(row * 64 + piece, 8, stride=8)

    def chain(state, row, order, ends, starts):
        for c in order:
            line = pl.ds(pl.multiple_of(row * 64 + c * 8, 8), 8)
            starts[line, :] = state
            state = prod[line, :] * state + ends[line, :]
        return state

    def carry_on(held, row, odd):
        ahead, behind = held
        ahead = ahead * links_up(heights, row)
        if odd:
            ahead = chain(ahead, row, left, end_rl, in_rl)
            behind = chain(behind, row, left, back_lr, tail_lr)
        else:
            ahead = chain(ahead, row, right, end_lr, in_lr)
            behind = chain(behind, row, right, back_rl, tail_rl)
        return (ahead, behind * links_up(heights, row + 1))

    def carry_back(held, row, odd):
        behind, ahead = held
        behind = behind * links_up(heights, row + 1)
        if odd:
            behind = chain(behind, row, right, end_lr, in_lr)
            ahead = chain(ahead, row, right, back_rl, tail_rl)
        else:
            behind = chain(behind, row, left, end_rl, in_rl)
            ahead = chain(ahead, row, left, back_lr, tail_lr)
        return (behind, ahead * links_up(heights, row))

    def ascend(row):
        keep = links_up(heights, row)
        for k in range(width // group):
            lanes = slice(k * group, (k + 1) * group)
            whole = lr = rl = mlr = mrl = None
            for c in range(8):
                lines = pl.ds(pl.multiple_of(row * 64 + c * 8, 8), 8)
                spot = slice(c * 8, c * 8 + 8)
                a, s, g = (a_ref[lines, lanes], s_ref[lines, lanes], g_ref[lines, lanes])
                before, here = [
                    pl.ds(pl.multiple_of((row + step) * 64 + c * 8, 8), 8) for step in range(2)
                ]
                state_h = a * (down_ref[before, lanes] * keep) + s
                down_ref[here, lanes] = state_h
                lam = g + col_m[spot, lanes] * keep
                col_m[spot, lanes] = a * lam
                up_ref[lines, lanes] = lam
                if c == 0:
                    whole, lr, rl, mlr, mrl = (a, s, s, a * g, a * g)
                else:
                    lr = a * lr + s
                    rl = rl + whole * s
                    whole = whole * a
                    mlr = mlr + whole * g
                    mrl = a * (mrl + g)
            for j in range(group // 128):
                spot = packed(row, k * (group // 128) + j)
                piece = slice(j * 128, (j + 1) * 128)
                prod[spot, :] = whole[:, piece]
                end_lr[spot, :] = lr[:, piece]
                end_rl[spot, :] = rl[:, piece]
                back_lr[spot, :] = mlr[:, piece]
                back_rl[spot, :] = mrl[:, piece]

    def ascend_two(step, held):
        row = 2 * step + 1
        held = carry_on(held, row - 1, False)
        ascend(row)
        held = carry_on(held, row, True)
        ascend(row + 1)
        return held

    ascend(0)
    held = lax.fori_loop(0, devices - 1, ascend_two, (nothing,) * 2)
    held = carry_on(held, rows - 2, False)
    ascend(rows - 1)
    carry_on(held, rows - 1, True)
    col_h[...] = jnp.zeros_like(col_h)
    col_m[...] = jnp.zeros_like(col_m)

    def descend(row):
        keep = links_up(heights, row + 1)

        def edge(ref, k):
            pieces = [ref[packed(row, k * (group // 128) + j), :] for j in range(group // 128)]
            return pieces[0] if len(pieces) == 1 else jnp.concatenate(pieces, axis=1)

        for k in range(width // group):
            lanes = slice(k * group, (k + 1) * group)
            h_right, m_left = (edge(in_lr, k), edge(tail_rl, k))
            for c in range(8):
                lines = pl.ds(pl.multiple_of(row * 64 + c * 8, 8), 8)
                spot = slice(c * 8, c * 8 + 8)
                a, s, g = (a_ref[lines, lanes], s_ref[lines, lanes], g_ref[lines, lanes])
                h_right = a * h_right + s
                lam = g + m_left
                m_left = a * lam
                row_h[spot, lanes] = h_right
                row_m[spot, lanes] = lam
            h_left, m_right = (edge(in_rl, k), edge(tail_lr, k))
            for c in range(7, -1, -1):
                lines = pl.ds(pl.multiple_of(row * 64 + c * 8, 8), 8)
                spot = slice(c * 8, c * 8 + 8)
                a, s, g = (a_ref[lines, lanes], s_ref[lines, lanes], g_ref[lines, lanes])
                h_left = a * h_left + s
                lam_lr = g + m_right
                m_right = a * lam_lr
                here = pl.ds(pl.multiple_of((row + 1) * 64 + c * 8, 8), 8)
                h_down, lam_up = (down_ref[here, lanes], up_ref[lines, lanes])
                h_up = a * (col_h[spot, lanes] * keep) + s
                col_h[spot, lanes] = h_up
                lam_down = g + col_m[spot, lanes] * keep
                col_m[spot, lanes] = a * lam_down
                h_right, lam_rl = (row_h[spot, lanes], row_m[spot, lanes])
                lam_sum = (lam_lr + lam_rl) + (lam_down + lam_up)
                s_ref[lines, lanes] = (h_right + h_left) + (h_down + h_up)
                up_ref[lines, lanes] = lam_sum
                g_ref[lines, lanes] = (
                    (lam_lr * h_right + lam_rl * h_left)
                    + (lam_down * h_down + lam_up * h_up)
                    - s * lam_sum
                )

    def descend_two(step, held):
        row = rows - 1 - 2 * step
        held = carry_back(held, row - 1, False)
        descend(row)
        held = carry_back(held, row - 2, True)
        descend(row - 1)
        return held

    held = carry_back((nothing,) * 2, rows - 1, True)
    held = lax.fori_loop(0, devices - 1, descend_two, held)
    carry_back(held, 0, False)
    descend(1)
    descend(0)
    decay_acc[...] = jnp.zeros_like(decay_acc)
    gather_e, gather_b, gather_c = (spread_e[:part], spread_bc[:PROJ, :128], spread_bc[:PROJ, 128:])

    def finish(tile, carry):
        lines = pl.ds(pl.multiple_of(tile * pos, pos), pos)
        delta = delta_keep[tile]
        delta_low = delta.astype(bf16)
        of_b, of_c = (coef_keep[lines, :128], coef_keep[lines, 128:])
        grad_b = grad_c = None
        of_y, of_step, of_sum = ([], [], [])
        for k in range(width // 128):
            lanes = slice(k * 128, (k + 1) * 128)
            h_sum, lam_sum = (s_ref[lines, lanes], up_ref[lines, lanes])
            of_step.append((g_ref[lines, lanes] * rate_row[:, lanes]).astype(bf16))
            of_y.append((h_sum * of_c).astype(bf16))
            of_sum.append((lam_sum * of_b).astype(bf16))
            term_b, term_c = (lam_sum * source_ref[lines, lanes], h_sum * mix_ref[lines, lanes])
            grad_b = term_b if grad_b is None else grad_b + term_b
            grad_c = term_c if grad_c is None else grad_c + term_c
        of_y, of_step, of_sum = [jnp.concatenate(x, axis=1) for x in (of_y, of_step, of_sum)]
        decay_acc[...] += dot(delta_low, of_step, (1, 0))
        y_keep[tile] = jnp.transpose(dot(of_y, gather_e, (1, 1)))
        steps_keep[tile] = jnp.transpose(dot(of_step, gather_e, (1, 1)))
        sums_keep[tile] = jnp.transpose(dot(of_sum, gather_e, (1, 1)))
        coefs_keep[tile] = dot(gather_b, grad_b.astype(bf16), (1, 1)) + dot(gather_c, grad_c.astype(bf16), (1, 1))
        return carry

    lax.fori_loop(0, devices, finish, 0, unroll=8)
    step_grad = jnp.zeros((part, 16), f32)
    for tile in range(devices):
        sums, coefs = (sums_keep[tile], coefs_keep[tile])
        pre_grad = (steps_keep[tile] + got[tile, :part] * sums) * step_keep[tile]
        send[tile, :part] = y_keep[tile]
        send[tile, part : 2 * part] = delta_keep[tile] * sums
        send[tile, 2 * part : 2 * part + 16] = coefs[:16] + fine_dot(step_own, pre_grad, (0, 0))
        send[tile, 2 * part + 16 :] = coefs[16:]
        step_grad = step_grad + fine_dot(pre_grad, got[tile, 2 * part : 2 * part + 16], (1, 1))
    decay_grad = jnp.where(one_channel, decay_acc[...], 0.0)
    decay_high, decay_low = split(decay_grad)
    decay_grad = dot(decay_high, by_state, (1, 1)) + dot(decay_low, by_state, (1, 1))
    spot = (iota((part, small.shape[1]), 1) == iota((part, small.shape[1]), 0) + place[0] * part).astype(bf16)
    for at, value in ((0, step_grad), (16, decay_grad)):
        high, low = split(value)
        small[at : at + 16] = dot(high, spot, (0, 0)) + dot(low, spot, (0, 0))


def mix_kernel(
    heights, place, group, got, small_in, low, low_halo, cot, conv_own, conv_halo, pre, gate_in, grad_in,
    select_rows, table, tok, in_w, out_t, conv_kernel, norm_gain, norm_bias,
    layer_out, act_out, near, far, gate_grad_out, keep, give,
    grads, gated_ref, inner_ref, moved_ref, sums_ref, *, pair,
):
    devices, length, pos = got.shape
    model, inner_width = out_t.shape
    part = inner_width // devices
    lane = iota((1, pos), 1)
    prev, following = row_masks(heights, place[0])
    proj_grad = got[0, 2 * part :]
    for k in range(1, devices):
        proj_grad = proj_grad + got[k, 2 * part :]
    proj_grad = proj_grad.astype(bf16)
    together = max(1, 48 // part)
    for first in range(0, devices, together):
        members = range(first, first + together)
        rows = slice(first * part, (first + together) * part)
        y = jnp.concatenate([got[k, :part] for k in members], axis=0)
        inner_grad = jnp.concatenate([got[k, part : 2 * part] for k in members], axis=0)
        pre_act, gate, gated_grad = (pre[rows], gate_in[rows], grad_in[rows])
        skip = table[rows, SKIP : SKIP + 1]
        sig_pre, sig_gate = (sigmoid(pre_act), sigmoid(gate))
        inner = (pre_act * sig_pre).astype(bf16)
        inner_ref[rows] = inner
        inner = inner.astype(f32)
        silu_gate = gate * sig_gate
        mix_grad = gated_grad * silu_gate
        inner_grad = inner_grad + mix_grad * skip + dot(select_rows[rows], proj_grad, (1, 0))
        act_grad = inner_grad * (sig_pre * (1.0 + pre_act * (1.0 - sig_pre)))
        act_out[rows] = act_grad
        y_all = y + skip * inner
        gated_ref[rows] = (y_all * silu_gate).astype(bf16)
        gate_grad_out[rows] = (gated_grad * y_all * (sig_gate * (1.0 + gate * (1.0 - sig_gate)))).astype(bf16)
        field = conv_own[rows]
        upper, lower = rows_around(field, conv_halo[rows])
        fields = (upper * prev, field, lower * following)
        sums = jnp.where(lane == 9, jnp.sum(act_grad, axis=1, keepdims=True), 0.0)
        sums = jnp.where(lane == 10, jnp.sum(mix_grad * inner, axis=1, keepdims=True), sums)
        for b, moved in enumerate((from_right(act_grad), act_grad, from_left(act_grad))):
            moved_ref[b, rows] = moved.astype(bf16)
            for a in range(3):
                sums = jnp.where(lane == 3 * a + b, jnp.sum(moved * fields[a], axis=1, keepdims=True), sums)
        sums_ref[rows] = sums
    half = inner_width // 2
    top, bottom = (act_out[:half], act_out[half:])
    up = jnp.where(lane < 64, top, pltpu.roll(bottom, 64, 1))
    down = jnp.where(lane < 64, pltpu.roll(top, 64, 1), bottom)
    even = place[0] % 2 == 0
    near[...] = jnp.where(even, down, up)
    far[...] = jnp.where(even, up, down)
    gated, gate_grad = (gated_ref[...], gate_grad_out[...])
    natural = dot(gated, column_order(pos), (1, 0)).astype(bf16)
    layer = jnp.transpose(dot(out_t[...], natural, (1, 0)))
    layer_out[...] = (tok[...].astype(f32) + layer).astype(bf16)

    low_in = low[...]
    upper, lower = rows_around(low_in.astype(f32), low_halo[...].astype(f32))
    which = iota((16, 1), 0)
    masks = jnp.where(which == 0, prev, jnp.where(which == 1, 1.0, following))
    left_hand = jnp.concatenate(
        [(upper * prev).astype(bf16), low_in, (lower * following).astype(bf16), masks.astype(bf16)], axis=0
    )
    blocks = inner_width // 128
    gate_at, out_at, small_at = [k * blocks * model for k in (1, 2, 3)]
    ones = jnp.ones((16, pos), bf16)
    totals = [[], []]
    gain_sum = jnp.zeros((model, 128), f32)
    for n in range(blocks):
        columns = slice(n * 128, (n + 1) * 128)
        in_conv = conv_total = None
        for b in range(3):
            part_b = dot(left_hand, moved_ref[b, columns], (1, 1))
            for a in range(3):
                tap = conv_kernel[a, b : b + 1, columns]
                term = tap * part_b[a * model : (a + 1) * model]
                total = tap * part_b[3 * model + a : 3 * model + a + 1]
                in_conv = term if in_conv is None else in_conv + term
                conv_total = total if conv_total is None else conv_total + total
        in_gate = dot(low_in, gate_grad[columns], (1, 1))
        grads[n * model : (n + 1) * model] = in_conv
        grads[gate_at + n * model : gate_at + (n + 1) * model] = in_gate
        grads[out_at + n * model : out_at + (n + 1) * model] = dot(cot[...], gated[columns], (1, 1))
        totals[0].append(conv_total)
        totals[1].append(dot(ones, gate_grad[columns], (1, 1))[0:1])
        conv_w = in_w[:, columns].astype(f32)
        gate_w = in_w[:, inner_width + n * 128 : inner_width + (n + 1) * 128].astype(f32)
        gain_sum = gain_sum + (conv_w * in_conv + gate_w * in_gate)
    sums = jnp.broadcast_to(jnp.concatenate(totals[0] + totals[1], axis=1), (16, 2 * inner_width))
    sums_high, sums_low = split(sums)
    shift_row = (dot(sums_high, in_w[...], (1, 1)) + dot(sums_low, in_w[...], (1, 1)))[0:1]
    gain_row = patch_sums(gain_sum)
    gain_row = (gain_row - norm_bias[...].reshape(1, model) * shift_row) / norm_gain[...].reshape(1, model)
    high, mid = split(sums_ref[...])
    rest = (sums_ref[...] - high.astype(f32) - mid.astype(f32)).astype(bf16)
    chosen = (iota((16, pos), 0) == iota((16, pos), 1)).astype(bf16)
    sums = dot(chosen, high, (1, 1)) + (dot(chosen, mid, (1, 1)) + dot(chosen, rest, (1, 1)))
    norms = jnp.concatenate([gain_row, shift_row], axis=1)
    sums = jnp.where(iota((16, 1), 0) == NORM_AT - TAPS_AT, norms, sums)
    smalls = jnp.concatenate([dot(proj_grad, inner_ref[...], (1, 1)), small_in[...], sums], axis=0)
    put_blocks(grads, small_at, smalls)
    small_at = small_at + blocks * SMALL
    grads[small_at:] = jnp.zeros((grads.shape[0] - small_at, 128), f32)
    own = group[0] % 2
    if pair:
        count = keep.shape[0] // 2
        height = group[0] // 2
        for ref, side in ((keep, own), (give, 1 - own)):
            for k, at in enumerate((height, 1 - height)):
                ref[k * count : (k + 1) * count] = grads[pl.ds(pl.multiple_of((2 * side + at) * count, count), count)]
    else:
        count = keep.shape[0]
        keep[...] = grads[pl.ds(pl.multiple_of(own * count, count), count)]
        give[...] = grads[pl.ds(pl.multiple_of((1 - own) * count, count), count)]


def exit_kernel(
    heights, place, act, from_above, from_below, gate_grad, table, tok, cot, in_w,
    tokens_grad,
):
    inner_width, pos = act.shape
    model = in_w.shape[0]
    lane = iota((1, pos), 1)
    even = place[0] % 2 == 0
    above, below = (
        jnp.where(even, from_above[...], from_below[...]), jnp.where(even, from_below[...], from_above[...])
    )
    halo_top = jnp.where(lane < 64, below, pltpu.roll(above, 64, 1))
    halo_bottom = jnp.where(lane < 64, pltpu.roll(below, 64, 1), above)
    act_grad = act[...]
    prev, following = row_masks(heights, place[0])
    upper, lower = rows_around(act_grad, jnp.concatenate([halo_top, halo_bottom], axis=0))
    columns = table[...]
    taps = [[columns[:, 8 - 3 * a - b : 9 - 3 * a - b] for b in range(3)] for a in range(3)]
    conv_grad = conv_tile(upper * prev, act_grad, lower * following, taps).astype(bf16)
    halves = jnp.concatenate([conv_grad, gate_grad[...]], axis=0)
    halves = dot(halves, column_order(pos), (1, 0)).astype(bf16)
    normed_grad = dot(in_w[...], halves, (1, 0))
    xhat, inverse = normalized(flipped(tok[...]))
    scaled = normed_grad * columns[:model, GAIN : GAIN + 1]
    x_grad = (
        scaled
        - jnp.mean(scaled, axis=0, keepdims=True)
        - xhat * jnp.mean(scaled * xhat, axis=0, keepdims=True)
    ) * inverse
    x_grad = jnp.transpose(x_grad)
    tokens_grad[...] = (x_grad + cot[...].astype(f32)).astype(bf16)


def deal_kernel(group, *refs, members, pair):
    pieces, ordered = (refs[:members], refs[-1])
    (
        gain_grad, shift_grad, inproj, kernel_grad, offset, select, stepproj, stepbias, decay, skip, outproj,
    ) = refs[members:-1]
    model, inner_width = outproj.shape
    blocks = inner_width // 128
    rank = stepproj.shape[0]
    states = decay.shape[0]
    count = pieces[0].shape[0]
    for k, piece in enumerate(pieces):
        if pair:
            core, height = (group[0] % 2, group[0] // 2)
            core = 1 - core if k // 2 else core
            height = 1 - height if k % 2 else height
            slot = core * 2 + height
        else:
            slot = k % 2 * (members // 2) + k // 2
        ordered[pl.ds(pl.multiple_of(slot * count, count), count)] = piece[...]

    def rows(start, count):
        return ordered[start : start + count]

    for k in range(2 * blocks):
        inproj[:, k * 128 : (k + 1) * 128] = rows(k * model, model)
    start = 2 * blocks * model
    for k in range(blocks):
        outproj[:, k * 128 : (k + 1) * 128] = rows(start + k * model, model)
    start = start + blocks * model
    small = jnp.concatenate([rows(start + k * SMALL, SMALL) for k in range(blocks)], axis=1)
    select[:rank] = small[:rank]
    select[rank:] = small[IN:PROJ]
    stepproj[...] = small[STEP_AT : STEP_AT + rank]
    stepbias[...] = small[STEP_AT + ONE : STEP_AT + ONE + 1].reshape(stepbias.shape)
    decay[...] = small[DECAY_AT : DECAY_AT + states]
    for k in range(3):
        kernel_grad[k] = small[TAPS_AT + 3 * k : TAPS_AT + 3 * k + 3]
    offset[...] = small[OFFSET_AT : OFFSET_AT + 1].reshape(offset.shape)
    skip[...] = small[SKIP_AT : SKIP_AT + 1].reshape(skip.shape)
    norms = small[NORM_AT : NORM_AT + 1]
    gain_grad[...] = norms[:, :model].reshape(gain_grad.shape)
    shift_grad[...] = norms[:, model:].reshape(shift_grad.shape)


def vmem_call(kernel, out_shape, scalars, arrays, weights=(), scratch=(), limit=16):
    scalars = [pltpu.with_memory_space_constraint(x, pltpu.HBM) if x.ndim == 2 else x for x in scalars]
    arrays = [pltpu.with_memory_space_constraint(x, pltpu.VMEM) for x in arrays]
    arrays += [pltpu.with_memory_space_constraint(x, pltpu.HBM) for x in weights]
    return pl.pallas_call(
        kernel,
        out_shape=out_shape,
        in_specs=[pl.BlockSpec(memory_space=pltpu.SMEM)] * len(scalars)
        + [pl.BlockSpec(memory_space=pltpu.VMEM)] * len(arrays),
        out_specs=[pl.BlockSpec(memory_space=pltpu.VMEM)] * len(out_shape),
        scratch_shapes=list(scratch),
        compiler_params=pltpu.CompilerParams(vmem_limit_bytes=limit * 1024 * 1024),
    )(*scalars, *arrays)


def struct(*shape, dtype=f32):
    return jax.ShapeDtypeStruct(shape, dtype)


def inside(*shape, dtype=f32):
    return pltpu.VMEM(shape, dtype)


def scan_call(heights, place, got, table, states):
    devices, length, pos = got.shape
    inner_width = table.shape[0]
    part = inner_width // devices
    width = -(-part * states // 128) * 128
    total = devices * pos
    span = 256 if width % 256 == 0 else 128
    group = 768 if width % 768 == 0 else span
    big = pltpu.VMEM((total, width), f32)
    line = pltpu.VMEM((2 * devices * 64, 128), f32)
    column = pltpu.VMEM((pos // 2, width), f32)
    own = pltpu.VMEM((devices, part, pos), f32)
    return vmem_call(
        functools.partial(scan_kernel, part=part, states=states, span=span, group=group),
        [inside(devices, length, pos), inside(32, inner_width)],
        [heights, place],
        [got, table],
        (),
        [big] * 3
        + [pltpu.VMEM((total + pos // 2, width), f32)]
        + [big] * 3
        + [column] * 4
        + [line] * 9
        + [pltpu.VMEM((total, 2 * part), bf16)] * 3
        + [pltpu.VMEM((total, 256), f32)]
        + [own] * 5
        + [pltpu.VMEM((devices, PROJ, pos), f32), pltpu.VMEM((part, width), f32)],
        limit=36 if total <= 1024 else 60,
    )


def on_device(
    tokens, heights, cotangent, norm_gain, norm_bias, in_weight, conv_kernel, conv_bias, select_weight,
    step_weight, step_bias, decay_log, skip_gain, out_weight,
):
    _, tile_rows, grid_cols, model = tokens.shape
    inner_width = out_weight.shape[0]
    states = decay_log.shape[1]
    rank = step_weight.shape[0]
    devices = lax.axis_size("seq")
    groups = lax.axis_size("dp")
    place = lax.axis_index("seq").reshape(1)
    group = lax.axis_index("dp").reshape(1)
    pair = groups == 4
    pos = tile_rows * grid_cols
    part = inner_width // devices
    length = 2 * part + PROJ
    near_pairs = [(i, i ^ 1) for i in range(devices)]
    far_pairs = [(i, (i - 1 + 2 * (i % 2)) % devices) for i in range(devices)]

    tok, cot = (tokens.reshape(pos, model), cotangent.reshape(pos, model))
    even = place[0] % 2 == 0
    upper, lower = (tok[:grid_cols].astype(f32), tok[grid_cols:].astype(f32))
    above = lax.ppermute(jnp.where(even, upper, lower), "seq", far_pairs)
    below = lax.ppermute(jnp.where(even, lower, upper), "seq", near_pairs)
    above, group = lax.optimization_barrier((above, group))
    out_t = out_weight.T
    channels = inside(inner_width, pos)
    narrow = inside(model, pos, dtype=bf16)
    conv_own, gate, gated_grad, mix, low, cot_in, conv_rows, select_rows, table = vmem_call(
        own_kernel,
        [channels] * 4
        + [narrow] * 2
        + [inside(inner_width, model, dtype=bf16), inside(inner_width, PROJ, dtype=bf16), inside(inner_width, TABLE)],
        [],
        [],
        [
            tok, cot, in_weight, out_t, select_weight.T, conv_kernel, conv_bias, step_weight, step_bias,
            decay_log.T, skip_gain, norm_gain, norm_bias,
        ],
        [pltpu.VMEM((TABLE, inner_width), f32)],
    )
    sent, conv_halo, pre_act, low_halo = vmem_call(
        entry_kernel,
        [inside(devices, length, pos), channels, channels, narrow],
        [heights, place],
        [above, below, conv_own, mix, conv_rows, select_rows, table],
    )
    got = lax.all_to_all(sent, "seq", 0, 0, tiled=True)
    sent, small = scan_call(heights, place, got, table, states)
    got = lax.all_to_all(sent, "seq", 0, 0, tiled=True)
    blocks = inner_width // 128
    whole = -(-blocks * (3 * model + SMALL) // 2048) * 2048
    half = whole // 2
    layer_out, act_grad, near, far, gate_grad, keep, give = vmem_call(
        functools.partial(mix_kernel, pair=pair),
        [struct(pos, model, dtype=bf16), channels]
        + [inside(inner_width // 2, pos)] * 2
        + [inside(inner_width, pos, dtype=bf16)]
        + [inside(half, 128)] * 2,
        [heights, place, group],
        [
            got, small, low, low_halo, cot_in, conv_own, conv_halo, pre_act, gate, gated_grad, select_rows, table,
        ],
        [tok, in_weight, out_t, conv_kernel, norm_gain, norm_bias],
        [
            pltpu.VMEM((whole, 128), f32), pltpu.VMEM((inner_width, pos), bf16), pltpu.VMEM((inner_width, pos), bf16),
            pltpu.VMEM((3, inner_width, pos), bf16), pltpu.VMEM((inner_width, pos), f32),
        ],
    )
    from_above = lax.ppermute(far, "seq", far_pairs)
    from_below = lax.ppermute(near, "seq", near_pairs)
    swap = [(i, i ^ 1) for i in range(groups)]
    taken = lax.ppermute(give, "dp", swap)
    count = half // (groups // 2)
    if pair:
        across = [(i, i ^ 2) for i in range(groups)]
        other = lax.ppermute(keep[count:] + taken[count:], "dp", across)
        piece = keep[:count] + taken[:count]
    else:
        same_core = [list(range(c, groups, 2)) for c in range(2)]
        pieces = (keep + taken).reshape(groups // 2, count, 128)
        pieces = lax.all_to_all(pieces, "dp", 0, 0, tiled=True, axis_index_groups=same_core)
        piece, other = (pieces[0], jnp.sum(pieces[1:], axis=0))
    other, from_above, from_below = lax.optimization_barrier((other, from_above, from_below))
    shares = (piece + other).reshape(devices, count // devices, 128)
    shares = lax.all_to_all(shares, "seq", 0, 0, tiled=True)
    share = jnp.broadcast_to(jnp.sum(shares, axis=0), shares.shape)
    mine = lax.all_to_all(share, "seq", 0, 0, tiled=True).reshape(count, 128)
    mine, from_above, from_below = lax.optimization_barrier((mine, from_above, from_below))
    (tokens_grad,) = vmem_call(
        exit_kernel,
        [struct(pos, model, dtype=bf16)],
        [heights, place],
        [act_grad, from_above, from_below, gate_grad, table],
        [tok, cot, in_weight],
    )
    if pair:
        from_y = lax.ppermute(mine, "dp", across)
        from_y, tokens_grad = lax.optimization_barrier((from_y, tokens_grad))
        pieces = [mine, from_y, lax.ppermute(mine, "dp", swap), lax.ppermute(from_y, "dp", swap)]
    else:
        pieces = list(lax.all_gather(mine, "dp"))
    gain, shift, inproj, kernel, offset, select, stepproj, stepbias, decay, skip, outproj = vmem_call(
        functools.partial(deal_kernel, members=len(pieces), pair=pair),
        [
            struct(model), struct(model), struct(model, 2 * inner_width), struct(3, 3, inner_width),
            struct(inner_width), struct(rank + 2 * states, inner_width), struct(rank, inner_width),
            struct(inner_width), struct(states, inner_width), struct(inner_width), struct(model, inner_width),
        ],
        [group],
        pieces,
        (),
        [pltpu.VMEM((whole, 128), f32)],
    )
    shape = tokens.shape
    return (
        layer_out.reshape(shape), tokens_grad.reshape(shape), gain, shift, inproj, kernel, offset, select.T,
        stepproj, stepbias, decay.T, skip, outproj.T,
    )


def solution(mesh):
    tile, whole = (P("dp", "seq", None, None), P())
    return jax.shard_map(
        on_device,
        mesh=mesh,
        in_specs=(tile, P("dp", None), tile) + (whole,) * 11,
        out_specs=(tile, tile) + (whole,) * 11,
        check_vma=False,
    )
```

```python
import functools

import jax
import jax.numpy as jnp
from jax import lax
from jax.experimental import pallas as pl
from jax.experimental.pallas import tpu as pltpu
from jax.sharding import PartitionSpec as P

epsilon = 1e-05
f32, bf16 = (jnp.float32, jnp.bfloat16)
ONE, IN, OUT, PROJ = (12, 16, 32, 48)
BIAS, SKIP, GAIN, SHIFT, STEP, DECAY, TABLE = (9, 10, 11, 12, 16, 32, 48)
STEP_AT, DECAY_AT, TAPS_AT, OFFSET_AT, SKIP_AT, NORM_AT, SMALL = (48, 64, 80, 89, 90, 95, 96)


def dot(a, b, over):
    return lax.dot_general(a, b, (((over[0],), (over[1],)), ((), ())), preferred_element_type=f32)


def split(value):
    high = value.astype(bf16)
    return (high, (value - high.astype(f32)).astype(bf16))


def fine_dot(a, b, over):
    (a_high, a_low), (b_high, b_low) = (split(a), split(b))
    return dot(a_high, b_high, over) + (dot(a_low, b_high, over) + dot(a_high, b_low, over))


def iota(shape, dim):
    return lax.broadcasted_iota(jnp.int32, shape, dim)


def sigmoid(v):
    return 1.0 / (1.0 + jnp.exp(-v))


def links_up(heights, row):
    end = jnp.int32(0)
    same = row > 0
    for k in range(heights.shape[1]):
        end = end + heights[0, k]
        same = same & (end != row)
    return jnp.where(same, 1.0, 0.0).astype(f32)


def row_masks(heights, place):
    lane = iota((1, 128), 1)
    flags = [links_up(heights, 2 * place + k) for k in range(3)]
    return (jnp.where(lane < 64, flags[0], flags[1]), jnp.where(lane < 64, flags[1], flags[2]))


def rows_around(own, halo):
    lane = iota((1, 128), 1)
    upper = pltpu.roll(jnp.where(lane < 64, own, halo), 64, 1)
    lower = pltpu.roll(jnp.where(lane < 64, halo, own), 64, 1)
    return (upper, lower)


def from_left(tile):
    place = iota((1, 128), 1) & 63
    wrapped = jnp.where(place == 0, 0.0, pltpu.roll(tile, 73, 1))
    return jnp.where(place < 8, wrapped, pltpu.roll(tile, 8, 1))


def from_right(tile):
    place = iota((1, 128), 1) & 63
    wrapped = jnp.where(place == 63, 0.0, pltpu.roll(tile, 55, 1))
    return jnp.where(place >= 56, wrapped, pltpu.roll(tile, 120, 1))


def conv_tile(upper, own, lower, taps):
    left, middle, right = [
        taps[0][b] * upper + taps[1][b] * own + taps[2][b] * lower for b in range(3)
    ]
    return middle + (from_left(left) + from_right(right))


def normalized(x):
    centred = x - jnp.mean(x, axis=0, keepdims=True)
    inverse = lax.rsqrt(jnp.mean(centred * centred, axis=0, keepdims=True) + epsilon)
    return (centred * inverse, inverse)


def eye(size):
    return (iota((size, size), 0) == iota((size, size), 1)).astype(bf16)


def flipped(value):
    pieces = [value[:, k : k + 128] for k in range(0, value.shape[1], 128)]
    return jnp.concatenate([dot(eye(piece.shape[1]), piece, (1, 1)) for piece in pieces], axis=0)


def flipped_fine(value):
    high, low = split(value)
    rest = (value - high.astype(f32) - low.astype(f32)).astype(bf16)
    return flipped(high) + (flipped(low) + flipped(rest))


def patch_sums(value):
    high, low = split(value)
    ones = jnp.ones((8, value.shape[1]), bf16)
    return (dot(ones, high, (1, 1)) + dot(ones, low, (1, 1)))[0:1]


def put_blocks(ref, start, value):
    for k in range(value.shape[1] // 128):
        ref[start + k * value.shape[0] : start + (k + 1) * value.shape[0]] = value[:, k * 128 : (k + 1) * 128]


def column_order(pos):
    new, old = (iota((pos, pos), 0), iota((pos, pos), 1))
    source = (new & ~63) | ((new & 7) << 3) | ((new >> 3) & 7)
    return (source == old).astype(bf16)


def lane_maps(part, states, width):
    lane = iota((1, width), 1)
    channel = jnp.floor((lane.astype(f32) + 0.5) * (1.0 / states)).astype(jnp.int32)
    return (channel, lane - channel * states, channel < part)


def entered(rows):
    return dot(flipped(rows).astype(bf16), column_order(rows.shape[0]), (1, 0))


def own_kernel(
    tok, cot, in_w, out_t, select_t, conv_kernel, conv_bias, step_weight, step_bias, decay_t, skip_gain,
    norm_gain, norm_bias,
    conv_out, gate_out, grad_out, mix_out, low_out, cot_out, conv_rows, select_rows, table, table_t, in_keep,
):
    model, inner_width = out_t.shape
    states = decay_t.shape[0]
    rank = step_weight.shape[0]
    in_keep[...] = in_w[...]
    in_rows = flipped(in_w[...]).astype(bf16)
    conv_rows[...] = in_rows[:inner_width]
    out_rows = flipped(out_t[...]).astype(bf16)
    chosen = iota((PROJ, select_t.shape[0]), 0)
    chosen = jnp.where(chosen < rank, chosen, jnp.where(chosen < IN, -1, chosen - IN + rank))
    chosen = (chosen == iota((PROJ, select_t.shape[0]), 1)).astype(bf16)
    select_rows[...] = flipped(dot(chosen, select_t[...], (1, 0)).astype(bf16)).astype(bf16)
    table_t[...] = jnp.zeros_like(table_t)
    for k in range(3):
        table_t[3 * k : 3 * k + 3] = conv_kernel[k]
    table_t[BIAS : BIAS + 1] = conv_bias[...].reshape(1, inner_width)
    table_t[SKIP : SKIP + 1] = skip_gain[...].reshape(1, inner_width)
    table_t[GAIN : GAIN + 1, :model] = norm_gain[...].reshape(1, model)
    table_t[SHIFT : SHIFT + 1, :model] = norm_bias[...].reshape(1, model)
    table_t[STEP : STEP + rank] = step_weight[...]
    table_t[STEP + ONE : STEP + ONE + 1] = step_bias[...].reshape(1, inner_width)
    table_t[DECAY : DECAY + states] = decay_t[...]
    columns = flipped_fine(table_t[...])
    table[...] = columns
    gain, shift = (columns[:model, GAIN : GAIN + 1], columns[:model, SHIFT : SHIFT + 1])
    low = (normalized(entered(tok[...]))[0] * gain + shift).astype(bf16)
    cot_in = entered(cot[...]).astype(bf16)
    low_out[...] = low
    cot_out[...] = cot_in
    both = dot(in_rows, low, (1, 0))
    conv_out[...] = both[:inner_width]
    gate = both[inner_width:]
    gated_grad = dot(out_rows, cot_in, (1, 0))
    gate_out[...] = gate
    grad_out[...] = gated_grad
    mix_out[...] = gated_grad * (gate * sigmoid(gate))


def entry_kernel(
    heights, place, above, below, conv_own, mix, conv_rows, select_rows, table,
    send, halo_out, pre_out, low_halo_out,
):
    devices = send.shape[0]
    inner_width = conv_own.shape[0]
    model = conv_rows.shape[1]
    part = inner_width // devices
    columns = table[...]
    gain, shift = (columns[:model, GAIN : GAIN + 1], columns[:model, SHIFT : SHIFT + 1])
    even = place[0] % 2 == 0
    halo = jnp.concatenate(
        [jnp.where(even, below[...], above[...]), jnp.where(even, above[...], below[...])], axis=0
    ).astype(bf16)
    low_halo = (normalized(entered(halo))[0] * gain + shift).astype(bf16)
    low_halo_out[...] = low_halo
    around = dot(conv_rows[...], low_halo, (1, 0))
    halo_out[...] = around
    conv_in = conv_own[...]
    prev, following = row_masks(heights, place[0])
    upper, lower = rows_around(conv_in, around)
    taps = [[columns[:, 3 * a + b : 3 * a + b + 1] for b in range(3)] for a in range(3)]
    pre_act = columns[:, BIAS : BIAS + 1] + conv_tile(upper * prev, conv_in, lower * following, taps)
    inner = (pre_act * sigmoid(pre_act)).astype(bf16)
    proj = dot(flipped(select_rows[...]).astype(bf16), inner, (1, 0))
    proj = jnp.where(iota(proj.shape, 0) == ONE, 1.0, proj)
    pre_out[...] = pre_act
    inner = inner.astype(f32)
    for k in range(devices):
        send[k, :part] = inner[k * part : (k + 1) * part]
        send[k, part : 2 * part] = mix[k * part : (k + 1) * part]
        send[k, 2 * part :] = proj


def scan_kernel(
    heights, place, got, table,
    send, small,
    a_ref, s_ref, g_ref, down_ref, up_ref, source_ref, mix_ref, col_h, col_m, row_h, row_m,
    prod, end_lr, end_rl, back_lr, back_rl, in_lr, in_rl, tail_lr, tail_rl,
    lhs_d, lhs_u, lhs_m, coef_keep, step_keep, delta_keep, y_keep, steps_keep, sums_keep, coefs_keep, decay_acc, *, part, states, span, group,
):
    devices, _, pos = got.shape
    rows = 2 * devices
    width = a_ref.shape[1]
    own_rows = table[pl.ds(pl.multiple_of(place[0] * part, 4), part), :]
    channel, state, live = lane_maps(part, states, width)
    twice = iota((2 * part, 1), 0)
    twice = jnp.where(twice >= part, twice - part, twice)
    spread_e = ((twice == channel) & live).astype(bf16)
    coef = iota((2 * PROJ, 1), 0)
    coef = jnp.where(coef >= PROJ, coef - PROJ, coef)
    near = state[:, :128]
    spread_bc = jnp.concatenate([coef - IN == near, coef - OUT == near], axis=1).astype(bf16)
    by_state = ((iota((states, 1), 0) == state) & live).astype(bf16)
    rate = -jnp.exp(own_rows[:, DECAY : DECAY + states])
    one_channel = (iota((part, 1), 0) == channel) & live
    rate_high, rate_low = split(rate)
    rate_rest = split(rate - rate_high.astype(f32) - rate_low.astype(f32))[0]
    rate_row = sum(dot(piece, by_state, (1, 0)) for piece in (rate_high, rate_low, rate_rest))
    rate_row = jnp.sum(jnp.where(one_channel, rate_row, 0.0), axis=0, keepdims=True)
    rate_two = rate_row * 1.4426950408889634
    step_own = own_rows[:, STEP : STEP + 16]
    step_high, step_low = split(step_own)
    step_three = jnp.concatenate([step_high, step_high, step_low], axis=1)

    def turned(value):
        return jnp.transpose(jnp.concatenate(split(value), axis=0))

    for tile in range(devices):
        lines = slice(tile * pos, (tile + 1) * pos)
        inner_own = got[tile, :part]
        proj = got[tile, 2 * part :]
        high, low = split(proj[:16])
        pre_step = dot(step_three, jnp.concatenate([high, low, high], axis=0), (1, 0))
        tail = jnp.exp(-jnp.abs(pre_step))
        tail = jnp.where(tail < 1e-3, tail * (1.0 - 0.5 * tail), jnp.log(1.0 + tail))
        delta = jnp.maximum(pre_step, 0.0) + tail
        step_keep[tile] = sigmoid(pre_step)
        delta_keep[tile] = delta
        lhs_d[lines, :] = turned(delta)
        lhs_u[lines, :] = turned(delta * inner_own)
        lhs_m[lines, :] = turned(got[tile, part : 2 * part])
        coef_keep[lines, :] = dot(turned(proj), spread_bc, (1, 0))

    for k in range(width // span):
        lanes = slice(k * span, (k + 1) * span)

        def prepare(tile, carry):
            lines = pl.ds(pl.multiple_of(tile * pos, pos), pos)
            of_delta, of_source, of_mix = (lhs_d[lines, :], lhs_u[lines, :], lhs_m[lines, :])
            a_ref[lines, lanes] = jnp.exp2(dot(of_delta, spread_e[:, lanes], (1, 0)) * rate_two[:, lanes])
            source = dot(of_source, spread_e[:, lanes], (1, 0))
            mix = dot(of_mix, spread_e[:, lanes], (1, 0))
            source_ref[lines, lanes] = source
            mix_ref[lines, lanes] = mix
            for j in range(span // 128):
                tile_lanes = slice(k * span + j * 128, k * span + (j + 1) * 128)
                piece = slice(j * 128, (j + 1) * 128)
                s_ref[lines, tile_lanes] = source[:, piece] * coef_keep[lines, :128]
                g_ref[lines, tile_lanes] = mix[:, piece] * coef_keep[lines, 128:]
            return carry

        lax.fori_loop(0, devices, prepare, 0, unroll=8)
    down_ref[:64] = jnp.zeros((64, width), f32)
    col_m[...] = jnp.zeros_like(col_m)
    right, left = (range(8), range(7, -1, -1))
    nothing = jnp.zeros((8, 128), f32)

    def packed(row, piece):
        return pl.ds(row * 64 + piece, 8, stride=8)

    def chain(state, row, order, ends, starts):
        for c in order:
            line = pl.ds(pl.multiple_of(row * 64 + c * 8, 8), 8)
            starts[line, :] = state
            state = prod[line, :] * state + ends[line, :]
        return state

    def carry_on(held, row, odd):
        ahead, behind = held
        ahead = ahead * links_up(heights, row)
        if odd:
            ahead = chain(ahead, row, left, end_rl, in_rl)
            behind = chain(behind, row, left, back_lr, tail_lr)
        else:
            ahead = chain(ahead, row, right, end_lr, in_lr)
            behind = chain(behind, row, right, back_rl, tail_rl)
        return (ahead, behind * links_up(heights, row + 1))

    def carry_back(held, row, odd):
        behind, ahead = held
        behind = behind * links_up(heights, row + 1)
        if odd:
            behind = chain(behind, row, right, end_lr, in_lr)
            ahead = chain(ahead, row, right, back_rl, tail_rl)
        else:
            behind = chain(behind, row, left, end_rl, in_rl)
            ahead = chain(ahead, row, left, back_lr, tail_lr)
        return (behind, ahead * links_up(heights, row))

    def ascend(row):
        keep = links_up(heights, row)
        for k in range(width // group):
            lanes = slice(k * group, (k + 1) * group)
            whole = lr = rl = mlr = mrl = None
            for c in range(8):
                lines = pl.ds(pl.multiple_of(row * 64 + c * 8, 8), 8)
                spot = slice(c * 8, c * 8 + 8)
                a, s, g = (a_ref[lines, lanes], s_ref[lines, lanes], g_ref[lines, lanes])
                before, here = [
                    pl.ds(pl.multiple_of((row + step) * 64 + c * 8, 8), 8) for step in range(2)
                ]
                state_h = a * (down_ref[before, lanes] * keep) + s
                down_ref[here, lanes] = state_h
                lam = g + col_m[spot, lanes] * keep
                col_m[spot, lanes] = a * lam
                up_ref[lines, lanes] = lam
                if c == 0:
                    whole, lr, rl, mlr, mrl = (a, s, s, a * g, a * g)
                else:
                    lr = a * lr + s
                    rl = rl + whole * s
                    whole = whole * a
                    mlr = mlr + whole * g
                    mrl = a * (mrl + g)
            for j in range(group // 128):
                spot = packed(row, k * (group // 128) + j)
                piece = slice(j * 128, (j + 1) * 128)
                prod[spot, :] = whole[:, piece]
                end_lr[spot, :] = lr[:, piece]
                end_rl[spot, :] = rl[:, piece]
                back_lr[spot, :] = mlr[:, piece]
                back_rl[spot, :] = mrl[:, piece]

    def ascend_two(step, held):
        row = 2 * step + 1
        held = carry_on(held, row - 1, False)
        ascend(row)
        held = carry_on(held, row, True)
        ascend(row + 1)
        return held

    ascend(0)
    held = lax.fori_loop(0, devices - 1, ascend_two, (nothing,) * 2)
    held = carry_on(held, rows - 2, False)
    ascend(rows - 1)
    carry_on(held, rows - 1, True)
    col_h[...] = jnp.zeros_like(col_h)
    col_m[...] = jnp.zeros_like(col_m)

    def descend(row):
        keep = links_up(heights, row + 1)

        def edge(ref, k):
            pieces = [ref[packed(row, k * (group // 128) + j), :] for j in range(group // 128)]
            return pieces[0] if len(pieces) == 1 else jnp.concatenate(pieces, axis=1)

        for k in range(width // group):
            lanes = slice(k * group, (k + 1) * group)
            h_right, m_left = (edge(in_lr, k), edge(tail_rl, k))
            for c in range(8):
                lines = pl.ds(pl.multiple_of(row * 64 + c * 8, 8), 8)
                spot = slice(c * 8, c * 8 + 8)
                a, s, g = (a_ref[lines, lanes], s_ref[lines, lanes], g_ref[lines, lanes])
                h_right = a * h_right + s
                lam = g + m_left
                m_left = a * lam
                row_h[spot, lanes] = h_right
                row_m[spot, lanes] = lam
            h_left, m_right = (edge(in_rl, k), edge(tail_lr, k))
            for c in range(7, -1, -1):
                lines = pl.ds(pl.multiple_of(row * 64 + c * 8, 8), 8)
                spot = slice(c * 8, c * 8 + 8)
                a, s, g = (a_ref[lines, lanes], s_ref[lines, lanes], g_ref[lines, lanes])
                h_left = a * h_left + s
                lam_lr = g + m_right
                m_right = a * lam_lr
                here = pl.ds(pl.multiple_of((row + 1) * 64 + c * 8, 8), 8)
                h_down, lam_up = (down_ref[here, lanes], up_ref[lines, lanes])
                h_up = a * (col_h[spot, lanes] * keep) + s
                col_h[spot, lanes] = h_up
                lam_down = g + col_m[spot, lanes] * keep
                col_m[spot, lanes] = a * lam_down
                h_right, lam_rl = (row_h[spot, lanes], row_m[spot, lanes])
                lam_sum = (lam_lr + lam_rl) + (lam_down + lam_up)
                s_ref[lines, lanes] = (h_right + h_left) + (h_down + h_up)
                up_ref[lines, lanes] = lam_sum
                g_ref[lines, lanes] = (
                    (lam_lr * h_right + lam_rl * h_left)
                    + (lam_down * h_down + lam_up * h_up)
                    - s * lam_sum
                )

    def descend_two(step, held):
        row = rows - 1 - 2 * step
        held = carry_back(held, row - 1, False)
        descend(row)
        held = carry_back(held, row - 2, True)
        descend(row - 1)
        return held

    held = carry_back((nothing,) * 2, rows - 1, True)
    held = lax.fori_loop(0, devices - 1, descend_two, held)
    carry_back(held, 0, False)
    descend(1)
    descend(0)
    decay_acc[...] = jnp.zeros_like(decay_acc)
    gather_e, gather_b, gather_c = (spread_e[:part], spread_bc[:PROJ, :128], spread_bc[:PROJ, 128:])

    def finish(tile, carry):
        lines = pl.ds(pl.multiple_of(tile * pos, pos), pos)
        delta = delta_keep[tile]
        delta_low = delta.astype(bf16)
        of_b, of_c = (coef_keep[lines, :128], coef_keep[lines, 128:])
        grad_b = grad_c = None
        of_y, of_step, of_sum = ([], [], [])
        for k in range(width // 128):
            lanes = slice(k * 128, (k + 1) * 128)
            h_sum, lam_sum = (s_ref[lines, lanes], up_ref[lines, lanes])
            of_step.append((g_ref[lines, lanes] * rate_row[:, lanes]).astype(bf16))
            of_y.append((h_sum * of_c).astype(bf16))
            of_sum.append((lam_sum * of_b).astype(bf16))
            term_b, term_c = (lam_sum * source_ref[lines, lanes], h_sum * mix_ref[lines, lanes])
            grad_b = term_b if grad_b is None else grad_b + term_b
            grad_c = term_c if grad_c is None else grad_c + term_c
        of_y, of_step, of_sum = [jnp.concatenate(x, axis=1) for x in (of_y, of_step, of_sum)]
        decay_acc[...] += dot(delta_low, of_step, (1, 0))
        y_keep[tile] = jnp.transpose(dot(of_y, gather_e, (1, 1)))
        steps_keep[tile] = jnp.transpose(dot(of_step, gather_e, (1, 1)))
        sums_keep[tile] = jnp.transpose(dot(of_sum, gather_e, (1, 1)))
        coefs_keep[tile] = dot(gather_b, grad_b.astype(bf16), (1, 1)) + dot(gather_c, grad_c.astype(bf16), (1, 1))
        return carry

    lax.fori_loop(0, devices, finish, 0, unroll=8)
    step_grad = jnp.zeros((part, 16), f32)
    for tile in range(devices):
        sums, coefs = (sums_keep[tile], coefs_keep[tile])
        pre_grad = (steps_keep[tile] + got[tile, :part] * sums) * step_keep[tile]
        send[tile, :part] = y_keep[tile]
        send[tile, part : 2 * part] = delta_keep[tile] * sums
        send[tile, 2 * part : 2 * part + 16] = coefs[:16] + fine_dot(step_own, pre_grad, (0, 0))
        send[tile, 2 * part + 16 :] = coefs[16:]
        step_grad = step_grad + fine_dot(pre_grad, got[tile, 2 * part : 2 * part + 16], (1, 1))
    decay_grad = jnp.where(one_channel, decay_acc[...], 0.0)
    decay_high, decay_low = split(decay_grad)
    decay_grad = dot(decay_high, by_state, (1, 1)) + dot(decay_low, by_state, (1, 1))
    spot = (iota((part, small.shape[1]), 1) == iota((part, small.shape[1]), 0) + place[0] * part).astype(bf16)
    for at, value in ((0, step_grad), (16, decay_grad)):
        high, low = split(value)
        small[at : at + 16] = dot(high, spot, (0, 0)) + dot(low, spot, (0, 0))


def mix_kernel(
    heights, place, group, got, small_in, low, low_halo, cot, conv_own, conv_halo, pre, gate_in, grad_in,
    select_rows, table, table_t, in_w,
    act_out, near, far, gate_grad_out, gated_ref, keep, give,
    grads, inner_ref, moved_ref, sums_ref, *, pair,
):
    devices, length, pos = got.shape
    model, inner_width = (low.shape[0], pre.shape[0])
    part = inner_width // devices
    lane = iota((1, pos), 1)
    prev, following = row_masks(heights, place[0])
    proj_grad = got[0, 2 * part :]
    for k in range(1, devices):
        proj_grad = proj_grad + got[k, 2 * part :]
    proj_grad = proj_grad.astype(bf16)
    together = max(1, 48 // part)
    for first in range(0, devices, together):
        members = range(first, first + together)
        rows = slice(first * part, (first + together) * part)
        y = jnp.concatenate([got[k, :part] for k in members], axis=0)
        inner_grad = jnp.concatenate([got[k, part : 2 * part] for k in members], axis=0)
        pre_act, gate, gated_grad = (pre[rows], gate_in[rows], grad_in[rows])
        skip = table[rows, SKIP : SKIP + 1]
        sig_pre, sig_gate = (sigmoid(pre_act), sigmoid(gate))
        inner = (pre_act * sig_pre).astype(bf16)
        inner_ref[rows] = inner
        inner = inner.astype(f32)
        silu_gate = gate * sig_gate
        mix_grad = gated_grad * silu_gate
        inner_grad = inner_grad + mix_grad * skip + dot(select_rows[rows], proj_grad, (1, 0))
        act_grad = inner_grad * (sig_pre * (1.0 + pre_act * (1.0 - sig_pre)))
        act_out[rows] = act_grad
        y_all = y + skip * inner
        gated_ref[rows] = (y_all * silu_gate).astype(bf16)
        gate_grad_out[rows] = (gated_grad * y_all * (sig_gate * (1.0 + gate * (1.0 - sig_gate)))).astype(bf16)
        field = conv_own[rows]
        upper, lower = rows_around(field, conv_halo[rows])
        fields = (upper * prev, field, lower * following)
        sums = jnp.where(lane == 9, jnp.sum(act_grad, axis=1, keepdims=True), 0.0)
        sums = jnp.where(lane == 10, jnp.sum(mix_grad * inner, axis=1, keepdims=True), sums)
        for b, moved in enumerate((from_right(act_grad), act_grad, from_left(act_grad))):
            moved_ref[b, rows] = moved.astype(bf16)
            for a in range(3):
                sums = jnp.where(lane == 3 * a + b, jnp.sum(moved * fields[a], axis=1, keepdims=True), sums)
        sums_ref[rows] = sums
    conv_w = in_w[:, :inner_width].astype(f32)
    beyond = None
    for b in range(3):
        weights = [conv_w * table_t[3 * a + b : 3 * a + b + 1] for a in (0, 2)]
        term = dot(jnp.concatenate(weights, axis=0).astype(bf16), moved_ref[b], (1, 0))
        beyond = term if beyond is None else beyond + term
    beyond = jnp.where(lane < 64, beyond[:model] * prev, beyond[model:] * following)
    top, bottom = (beyond[: model // 2], beyond[model // 2 :])
    up = jnp.where(lane < 64, top, pltpu.roll(bottom, 64, 1))
    down = jnp.where(lane < 64, pltpu.roll(top, 64, 1), bottom)
    even = place[0] % 2 == 0
    near[...] = jnp.where(even, down, up)
    far[...] = jnp.where(even, up, down)
    gated, gate_grad = (gated_ref[...], gate_grad_out[...])

    low_in = low[...]
    upper, lower = rows_around(low_in.astype(f32), low_halo[...].astype(f32))
    which = iota((16, 1), 0)
    masks = jnp.where(which == 0, prev, jnp.where(which == 1, 1.0, following))
    left_hand = jnp.concatenate(
        [(upper * prev).astype(bf16), low_in, (lower * following).astype(bf16), masks.astype(bf16)], axis=0
    )
    blocks = inner_width // 128
    gate_at, out_at, small_at = [k * blocks * model for k in (1, 2, 3)]
    ones = jnp.ones((16, pos), bf16)
    totals = [[], []]
    gain_sum = jnp.zeros((model, 128), f32)
    for n in range(blocks):
        columns = slice(n * 128, (n + 1) * 128)
        in_conv = conv_total = None
        for b in range(3):
            part_b = dot(left_hand, moved_ref[b, columns], (1, 1))
            for a in range(3):
                tap = table_t[3 * a + b : 3 * a + b + 1, columns]
                term = tap * part_b[a * model : (a + 1) * model]
                total = tap * part_b[3 * model + a : 3 * model + a + 1]
                in_conv = term if in_conv is None else in_conv + term
                conv_total = total if conv_total is None else conv_total + total
        in_gate = dot(low_in, gate_grad[columns], (1, 1))
        grads[n * model : (n + 1) * model] = in_conv
        grads[gate_at + n * model : gate_at + (n + 1) * model] = in_gate
        grads[out_at + n * model : out_at + (n + 1) * model] = dot(cot[...], gated[columns], (1, 1))
        totals[0].append(conv_total)
        totals[1].append(dot(ones, gate_grad[columns], (1, 1))[0:1])
        conv_w = in_w[:, columns].astype(f32)
        gate_w = in_w[:, inner_width + n * 128 : inner_width + (n + 1) * 128].astype(f32)
        gain_sum = gain_sum + (conv_w * in_conv + gate_w * in_gate)
    sums = jnp.broadcast_to(jnp.concatenate(totals[0] + totals[1], axis=1), (16, 2 * inner_width))
    sums_high, sums_low = split(sums)
    shift_row = (dot(sums_high, in_w[...], (1, 1)) + dot(sums_low, in_w[...], (1, 1)))[0:1]
    gain_row = patch_sums(gain_sum)
    gain, shift = (table_t[GAIN : GAIN + 1, :model], table_t[SHIFT : SHIFT + 1, :model])
    gain_row = (gain_row - shift * shift_row) / gain
    high, mid = split(sums_ref[...])
    rest = (sums_ref[...] - high.astype(f32) - mid.astype(f32)).astype(bf16)
    chosen = (iota((16, pos), 0) == iota((16, pos), 1)).astype(bf16)
    sums = dot(chosen, high, (1, 1)) + (dot(chosen, mid, (1, 1)) + dot(chosen, rest, (1, 1)))
    norms = jnp.concatenate([gain_row, shift_row], axis=1)
    sums = jnp.where(iota((16, 1), 0) == NORM_AT - TAPS_AT, norms, sums)
    smalls = jnp.concatenate([dot(proj_grad, inner_ref[...], (1, 1)), small_in[...], sums], axis=0)
    put_blocks(grads, small_at, smalls)
    small_at = small_at + blocks * SMALL
    grads[small_at:] = jnp.zeros((grads.shape[0] - small_at, 128), f32)
    own = group[0] % 2
    if pair:
        count = keep.shape[0] // 2
        height = group[0] // 2
        for ref, side in ((keep, own), (give, 1 - own)):
            for k, at in enumerate((height, 1 - height)):
                ref[k * count : (k + 1) * count] = grads[pl.ds(pl.multiple_of((2 * side + at) * count, count), count)]
    else:
        count = keep.shape[0]
        keep[...] = grads[pl.ds(pl.multiple_of(own * count, count), count)]
        give[...] = grads[pl.ds(pl.multiple_of((1 - own) * count, count), count)]


def exit_kernel(
    heights, place, act, from_above, from_below, gate_grad, gated, table, in_w, tok, cot, out_t,
    tokens_grad, layer_out,
):
    inner_width, pos = act.shape
    model = in_w.shape[0]
    lane = iota((1, pos), 1)
    even = place[0] % 2 == 0
    above, below = (
        jnp.where(even, from_above[...], from_below[...]), jnp.where(even, from_below[...], from_above[...])
    )
    top = jnp.where(lane < 64, above, pltpu.roll(below, 64, 1))
    bottom = jnp.where(lane < 64, pltpu.roll(above, 64, 1), below)
    beyond_high, beyond_low = split(jnp.concatenate([top, bottom], axis=0))
    act_grad = act[...]
    prev, following = row_masks(heights, place[0])
    upper, lower = rows_around(act_grad, jnp.zeros_like(act_grad))
    columns = table[...]
    taps = [[columns[:, 8 - 3 * a - b : 9 - 3 * a - b] for b in range(3)] for a in range(3)]
    conv_grad = conv_tile(upper * prev, act_grad, lower * following, taps).astype(bf16)
    natural = jnp.concatenate([conv_grad, gate_grad[...], gated[...]], axis=0)
    order = column_order(pos)
    natural = dot(natural, order, (1, 0)).astype(bf16)
    layer = jnp.transpose(dot(out_t[...], natural[2 * inner_width :], (1, 0)))
    layer_out[...] = (tok[...].astype(f32) + layer).astype(bf16)
    normed_grad = dot(in_w[...], natural[: 2 * inner_width], (1, 0))
    normed_grad = normed_grad + (dot(beyond_high, order, (1, 0)) + dot(beyond_low, order, (1, 0)))
    xhat, inverse = normalized(flipped(tok[...]))
    scaled = normed_grad * columns[:model, GAIN : GAIN + 1]
    x_grad = (
        scaled
        - jnp.mean(scaled, axis=0, keepdims=True)
        - xhat * jnp.mean(scaled * xhat, axis=0, keepdims=True)
    ) * inverse
    x_grad = jnp.transpose(x_grad)
    tokens_grad[...] = (x_grad + cot[...].astype(f32)).astype(bf16)


def deal_kernel(group, *refs, members, pair):
    pieces, ordered = (refs[:members], refs[-1])
    (
        gain_grad, shift_grad, inproj, kernel_grad, offset, select, stepproj, stepbias, decay, skip, outproj,
    ) = refs[members:-1]
    model, inner_width = outproj.shape
    blocks = inner_width // 128
    rank = stepproj.shape[0]
    states = decay.shape[0]
    count = pieces[0].shape[0]
    for k, piece in enumerate(pieces):
        if pair:
            core, height = (group[0] % 2, group[0] // 2)
            core = 1 - core if k // 2 else core
            height = 1 - height if k % 2 else height
            slot = core * 2 + height
        else:
            slot = k % 2 * (members // 2) + k // 2
        ordered[pl.ds(pl.multiple_of(slot * count, count), count)] = piece[...]

    def rows(start, count):
        return ordered[start : start + count]

    for k in range(2 * blocks):
        inproj[:, k * 128 : (k + 1) * 128] = rows(k * model, model)
    start = 2 * blocks * model
    for k in range(blocks):
        outproj[:, k * 128 : (k + 1) * 128] = rows(start + k * model, model)
    start = start + blocks * model
    small = jnp.concatenate([rows(start + k * SMALL, SMALL) for k in range(blocks)], axis=1)
    select[:rank] = small[:rank]
    select[rank:] = small[IN:PROJ]
    stepproj[...] = small[STEP_AT : STEP_AT + rank]
    stepbias[...] = small[STEP_AT + ONE : STEP_AT + ONE + 1].reshape(stepbias.shape)
    decay[...] = small[DECAY_AT : DECAY_AT + states]
    for k in range(3):
        kernel_grad[k] = small[TAPS_AT + 3 * k : TAPS_AT + 3 * k + 3]
    offset[...] = small[OFFSET_AT : OFFSET_AT + 1].reshape(offset.shape)
    skip[...] = small[SKIP_AT : SKIP_AT + 1].reshape(skip.shape)
    norms = small[NORM_AT : NORM_AT + 1]
    gain_grad[...] = norms[:, :model].reshape(gain_grad.shape)
    shift_grad[...] = norms[:, model:].reshape(shift_grad.shape)


def vmem_call(kernel, out_shape, scalars, arrays, weights=(), scratch=(), limit=16):
    scalars = [pltpu.with_memory_space_constraint(x, pltpu.HBM) if x.ndim == 2 else x for x in scalars]
    arrays = [pltpu.with_memory_space_constraint(x, pltpu.VMEM) for x in arrays]
    arrays += [pltpu.with_memory_space_constraint(x, pltpu.HBM) for x in weights]
    return pl.pallas_call(
        kernel,
        out_shape=out_shape,
        in_specs=[pl.BlockSpec(memory_space=pltpu.SMEM)] * len(scalars)
        + [pl.BlockSpec(memory_space=pltpu.VMEM)] * len(arrays),
        out_specs=[pl.BlockSpec(memory_space=pltpu.VMEM)] * len(out_shape),
        scratch_shapes=list(scratch),
        compiler_params=pltpu.CompilerParams(vmem_limit_bytes=limit * 1024 * 1024),
    )(*scalars, *arrays)


def struct(*shape, dtype=f32):
    return jax.ShapeDtypeStruct(shape, dtype)


def inside(*shape, dtype=f32):
    return pltpu.VMEM(shape, dtype)


def scan_call(heights, place, got, table, states):
    devices, length, pos = got.shape
    inner_width = table.shape[0]
    part = inner_width // devices
    width = -(-part * states // 128) * 128
    total = devices * pos
    span = 256 if width % 256 == 0 else 128
    group = 768 if width % 768 == 0 else span
    big = pltpu.VMEM((total, width), f32)
    line = pltpu.VMEM((2 * devices * 64, 128), f32)
    column = pltpu.VMEM((pos // 2, width), f32)
    own = pltpu.VMEM((devices, part, pos), f32)
    return vmem_call(
        functools.partial(scan_kernel, part=part, states=states, span=span, group=group),
        [inside(devices, length, pos), inside(32, inner_width)],
        [heights, place],
        [got, table],
        (),
        [big] * 3
        + [pltpu.VMEM((total + pos // 2, width), f32)]
        + [big] * 3
        + [column] * 4
        + [line] * 9
        + [pltpu.VMEM((total, 2 * part), bf16)] * 3
        + [pltpu.VMEM((total, 256), f32)]
        + [own] * 5
        + [pltpu.VMEM((devices, PROJ, pos), f32), pltpu.VMEM((part, width), f32)],
        limit=36 if total <= 1024 else 60,
    )


def on_device(
    tokens, heights, cotangent, norm_gain, norm_bias, in_weight, conv_kernel, conv_bias, select_weight,
    step_weight, step_bias, decay_log, skip_gain, out_weight,
):
    _, tile_rows, grid_cols, model = tokens.shape
    inner_width = out_weight.shape[0]
    states = decay_log.shape[1]
    rank = step_weight.shape[0]
    devices = lax.axis_size("seq")
    groups = lax.axis_size("dp")
    place = lax.axis_index("seq").reshape(1)
    group = lax.axis_index("dp").reshape(1)
    pair = groups == 4
    pos = tile_rows * grid_cols
    part = inner_width // devices
    length = 2 * part + PROJ
    near_pairs = [(i, i ^ 1) for i in range(devices)]
    far_pairs = [(i, (i - 1 + 2 * (i % 2)) % devices) for i in range(devices)]

    tok, cot = (tokens.reshape(pos, model), cotangent.reshape(pos, model))
    even = place[0] % 2 == 0
    upper, lower = (tok[:grid_cols].astype(f32), tok[grid_cols:].astype(f32))
    above = lax.ppermute(jnp.where(even, upper, lower), "seq", far_pairs)
    below = lax.ppermute(jnp.where(even, lower, upper), "seq", near_pairs)
    above, group = lax.optimization_barrier((above, group))
    out_t = out_weight.T
    channels = inside(inner_width, pos)
    narrow = inside(model, pos, dtype=bf16)
    conv_own, gate, gated_grad, mix, low, cot_in, conv_rows, select_rows, table, table_t, in_keep = vmem_call(
        own_kernel,
        [channels] * 4
        + [narrow] * 2
        + [
            inside(inner_width, model, dtype=bf16), inside(inner_width, PROJ, dtype=bf16), inside(inner_width, TABLE),
            inside(TABLE, inner_width), inside(model, 2 * inner_width, dtype=bf16),
        ],
        [],
        [],
        [
            tok, cot, in_weight, out_t, select_weight.T, conv_kernel, conv_bias, step_weight, step_bias,
            decay_log.T, skip_gain, norm_gain, norm_bias,
        ],
    )
    sent, conv_halo, pre_act, low_halo = vmem_call(
        entry_kernel,
        [inside(devices, length, pos), channels, channels, narrow],
        [heights, place],
        [above, below, conv_own, mix, conv_rows, select_rows, table],
    )
    got = lax.all_to_all(sent, "seq", 0, 0, tiled=True)
    sent, small = scan_call(heights, place, got, table, states)
    got = lax.all_to_all(sent, "seq", 0, 0, tiled=True)
    blocks = inner_width // 128
    whole = -(-blocks * (3 * model + SMALL) // 2048) * 2048
    half = whole // 2
    act_grad, near, far, gate_grad, gated, keep, give = vmem_call(
        functools.partial(mix_kernel, pair=pair),
        [channels]
        + [inside(model // 2, pos)] * 2
        + [inside(inner_width, pos, dtype=bf16)] * 2
        + [inside(half, 128)] * 2,
        [heights, place, group],
        [
            got, small, low, low_halo, cot_in, conv_own, conv_halo, pre_act, gate, gated_grad, select_rows, table,
            table_t, in_keep,
        ],
        (),
        [
            pltpu.VMEM((whole, 128), f32), pltpu.VMEM((inner_width, pos), bf16),
            pltpu.VMEM((3, inner_width, pos), bf16), pltpu.VMEM((inner_width, pos), f32),
        ],
    )
    from_above = lax.ppermute(far, "seq", far_pairs)
    from_below = lax.ppermute(near, "seq", near_pairs)
    swap = [(i, i ^ 1) for i in range(groups)]
    taken = lax.ppermute(give, "dp", swap)
    count = half // (groups // 2)
    if pair:
        across = [(i, i ^ 2) for i in range(groups)]
        other = lax.ppermute(keep[count:] + taken[count:], "dp", across)
        piece = keep[:count] + taken[:count]
    else:
        same_core = [list(range(c, groups, 2)) for c in range(2)]
        pieces = (keep + taken).reshape(groups // 2, count, 128)
        pieces = lax.all_to_all(pieces, "dp", 0, 0, tiled=True, axis_index_groups=same_core)
        piece, other = (pieces[0], jnp.sum(pieces[1:], axis=0))
    other, from_above, from_below = lax.optimization_barrier((other, from_above, from_below))
    shares = (piece + other).reshape(devices, count // devices, 128)
    shares = lax.all_to_all(shares, "seq", 0, 0, tiled=True)
    share = jnp.broadcast_to(jnp.sum(shares, axis=0), shares.shape)
    mine = lax.all_to_all(share, "seq", 0, 0, tiled=True).reshape(count, 128)
    mine, from_above, from_below = lax.optimization_barrier((mine, from_above, from_below))
    tokens_grad, layer_out = vmem_call(
        exit_kernel,
        [struct(pos, model, dtype=bf16)] * 2,
        [heights, place],
        [act_grad, from_above, from_below, gate_grad, gated, table, in_keep],
        [tok, cot, out_t],
    )
    if pair:
        from_y = lax.ppermute(mine, "dp", across)
        from_y, tokens_grad = lax.optimization_barrier((from_y, tokens_grad))
        pieces = [mine, from_y, lax.ppermute(mine, "dp", swap), lax.ppermute(from_y, "dp", swap)]
    else:
        pieces = list(lax.all_gather(mine, "dp"))
    gain, shift, inproj, kernel, offset, select, stepproj, stepbias, decay, skip, outproj = vmem_call(
        functools.partial(deal_kernel, members=len(pieces), pair=pair),
        [
            struct(model), struct(model), struct(model, 2 * inner_width), struct(3, 3, inner_width),
            struct(inner_width), struct(rank + 2 * states, inner_width), struct(rank, inner_width),
            struct(inner_width), struct(states, inner_width), struct(inner_width), struct(model, inner_width),
        ],
        [group],
        pieces,
        (),
        [pltpu.VMEM((whole, 128), f32)],
    )
    shape = tokens.shape
    return (
        layer_out.reshape(shape), tokens_grad.reshape(shape), gain, shift, inproj, kernel, offset, select.T,
        stepproj, stepbias, decay.T, skip, outproj.T,
    )


def solution(mesh):
    tile, whole = (P("dp", "seq", None, None), P())
    return jax.shard_map(
        on_device,
        mesh=mesh,
        in_specs=(tile, P("dp", None), tile) + (whole,) * 11,
        out_specs=(tile, tile) + (whole,) * 11,
        check_vma=False,
    )
```

```python
import functools

import jax
import jax.numpy as jnp
from jax import lax
from jax.experimental import pallas as pl
from jax.experimental.pallas import tpu as pltpu
from jax.sharding import PartitionSpec as P

epsilon = 1e-05
f32, bf16 = (jnp.float32, jnp.bfloat16)
ONE, IN, OUT, PROJ = (12, 16, 32, 48)
BIAS, SKIP, GAIN, SHIFT, STEP, DECAY, TABLE = (9, 10, 11, 12, 16, 32, 48)
STEP_AT, DECAY_AT, TAPS_AT, OFFSET_AT, SKIP_AT, NORM_AT, SMALL = (48, 64, 80, 89, 90, 95, 96)


def dot(a, b, over):
    return lax.dot_general(a, b, (((over[0],), (over[1],)), ((), ())), preferred_element_type=f32)


def split(value):
    high = value.astype(bf16)
    return (high, (value - high.astype(f32)).astype(bf16))


def fine_dot(a, b, over):
    (a_high, a_low), (b_high, b_low) = (split(a), split(b))
    return dot(a_high, b_high, over) + (dot(a_low, b_high, over) + dot(a_high, b_low, over))


def iota(shape, dim):
    return lax.broadcasted_iota(jnp.int32, shape, dim)


def sigmoid(v):
    return 1.0 / (1.0 + jnp.exp(-v))


def links_up(heights, row):
    if row == 0:
        return 0.0
    end = jnp.int32(0)
    same = True
    for k in range(heights.shape[1]):
        end = end + heights[0, k]
        same = same & (end != row)
    return jnp.where(same, 1.0, 0.0).astype(f32)


def row_masks(links, place):
    lane = iota((1, 128), 1)
    flags = [links[2 * place + k, 0:1] for k in range(3)]
    return (jnp.where(lane < 64, flags[0], flags[1]), jnp.where(lane < 64, flags[1], flags[2]))


def rows_around(own, halo):
    lane = iota((1, 128), 1)
    upper = pltpu.roll(jnp.where(lane < 64, own, halo), 64, 1)
    lower = pltpu.roll(jnp.where(lane < 64, halo, own), 64, 1)
    return (upper, lower)


def from_left(tile):
    place = iota((1, 128), 1) & 63
    wrapped = jnp.where(place == 0, 0.0, pltpu.roll(tile, 73, 1))
    return jnp.where(place < 8, wrapped, pltpu.roll(tile, 8, 1))


def from_right(tile):
    place = iota((1, 128), 1) & 63
    wrapped = jnp.where(place == 63, 0.0, pltpu.roll(tile, 55, 1))
    return jnp.where(place >= 56, wrapped, pltpu.roll(tile, 120, 1))


def conv_tile(upper, own, lower, taps):
    left, middle, right = [
        taps[0][b] * upper + taps[1][b] * own + taps[2][b] * lower for b in range(3)
    ]
    return middle + (from_left(left) + from_right(right))


def normalized(x):
    centred = x - jnp.mean(x, axis=0, keepdims=True)
    inverse = lax.rsqrt(jnp.mean(centred * centred, axis=0, keepdims=True) + epsilon)
    return (centred * inverse, inverse)


def eye(size):
    return (iota((size, size), 0) == iota((size, size), 1)).astype(bf16)


def flipped(value):
    pieces = [value[:, k : k + 128] for k in range(0, value.shape[1], 128)]
    return jnp.concatenate([dot(eye(piece.shape[1]), piece, (1, 1)) for piece in pieces], axis=0)


def flipped_fine(value):
    high, low = split(value)
    rest = (value - high.astype(f32) - low.astype(f32)).astype(bf16)
    return flipped(high) + (flipped(low) + flipped(rest))


def patch_sums(value):
    high, low = split(value)
    ones = jnp.ones((8, value.shape[1]), bf16)
    return (dot(ones, high, (1, 1)) + dot(ones, low, (1, 1)))[0:1]


def put_blocks(ref, start, value):
    for k in range(value.shape[1] // 128):
        ref[start + k * value.shape[0] : start + (k + 1) * value.shape[0]] = value[:, k * 128 : (k + 1) * 128]


def column_order(pos):
    new, old = (iota((pos, pos), 0), iota((pos, pos), 1))
    source = (new & ~63) | ((new & 7) << 3) | ((new >> 3) & 7)
    return (source == old).astype(bf16)


def lane_maps(part, states, width):
    lane = iota((1, width), 1)
    channel = jnp.floor((lane.astype(f32) + 0.5) * (1.0 / states)).astype(jnp.int32)
    return (channel, lane - channel * states, channel < part)


def entered(rows):
    return dot(flipped(rows).astype(bf16), column_order(rows.shape[0]), (1, 0))


def own_kernel(
    heights, tok, cot, in_w, out_t, select_t, conv_kernel, conv_bias, step_weight, step_bias, decay_t, skip_gain,
    norm_gain, norm_bias,
    conv_out, gate_out, grad_out, mix_out, low_out, cot_out, conv_rows, select_rows, table, table_t, in_keep, links,
):
    model, inner_width = out_t.shape
    states = decay_t.shape[0]
    rank = step_weight.shape[0]
    in_keep[...] = in_w[...]
    for row in range(links.shape[0]):
        links[row] = jnp.full(links.shape[1:], links_up(heights, row), f32)
    in_rows = flipped(in_w[...]).astype(bf16)
    conv_rows[...] = in_rows[:inner_width]
    out_rows = flipped(out_t[...]).astype(bf16)
    chosen = iota((PROJ, select_t.shape[0]), 0)
    chosen = jnp.where(chosen < rank, chosen, jnp.where(chosen < IN, -1, chosen - IN + rank))
    chosen = (chosen == iota((PROJ, select_t.shape[0]), 1)).astype(bf16)
    select_rows[...] = flipped(dot(chosen, select_t[...], (1, 0)).astype(bf16)).astype(bf16)
    table_t[...] = jnp.zeros_like(table_t)
    for k in range(3):
        table_t[3 * k : 3 * k + 3] = conv_kernel[k]
    table_t[BIAS : BIAS + 1] = conv_bias[...].reshape(1, inner_width)
    table_t[SKIP : SKIP + 1] = skip_gain[...].reshape(1, inner_width)
    table_t[GAIN : GAIN + 1, :model] = norm_gain[...].reshape(1, model)
    table_t[SHIFT : SHIFT + 1, :model] = norm_bias[...].reshape(1, model)
    table_t[STEP : STEP + rank] = step_weight[...]
    table_t[STEP + ONE : STEP + ONE + 1] = step_bias[...].reshape(1, inner_width)
    table_t[DECAY : DECAY + states] = decay_t[...]
    columns = flipped_fine(table_t[...])
    table[...] = columns
    gain, shift = (columns[:model, GAIN : GAIN + 1], columns[:model, SHIFT : SHIFT + 1])
    low = (normalized(entered(tok[...]))[0] * gain + shift).astype(bf16)
    cot_in = entered(cot[...]).astype(bf16)
    low_out[...] = low
    cot_out[...] = cot_in
    both = dot(in_rows, low, (1, 0))
    conv_out[...] = both[:inner_width]
    gate = both[inner_width:]
    gated_grad = dot(out_rows, cot_in, (1, 0))
    gate_out[...] = gate
    grad_out[...] = gated_grad
    mix_out[...] = gated_grad * (gate * sigmoid(gate))


def entry_kernel(
    place, above, below, conv_own, mix, conv_rows, select_rows, table, links,
    send, halo_out, pre_out, low_halo_out,
):
    devices = send.shape[0]
    inner_width = conv_own.shape[0]
    model = conv_rows.shape[1]
    part = inner_width // devices
    columns = table[...]
    gain, shift = (columns[:model, GAIN : GAIN + 1], columns[:model, SHIFT : SHIFT + 1])
    even = place[0] % 2 == 0
    halo = jnp.concatenate(
        [jnp.where(even, below[...], above[...]), jnp.where(even, above[...], below[...])], axis=0
    ).astype(bf16)
    low_halo = (normalized(entered(halo))[0] * gain + shift).astype(bf16)
    low_halo_out[...] = low_halo
    around = dot(conv_rows[...], low_halo, (1, 0))
    halo_out[...] = around
    conv_in = conv_own[...]
    prev, following = row_masks(links, place[0])
    upper, lower = rows_around(conv_in, around)
    taps = [[columns[:, 3 * a + b : 3 * a + b + 1] for b in range(3)] for a in range(3)]
    pre_act = columns[:, BIAS : BIAS + 1] + conv_tile(upper * prev, conv_in, lower * following, taps)
    inner = (pre_act * sigmoid(pre_act)).astype(bf16)
    proj = dot(flipped(select_rows[...]).astype(bf16), inner, (1, 0))
    proj = jnp.where(iota(proj.shape, 0) == ONE, 1.0, proj)
    pre_out[...] = pre_act
    inner = inner.astype(f32)
    for k in range(devices):
        send[k, :part] = inner[k * part : (k + 1) * part]
        send[k, part : 2 * part] = mix[k * part : (k + 1) * part]
        send[k, 2 * part :] = proj


def scan_kernel(
    place, got, table, links,
    send, small,
    a_ref, s_ref, g_ref, down_ref, up_ref, source_ref, mix_ref, col_h, col_m, row_h, row_m,
    prod, end_lr, end_rl, back_lr, back_rl, in_lr, in_rl, tail_lr, tail_rl,
    lhs_d, lhs_u, lhs_m, coef_keep, step_keep, delta_keep, y_keep, steps_keep, sums_keep, coefs_keep, decay_acc, *, part, states, span, group,
):
    devices, _, pos = got.shape
    rows = 2 * devices
    width = a_ref.shape[1]
    own_rows = table[pl.ds(pl.multiple_of(place[0] * part, 4), part), :]
    channel, state, live = lane_maps(part, states, width)
    twice = iota((2 * part, 1), 0)
    twice = jnp.where(twice >= part, twice - part, twice)
    spread_e = ((twice == channel) & live).astype(bf16)
    coef = iota((2 * PROJ, 1), 0)
    coef = jnp.where(coef >= PROJ, coef - PROJ, coef)
    near = state[:, :128]
    spread_bc = jnp.concatenate([coef - IN == near, coef - OUT == near], axis=1).astype(bf16)
    by_state = ((iota((states, 1), 0) == state) & live).astype(bf16)
    rate = -jnp.exp(own_rows[:, DECAY : DECAY + states])
    one_channel = (iota((part, 1), 0) == channel) & live
    rate_high, rate_low = split(rate)
    rate_rest = split(rate - rate_high.astype(f32) - rate_low.astype(f32))[0]
    rate_row = sum(dot(piece, by_state, (1, 0)) for piece in (rate_high, rate_low, rate_rest))
    rate_row = jnp.sum(jnp.where(one_channel, rate_row, 0.0), axis=0, keepdims=True)
    rate_two = rate_row * 1.4426950408889634
    step_own = own_rows[:, STEP : STEP + 16]
    step_high, step_low = split(step_own)
    step_three = jnp.concatenate([step_high, step_high, step_low], axis=1)

    def turned(value):
        return jnp.transpose(jnp.concatenate(split(value), axis=0))

    for tile in range(devices):
        lines = slice(tile * pos, (tile + 1) * pos)
        inner_own = got[tile, :part]
        proj = got[tile, 2 * part :]
        high, low = split(proj[:16])
        pre_step = dot(step_three, jnp.concatenate([high, low, high], axis=0), (1, 0))
        tail = jnp.exp(-jnp.abs(pre_step))
        tail = jnp.where(tail < 1e-3, tail * (1.0 - 0.5 * tail), jnp.log(1.0 + tail))
        delta = jnp.maximum(pre_step, 0.0) + tail
        step_keep[tile] = sigmoid(pre_step)
        delta_keep[tile] = delta
        lhs_d[lines, :] = turned(delta)
        lhs_u[lines, :] = turned(delta * inner_own)
        lhs_m[lines, :] = turned(got[tile, part : 2 * part])
        coef_keep[lines, :] = dot(turned(proj), spread_bc, (1, 0))

    for k in range(width // span):
        lanes = slice(k * span, (k + 1) * span)

        def prepare(tile, carry):
            lines = pl.ds(pl.multiple_of(tile * pos, pos), pos)
            of_delta, of_source, of_mix = (lhs_d[lines, :], lhs_u[lines, :], lhs_m[lines, :])
            a_ref[lines, lanes] = jnp.exp2(dot(of_delta, spread_e[:, lanes], (1, 0)) * rate_two[:, lanes])
            source = dot(of_source, spread_e[:, lanes], (1, 0))
            mix = dot(of_mix, spread_e[:, lanes], (1, 0))
            source_ref[lines, lanes] = source
            mix_ref[lines, lanes] = mix
            for j in range(span // 128):
                tile_lanes = slice(k * span + j * 128, k * span + (j + 1) * 128)
                piece = slice(j * 128, (j + 1) * 128)
                s_ref[lines, tile_lanes] = source[:, piece] * coef_keep[lines, :128]
                g_ref[lines, tile_lanes] = mix[:, piece] * coef_keep[lines, 128:]
            return carry

        lax.fori_loop(0, devices, prepare, 0, unroll=8)
    down_ref[:64] = jnp.zeros((64, width), f32)
    col_m[...] = jnp.zeros_like(col_m)
    right, left = (range(8), range(7, -1, -1))
    nothing = jnp.zeros((8, 128), f32)

    def packed(row, piece):
        return pl.ds(row * 64 + piece, 8, stride=8)

    def chain(state, row, order, ends, starts):
        for c in order:
            line = pl.ds(pl.multiple_of(row * 64 + c * 8, 8), 8)
            starts[line, :] = state
            state = prod[line, :] * state + ends[line, :]
        return state

    def link(row):
        return links[row]

    def carry_on(held, row, odd):
        ahead, behind = held
        ahead = ahead * link(row)
        if odd:
            ahead = chain(ahead, row, left, end_rl, in_rl)
            behind = chain(behind, row, left, back_lr, tail_lr)
        else:
            ahead = chain(ahead, row, right, end_lr, in_lr)
            behind = chain(behind, row, right, back_rl, tail_rl)
        return (ahead, behind * link(row + 1))

    def carry_back(held, row, odd):
        behind, ahead = held
        behind = behind * link(row + 1)
        if odd:
            behind = chain(behind, row, right, end_lr, in_lr)
            ahead = chain(ahead, row, right, back_rl, tail_rl)
        else:
            behind = chain(behind, row, left, end_rl, in_rl)
            ahead = chain(ahead, row, left, back_lr, tail_lr)
        return (behind, ahead * link(row))

    def wide_link(row):
        return jnp.concatenate([links[row]] * (group // 128), axis=1)

    def ascend(row):
        keep = wide_link(row)
        for k in range(width // group):
            lanes = slice(k * group, (k + 1) * group)
            whole = lr = rl = mlr = mrl = None
            for c in range(8):
                lines = pl.ds(pl.multiple_of(row * 64 + c * 8, 8), 8)
                spot = slice(c * 8, c * 8 + 8)
                a, s, g = (a_ref[lines, lanes], s_ref[lines, lanes], g_ref[lines, lanes])
                before, here = [
                    pl.ds(pl.multiple_of((row + step) * 64 + c * 8, 8), 8) for step in range(2)
                ]
                state_h = a * (down_ref[before, lanes] * keep) + s
                down_ref[here, lanes] = state_h
                lam = g + col_m[spot, lanes] * keep
                col_m[spot, lanes] = a * lam
                up_ref[lines, lanes] = lam
                if c == 0:
                    whole, lr, rl, mlr, mrl = (a, s, s, a * g, a * g)
                else:
                    lr = a * lr + s
                    rl = rl + whole * s
                    whole = whole * a
                    mlr = mlr + whole * g
                    mrl = a * (mrl + g)
            for j in range(group // 128):
                spot = packed(row, k * (group // 128) + j)
                piece = slice(j * 128, (j + 1) * 128)
                prod[spot, :] = whole[:, piece]
                end_lr[spot, :] = lr[:, piece]
                end_rl[spot, :] = rl[:, piece]
                back_lr[spot, :] = mlr[:, piece]
                back_rl[spot, :] = mrl[:, piece]

    def ascend_two(step, held):
        row = 2 * step + 1
        held = carry_on(held, row - 1, False)
        ascend(row)
        held = carry_on(held, row, True)
        ascend(row + 1)
        return held

    ascend(0)
    held = lax.fori_loop(0, devices - 1, ascend_two, (nothing,) * 2)
    held = carry_on(held, rows - 2, False)
    ascend(rows - 1)
    carry_on(held, rows - 1, True)
    col_h[...] = jnp.zeros_like(col_h)
    col_m[...] = jnp.zeros_like(col_m)

    def descend(row):
        keep = wide_link(row + 1)

        def edge(ref, k):
            pieces = [ref[packed(row, k * (group // 128) + j), :] for j in range(group // 128)]
            return pieces[0] if len(pieces) == 1 else jnp.concatenate(pieces, axis=1)

        for k in range(width // group):
            lanes = slice(k * group, (k + 1) * group)
            h_right, m_left = (edge(in_lr, k), edge(tail_rl, k))
            for c in range(8):
                lines = pl.ds(pl.multiple_of(row * 64 + c * 8, 8), 8)
                spot = slice(c * 8, c * 8 + 8)
                a, s, g = (a_ref[lines, lanes], s_ref[lines, lanes], g_ref[lines, lanes])
                h_right = a * h_right + s
                lam = g + m_left
                m_left = a * lam
                row_h[spot, lanes] = h_right
                row_m[spot, lanes] = lam
            h_left, m_right = (edge(in_rl, k), edge(tail_lr, k))
            for c in range(7, -1, -1):
                lines = pl.ds(pl.multiple_of(row * 64 + c * 8, 8), 8)
                spot = slice(c * 8, c * 8 + 8)
                a, s, g = (a_ref[lines, lanes], s_ref[lines, lanes], g_ref[lines, lanes])
                h_left = a * h_left + s
                lam_lr = g + m_right
                m_right = a * lam_lr
                here = pl.ds(pl.multiple_of((row + 1) * 64 + c * 8, 8), 8)
                h_down, lam_up = (down_ref[here, lanes], up_ref[lines, lanes])
                h_up = a * (col_h[spot, lanes] * keep) + s
                col_h[spot, lanes] = h_up
                lam_down = g + col_m[spot, lanes] * keep
                col_m[spot, lanes] = a * lam_down
                h_right, lam_rl = (row_h[spot, lanes], row_m[spot, lanes])
                lam_sum = (lam_lr + lam_rl) + (lam_down + lam_up)
                s_ref[lines, lanes] = (h_right + h_left) + (h_down + h_up)
                up_ref[lines, lanes] = lam_sum
                g_ref[lines, lanes] = (
                    (lam_lr * h_right + lam_rl * h_left)
                    + (lam_down * h_down + lam_up * h_up)
                    - s * lam_sum
                )

    def descend_two(step, held):
        row = rows - 1 - 2 * step
        held = carry_back(held, row - 1, False)
        descend(row)
        held = carry_back(held, row - 2, True)
        descend(row - 1)
        return held

    held = carry_back((nothing,) * 2, rows - 1, True)
    held = lax.fori_loop(0, devices - 1, descend_two, held)
    carry_back(held, 0, False)
    descend(1)
    descend(0)
    decay_acc[...] = jnp.zeros_like(decay_acc)
    gather_e, gather_b, gather_c = (spread_e[:part], spread_bc[:PROJ, :128], spread_bc[:PROJ, 128:])

    def finish(tile, carry):
        lines = pl.ds(pl.multiple_of(tile * pos, pos), pos)
        delta = delta_keep[tile]
        delta_low = delta.astype(bf16)
        of_b, of_c = (coef_keep[lines, :128], coef_keep[lines, 128:])
        grad_b = grad_c = None
        of_y, of_step, of_sum = ([], [], [])
        for k in range(width // 128):
            lanes = slice(k * 128, (k + 1) * 128)
            h_sum, lam_sum = (s_ref[lines, lanes], up_ref[lines, lanes])
            of_step.append((g_ref[lines, lanes] * rate_row[:, lanes]).astype(bf16))
            of_y.append((h_sum * of_c).astype(bf16))
            of_sum.append((lam_sum * of_b).astype(bf16))
            term_b, term_c = (lam_sum * source_ref[lines, lanes], h_sum * mix_ref[lines, lanes])
            grad_b = term_b if grad_b is None else grad_b + term_b
            grad_c = term_c if grad_c is None else grad_c + term_c
        of_y, of_step, of_sum = [jnp.concatenate(x, axis=1) for x in (of_y, of_step, of_sum)]
        decay_acc[...] += dot(delta_low, of_step, (1, 0))
        y_keep[tile] = jnp.transpose(dot(of_y, gather_e, (1, 1)))
        steps_keep[tile] = jnp.transpose(dot(of_step, gather_e, (1, 1)))
        sums_keep[tile] = jnp.transpose(dot(of_sum, gather_e, (1, 1)))
        coefs_keep[tile] = dot(gather_b, grad_b.astype(bf16), (1, 1)) + dot(gather_c, grad_c.astype(bf16), (1, 1))
        return carry

    lax.fori_loop(0, devices, finish, 0, unroll=8)
    step_grad = jnp.zeros((part, 16), f32)
    for tile in range(devices):
        sums, coefs = (sums_keep[tile], coefs_keep[tile])
        pre_grad = (steps_keep[tile] + got[tile, :part] * sums) * step_keep[tile]
        send[tile, :part] = y_keep[tile]
        send[tile, part : 2 * part] = delta_keep[tile] * sums
        send[tile, 2 * part : 2 * part + 16] = coefs[:16] + fine_dot(step_own, pre_grad, (0, 0))
        send[tile, 2 * part + 16 :] = coefs[16:]
        step_grad = step_grad + fine_dot(pre_grad, got[tile, 2 * part : 2 * part + 16], (1, 1))
    decay_grad = jnp.where(one_channel, decay_acc[...], 0.0)
    decay_high, decay_low = split(decay_grad)
    decay_grad = dot(decay_high, by_state, (1, 1)) + dot(decay_low, by_state, (1, 1))
    spot = (iota((part, small.shape[1]), 1) == iota((part, small.shape[1]), 0) + place[0] * part).astype(bf16)
    for at, value in ((0, step_grad), (16, decay_grad)):
        high, low = split(value)
        small[at : at + 16] = dot(high, spot, (0, 0)) + dot(low, spot, (0, 0))


def mix_kernel(
    place, group, got, small_in, low, low_halo, cot, conv_own, conv_halo, pre, gate_in, grad_in,
    select_rows, table, table_t, in_w, links,
    act_out, near, far, gate_grad_out, gated_ref, keep, give,
    grads, inner_ref, moved_ref, sums_ref, *, pair,
):
    devices, length, pos = got.shape
    model, inner_width = (low.shape[0], pre.shape[0])
    part = inner_width // devices
    lane = iota((1, pos), 1)
    prev, following = row_masks(links, place[0])
    proj_grad = got[0, 2 * part :]
    for k in range(1, devices):
        proj_grad = proj_grad + got[k, 2 * part :]
    proj_grad = proj_grad.astype(bf16)
    together = max(1, 48 // part)
    for first in range(0, devices, together):
        members = range(first, first + together)
        rows = slice(first * part, (first + together) * part)
        y = jnp.concatenate([got[k, :part] for k in members], axis=0)
        inner_grad = jnp.concatenate([got[k, part : 2 * part] for k in members], axis=0)
        pre_act, gate, gated_grad = (pre[rows], gate_in[rows], grad_in[rows])
        skip = table[rows, SKIP : SKIP + 1]
        sig_pre, sig_gate = (sigmoid(pre_act), sigmoid(gate))
        inner = (pre_act * sig_pre).astype(bf16)
        inner_ref[rows] = inner
        inner = inner.astype(f32)
        silu_gate = gate * sig_gate
        mix_grad = gated_grad * silu_gate
        inner_grad = inner_grad + mix_grad * skip + dot(select_rows[rows], proj_grad, (1, 0))
        act_grad = inner_grad * (sig_pre * (1.0 + pre_act * (1.0 - sig_pre)))
        act_out[rows] = act_grad
        y_all = y + skip * inner
        gated_ref[rows] = (y_all * silu_gate).astype(bf16)
        gate_grad_out[rows] = (gated_grad * y_all * (sig_gate * (1.0 + gate * (1.0 - sig_gate)))).astype(bf16)
        field = conv_own[rows]
        upper, lower = rows_around(field, conv_halo[rows])
        fields = (upper * prev, field, lower * following)
        sums = jnp.where(lane == 9, jnp.sum(act_grad, axis=1, keepdims=True), 0.0)
        sums = jnp.where(lane == 10, jnp.sum(mix_grad * inner, axis=1, keepdims=True), sums)
        for b, moved in enumerate((from_right(act_grad), act_grad, from_left(act_grad))):
            moved_ref[b, rows] = moved.astype(bf16)
            for a in range(3):
                sums = jnp.where(lane == 3 * a + b, jnp.sum(moved * fields[a], axis=1, keepdims=True), sums)
        sums_ref[rows] = sums
    conv_w = in_w[:, :inner_width].astype(f32)
    beyond = None
    for b in range(3):
        weights = [conv_w * table_t[3 * a + b : 3 * a + b + 1] for a in (0, 2)]
        term = dot(jnp.concatenate(weights, axis=0).astype(bf16), moved_ref[b], (1, 0))
        beyond = term if beyond is None else beyond + term
    beyond = jnp.where(lane < 64, beyond[:model] * prev, beyond[model:] * following)
    top, bottom = (beyond[: model // 2], beyond[model // 2 :])
    up = jnp.where(lane < 64, top, pltpu.roll(bottom, 64, 1))
    down = jnp.where(lane < 64, pltpu.roll(top, 64, 1), bottom)
    even = place[0] % 2 == 0
    near[...] = jnp.where(even, down, up)
    far[...] = jnp.where(even, up, down)
    gated, gate_grad = (gated_ref[...], gate_grad_out[...])

    low_in = low[...]
    upper, lower = rows_around(low_in.astype(f32), low_halo[...].astype(f32))
    which = iota((16, 1), 0)
    masks = jnp.where(which == 0, prev, jnp.where(which == 1, 1.0, following))
    left_hand = jnp.concatenate(
        [(upper * prev).astype(bf16), low_in, (lower * following).astype(bf16), masks.astype(bf16)], axis=0
    )
    blocks = inner_width // 128
    gate_at, out_at, small_at = [k * blocks * model for k in (1, 2, 3)]
    ones = jnp.ones((16, pos), bf16)
    totals = [[], []]
    gain_sum = jnp.zeros((model, 128), f32)
    for n in range(blocks):
        columns = slice(n * 128, (n + 1) * 128)
        in_conv = conv_total = None
        for b in range(3):
            part_b = dot(left_hand, moved_ref[b, columns], (1, 1))
            for a in range(3):
                tap = table_t[3 * a + b : 3 * a + b + 1, columns]
                term = tap * part_b[a * model : (a + 1) * model]
                total = tap * part_b[3 * model + a : 3 * model + a + 1]
                in_conv = term if in_conv is None else in_conv + term
                conv_total = total if conv_total is None else conv_total + total
        in_gate = dot(low_in, gate_grad[columns], (1, 1))
        grads[n * model : (n + 1) * model] = in_conv
        grads[gate_at + n * model : gate_at + (n + 1) * model] = in_gate
        grads[out_at + n * model : out_at + (n + 1) * model] = dot(cot[...], gated[columns], (1, 1))
        totals[0].append(conv_total)
        totals[1].append(dot(ones, gate_grad[columns], (1, 1))[0:1])
        conv_w = in_w[:, columns].astype(f32)
        gate_w = in_w[:, inner_width + n * 128 : inner_width + (n + 1) * 128].astype(f32)
        gain_sum = gain_sum + (conv_w * in_conv + gate_w * in_gate)
    sums = jnp.broadcast_to(jnp.concatenate(totals[0] + totals[1], axis=1), (16, 2 * inner_width))
    sums_high, sums_low = split(sums)
    shift_row = (dot(sums_high, in_w[...], (1, 1)) + dot(sums_low, in_w[...], (1, 1)))[0:1]
    gain_row = patch_sums(gain_sum)
    gain, shift = (table_t[GAIN : GAIN + 1, :model], table_t[SHIFT : SHIFT + 1, :model])
    gain_row = (gain_row - shift * shift_row) / gain
    high, mid = split(sums_ref[...])
    rest = (sums_ref[...] - high.astype(f32) - mid.astype(f32)).astype(bf16)
    chosen = (iota((16, pos), 0) == iota((16, pos), 1)).astype(bf16)
    sums = dot(chosen, high, (1, 1)) + (dot(chosen, mid, (1, 1)) + dot(chosen, rest, (1, 1)))
    norms = jnp.concatenate([gain_row, shift_row], axis=1)
    sums = jnp.where(iota((16, 1), 0) == NORM_AT - TAPS_AT, norms, sums)
    smalls = jnp.concatenate([dot(proj_grad, inner_ref[...], (1, 1)), small_in[...], sums], axis=0)
    put_blocks(grads, small_at, smalls)
    small_at = small_at + blocks * SMALL
    grads[small_at:] = jnp.zeros((grads.shape[0] - small_at, 128), f32)
    own = group[0] % 2
    if pair:
        count = keep.shape[0] // 2
        height = group[0] // 2
        for ref, side in ((keep, own), (give, 1 - own)):
            for k, at in enumerate((height, 1 - height)):
                ref[k * count : (k + 1) * count] = grads[pl.ds(pl.multiple_of((2 * side + at) * count, count), count)]
    else:
        count = keep.shape[0]
        keep[...] = grads[pl.ds(pl.multiple_of(own * count, count), count)]
        give[...] = grads[pl.ds(pl.multiple_of((1 - own) * count, count), count)]


def exit_kernel(
    place, act, from_above, from_below, gate_grad, gated, table, in_w, links, tok, cot, out_t,
    tokens_grad, layer_out,
):
    inner_width, pos = act.shape
    model = in_w.shape[0]
    lane = iota((1, pos), 1)
    even = place[0] % 2 == 0
    above, below = (
        jnp.where(even, from_above[...], from_below[...]), jnp.where(even, from_below[...], from_above[...])
    )
    top = jnp.where(lane < 64, above, pltpu.roll(below, 64, 1))
    bottom = jnp.where(lane < 64, pltpu.roll(above, 64, 1), below)
    beyond_high, beyond_low = split(jnp.concatenate([top, bottom], axis=0))
    act_grad = act[...]
    prev, following = row_masks(links, place[0])
    upper, lower = rows_around(act_grad, jnp.zeros_like(act_grad))
    columns = table[...]
    taps = [[columns[:, 8 - 3 * a - b : 9 - 3 * a - b] for b in range(3)] for a in range(3)]
    conv_grad = conv_tile(upper * prev, act_grad, lower * following, taps).astype(bf16)
    natural = jnp.concatenate([conv_grad, gate_grad[...], gated[...]], axis=0)
    order = column_order(pos)
    natural = dot(natural, order, (1, 0)).astype(bf16)
    layer = jnp.transpose(dot(out_t[...], natural[2 * inner_width :], (1, 0)))
    layer_out[...] = (tok[...].astype(f32) + layer).astype(bf16)
    normed_grad = dot(in_w[...], natural[: 2 * inner_width], (1, 0))
    normed_grad = normed_grad + (dot(beyond_high, order, (1, 0)) + dot(beyond_low, order, (1, 0)))
    xhat, inverse = normalized(flipped(tok[...]))
    scaled = normed_grad * columns[:model, GAIN : GAIN + 1]
    x_grad = (
        scaled
        - jnp.mean(scaled, axis=0, keepdims=True)
        - xhat * jnp.mean(scaled * xhat, axis=0, keepdims=True)
    ) * inverse
    x_grad = jnp.transpose(x_grad)
    tokens_grad[...] = (x_grad + cot[...].astype(f32)).astype(bf16)


def deal_kernel(group, *refs, members, pair):
    pieces, ordered = (refs[:members], refs[-1])
    (
        gain_grad, shift_grad, inproj, kernel_grad, offset, select, stepproj, stepbias, decay, skip, outproj,
    ) = refs[members:-1]
    model, inner_width = outproj.shape
    blocks = inner_width // 128
    rank = stepproj.shape[0]
    states = decay.shape[0]
    count = pieces[0].shape[0]
    for k, piece in enumerate(pieces):
        if pair:
            core, height = (group[0] % 2, group[0] // 2)
            core = 1 - core if k // 2 else core
            height = 1 - height if k % 2 else height
            slot = core * 2 + height
        else:
            slot = k % 2 * (members // 2) + k // 2
        ordered[pl.ds(pl.multiple_of(slot * count, count), count)] = piece[...]

    def rows(start, count):
        return ordered[start : start + count]

    for k in range(2 * blocks):
        inproj[:, k * 128 : (k + 1) * 128] = rows(k * model, model)
    start = 2 * blocks * model
    for k in range(blocks):
        outproj[:, k * 128 : (k + 1) * 128] = rows(start + k * model, model)
    start = start + blocks * model
    small = jnp.concatenate([rows(start + k * SMALL, SMALL) for k in range(blocks)], axis=1)
    select[:rank] = small[:rank]
    select[rank:] = small[IN:PROJ]
    stepproj[...] = small[STEP_AT : STEP_AT + rank]
    stepbias[...] = small[STEP_AT + ONE : STEP_AT + ONE + 1].reshape(stepbias.shape)
    decay[...] = small[DECAY_AT : DECAY_AT + states]
    for k in range(3):
        kernel_grad[k] = small[TAPS_AT + 3 * k : TAPS_AT + 3 * k + 3]
    offset[...] = small[OFFSET_AT : OFFSET_AT + 1].reshape(offset.shape)
    skip[...] = small[SKIP_AT : SKIP_AT + 1].reshape(skip.shape)
    norms = small[NORM_AT : NORM_AT + 1]
    gain_grad[...] = norms[:, :model].reshape(gain_grad.shape)
    shift_grad[...] = norms[:, model:].reshape(shift_grad.shape)


def vmem_call(kernel, out_shape, scalars, arrays, weights=(), scratch=(), limit=16):
    scalars = [pltpu.with_memory_space_constraint(x, pltpu.HBM) if x.ndim == 2 else x for x in scalars]
    arrays = [pltpu.with_memory_space_constraint(x, pltpu.VMEM) for x in arrays]
    arrays += [pltpu.with_memory_space_constraint(x, pltpu.HBM) for x in weights]
    return pl.pallas_call(
        kernel,
        out_shape=out_shape,
        in_specs=[pl.BlockSpec(memory_space=pltpu.SMEM)] * len(scalars)
        + [pl.BlockSpec(memory_space=pltpu.VMEM)] * len(arrays),
        out_specs=[pl.BlockSpec(memory_space=pltpu.VMEM)] * len(out_shape),
        scratch_shapes=list(scratch),
        compiler_params=pltpu.CompilerParams(vmem_limit_bytes=limit * 1024 * 1024),
    )(*scalars, *arrays)


def struct(*shape, dtype=f32):
    return jax.ShapeDtypeStruct(shape, dtype)


def inside(*shape, dtype=f32):
    return pltpu.VMEM(shape, dtype)


def scan_call(place, got, table, links, states):
    devices, length, pos = got.shape
    inner_width = table.shape[0]
    part = inner_width // devices
    width = -(-part * states // 128) * 128
    total = devices * pos
    span = 256 if width % 256 == 0 else 128
    group = 768 if width % 768 == 0 else span
    big = pltpu.VMEM((total, width), f32)
    line = pltpu.VMEM((2 * devices * 64, 128), f32)
    column = pltpu.VMEM((pos // 2, width), f32)
    own = pltpu.VMEM((devices, part, pos), f32)
    return vmem_call(
        functools.partial(scan_kernel, part=part, states=states, span=span, group=group),
        [inside(devices, length, pos), inside(32, inner_width)],
        [place],
        [got, table, links],
        (),
        [big] * 3
        + [pltpu.VMEM((total + pos // 2, width), f32)]
        + [big] * 3
        + [column] * 4
        + [line] * 9
        + [pltpu.VMEM((total, 2 * part), bf16)] * 3
        + [pltpu.VMEM((total, 256), f32)]
        + [own] * 5
        + [pltpu.VMEM((devices, PROJ, pos), f32), pltpu.VMEM((part, width), f32)],
        limit=36 if total <= 1024 else 60,
    )


def on_device(
    tokens, heights, cotangent, norm_gain, norm_bias, in_weight, conv_kernel, conv_bias, select_weight,
    step_weight, step_bias, decay_log, skip_gain, out_weight,
):
    _, tile_rows, grid_cols, model = tokens.shape
    inner_width = out_weight.shape[0]
    states = decay_log.shape[1]
    rank = step_weight.shape[0]
    devices = lax.axis_size("seq")
    groups = lax.axis_size("dp")
    place = lax.axis_index("seq").reshape(1)
    group = lax.axis_index("dp").reshape(1)
    pair = groups == 4
    pos = tile_rows * grid_cols
    part = inner_width // devices
    length = 2 * part + PROJ
    near_pairs = [(i, i ^ 1) for i in range(devices)]
    far_pairs = [(i, (i - 1 + 2 * (i % 2)) % devices) for i in range(devices)]

    tok, cot = (tokens.reshape(pos, model), cotangent.reshape(pos, model))
    even = place[0] % 2 == 0
    upper, lower = (tok[:grid_cols].astype(f32), tok[grid_cols:].astype(f32))
    above = lax.ppermute(jnp.where(even, upper, lower), "seq", far_pairs)
    below = lax.ppermute(jnp.where(even, lower, upper), "seq", near_pairs)
    above, group = lax.optimization_barrier((above, group))
    out_t = out_weight.T
    channels = inside(inner_width, pos)
    narrow = inside(model, pos, dtype=bf16)
    conv_own, gate, gated_grad, mix, low, cot_in, conv_rows, select_rows, table, table_t, in_keep, links = vmem_call(
        own_kernel,
        [channels] * 4
        + [narrow] * 2
        + [
            inside(inner_width, model, dtype=bf16), inside(inner_width, PROJ, dtype=bf16), inside(inner_width, TABLE),
            inside(TABLE, inner_width), inside(model, 2 * inner_width, dtype=bf16),
            inside(2 * devices + 1, 8, 128),
        ],
        [heights],
        [],
        [
            tok, cot, in_weight, out_t, select_weight.T, conv_kernel, conv_bias, step_weight, step_bias,
            decay_log.T, skip_gain, norm_gain, norm_bias,
        ],
    )
    sent, conv_halo, pre_act, low_halo = vmem_call(
        entry_kernel,
        [inside(devices, length, pos), channels, channels, narrow],
        [place],
        [above, below, conv_own, mix, conv_rows, select_rows, table, links],
    )
    got = lax.all_to_all(sent, "seq", 0, 0, tiled=True)
    sent, small = scan_call(place, got, table, links, states)
    got = lax.all_to_all(sent, "seq", 0, 0, tiled=True)
    blocks = inner_width // 128
    whole = -(-blocks * (3 * model + SMALL) // 2048) * 2048
    half = whole // 2
    act_grad, near, far, gate_grad, gated, keep, give = vmem_call(
        functools.partial(mix_kernel, pair=pair),
        [channels]
        + [inside(model // 2, pos)] * 2
        + [inside(inner_width, pos, dtype=bf16)] * 2
        + [inside(half, 128)] * 2,
        [place, group],
        [
            got, small, low, low_halo, cot_in, conv_own, conv_halo, pre_act, gate, gated_grad, select_rows, table,
            table_t, in_keep, links,
        ],
        (),
        [
            pltpu.VMEM((whole, 128), f32), pltpu.VMEM((inner_width, pos), bf16),
            pltpu.VMEM((3, inner_width, pos), bf16), pltpu.VMEM((inner_width, pos), f32),
        ],
    )
    from_above = lax.ppermute(far, "seq", far_pairs)
    from_below = lax.ppermute(near, "seq", near_pairs)
    swap = [(i, i ^ 1) for i in range(groups)]
    taken = lax.ppermute(give, "dp", swap)
    count = half // (groups // 2)
    if pair:
        across = [(i, i ^ 2) for i in range(groups)]
        other = lax.ppermute(keep[count:] + taken[count:], "dp", across)
        piece = keep[:count] + taken[:count]
    else:
        same_core = [list(range(c, groups, 2)) for c in range(2)]
        pieces = (keep + taken).reshape(groups // 2, count, 128)
        pieces = lax.all_to_all(pieces, "dp", 0, 0, tiled=True, axis_index_groups=same_core)
        piece, other = (pieces[0], jnp.sum(pieces[1:], axis=0))
    other, from_above, from_below = lax.optimization_barrier((other, from_above, from_below))
    shares = (piece + other).reshape(devices, count // devices, 128)
    shares = lax.all_to_all(shares, "seq", 0, 0, tiled=True)
    share = jnp.broadcast_to(jnp.sum(shares, axis=0), shares.shape)
    mine = lax.all_to_all(share, "seq", 0, 0, tiled=True).reshape(count, 128)
    mine, from_above, from_below = lax.optimization_barrier((mine, from_above, from_below))
    tokens_grad, layer_out = vmem_call(
        exit_kernel,
        [struct(pos, model, dtype=bf16)] * 2,
        [place],
        [act_grad, from_above, from_below, gate_grad, gated, table, in_keep, links],
        [tok, cot, out_t],
    )
    if pair:
        from_y = lax.ppermute(mine, "dp", across)
        from_y, tokens_grad = lax.optimization_barrier((from_y, tokens_grad))
        pieces = [mine, from_y, lax.ppermute(mine, "dp", swap), lax.ppermute(from_y, "dp", swap)]
    else:
        pieces = list(lax.all_gather(mine, "dp"))
    gain, shift, inproj, kernel, offset, select, stepproj, stepbias, decay, skip, outproj = vmem_call(
        functools.partial(deal_kernel, members=len(pieces), pair=pair),
        [
            struct(model), struct(model), struct(model, 2 * inner_width), struct(3, 3, inner_width),
            struct(inner_width), struct(rank + 2 * states, inner_width), struct(rank, inner_width),
            struct(inner_width), struct(states, inner_width), struct(inner_width), struct(model, inner_width),
        ],
        [group],
        pieces,
        (),
        [pltpu.VMEM((whole, 128), f32)],
    )
    shape = tokens.shape
    return (
        layer_out.reshape(shape), tokens_grad.reshape(shape), gain, shift, inproj, kernel, offset, select.T,
        stepproj, stepbias, decay.T, skip, outproj.T,
    )


def solution(mesh):
    tile, whole = (P("dp", "seq", None, None), P())
    return jax.shard_map(
        on_device,
        mesh=mesh,
        in_specs=(tile, P("dp", None), tile) + (whole,) * 11,
        out_specs=(tile, tile) + (whole,) * 11,
        check_vma=False,
    )
```

```python
import functools

import jax
import jax.numpy as jnp
from jax import lax
from jax.experimental import pallas as pl
from jax.experimental.pallas import tpu as pltpu
from jax.sharding import PartitionSpec as P

epsilon = 1e-05
f32, bf16 = (jnp.float32, jnp.bfloat16)
ONE, IN, OUT, PROJ = (12, 16, 32, 48)
BIAS, SKIP, GAIN, SHIFT, STEP, DECAY, TABLE = (9, 10, 11, 12, 16, 32, 48)
STEP_AT, DECAY_AT, TAPS_AT, OFFSET_AT, SKIP_AT, NORM_AT, SMALL = (48, 64, 80, 89, 90, 95, 96)


def dot(a, b, over):
    return lax.dot_general(a, b, (((over[0],), (over[1],)), ((), ())), preferred_element_type=f32)


def split(value):
    high = value.astype(bf16)
    return (high, (value - high.astype(f32)).astype(bf16))


def fine_dot(a, b, over):
    (a_high, a_low), (b_high, b_low) = (split(a), split(b))
    return dot(a_high, b_high, over) + (dot(a_low, b_high, over) + dot(a_high, b_low, over))


def iota(shape, dim):
    return lax.broadcasted_iota(jnp.int32, shape, dim)


def sigmoid(v):
    return 1.0 / (1.0 + jnp.exp(-v))


def links_up(heights, row):
    if row == 0:
        return 0.0
    end = jnp.int32(0)
    same = True
    for k in range(heights.shape[1]):
        end = end + heights[0, k]
        same = same & (end != row)
    return jnp.where(same, 1.0, 0.0).astype(f32)


def row_masks(links, place):
    lane = iota((1, 128), 1)
    flags = [links[2 * place + k, 0:1] for k in range(3)]
    return (jnp.where(lane < 64, flags[0], flags[1]), jnp.where(lane < 64, flags[1], flags[2]))


def rows_around(own, halo):
    lane = iota((1, 128), 1)
    upper = pltpu.roll(jnp.where(lane < 64, own, halo), 64, 1)
    lower = pltpu.roll(jnp.where(lane < 64, halo, own), 64, 1)
    return (upper, lower)


def from_left(tile):
    place = iota((1, 128), 1) & 63
    wrapped = jnp.where(place == 0, 0.0, pltpu.roll(tile, 73, 1))
    return jnp.where(place < 8, wrapped, pltpu.roll(tile, 8, 1))


def from_right(tile):
    place = iota((1, 128), 1) & 63
    wrapped = jnp.where(place == 63, 0.0, pltpu.roll(tile, 55, 1))
    return jnp.where(place >= 56, wrapped, pltpu.roll(tile, 120, 1))


def conv_tile(upper, own, lower, taps):
    left, middle, right = [
        taps[0][b] * upper + taps[1][b] * own + taps[2][b] * lower for b in range(3)
    ]
    return middle + (from_left(left) + from_right(right))


def normalized(x):
    centred = x - jnp.mean(x, axis=0, keepdims=True)
    inverse = lax.rsqrt(jnp.mean(centred * centred, axis=0, keepdims=True) + epsilon)
    return (centred * inverse, inverse)


def eye(size):
    return (iota((size, size), 0) == iota((size, size), 1)).astype(bf16)


def flipped(value):
    pieces = [value[:, k : k + 128] for k in range(0, value.shape[1], 128)]
    return jnp.concatenate([dot(eye(piece.shape[1]), piece, (1, 1)) for piece in pieces], axis=0)


def flipped_fine(value):
    high, low = split(value)
    rest = (value - high.astype(f32) - low.astype(f32)).astype(bf16)
    return flipped(high) + (flipped(low) + flipped(rest))


def patch_sums(value):
    high, low = split(value)
    ones = jnp.ones((8, value.shape[1]), bf16)
    return (dot(ones, high, (1, 1)) + dot(ones, low, (1, 1)))[0:1]


def put_blocks(ref, start, value):
    for k in range(value.shape[1] // 128):
        ref[start + k * value.shape[0] : start + (k + 1) * value.shape[0]] = value[:, k * 128 : (k + 1) * 128]


def column_order(pos):
    new, old = (iota((pos, pos), 0), iota((pos, pos), 1))
    source = (new & ~63) | ((new & 7) << 3) | ((new >> 3) & 7)
    return (source == old).astype(bf16)


def lane_maps(part, states, width):
    lane = iota((1, width), 1)
    channel = jnp.floor((lane.astype(f32) + 0.5) * (1.0 / states)).astype(jnp.int32)
    return (channel, lane - channel * states, channel < part)


def entered(rows):
    return dot(flipped(rows).astype(bf16), column_order(rows.shape[0]), (1, 0))


def own_kernel(
    heights, tok, cot, in_w, out_t, select_t, conv_kernel, conv_bias, step_weight, step_bias, decay_t, skip_gain,
    norm_gain, norm_bias,
    conv_out, gate_out, grad_out, mix_out, low_out, cot_out, conv_rows, select_rows, table, table_t, in_keep, links,
):
    model, inner_width = out_t.shape
    states = decay_t.shape[0]
    rank = step_weight.shape[0]
    in_keep[...] = in_w[...]
    for row in range(links.shape[0]):
        links[row] = jnp.full(links.shape[1:], links_up(heights, row), f32)
    in_rows = flipped(in_w[...]).astype(bf16)
    conv_rows[...] = in_rows[:inner_width]
    out_rows = flipped(out_t[...]).astype(bf16)
    chosen = iota((PROJ, select_t.shape[0]), 0)
    chosen = jnp.where(chosen < rank, chosen, jnp.where(chosen < IN, -1, chosen - IN + rank))
    chosen = (chosen == iota((PROJ, select_t.shape[0]), 1)).astype(bf16)
    select_rows[...] = flipped(dot(chosen, select_t[...], (1, 0)).astype(bf16)).astype(bf16)
    table_t[...] = jnp.zeros_like(table_t)
    for k in range(3):
        table_t[3 * k : 3 * k + 3] = conv_kernel[k]
    table_t[BIAS : BIAS + 1] = conv_bias[...].reshape(1, inner_width)
    table_t[SKIP : SKIP + 1] = skip_gain[...].reshape(1, inner_width)
    table_t[GAIN : GAIN + 1, :model] = norm_gain[...].reshape(1, model)
    table_t[SHIFT : SHIFT + 1, :model] = norm_bias[...].reshape(1, model)
    table_t[STEP : STEP + rank] = step_weight[...]
    table_t[STEP + ONE : STEP + ONE + 1] = step_bias[...].reshape(1, inner_width)
    table_t[DECAY : DECAY + states] = decay_t[...]
    columns = flipped_fine(table_t[...])
    table[...] = columns
    gain, shift = (columns[:model, GAIN : GAIN + 1], columns[:model, SHIFT : SHIFT + 1])
    low = (normalized(entered(tok[...]))[0] * gain + shift).astype(bf16)
    cot_in = entered(cot[...]).astype(bf16)
    low_out[...] = low
    cot_out[...] = cot_in
    both = dot(in_rows, low, (1, 0))
    conv_out[...] = both[:inner_width]
    gate = both[inner_width:]
    gated_grad = dot(out_rows, cot_in, (1, 0))
    gate_out[...] = gate
    grad_out[...] = gated_grad
    mix_out[...] = gated_grad * (gate * sigmoid(gate))


def entry_kernel(
    place, above, below, conv_own, mix, conv_rows, select_rows, table, links,
    send, halo_out, pre_out, low_halo_out,
):
    devices = send.shape[0]
    inner_width = conv_own.shape[0]
    model = conv_rows.shape[1]
    part = inner_width // devices
    columns = table[...]
    gain, shift = (columns[:model, GAIN : GAIN + 1], columns[:model, SHIFT : SHIFT + 1])
    even = place[0] % 2 == 0
    halo = jnp.concatenate(
        [jnp.where(even, below[...], above[...]), jnp.where(even, above[...], below[...])], axis=0
    ).astype(bf16)
    low_halo = (normalized(entered(halo))[0] * gain + shift).astype(bf16)
    low_halo_out[...] = low_halo
    around = dot(conv_rows[...], low_halo, (1, 0))
    halo_out[...] = around
    conv_in = conv_own[...]
    prev, following = row_masks(links, place[0])
    upper, lower = rows_around(conv_in, around)
    taps = [[columns[:, 3 * a + b : 3 * a + b + 1] for b in range(3)] for a in range(3)]
    pre_act = columns[:, BIAS : BIAS + 1] + conv_tile(upper * prev, conv_in, lower * following, taps)
    inner = (pre_act * sigmoid(pre_act)).astype(bf16)
    proj = dot(flipped(select_rows[...]).astype(bf16), inner, (1, 0))
    proj = jnp.where(iota(proj.shape, 0) == ONE, 1.0, proj)
    pre_out[...] = pre_act
    inner = inner.astype(f32)
    for k in range(devices):
        send[k, :part] = inner[k * part : (k + 1) * part]
        send[k, part : 2 * part] = mix[k * part : (k + 1) * part]
        send[k, 2 * part :] = proj


def scan_kernel(
    place, got, table, links,
    send, small,
    a_ref, s_ref, g_ref, down_ref, up_ref, source_ref, mix_ref, col_h, col_m, row_h, row_m,
    prod, end_lr, end_rl, back_lr, back_rl, in_lr, in_rl, tail_lr, tail_rl,
    lhs_d, lhs_u, lhs_m, coef_keep, step_keep, delta_keep, y_keep, steps_keep, sums_keep, coefs_keep, decay_acc, *, part, states, span, group,
):
    devices, _, pos = got.shape
    rows = 2 * devices
    width = a_ref.shape[1]
    own_rows = table[pl.ds(pl.multiple_of(place[0] * part, 4), part), :]
    channel, state, live = lane_maps(part, states, width)
    twice = iota((2 * part, 1), 0)
    twice = jnp.where(twice >= part, twice - part, twice)
    spread_e = ((twice == channel) & live).astype(bf16)
    coef = iota((2 * PROJ, 1), 0)
    coef = jnp.where(coef >= PROJ, coef - PROJ, coef)
    near = state[:, :128]
    spread_bc = jnp.concatenate([coef - IN == near, coef - OUT == near], axis=1).astype(bf16)
    by_state = ((iota((states, 1), 0) == state) & live).astype(bf16)
    rate = -jnp.exp(own_rows[:, DECAY : DECAY + states])
    one_channel = (iota((part, 1), 0) == channel) & live
    rate_high, rate_low = split(rate)
    rate_rest = split(rate - rate_high.astype(f32) - rate_low.astype(f32))[0]
    rate_row = sum(dot(piece, by_state, (1, 0)) for piece in (rate_high, rate_low, rate_rest))
    rate_row = jnp.sum(jnp.where(one_channel, rate_row, 0.0), axis=0, keepdims=True)
    rate_two = rate_row * 1.4426950408889634
    step_own = own_rows[:, STEP : STEP + 16]
    step_high, step_low = split(step_own)
    step_three = jnp.concatenate([step_high, step_high, step_low], axis=1)

    def turned(value):
        return jnp.transpose(jnp.concatenate(split(value), axis=0))

    for tile in range(devices):
        lines = slice(tile * pos, (tile + 1) * pos)
        inner_own = got[tile, :part]
        proj = got[tile, 2 * part :]
        high, low = split(proj[:16])
        pre_step = dot(step_three, jnp.concatenate([high, low, high], axis=0), (1, 0))
        tail = jnp.exp(-jnp.abs(pre_step))
        tail = jnp.where(tail < 1e-3, tail * (1.0 - 0.5 * tail), jnp.log(1.0 + tail))
        delta = jnp.maximum(pre_step, 0.0) + tail
        step_keep[tile] = sigmoid(pre_step)
        delta_keep[tile] = delta
        lhs_d[lines, :] = turned(delta)
        lhs_u[lines, :] = turned(delta * inner_own)
        lhs_m[lines, :] = turned(got[tile, part : 2 * part])
        coef_keep[lines, :] = dot(turned(proj), spread_bc, (1, 0))

    for k in range(width // span):
        lanes = slice(k * span, (k + 1) * span)

        def prepare(tile, carry):
            lines = pl.ds(pl.multiple_of(tile * pos, pos), pos)
            of_delta, of_source, of_mix = (lhs_d[lines, :], lhs_u[lines, :], lhs_m[lines, :])
            a_ref[lines, lanes] = jnp.exp2(dot(of_delta, spread_e[:, lanes], (1, 0)) * rate_two[:, lanes])
            source = dot(of_source, spread_e[:, lanes], (1, 0))
            mix = dot(of_mix, spread_e[:, lanes], (1, 0))
            source_ref[lines, lanes] = source
            mix_ref[lines, lanes] = mix
            for j in range(span // 128):
                tile_lanes = slice(k * span + j * 128, k * span + (j + 1) * 128)
                piece = slice(j * 128, (j + 1) * 128)
                s_ref[lines, tile_lanes] = source[:, piece] * coef_keep[lines, :128]
                g_ref[lines, tile_lanes] = mix[:, piece] * coef_keep[lines, 128:]
            return carry

        lax.fori_loop(0, devices, prepare, 0, unroll=8)
    down_ref[:64] = jnp.zeros((64, width), f32)
    col_m[...] = jnp.zeros_like(col_m)
    right, left = (range(8), range(7, -1, -1))
    nothing = jnp.zeros((8, 128), f32)

    def packed(row, piece):
        return pl.ds(row * 64 + piece, 8, stride=8)

    def chain(state, row, order, ends, starts):
        for c in order:
            line = pl.ds(pl.multiple_of(row * 64 + c * 8, 8), 8)
            starts[line, :] = state
            state = prod[line, :] * state + ends[line, :]
        return state

    def link(row):
        return links[row]

    def carry_on(held, row, odd):
        ahead, behind = held
        ahead = ahead * link(row)
        if odd:
            ahead = chain(ahead, row, left, end_rl, in_rl)
            behind = chain(behind, row, left, back_lr, tail_lr)
        else:
            ahead = chain(ahead, row, right, end_lr, in_lr)
            behind = chain(behind, row, right, back_rl, tail_rl)
        return (ahead, behind * link(row + 1))

    def carry_back(held, row, odd):
        behind, ahead = held
        behind = behind * link(row + 1)
        if odd:
            behind = chain(behind, row, right, end_lr, in_lr)
            ahead = chain(ahead, row, right, back_rl, tail_rl)
        else:
            behind = chain(behind, row, left, end_rl, in_rl)
            ahead = chain(ahead, row, left, back_lr, tail_lr)
        return (behind, ahead * link(row))

    def wide_link(row):
        return jnp.concatenate([links[row]] * (group // 128), axis=1)

    def ascend(row):
        keep = wide_link(row)
        for k in range(width // group):
            lanes = slice(k * group, (k + 1) * group)
            whole = lr = rl = mlr = mrl = None
            for c in range(8):
                lines = pl.ds(pl.multiple_of(row * 64 + c * 8, 8), 8)
                spot = slice(c * 8, c * 8 + 8)
                a, s, g = (a_ref[lines, lanes], s_ref[lines, lanes], g_ref[lines, lanes])
                before, here = [
                    pl.ds(pl.multiple_of((row + step) * 64 + c * 8, 8), 8) for step in range(2)
                ]
                state_h = a * (down_ref[before, lanes] * keep) + s
                down_ref[here, lanes] = state_h
                lam = g + col_m[spot, lanes] * keep
                col_m[spot, lanes] = a * lam
                up_ref[lines, lanes] = lam
                if c == 0:
                    whole, lr, rl, mlr, mrl = (a, s, s, a * g, a * g)
                else:
                    lr = a * lr + s
                    rl = rl + whole * s
                    whole = whole * a
                    mlr = mlr + whole * g
                    mrl = a * (mrl + g)
            for j in range(group // 128):
                spot = packed(row, k * (group // 128) + j)
                piece = slice(j * 128, (j + 1) * 128)
                prod[spot, :] = whole[:, piece]
                end_lr[spot, :] = lr[:, piece]
                end_rl[spot, :] = rl[:, piece]
                back_lr[spot, :] = mlr[:, piece]
                back_rl[spot, :] = mrl[:, piece]

    def ascend_two(step, held):
        row = 2 * step + 1
        held = carry_on(held, row - 1, False)
        ascend(row)
        held = carry_on(held, row, True)
        ascend(row + 1)
        return held

    ascend(0)
    held = lax.fori_loop(0, devices - 1, ascend_two, (nothing,) * 2)
    held = carry_on(held, rows - 2, False)
    ascend(rows - 1)
    carry_on(held, rows - 1, True)
    col_h[...] = jnp.zeros_like(col_h)
    col_m[...] = jnp.zeros_like(col_m)

    def descend(row):
        keep = wide_link(row + 1)

        def edge(ref, k):
            pieces = [ref[packed(row, k * (group // 128) + j), :] for j in range(group // 128)]
            return pieces[0] if len(pieces) == 1 else jnp.concatenate(pieces, axis=1)

        for k in range(width // group):
            lanes = slice(k * group, (k + 1) * group)
            h_right, m_left = (edge(in_lr, k), edge(tail_rl, k))
            for c in range(8):
                lines = pl.ds(pl.multiple_of(row * 64 + c * 8, 8), 8)
                spot = slice(c * 8, c * 8 + 8)
                a, s, g = (a_ref[lines, lanes], s_ref[lines, lanes], g_ref[lines, lanes])
                h_right = a * h_right + s
                lam = g + m_left
                m_left = a * lam
                row_h[spot, lanes] = h_right
                row_m[spot, lanes] = lam
            h_left, m_right = (edge(in_rl, k), edge(tail_lr, k))
            for c in range(7, -1, -1):
                lines = pl.ds(pl.multiple_of(row * 64 + c * 8, 8), 8)
                spot = slice(c * 8, c * 8 + 8)
                a, s, g = (a_ref[lines, lanes], s_ref[lines, lanes], g_ref[lines, lanes])
                h_left = a * h_left + s
                lam_lr = g + m_right
                m_right = a * lam_lr
                here = pl.ds(pl.multiple_of((row + 1) * 64 + c * 8, 8), 8)
                h_down, lam_up = (down_ref[here, lanes], up_ref[lines, lanes])
                h_up = a * (col_h[spot, lanes] * keep) + s
                col_h[spot, lanes] = h_up
                lam_down = g + col_m[spot, lanes] * keep
                col_m[spot, lanes] = a * lam_down
                h_right, lam_rl = (row_h[spot, lanes], row_m[spot, lanes])
                lam_sum = (lam_lr + lam_rl) + (lam_down + lam_up)
                s_ref[lines, lanes] = (h_right + h_left) + (h_down + h_up)
                up_ref[lines, lanes] = lam_sum
                g_ref[lines, lanes] = (
                    (lam_lr * h_right + lam_rl * h_left)
                    + (lam_down * h_down + lam_up * h_up)
                    - s * lam_sum
                )

    def descend_two(step, held):
        row = rows - 1 - 2 * step
        held = carry_back(held, row - 1, False)
        descend(row)
        held = carry_back(held, row - 2, True)
        descend(row - 1)
        return held

    held = carry_back((nothing,) * 2, rows - 1, True)
    held = lax.fori_loop(0, devices - 1, descend_two, held)
    carry_back(held, 0, False)
    descend(1)
    descend(0)
    decay_acc[...] = jnp.zeros_like(decay_acc)
    gather_e, gather_b, gather_c = (spread_e[:part], spread_bc[:PROJ, :128], spread_bc[:PROJ, 128:])

    def finish(tile, carry):
        lines = pl.ds(pl.multiple_of(tile * pos, pos), pos)
        delta = delta_keep[tile]
        delta_low = delta.astype(bf16)
        of_b, of_c = (coef_keep[lines, :128], coef_keep[lines, 128:])
        grad_b = grad_c = None
        of_y, of_step, of_sum = ([], [], [])
        for k in range(width // 128):
            lanes = slice(k * 128, (k + 1) * 128)
            h_sum, lam_sum = (s_ref[lines, lanes], up_ref[lines, lanes])
            of_step.append((g_ref[lines, lanes] * rate_row[:, lanes]).astype(bf16))
            of_y.append((h_sum * of_c).astype(bf16))
            of_sum.append((lam_sum * of_b).astype(bf16))
            term_b, term_c = (lam_sum * source_ref[lines, lanes], h_sum * mix_ref[lines, lanes])
            grad_b = term_b if grad_b is None else grad_b + term_b
            grad_c = term_c if grad_c is None else grad_c + term_c
        of_y, of_step, of_sum = [jnp.concatenate(x, axis=1) for x in (of_y, of_step, of_sum)]
        decay_acc[...] += dot(delta_low, of_step, (1, 0))
        y_keep[tile] = jnp.transpose(dot(of_y, gather_e, (1, 1)))
        steps_keep[tile] = jnp.transpose(dot(of_step, gather_e, (1, 1)))
        sums_keep[tile] = jnp.transpose(dot(of_sum, gather_e, (1, 1)))
        coefs_keep[tile] = dot(gather_b, grad_b.astype(bf16), (1, 1)) + dot(gather_c, grad_c.astype(bf16), (1, 1))
        return carry

    lax.fori_loop(0, devices, finish, 0, unroll=8)
    pre_grads = []
    for tile in range(devices):
        sums = sums_keep[tile]
        pre_grads.append((steps_keep[tile] + got[tile, :part] * sums) * step_keep[tile])
        send[tile, :part] = y_keep[tile]
        send[tile, part : 2 * part] = delta_keep[tile] * sums
        send[tile, 2 * part + 16 :] = coefs_keep[tile, 16:]
    pre_grads = jnp.concatenate(pre_grads, axis=1)
    ranks = jnp.concatenate([got[tile, 2 * part : 2 * part + 16] for tile in range(devices)], axis=1)
    rank_grad = fine_dot(step_own, pre_grads, (0, 0))
    for tile in range(devices):
        send[tile, 2 * part : 2 * part + 16] = coefs_keep[tile, :16] + rank_grad[:, tile * pos : (tile + 1) * pos]
    step_grad = fine_dot(pre_grads, ranks, (1, 1))
    decay_grad = jnp.where(one_channel, decay_acc[...], 0.0)
    decay_high, decay_low = split(decay_grad)
    decay_grad = dot(decay_high, by_state, (1, 1)) + dot(decay_low, by_state, (1, 1))
    spot = (iota((part, small.shape[1]), 1) == iota((part, small.shape[1]), 0) + place[0] * part).astype(bf16)
    for at, value in ((0, step_grad), (16, decay_grad)):
        high, low = split(value)
        small[at : at + 16] = dot(high, spot, (0, 0)) + dot(low, spot, (0, 0))


def mix_kernel(
    place, group, got, small_in, low, low_halo, cot, conv_own, conv_halo, pre, gate_in, grad_in,
    select_rows, table, table_t, in_w, links,
    act_out, near, far, gate_grad_out, gated_ref, keep, give,
    grads, inner_ref, moved_ref, sums_ref, *, pair,
):
    devices, length, pos = got.shape
    model, inner_width = (low.shape[0], pre.shape[0])
    part = inner_width // devices
    lane = iota((1, pos), 1)
    prev, following = row_masks(links, place[0])
    proj_grad = got[0, 2 * part :]
    for k in range(1, devices):
        proj_grad = proj_grad + got[k, 2 * part :]
    proj_grad = proj_grad.astype(bf16)
    together = max(1, 48 // part)
    for first in range(0, devices, together):
        members = range(first, first + together)
        rows = slice(first * part, (first + together) * part)
        y = jnp.concatenate([got[k, :part] for k in members], axis=0)
        inner_grad = jnp.concatenate([got[k, part : 2 * part] for k in members], axis=0)
        pre_act, gate, gated_grad = (pre[rows], gate_in[rows], grad_in[rows])
        skip = table[rows, SKIP : SKIP + 1]
        sig_pre, sig_gate = (sigmoid(pre_act), sigmoid(gate))
        inner = (pre_act * sig_pre).astype(bf16)
        inner_ref[rows] = inner
        inner = inner.astype(f32)
        silu_gate = gate * sig_gate
        mix_grad = gated_grad * silu_gate
        inner_grad = inner_grad + mix_grad * skip + dot(select_rows[rows], proj_grad, (1, 0))
        act_grad = inner_grad * (sig_pre * (1.0 + pre_act * (1.0 - sig_pre)))
        act_out[rows] = act_grad
        y_all = y + skip * inner
        gated_ref[rows] = (y_all * silu_gate).astype(bf16)
        gate_grad_out[rows] = (gated_grad * y_all * (sig_gate * (1.0 + gate * (1.0 - sig_gate)))).astype(bf16)
        field = conv_own[rows]
        upper, lower = rows_around(field, conv_halo[rows])
        fields = (upper * prev, field, lower * following)
        sums = jnp.where(lane == 9, jnp.sum(act_grad, axis=1, keepdims=True), 0.0)
        sums = jnp.where(lane == 10, jnp.sum(mix_grad * inner, axis=1, keepdims=True), sums)
        for b, moved in enumerate((from_right(act_grad), act_grad, from_left(act_grad))):
            moved_ref[b, rows] = moved.astype(bf16)
            for a in range(3):
                sums = jnp.where(lane == 3 * a + b, jnp.sum(moved * fields[a], axis=1, keepdims=True), sums)
        sums_ref[rows] = sums
    conv_w = in_w[:, :inner_width].astype(f32)
    beyond = None
    for b in range(3):
        weights = [conv_w * table_t[3 * a + b : 3 * a + b + 1] for a in (0, 2)]
        term = dot(jnp.concatenate(weights, axis=0).astype(bf16), moved_ref[b], (1, 0))
        beyond = term if beyond is None else beyond + term
    beyond = jnp.where(lane < 64, beyond[:model] * prev, beyond[model:] * following)
    top, bottom = (beyond[: model // 2], beyond[model // 2 :])
    up = jnp.where(lane < 64, top, pltpu.roll(bottom, 64, 1))
    down = jnp.where(lane < 64, pltpu.roll(top, 64, 1), bottom)
    even = place[0] % 2 == 0
    near[...] = jnp.where(even, down, up)
    far[...] = jnp.where(even, up, down)
    gated, gate_grad = (gated_ref[...], gate_grad_out[...])

    low_in = low[...]
    upper, lower = rows_around(low_in.astype(f32), low_halo[...].astype(f32))
    which = iota((16, 1), 0)
    masks = jnp.where(which == 0, prev, jnp.where(which == 1, 1.0, following))
    left_hand = jnp.concatenate(
        [(upper * prev).astype(bf16), low_in, (lower * following).astype(bf16), masks.astype(bf16)], axis=0
    )
    blocks = inner_width // 128
    gate_at, out_at, small_at = [k * blocks * model for k in (1, 2, 3)]
    ones = jnp.ones((16, pos), bf16)
    totals = [[], []]
    gain_sum = jnp.zeros((model, 128), f32)
    for n in range(blocks):
        columns = slice(n * 128, (n + 1) * 128)
        in_conv = conv_total = None
        for b in range(3):
            part_b = dot(left_hand, moved_ref[b, columns], (1, 1))
            for a in range(3):
                tap = table_t[3 * a + b : 3 * a + b + 1, columns]
                term = tap * part_b[a * model : (a + 1) * model]
                total = tap * part_b[3 * model + a : 3 * model + a + 1]
                in_conv = term if in_conv is None else in_conv + term
                conv_total = total if conv_total is None else conv_total + total
        in_gate = dot(low_in, gate_grad[columns], (1, 1))
        grads[n * model : (n + 1) * model] = in_conv
        grads[gate_at + n * model : gate_at + (n + 1) * model] = in_gate
        grads[out_at + n * model : out_at + (n + 1) * model] = dot(cot[...], gated[columns], (1, 1))
        totals[0].append(conv_total)
        totals[1].append(dot(ones, gate_grad[columns], (1, 1))[0:1])
        conv_w = in_w[:, columns].astype(f32)
        gate_w = in_w[:, inner_width + n * 128 : inner_width + (n + 1) * 128].astype(f32)
        gain_sum = gain_sum + (conv_w * in_conv + gate_w * in_gate)
    sums = jnp.broadcast_to(jnp.concatenate(totals[0] + totals[1], axis=1), (16, 2 * inner_width))
    sums_high, sums_low = split(sums)
    shift_row = (dot(sums_high, in_w[...], (1, 1)) + dot(sums_low, in_w[...], (1, 1)))[0:1]
    gain_row = patch_sums(gain_sum)
    gain, shift = (table_t[GAIN : GAIN + 1, :model], table_t[SHIFT : SHIFT + 1, :model])
    gain_row = (gain_row - shift * shift_row) / gain
    high, mid = split(sums_ref[...])
    rest = (sums_ref[...] - high.astype(f32) - mid.astype(f32)).astype(bf16)
    chosen = (iota((16, pos), 0) == iota((16, pos), 1)).astype(bf16)
    sums = dot(chosen, high, (1, 1)) + (dot(chosen, mid, (1, 1)) + dot(chosen, rest, (1, 1)))
    norms = jnp.concatenate([gain_row, shift_row], axis=1)
    sums = jnp.where(iota((16, 1), 0) == NORM_AT - TAPS_AT, norms, sums)
    smalls = jnp.concatenate([dot(proj_grad, inner_ref[...], (1, 1)), small_in[...], sums], axis=0)
    put_blocks(grads, small_at, smalls)
    small_at = small_at + blocks * SMALL
    grads[small_at:] = jnp.zeros((grads.shape[0] - small_at, 128), f32)
    own = group[0] % 2
    if pair:
        count = keep.shape[0] // 2
        height = group[0] // 2
        for ref, side in ((keep, own), (give, 1 - own)):
            for k, at in enumerate((height, 1 - height)):
                ref[k * count : (k + 1) * count] = grads[pl.ds(pl.multiple_of((2 * side + at) * count, count), count)]
    else:
        count = keep.shape[0]
        keep[...] = grads[pl.ds(pl.multiple_of(own * count, count), count)]
        give[...] = grads[pl.ds(pl.multiple_of((1 - own) * count, count), count)]


def exit_kernel(
    place, act, from_above, from_below, gate_grad, gated, table, in_w, links, tok, cot, out_t,
    tokens_grad, layer_out,
):
    inner_width, pos = act.shape
    model = in_w.shape[0]
    lane = iota((1, pos), 1)
    even = place[0] % 2 == 0
    above, below = (
        jnp.where(even, from_above[...], from_below[...]), jnp.where(even, from_below[...], from_above[...])
    )
    top = jnp.where(lane < 64, above, pltpu.roll(below, 64, 1))
    bottom = jnp.where(lane < 64, pltpu.roll(above, 64, 1), below)
    beyond_high, beyond_low = split(jnp.concatenate([top, bottom], axis=0))
    act_grad = act[...]
    prev, following = row_masks(links, place[0])
    upper, lower = rows_around(act_grad, jnp.zeros_like(act_grad))
    columns = table[...]
    taps = [[columns[:, 8 - 3 * a - b : 9 - 3 * a - b] for b in range(3)] for a in range(3)]
    conv_grad = conv_tile(upper * prev, act_grad, lower * following, taps).astype(bf16)
    natural = jnp.concatenate([conv_grad, gate_grad[...], gated[...]], axis=0)
    order = column_order(pos)
    natural = dot(natural, order, (1, 0)).astype(bf16)
    layer = jnp.transpose(dot(out_t[...], natural[2 * inner_width :], (1, 0)))
    layer_out[...] = (tok[...].astype(f32) + layer).astype(bf16)
    normed_grad = dot(in_w[...], natural[: 2 * inner_width], (1, 0))
    normed_grad = normed_grad + (dot(beyond_high, order, (1, 0)) + dot(beyond_low, order, (1, 0)))
    xhat, inverse = normalized(flipped(tok[...]))
    scaled = normed_grad * columns[:model, GAIN : GAIN + 1]
    x_grad = (
        scaled
        - jnp.mean(scaled, axis=0, keepdims=True)
        - xhat * jnp.mean(scaled * xhat, axis=0, keepdims=True)
    ) * inverse
    x_grad = jnp.transpose(x_grad)
    tokens_grad[...] = (x_grad + cot[...].astype(f32)).astype(bf16)


def deal_kernel(group, *refs, members, pair):
    pieces, ordered = (refs[:members], refs[-1])
    (
        gain_grad, shift_grad, inproj, kernel_grad, offset, select, stepproj, stepbias, decay, skip, outproj,
    ) = refs[members:-1]
    model, inner_width = outproj.shape
    blocks = inner_width // 128
    rank = stepproj.shape[0]
    states = decay.shape[0]
    count = pieces[0].shape[0]
    for k, piece in enumerate(pieces):
        if pair:
            core, height = (group[0] % 2, group[0] // 2)
            core = 1 - core if k // 2 else core
            height = 1 - height if k % 2 else height
            slot = core * 2 + height
        else:
            slot = k % 2 * (members // 2) + k // 2
        ordered[pl.ds(pl.multiple_of(slot * count, count), count)] = piece[...]

    def rows(start, count):
        return ordered[start : start + count]

    for k in range(2 * blocks):
        inproj[:, k * 128 : (k + 1) * 128] = rows(k * model, model)
    start = 2 * blocks * model
    for k in range(blocks):
        outproj[:, k * 128 : (k + 1) * 128] = rows(start + k * model, model)
    start = start + blocks * model
    small = jnp.concatenate([rows(start + k * SMALL, SMALL) for k in range(blocks)], axis=1)
    select[:rank] = small[:rank]
    select[rank:] = small[IN:PROJ]
    stepproj[...] = small[STEP_AT : STEP_AT + rank]
    stepbias[...] = small[STEP_AT + ONE : STEP_AT + ONE + 1].reshape(stepbias.shape)
    decay[...] = small[DECAY_AT : DECAY_AT + states]
    for k in range(3):
        kernel_grad[k] = small[TAPS_AT + 3 * k : TAPS_AT + 3 * k + 3]
    offset[...] = small[OFFSET_AT : OFFSET_AT + 1].reshape(offset.shape)
    skip[...] = small[SKIP_AT : SKIP_AT + 1].reshape(skip.shape)
    norms = small[NORM_AT : NORM_AT + 1]
    gain_grad[...] = norms[:, :model].reshape(gain_grad.shape)
    shift_grad[...] = norms[:, model:].reshape(shift_grad.shape)


def vmem_call(kernel, out_shape, scalars, arrays, weights=(), scratch=(), limit=16):
    scalars = [pltpu.with_memory_space_constraint(x, pltpu.HBM) if x.ndim == 2 else x for x in scalars]
    arrays = [pltpu.with_memory_space_constraint(x, pltpu.VMEM) for x in arrays]
    arrays += [pltpu.with_memory_space_constraint(x, pltpu.HBM) for x in weights]
    return pl.pallas_call(
        kernel,
        out_shape=out_shape,
        in_specs=[pl.BlockSpec(memory_space=pltpu.SMEM)] * len(scalars)
        + [pl.BlockSpec(memory_space=pltpu.VMEM)] * len(arrays),
        out_specs=[pl.BlockSpec(memory_space=pltpu.VMEM)] * len(out_shape),
        scratch_shapes=list(scratch),
        compiler_params=pltpu.CompilerParams(vmem_limit_bytes=limit * 1024 * 1024),
    )(*scalars, *arrays)


def struct(*shape, dtype=f32):
    return jax.ShapeDtypeStruct(shape, dtype)


def inside(*shape, dtype=f32):
    return pltpu.VMEM(shape, dtype)


def scan_call(place, got, table, links, states):
    devices, length, pos = got.shape
    inner_width = table.shape[0]
    part = inner_width // devices
    width = -(-part * states // 128) * 128
    total = devices * pos
    span = 256 if width % 256 == 0 else 128
    group = 768 if width % 768 == 0 else span
    big = pltpu.VMEM((total, width), f32)
    line = pltpu.VMEM(((2 * devices + 1) * 64, 128), f32)
    column = pltpu.VMEM((pos // 2, width), f32)
    own = pltpu.VMEM((devices, part, pos), f32)
    return vmem_call(
        functools.partial(scan_kernel, part=part, states=states, span=span, group=group),
        [inside(devices, length, pos), inside(32, inner_width)],
        [place],
        [got, table, links],
        (),
        [big] * 3
        + [pltpu.VMEM((total + pos // 2, width), f32)]
        + [big] * 3
        + [column] * 4
        + [line] * 9
        + [pltpu.VMEM((total, 2 * part), bf16)] * 3
        + [pltpu.VMEM((total, 256), f32)]
        + [own] * 5
        + [pltpu.VMEM((devices, PROJ, pos), f32), pltpu.VMEM((part, width), f32)],
        limit=36 if total <= 1024 else 60,
    )


def on_device(
    tokens, heights, cotangent, norm_gain, norm_bias, in_weight, conv_kernel, conv_bias, select_weight,
    step_weight, step_bias, decay_log, skip_gain, out_weight,
):
    _, tile_rows, grid_cols, model = tokens.shape
    inner_width = out_weight.shape[0]
    states = decay_log.shape[1]
    rank = step_weight.shape[0]
    devices = lax.axis_size("seq")
    groups = lax.axis_size("dp")
    place = lax.axis_index("seq").reshape(1)
    group = lax.axis_index("dp").reshape(1)
    pair = groups == 4
    pos = tile_rows * grid_cols
    part = inner_width // devices
    length = 2 * part + PROJ
    near_pairs = [(i, i ^ 1) for i in range(devices)]
    far_pairs = [(i, (i - 1 + 2 * (i % 2)) % devices) for i in range(devices)]

    tok, cot = (tokens.reshape(pos, model), cotangent.reshape(pos, model))
    even = place[0] % 2 == 0
    upper, lower = (tok[:grid_cols].astype(f32), tok[grid_cols:].astype(f32))
    above = lax.ppermute(jnp.where(even, upper, lower), "seq", far_pairs)
    below = lax.ppermute(jnp.where(even, lower, upper), "seq", near_pairs)
    above, group = lax.optimization_barrier((above, group))
    out_t = out_weight.T
    channels = inside(inner_width, pos)
    narrow = inside(model, pos, dtype=bf16)
    conv_own, gate, gated_grad, mix, low, cot_in, conv_rows, select_rows, table, table_t, in_keep, links = vmem_call(
        own_kernel,
        [channels] * 4
        + [narrow] * 2
        + [
            inside(inner_width, model, dtype=bf16), inside(inner_width, PROJ, dtype=bf16), inside(inner_width, TABLE),
            inside(TABLE, inner_width), inside(model, 2 * inner_width, dtype=bf16),
            inside(2 * devices + 1, 8, 128),
        ],
        [heights],
        [],
        [
            tok, cot, in_weight, out_t, select_weight.T, conv_kernel, conv_bias, step_weight, step_bias,
            decay_log.T, skip_gain, norm_gain, norm_bias,
        ],
    )
    sent, conv_halo, pre_act, low_halo = vmem_call(
        entry_kernel,
        [inside(devices, length, pos), channels, channels, narrow],
        [place],
        [above, below, conv_own, mix, conv_rows, select_rows, table, links],
    )
    got = lax.all_to_all(sent, "seq", 0, 0, tiled=True)
    sent, small = scan_call(place, got, table, links, states)
    got = lax.all_to_all(sent, "seq", 0, 0, tiled=True)
    blocks = inner_width // 128
    whole = -(-blocks * (3 * model + SMALL) // 2048) * 2048
    half = whole // 2
    act_grad, near, far, gate_grad, gated, keep, give = vmem_call(
        functools.partial(mix_kernel, pair=pair),
        [channels]
        + [inside(model // 2, pos)] * 2
        + [inside(inner_width, pos, dtype=bf16)] * 2
        + [inside(half, 128)] * 2,
        [place, group],
        [
            got, small, low, low_halo, cot_in, conv_own, conv_halo, pre_act, gate, gated_grad, select_rows, table,
            table_t, in_keep, links,
        ],
        (),
        [
            pltpu.VMEM((whole, 128), f32), pltpu.VMEM((inner_width, pos), bf16),
            pltpu.VMEM((3, inner_width, pos), bf16), pltpu.VMEM((inner_width, pos), f32),
        ],
    )
    from_above = lax.ppermute(far, "seq", far_pairs)
    from_below = lax.ppermute(near, "seq", near_pairs)
    swap = [(i, i ^ 1) for i in range(groups)]
    taken = lax.ppermute(give, "dp", swap)
    count = half // (groups // 2)
    if pair:
        across = [(i, i ^ 2) for i in range(groups)]
        other = lax.ppermute(keep[count:] + taken[count:], "dp", across)
        piece = keep[:count] + taken[:count]
    else:
        same_core = [list(range(c, groups, 2)) for c in range(2)]
        pieces = (keep + taken).reshape(groups // 2, count, 128)
        pieces = lax.all_to_all(pieces, "dp", 0, 0, tiled=True, axis_index_groups=same_core)
        piece, other = (pieces[0], jnp.sum(pieces[1:], axis=0))
    other, from_above, from_below = lax.optimization_barrier((other, from_above, from_below))
    shares = (piece + other).reshape(devices, count // devices, 128)
    shares = lax.all_to_all(shares, "seq", 0, 0, tiled=True)
    share = jnp.broadcast_to(jnp.sum(shares, axis=0), shares.shape)
    mine = lax.all_to_all(share, "seq", 0, 0, tiled=True).reshape(count, 128)
    mine, from_above, from_below = lax.optimization_barrier((mine, from_above, from_below))
    tokens_grad, layer_out = vmem_call(
        exit_kernel,
        [struct(pos, model, dtype=bf16)] * 2,
        [place],
        [act_grad, from_above, from_below, gate_grad, gated, table, in_keep, links],
        [tok, cot, out_t],
    )
    if pair:
        from_y = lax.ppermute(mine, "dp", across)
        from_y, tokens_grad = lax.optimization_barrier((from_y, tokens_grad))
        pieces = [mine, from_y, lax.ppermute(mine, "dp", swap), lax.ppermute(from_y, "dp", swap)]
    else:
        pieces = list(lax.all_gather(mine, "dp"))
    gain, shift, inproj, kernel, offset, select, stepproj, stepbias, decay, skip, outproj = vmem_call(
        functools.partial(deal_kernel, members=len(pieces), pair=pair),
        [
            struct(model), struct(model), struct(model, 2 * inner_width), struct(3, 3, inner_width),
            struct(inner_width), struct(rank + 2 * states, inner_width), struct(rank, inner_width),
            struct(inner_width), struct(states, inner_width), struct(inner_width), struct(model, inner_width),
        ],
        [group],
        pieces,
        (),
        [pltpu.VMEM((whole, 128), f32)],
    )
    shape = tokens.shape
    return (
        layer_out.reshape(shape), tokens_grad.reshape(shape), gain, shift, inproj, kernel, offset, select.T,
        stepproj, stepbias, decay.T, skip, outproj.T,
    )


def solution(mesh):
    tile, whole = (P("dp", "seq", None, None), P())
    return jax.shard_map(
        on_device,
        mesh=mesh,
        in_specs=(tile, P("dp", None), tile) + (whole,) * 11,
        out_specs=(tile, tile) + (whole,) * 11,
        check_vma=False,
    )
```

```python
import functools

import jax
import jax.numpy as jnp
from jax import lax
from jax.experimental import pallas as pl
from jax.experimental.pallas import tpu as pltpu
from jax.sharding import PartitionSpec as P

epsilon = 1e-05
f32, bf16 = (jnp.float32, jnp.bfloat16)
ONE, IN, OUT, PROJ = (12, 16, 32, 48)
BIAS, SKIP, GAIN, SHIFT, STEP, DECAY, TABLE = (9, 10, 11, 12, 16, 32, 48)
STEP_AT, DECAY_AT, TAPS_AT, OFFSET_AT, SKIP_AT, NORM_AT, SMALL = (48, 64, 80, 89, 90, 95, 96)


def dot(a, b, over):
    return lax.dot_general(a, b, (((over[0],), (over[1],)), ((), ())), preferred_element_type=f32)


def split(value):
    high = value.astype(bf16)
    return (high, (value - high.astype(f32)).astype(bf16))


def fine_dot(a, b, over):
    (a_high, a_low), (b_high, b_low) = (split(a), split(b))
    return dot(a_high, b_high, over) + (dot(a_low, b_high, over) + dot(a_high, b_low, over))


def iota(shape, dim):
    return lax.broadcasted_iota(jnp.int32, shape, dim)


def sigmoid(v):
    return 1.0 / (1.0 + jnp.exp(-v))


def links_up(heights, row):
    if row == 0:
        return 0.0
    end = jnp.int32(0)
    same = True
    for k in range(heights.shape[1]):
        end = end + heights[0, k]
        same = same & (end != row)
    return jnp.where(same, 1.0, 0.0).astype(f32)


def row_masks(links, place):
    lane = iota((1, 128), 1)
    flags = [links[2 * place + k, 0:1] for k in range(3)]
    return (jnp.where(lane < 64, flags[0], flags[1]), jnp.where(lane < 64, flags[1], flags[2]))


def rows_around(own, halo):
    lane = iota((1, 128), 1)
    upper = pltpu.roll(jnp.where(lane < 64, own, halo), 64, 1)
    lower = pltpu.roll(jnp.where(lane < 64, halo, own), 64, 1)
    return (upper, lower)


def from_left(tile):
    place = iota((1, 128), 1) & 63
    wrapped = jnp.where(place == 0, 0.0, pltpu.roll(tile, 73, 1))
    return jnp.where(place < 8, wrapped, pltpu.roll(tile, 8, 1))


def from_right(tile):
    place = iota((1, 128), 1) & 63
    wrapped = jnp.where(place == 63, 0.0, pltpu.roll(tile, 55, 1))
    return jnp.where(place >= 56, wrapped, pltpu.roll(tile, 120, 1))


def conv_tile(upper, own, lower, taps):
    left, middle, right = [
        taps[0][b] * upper + taps[1][b] * own + taps[2][b] * lower for b in range(3)
    ]
    return middle + (from_left(left) + from_right(right))


def normalized(x):
    centred = x - jnp.mean(x, axis=0, keepdims=True)
    inverse = lax.rsqrt(jnp.mean(centred * centred, axis=0, keepdims=True) + epsilon)
    return (centred * inverse, inverse)


def eye(size):
    return (iota((size, size), 0) == iota((size, size), 1)).astype(bf16)


def flipped(value):
    pieces = [value[:, k : k + 128] for k in range(0, value.shape[1], 128)]
    return jnp.concatenate([dot(eye(piece.shape[1]), piece, (1, 1)) for piece in pieces], axis=0)


def flipped_fine(value):
    high, low = split(value)
    rest = (value - high.astype(f32) - low.astype(f32)).astype(bf16)
    return flipped(high) + (flipped(low) + flipped(rest))


def patch_sums(value):
    high, low = split(value)
    ones = jnp.ones((8, value.shape[1]), bf16)
    return (dot(ones, high, (1, 1)) + dot(ones, low, (1, 1)))[0:1]


def put_blocks(ref, start, value):
    for k in range(value.shape[1] // 128):
        ref[start + k * value.shape[0] : start + (k + 1) * value.shape[0]] = value[:, k * 128 : (k + 1) * 128]


def column_order(pos):
    new, old = (iota((pos, pos), 0), iota((pos, pos), 1))
    source = (new & ~63) | ((new & 7) << 3) | ((new >> 3) & 7)
    return (source == old).astype(bf16)


def lane_maps(part, states, width):
    lane = iota((1, width), 1)
    channel = jnp.floor((lane.astype(f32) + 0.5) * (1.0 / states)).astype(jnp.int32)
    return (channel, lane - channel * states, channel < part)


def entered(rows):
    return dot(flipped(rows).astype(bf16), column_order(rows.shape[0]), (1, 0))


def own_kernel(
    heights, place, tok, cot, in_w, out_t, select_t, conv_kernel, conv_bias, step_weight, step_bias, decay_t, skip_gain,
    norm_gain, norm_bias,
    conv_out, gate_out, grad_out, mix_out, low_out, cot_out, conv_rows, select_rows, table, table_t, in_keep, links,
    taps_wide, spread_e, spread_bc, by_state, one_channel, rates, step_three,
):
    model, inner_width = out_t.shape
    states = decay_t.shape[0]
    rank = step_weight.shape[0]
    in_keep[...] = in_w[...]
    for row in range(links.shape[0]):
        links[row] = jnp.full(links.shape[1:], links_up(heights, row), f32)
    in_rows = flipped(in_w[...]).astype(bf16)
    conv_rows[...] = in_rows[:inner_width]
    out_rows = flipped(out_t[...]).astype(bf16)
    chosen = iota((PROJ, select_t.shape[0]), 0)
    chosen = jnp.where(chosen < rank, chosen, jnp.where(chosen < IN, -1, chosen - IN + rank))
    chosen = (chosen == iota((PROJ, select_t.shape[0]), 1)).astype(bf16)
    select_rows[...] = flipped(dot(chosen, select_t[...], (1, 0)).astype(bf16)).astype(bf16)
    table_t[...] = jnp.zeros_like(table_t)
    for k in range(3):
        table_t[3 * k : 3 * k + 3] = conv_kernel[k]
    table_t[BIAS : BIAS + 1] = conv_bias[...].reshape(1, inner_width)
    table_t[SKIP : SKIP + 1] = skip_gain[...].reshape(1, inner_width)
    table_t[GAIN : GAIN + 1, :model] = norm_gain[...].reshape(1, model)
    table_t[SHIFT : SHIFT + 1, :model] = norm_bias[...].reshape(1, model)
    table_t[STEP : STEP + rank] = step_weight[...]
    table_t[STEP + ONE : STEP + ONE + 1] = step_bias[...].reshape(1, inner_width)
    table_t[DECAY : DECAY + states] = decay_t[...]
    columns = flipped_fine(table_t[...])
    table[...] = columns
    for k in range(taps_wide.shape[0]):
        taps_wide[k] = jnp.broadcast_to(columns[:, k : k + 1], taps_wide.shape[1:])
    gain, shift = (columns[:model, GAIN : GAIN + 1], columns[:model, SHIFT : SHIFT + 1])
    low = (normalized(entered(tok[...]))[0] * gain + shift).astype(bf16)
    cot_in = entered(cot[...]).astype(bf16)
    low_out[...] = low
    cot_out[...] = cot_in
    both = dot(in_rows, low, (1, 0))
    conv_out[...] = both[:inner_width]
    gate = both[inner_width:]
    gated_grad = dot(out_rows, cot_in, (1, 0))
    gate_out[...] = gate
    grad_out[...] = gated_grad
    mix_out[...] = gated_grad * (gate * sigmoid(gate))

    part, width = one_channel.shape
    own_rows = table[pl.ds(pl.multiple_of(place[0] * part, 4), part), :]
    channel, state, live = lane_maps(part, states, width)
    twice = iota((2 * part, 1), 0)
    twice = jnp.where(twice >= part, twice - part, twice)
    spread_e[...] = ((twice == channel) & live).astype(bf16)
    coef = iota((2 * PROJ, 1), 0)
    coef = jnp.where(coef >= PROJ, coef - PROJ, coef)
    first = state[:, :128]
    spread_bc[...] = jnp.concatenate([coef - IN == first, coef - OUT == first], axis=1).astype(bf16)
    of_state = ((iota((states, 1), 0) == state) & live).astype(bf16)
    by_state[...] = of_state
    mask = ((iota((part, 1), 0) == channel) & live).astype(f32)
    one_channel[...] = mask
    rate = -jnp.exp(own_rows[:, DECAY : DECAY + states])
    rate_high, rate_low = split(rate)
    rate_rest = split(rate - rate_high.astype(f32) - rate_low.astype(f32))[0]
    rate_row = sum(dot(piece, of_state, (1, 0)) for piece in (rate_high, rate_low, rate_rest))
    rate_row = jnp.sum(rate_row * mask, axis=0, keepdims=True)
    rates[...] = jnp.where(iota((8, 1), 0) == 0, rate_row, rate_row * 1.4426950408889634)
    step_high, step_low = split(own_rows[:, STEP : STEP + 16])
    step_three[...] = jnp.concatenate([step_high, step_high, step_low], axis=1)


def entry_kernel(
    place, above, below, conv_own, mix, conv_rows, select_rows, table, links, taps_wide,
    send, halo_out, pre_out, low_halo_out,
):
    devices = send.shape[0]
    inner_width = conv_own.shape[0]
    model = conv_rows.shape[1]
    part = inner_width // devices
    gain, shift = (table[:model, GAIN : GAIN + 1], table[:model, SHIFT : SHIFT + 1])
    even = place[0] % 2 == 0
    halo = jnp.concatenate(
        [jnp.where(even, below[...], above[...]), jnp.where(even, above[...], below[...])], axis=0
    ).astype(bf16)
    low_halo = (normalized(entered(halo))[0] * gain + shift).astype(bf16)
    low_halo_out[...] = low_halo
    around = dot(conv_rows[...], low_halo, (1, 0))
    halo_out[...] = around
    conv_in = conv_own[...]
    prev, following = row_masks(links, place[0])
    upper, lower = rows_around(conv_in, around)
    taps = [[taps_wide[3 * a + b] for b in range(3)] for a in range(3)]
    pre_act = taps_wide[BIAS] + conv_tile(upper * prev, conv_in, lower * following, taps)
    inner = (pre_act * sigmoid(pre_act)).astype(bf16)
    proj = dot(flipped(select_rows[...]).astype(bf16), inner, (1, 0))
    proj = jnp.where(iota(proj.shape, 0) == ONE, 1.0, proj)
    pre_out[...] = pre_act
    inner = inner.astype(f32)
    for k in range(devices):
        send[k, :part] = inner[k * part : (k + 1) * part]
        send[k, part : 2 * part] = mix[k * part : (k + 1) * part]
        send[k, 2 * part :] = proj


def scan_kernel(
    place, got, table, links, spread_e, spread_bc, by_state, one_channel, rates, step_three,
    send, small,
    a_ref, s_ref, g_ref, down_ref, up_ref, source_ref, mix_ref, col_h, col_m, row_h, row_m,
    prod, end_lr, end_rl, back_lr, back_rl, in_lr, in_rl, tail_lr, tail_rl,
    lhs_d, lhs_u, lhs_m, coef_keep, step_keep, delta_keep, y_keep, steps_keep, sums_keep, coefs_keep, decay_acc, *, part, states, span, group,
):
    devices, _, pos = got.shape
    rows = 2 * devices
    width = a_ref.shape[1]
    rate_row, rate_two = (rates[0:1], rates[1:2])
    step_own = table[pl.ds(pl.multiple_of(place[0] * part, 4), part), STEP : STEP + 16]

    def turned(value):
        return jnp.transpose(jnp.concatenate(split(value), axis=0))

    for tile in range(devices):
        lines = slice(tile * pos, (tile + 1) * pos)
        inner_own = got[tile, :part]
        proj = got[tile, 2 * part :]
        high, low = split(proj[:16])
        pre_step = dot(step_three[...], jnp.concatenate([high, low, high], axis=0), (1, 0))
        tail = jnp.exp(-jnp.abs(pre_step))
        tail = jnp.where(tail < 1e-3, tail * (1.0 - 0.5 * tail), jnp.log(1.0 + tail))
        delta = jnp.maximum(pre_step, 0.0) + tail
        step_keep[tile] = sigmoid(pre_step)
        delta_keep[tile] = delta
        lhs_d[lines, :] = turned(delta)
        lhs_u[lines, :] = turned(delta * inner_own)
        lhs_m[lines, :] = turned(got[tile, part : 2 * part])
        coef_keep[lines, :] = dot(turned(proj), spread_bc[...], (1, 0))

    for k in range(width // span):
        lanes = slice(k * span, (k + 1) * span)

        def prepare(tile, carry):
            lines = pl.ds(pl.multiple_of(tile * pos, pos), pos)
            of_delta, of_source, of_mix = (lhs_d[lines, :], lhs_u[lines, :], lhs_m[lines, :])
            a_ref[lines, lanes] = jnp.exp2(dot(of_delta, spread_e[:, lanes], (1, 0)) * rate_two[:, lanes])
            source = dot(of_source, spread_e[:, lanes], (1, 0))
            mix = dot(of_mix, spread_e[:, lanes], (1, 0))
            source_ref[lines, lanes] = source
            mix_ref[lines, lanes] = mix
            for j in range(span // 128):
                tile_lanes = slice(k * span + j * 128, k * span + (j + 1) * 128)
                piece = slice(j * 128, (j + 1) * 128)
                s_ref[lines, tile_lanes] = source[:, piece] * coef_keep[lines, :128]
                g_ref[lines, tile_lanes] = mix[:, piece] * coef_keep[lines, 128:]
            return carry

        lax.fori_loop(0, devices, prepare, 0, unroll=8)
    down_ref[:64] = jnp.zeros((64, width), f32)
    col_m[...] = jnp.zeros_like(col_m)
    right, left = (range(8), range(7, -1, -1))
    nothing = jnp.zeros((8, 128), f32)

    def packed(row, piece):
        return pl.ds(row * 64 + piece, 8, stride=8)

    def chain(state, row, order, ends, starts):
        for c in order:
            line = pl.ds(pl.multiple_of(row * 64 + c * 8, 8), 8)
            starts[line, :] = state
            state = prod[line, :] * state + ends[line, :]
        return state

    def link(row):
        return links[row]

    def carry_on(held, row, odd):
        ahead, behind = held
        ahead = ahead * link(row)
        if odd:
            ahead = chain(ahead, row, left, end_rl, in_rl)
            behind = chain(behind, row, left, back_lr, tail_lr)
        else:
            ahead = chain(ahead, row, right, end_lr, in_lr)
            behind = chain(behind, row, right, back_rl, tail_rl)
        return (ahead, behind * link(row + 1))

    def carry_back(held, row, odd):
        behind, ahead = held
        behind = behind * link(row + 1)
        if odd:
            behind = chain(behind, row, right, end_lr, in_lr)
            ahead = chain(ahead, row, right, back_rl, tail_rl)
        else:
            behind = chain(behind, row, left, end_rl, in_rl)
            ahead = chain(ahead, row, left, back_lr, tail_lr)
        return (behind, ahead * link(row))

    def wide_link(row):
        return jnp.concatenate([links[row]] * (group // 128), axis=1)

    def ascend(row):
        keep = wide_link(row)
        for k in range(width // group):
            lanes = slice(k * group, (k + 1) * group)
            whole = lr = rl = mlr = mrl = None
            for c in range(8):
                lines = pl.ds(pl.multiple_of(row * 64 + c * 8, 8), 8)
                spot = slice(c * 8, c * 8 + 8)
                a, s, g = (a_ref[lines, lanes], s_ref[lines, lanes], g_ref[lines, lanes])
                before, here = [
                    pl.ds(pl.multiple_of((row + step) * 64 + c * 8, 8), 8) for step in range(2)
                ]
                state_h = a * (down_ref[before, lanes] * keep) + s
                down_ref[here, lanes] = state_h
                lam = g + col_m[spot, lanes] * keep
                col_m[spot, lanes] = a * lam
                up_ref[lines, lanes] = lam
                if c == 0:
                    whole, lr, rl, mlr, mrl = (a, s, s, a * g, a * g)
                else:
                    lr = a * lr + s
                    rl = rl + whole * s
                    whole = whole * a
                    mlr = mlr + whole * g
                    mrl = a * (mrl + g)
            for j in range(group // 128):
                spot = packed(row, k * (group // 128) + j)
                piece = slice(j * 128, (j + 1) * 128)
                prod[spot, :] = whole[:, piece]
                end_lr[spot, :] = lr[:, piece]
                end_rl[spot, :] = rl[:, piece]
                back_lr[spot, :] = mlr[:, piece]
                back_rl[spot, :] = mrl[:, piece]

    def ascend_two(step, held):
        row = 2 * step + 1
        held = carry_on(held, row - 1, False)
        ascend(row)
        held = carry_on(held, row, True)
        ascend(row + 1)
        return held

    ascend(0)
    held = lax.fori_loop(0, devices - 1, ascend_two, (nothing,) * 2)
    held = carry_on(held, rows - 2, False)
    ascend(rows - 1)
    carry_on(held, rows - 1, True)
    col_h[...] = jnp.zeros_like(col_h)
    col_m[...] = jnp.zeros_like(col_m)

    def descend(row):
        keep = wide_link(row + 1)

        def edge(ref, k):
            pieces = [ref[packed(row, k * (group // 128) + j), :] for j in range(group // 128)]
            return pieces[0] if len(pieces) == 1 else jnp.concatenate(pieces, axis=1)

        for k in range(width // group):
            lanes = slice(k * group, (k + 1) * group)
            h_right, m_left = (edge(in_lr, k), edge(tail_rl, k))
            for c in range(8):
                lines = pl.ds(pl.multiple_of(row * 64 + c * 8, 8), 8)
                spot = slice(c * 8, c * 8 + 8)
                a, s, g = (a_ref[lines, lanes], s_ref[lines, lanes], g_ref[lines, lanes])
                h_right = a * h_right + s
                lam = g + m_left
                m_left = a * lam
                row_h[spot, lanes] = h_right
                row_m[spot, lanes] = lam
            h_left, m_right = (edge(in_rl, k), edge(tail_lr, k))
            for c in range(7, -1, -1):
                lines = pl.ds(pl.multiple_of(row * 64 + c * 8, 8), 8)
                spot = slice(c * 8, c * 8 + 8)
                a, s, g = (a_ref[lines, lanes], s_ref[lines, lanes], g_ref[lines, lanes])
                h_left = a * h_left + s
                lam_lr = g + m_right
                m_right = a * lam_lr
                here = pl.ds(pl.multiple_of((row + 1) * 64 + c * 8, 8), 8)
                h_down, lam_up = (down_ref[here, lanes], up_ref[lines, lanes])
                h_up = a * (col_h[spot, lanes] * keep) + s
                col_h[spot, lanes] = h_up
                lam_down = g + col_m[spot, lanes] * keep
                col_m[spot, lanes] = a * lam_down
                h_right, lam_rl = (row_h[spot, lanes], row_m[spot, lanes])
                lam_sum = (lam_lr + lam_rl) + (lam_down + lam_up)
                s_ref[lines, lanes] = (h_right + h_left) + (h_down + h_up)
                up_ref[lines, lanes] = lam_sum
                g_ref[lines, lanes] = (
                    (lam_lr * h_right + lam_rl * h_left)
                    + (lam_down * h_down + lam_up * h_up)
                    - s * lam_sum
                )

    def descend_two(step, held):
        row = rows - 1 - 2 * step
        held = carry_back(held, row - 1, False)
        descend(row)
        held = carry_back(held, row - 2, True)
        descend(row - 1)
        return held

    held = carry_back((nothing,) * 2, rows - 1, True)
    held = lax.fori_loop(0, devices - 1, descend_two, held)
    carry_back(held, 0, False)
    descend(1)
    descend(0)
    decay_acc[...] = jnp.zeros_like(decay_acc)
    gather_e, gather_b, gather_c = (spread_e[:part], spread_bc[:PROJ, :128], spread_bc[:PROJ, 128:])

    def finish(tile, carry):
        lines = pl.ds(pl.multiple_of(tile * pos, pos), pos)
        delta = delta_keep[tile]
        delta_low = delta.astype(bf16)
        of_b, of_c = (coef_keep[lines, :128], coef_keep[lines, 128:])
        grad_b = grad_c = None
        of_y, of_step, of_sum = ([], [], [])
        for k in range(width // 128):
            lanes = slice(k * 128, (k + 1) * 128)
            h_sum, lam_sum = (s_ref[lines, lanes], up_ref[lines, lanes])
            of_step.append((g_ref[lines, lanes] * rate_row[:, lanes]).astype(bf16))
            of_y.append((h_sum * of_c).astype(bf16))
            of_sum.append((lam_sum * of_b).astype(bf16))
            term_b, term_c = (lam_sum * source_ref[lines, lanes], h_sum * mix_ref[lines, lanes])
            grad_b = term_b if grad_b is None else grad_b + term_b
            grad_c = term_c if grad_c is None else grad_c + term_c
        of_y, of_step, of_sum = [jnp.concatenate(x, axis=1) for x in (of_y, of_step, of_sum)]
        decay_acc[...] += dot(delta_low, of_step, (1, 0))
        y_keep[tile] = jnp.transpose(dot(of_y, gather_e, (1, 1)))
        steps_keep[tile] = jnp.transpose(dot(of_step, gather_e, (1, 1)))
        sums_keep[tile] = jnp.transpose(dot(of_sum, gather_e, (1, 1)))
        coefs_keep[tile] = dot(gather_b, grad_b.astype(bf16), (1, 1)) + dot(gather_c, grad_c.astype(bf16), (1, 1))
        return carry

    lax.fori_loop(0, devices, finish, 0, unroll=8)
    pre_grads = []
    for tile in range(devices):
        sums = sums_keep[tile]
        pre_grads.append((steps_keep[tile] + got[tile, :part] * sums) * step_keep[tile])
        send[tile, :part] = y_keep[tile]
        send[tile, part : 2 * part] = delta_keep[tile] * sums
        send[tile, 2 * part + 16 :] = coefs_keep[tile, 16:]
    pre_grads = jnp.concatenate(pre_grads, axis=1)
    ranks = jnp.concatenate([got[tile, 2 * part : 2 * part + 16] for tile in range(devices)], axis=1)
    rank_grad = fine_dot(step_own, pre_grads, (0, 0))
    for tile in range(devices):
        send[tile, 2 * part : 2 * part + 16] = coefs_keep[tile, :16] + rank_grad[:, tile * pos : (tile + 1) * pos]
    step_grad = fine_dot(pre_grads, ranks, (1, 1))
    decay_grad = decay_acc[...] * one_channel[...]
    decay_high, decay_low = split(decay_grad)
    decay_grad = dot(decay_high, by_state[...], (1, 1)) + dot(decay_low, by_state[...], (1, 1))
    spot = (iota((part, small.shape[1]), 1) == iota((part, small.shape[1]), 0) + place[0] * part).astype(bf16)
    for at, value in ((0, step_grad), (16, decay_grad)):
        high, low = split(value)
        small[at : at + 16] = dot(high, spot, (0, 0)) + dot(low, spot, (0, 0))


def mix_kernel(
    place, group, got, small_in, low, low_halo, cot, conv_own, conv_halo, pre, gate_in, grad_in,
    select_rows, table, table_t, in_w, links,
    act_out, near, far, gate_grad_out, gated_ref, keep, give,
    grads, inner_ref, moved_ref, sums_ref, *, pair,
):
    devices, length, pos = got.shape
    model, inner_width = (low.shape[0], pre.shape[0])
    part = inner_width // devices
    lane = iota((1, pos), 1)
    prev, following = row_masks(links, place[0])
    proj_grad = got[0, 2 * part :]
    for k in range(1, devices):
        proj_grad = proj_grad + got[k, 2 * part :]
    proj_grad = proj_grad.astype(bf16)
    together = max(1, 48 // part)
    for first in range(0, devices, together):
        members = range(first, first + together)
        rows = slice(first * part, (first + together) * part)
        y = jnp.concatenate([got[k, :part] for k in members], axis=0)
        inner_grad = jnp.concatenate([got[k, part : 2 * part] for k in members], axis=0)
        pre_act, gate, gated_grad = (pre[rows], gate_in[rows], grad_in[rows])
        skip = table[rows, SKIP : SKIP + 1]
        sig_pre, sig_gate = (sigmoid(pre_act), sigmoid(gate))
        inner = (pre_act * sig_pre).astype(bf16)
        inner_ref[rows] = inner
        inner = inner.astype(f32)
        silu_gate = gate * sig_gate
        mix_grad = gated_grad * silu_gate
        inner_grad = inner_grad + mix_grad * skip + dot(select_rows[rows], proj_grad, (1, 0))
        act_grad = inner_grad * (sig_pre * (1.0 + pre_act * (1.0 - sig_pre)))
        act_out[rows] = act_grad
        y_all = y + skip * inner
        gated_ref[rows] = (y_all * silu_gate).astype(bf16)
        gate_grad_out[rows] = (gated_grad * y_all * (sig_gate * (1.0 + gate * (1.0 - sig_gate)))).astype(bf16)
        field = conv_own[rows]
        upper, lower = rows_around(field, conv_halo[rows])
        fields = (upper * prev, field, lower * following)
        sums = jnp.where(lane == 9, jnp.sum(act_grad, axis=1, keepdims=True), 0.0)
        sums = jnp.where(lane == 10, jnp.sum(mix_grad * inner, axis=1, keepdims=True), sums)
        for b, moved in enumerate((from_right(act_grad), act_grad, from_left(act_grad))):
            moved_ref[b, rows] = moved.astype(bf16)
            for a in range(3):
                sums = jnp.where(lane == 3 * a + b, jnp.sum(moved * fields[a], axis=1, keepdims=True), sums)
        sums_ref[rows] = sums
    conv_w = in_w[:, :inner_width].astype(f32)
    beyond = None
    for b in range(3):
        weights = [conv_w * table_t[3 * a + b : 3 * a + b + 1] for a in (0, 2)]
        term = dot(jnp.concatenate(weights, axis=0).astype(bf16), moved_ref[b], (1, 0))
        beyond = term if beyond is None else beyond + term
    beyond = jnp.where(lane < 64, beyond[:model] * prev, beyond[model:] * following)
    top, bottom = (beyond[: model // 2], beyond[model // 2 :])
    up = jnp.where(lane < 64, top, pltpu.roll(bottom, 64, 1))
    down = jnp.where(lane < 64, pltpu.roll(top, 64, 1), bottom)
    even = place[0] % 2 == 0
    near[...] = jnp.where(even, down, up)
    far[...] = jnp.where(even, up, down)
    gated, gate_grad = (gated_ref[...], gate_grad_out[...])

    low_in = low[...]
    upper, lower = rows_around(low_in.astype(f32), low_halo[...].astype(f32))
    which = iota((16, 1), 0)
    masks = jnp.where(which == 0, prev, jnp.where(which == 1, 1.0, following))
    left_hand = jnp.concatenate(
        [(upper * prev).astype(bf16), low_in, (lower * following).astype(bf16), masks.astype(bf16)], axis=0
    )
    blocks = inner_width // 128
    gate_at, out_at, small_at = [k * blocks * model for k in (1, 2, 3)]
    ones = jnp.ones((16, pos), bf16)
    totals = [[], []]
    gain_sum = jnp.zeros((model, 128), f32)
    for n in range(blocks):
        columns = slice(n * 128, (n + 1) * 128)
        in_conv = conv_total = None
        for b in range(3):
            part_b = dot(left_hand, moved_ref[b, columns], (1, 1))
            for a in range(3):
                tap = table_t[3 * a + b : 3 * a + b + 1, columns]
                term = tap * part_b[a * model : (a + 1) * model]
                total = tap * part_b[3 * model + a : 3 * model + a + 1]
                in_conv = term if in_conv is None else in_conv + term
                conv_total = total if conv_total is None else conv_total + total
        in_gate = dot(low_in, gate_grad[columns], (1, 1))
        grads[n * model : (n + 1) * model] = in_conv
        grads[gate_at + n * model : gate_at + (n + 1) * model] = in_gate
        grads[out_at + n * model : out_at + (n + 1) * model] = dot(cot[...], gated[columns], (1, 1))
        totals[0].append(conv_total)
        totals[1].append(dot(ones, gate_grad[columns], (1, 1))[0:1])
        conv_w = in_w[:, columns].astype(f32)
        gate_w = in_w[:, inner_width + n * 128 : inner_width + (n + 1) * 128].astype(f32)
        gain_sum = gain_sum + (conv_w * in_conv + gate_w * in_gate)
    sums = jnp.broadcast_to(jnp.concatenate(totals[0] + totals[1], axis=1), (16, 2 * inner_width))
    sums_high, sums_low = split(sums)
    shift_row = (dot(sums_high, in_w[...], (1, 1)) + dot(sums_low, in_w[...], (1, 1)))[0:1]
    gain_row = patch_sums(gain_sum)
    gain, shift = (table_t[GAIN : GAIN + 1, :model], table_t[SHIFT : SHIFT + 1, :model])
    gain_row = (gain_row - shift * shift_row) / gain
    high, mid = split(sums_ref[...])
    rest = (sums_ref[...] - high.astype(f32) - mid.astype(f32)).astype(bf16)
    chosen = (iota((16, pos), 0) == iota((16, pos), 1)).astype(bf16)
    sums = dot(chosen, high, (1, 1)) + (dot(chosen, mid, (1, 1)) + dot(chosen, rest, (1, 1)))
    norms = jnp.concatenate([gain_row, shift_row], axis=1)
    sums = jnp.where(iota((16, 1), 0) == NORM_AT - TAPS_AT, norms, sums)
    smalls = jnp.concatenate([dot(proj_grad, inner_ref[...], (1, 1)), small_in[...], sums], axis=0)
    put_blocks(grads, small_at, smalls)
    small_at = small_at + blocks * SMALL
    grads[small_at:] = jnp.zeros((grads.shape[0] - small_at, 128), f32)
    own = group[0] % 2
    if pair:
        count = keep.shape[0] // 2
        height = group[0] // 2
        for ref, side in ((keep, own), (give, 1 - own)):
            for k, at in enumerate((height, 1 - height)):
                ref[k * count : (k + 1) * count] = grads[pl.ds(pl.multiple_of((2 * side + at) * count, count), count)]
    else:
        count = keep.shape[0]
        keep[...] = grads[pl.ds(pl.multiple_of(own * count, count), count)]
        give[...] = grads[pl.ds(pl.multiple_of((1 - own) * count, count), count)]


def exit_kernel(
    place, act, from_above, from_below, gate_grad, gated, table, in_w, links, tok, cot, out_t,
    tokens_grad, layer_out,
):
    inner_width, pos = act.shape
    model = in_w.shape[0]
    lane = iota((1, pos), 1)
    even = place[0] % 2 == 0
    above, below = (
        jnp.where(even, from_above[...], from_below[...]), jnp.where(even, from_below[...], from_above[...])
    )
    top = jnp.where(lane < 64, above, pltpu.roll(below, 64, 1))
    bottom = jnp.where(lane < 64, pltpu.roll(above, 64, 1), below)
    beyond_high, beyond_low = split(jnp.concatenate([top, bottom], axis=0))
    act_grad = act[...]
    prev, following = row_masks(links, place[0])
    upper, lower = rows_around(act_grad, jnp.zeros_like(act_grad))
    columns = table[...]
    taps = [[columns[:, 8 - 3 * a - b : 9 - 3 * a - b] for b in range(3)] for a in range(3)]
    conv_grad = conv_tile(upper * prev, act_grad, lower * following, taps).astype(bf16)
    natural = jnp.concatenate([conv_grad, gate_grad[...], gated[...]], axis=0)
    order = column_order(pos)
    natural = dot(natural, order, (1, 0)).astype(bf16)
    layer = jnp.transpose(dot(out_t[...], natural[2 * inner_width :], (1, 0)))
    layer_out[...] = (tok[...].astype(f32) + layer).astype(bf16)
    normed_grad = dot(in_w[...], natural[: 2 * inner_width], (1, 0))
    normed_grad = normed_grad + (dot(beyond_high, order, (1, 0)) + dot(beyond_low, order, (1, 0)))
    xhat, inverse = normalized(flipped(tok[...]))
    scaled = normed_grad * columns[:model, GAIN : GAIN + 1]
    x_grad = (
        scaled
        - jnp.mean(scaled, axis=0, keepdims=True)
        - xhat * jnp.mean(scaled * xhat, axis=0, keepdims=True)
    ) * inverse
    x_grad = jnp.transpose(x_grad)
    tokens_grad[...] = (x_grad + cot[...].astype(f32)).astype(bf16)


def deal_kernel(group, *refs, members, pair):
    pieces, ordered = (refs[:members], refs[-1])
    (
        gain_grad, shift_grad, inproj, kernel_grad, offset, select, stepproj, stepbias, decay, skip, outproj,
    ) = refs[members:-1]
    model, inner_width = outproj.shape
    blocks = inner_width // 128
    rank = stepproj.shape[0]
    states = decay.shape[0]
    count = pieces[0].shape[0]
    for k, piece in enumerate(pieces):
        if pair:
            core, height = (group[0] % 2, group[0] // 2)
            core = 1 - core if k // 2 else core
            height = 1 - height if k % 2 else height
            slot = core * 2 + height
        else:
            slot = k % 2 * (members // 2) + k // 2
        ordered[pl.ds(pl.multiple_of(slot * count, count), count)] = piece[...]

    def rows(start, count):
        return ordered[start : start + count]

    for k in range(2 * blocks):
        inproj[:, k * 128 : (k + 1) * 128] = rows(k * model, model)
    start = 2 * blocks * model
    for k in range(blocks):
        outproj[:, k * 128 : (k + 1) * 128] = rows(start + k * model, model)
    start = start + blocks * model
    small = jnp.concatenate([rows(start + k * SMALL, SMALL) for k in range(blocks)], axis=1)
    select[:rank] = small[:rank]
    select[rank:] = small[IN:PROJ]
    stepproj[...] = small[STEP_AT : STEP_AT + rank]
    stepbias[...] = small[STEP_AT + ONE : STEP_AT + ONE + 1].reshape(stepbias.shape)
    decay[...] = small[DECAY_AT : DECAY_AT + states]
    for k in range(3):
        kernel_grad[k] = small[TAPS_AT + 3 * k : TAPS_AT + 3 * k + 3]
    offset[...] = small[OFFSET_AT : OFFSET_AT + 1].reshape(offset.shape)
    skip[...] = small[SKIP_AT : SKIP_AT + 1].reshape(skip.shape)
    norms = small[NORM_AT : NORM_AT + 1]
    gain_grad[...] = norms[:, :model].reshape(gain_grad.shape)
    shift_grad[...] = norms[:, model:].reshape(shift_grad.shape)


def vmem_call(kernel, out_shape, scalars, arrays, weights=(), scratch=(), limit=16):
    scalars = [pltpu.with_memory_space_constraint(x, pltpu.HBM) if x.ndim == 2 else x for x in scalars]
    arrays = [pltpu.with_memory_space_constraint(x, pltpu.VMEM) for x in arrays]
    arrays += [pltpu.with_memory_space_constraint(x, pltpu.HBM) for x in weights]
    return pl.pallas_call(
        kernel,
        out_shape=out_shape,
        in_specs=[pl.BlockSpec(memory_space=pltpu.SMEM)] * len(scalars)
        + [pl.BlockSpec(memory_space=pltpu.VMEM)] * len(arrays),
        out_specs=[pl.BlockSpec(memory_space=pltpu.VMEM)] * len(out_shape),
        scratch_shapes=list(scratch),
        compiler_params=pltpu.CompilerParams(vmem_limit_bytes=limit * 1024 * 1024),
    )(*scalars, *arrays)


def struct(*shape, dtype=f32):
    return jax.ShapeDtypeStruct(shape, dtype)


def inside(*shape, dtype=f32):
    return pltpu.VMEM(shape, dtype)


def scan_call(place, got, table, links, maps, states):
    devices, length, pos = got.shape
    inner_width = table.shape[0]
    part = inner_width // devices
    width = -(-part * states // 128) * 128
    total = devices * pos
    span = 256 if width % 256 == 0 else 128
    group = 768 if width % 768 == 0 else span
    big = pltpu.VMEM((total, width), f32)
    line = pltpu.VMEM(((2 * devices + 1) * 64, 128), f32)
    column = pltpu.VMEM((pos // 2, width), f32)
    own = pltpu.VMEM((devices, part, pos), f32)
    return vmem_call(
        functools.partial(scan_kernel, part=part, states=states, span=span, group=group),
        [inside(devices, length, pos), inside(32, inner_width)],
        [place],
        [got, table, links, *maps],
        (),
        [big] * 3
        + [pltpu.VMEM((total + pos // 2, width), f32)]
        + [big] * 3
        + [column] * 4
        + [line] * 9
        + [pltpu.VMEM((total, 2 * part), bf16)] * 3
        + [pltpu.VMEM((total, 256), f32)]
        + [own] * 5
        + [pltpu.VMEM((devices, PROJ, pos), f32), pltpu.VMEM((part, width), f32)],
        limit=36 if total <= 1024 else 60,
    )


def on_device(
    tokens, heights, cotangent, norm_gain, norm_bias, in_weight, conv_kernel, conv_bias, select_weight,
    step_weight, step_bias, decay_log, skip_gain, out_weight,
):
    _, tile_rows, grid_cols, model = tokens.shape
    inner_width = out_weight.shape[0]
    states = decay_log.shape[1]
    rank = step_weight.shape[0]
    devices = lax.axis_size("seq")
    groups = lax.axis_size("dp")
    place = lax.axis_index("seq").reshape(1)
    group = lax.axis_index("dp").reshape(1)
    pair = groups == 4
    pos = tile_rows * grid_cols
    part = inner_width // devices
    width = -(-part * states // 128) * 128
    length = 2 * part + PROJ
    near_pairs = [(i, i ^ 1) for i in range(devices)]
    far_pairs = [(i, (i - 1 + 2 * (i % 2)) % devices) for i in range(devices)]

    tok, cot = (tokens.reshape(pos, model), cotangent.reshape(pos, model))
    even = place[0] % 2 == 0
    upper, lower = (tok[:grid_cols].astype(f32), tok[grid_cols:].astype(f32))
    above = lax.ppermute(jnp.where(even, upper, lower), "seq", far_pairs)
    below = lax.ppermute(jnp.where(even, lower, upper), "seq", near_pairs)
    above, group = lax.optimization_barrier((above, group))
    out_t = out_weight.T
    channels = inside(inner_width, pos)
    narrow = inside(model, pos, dtype=bf16)
    conv_own, gate, gated_grad, mix, low, cot_in, conv_rows, select_rows, table, table_t, in_keep, links, taps_wide, *maps = vmem_call(
        own_kernel,
        [channels] * 4
        + [narrow] * 2
        + [
            inside(inner_width, model, dtype=bf16), inside(inner_width, PROJ, dtype=bf16), inside(inner_width, TABLE),
            inside(TABLE, inner_width), inside(model, 2 * inner_width, dtype=bf16),
            inside(2 * devices + 1, 8, 128), inside(BIAS + 1, inner_width, pos),
            inside(2 * part, width, dtype=bf16), inside(2 * PROJ, 256, dtype=bf16), inside(states, width, dtype=bf16),
            inside(part, width), inside(8, width), inside(part, 48, dtype=bf16),
        ],
        [heights, place],
        [],
        [
            tok, cot, in_weight, out_t, select_weight.T, conv_kernel, conv_bias, step_weight, step_bias,
            decay_log.T, skip_gain, norm_gain, norm_bias,
        ],
    )
    sent, conv_halo, pre_act, low_halo = vmem_call(
        entry_kernel,
        [inside(devices, length, pos), channels, channels, narrow],
        [place],
        [above, below, conv_own, mix, conv_rows, select_rows, table, links, taps_wide],
    )
    got = lax.all_to_all(sent, "seq", 0, 0, tiled=True)
    sent, small = scan_call(place, got, table, links, maps, states)
    got = lax.all_to_all(sent, "seq", 0, 0, tiled=True)
    blocks = inner_width // 128
    whole = -(-blocks * (3 * model + SMALL) // 2048) * 2048
    half = whole // 2
    act_grad, near, far, gate_grad, gated, keep, give = vmem_call(
        functools.partial(mix_kernel, pair=pair),
        [channels]
        + [inside(model // 2, pos)] * 2
        + [inside(inner_width, pos, dtype=bf16)] * 2
        + [inside(half, 128)] * 2,
        [place, group],
        [
            got, small, low, low_halo, cot_in, conv_own, conv_halo, pre_act, gate, gated_grad, select_rows, table,
            table_t, in_keep, links,
        ],
        (),
        [
            pltpu.VMEM((whole, 128), f32), pltpu.VMEM((inner_width, pos), bf16),
            pltpu.VMEM((3, inner_width, pos), bf16), pltpu.VMEM((inner_width, pos), f32),
        ],
    )
    from_above = lax.ppermute(far, "seq", far_pairs)
    from_below = lax.ppermute(near, "seq", near_pairs)
    swap = [(i, i ^ 1) for i in range(groups)]
    taken = lax.ppermute(give, "dp", swap)
    count = half // (groups // 2)
    if pair:
        across = [(i, i ^ 2) for i in range(groups)]
        other = lax.ppermute(keep[count:] + taken[count:], "dp", across)
        piece = keep[:count] + taken[:count]
    else:
        same_core = [list(range(c, groups, 2)) for c in range(2)]
        pieces = (keep + taken).reshape(groups // 2, count, 128)
        pieces = lax.all_to_all(pieces, "dp", 0, 0, tiled=True, axis_index_groups=same_core)
        piece, other = (pieces[0], jnp.sum(pieces[1:], axis=0))
    other, from_above, from_below = lax.optimization_barrier((other, from_above, from_below))
    shares = (piece + other).reshape(devices, count // devices, 128)
    shares = lax.all_to_all(shares, "seq", 0, 0, tiled=True)
    share = jnp.broadcast_to(jnp.sum(shares, axis=0), shares.shape)
    mine = lax.all_to_all(share, "seq", 0, 0, tiled=True).reshape(count, 128)
    mine, from_above, from_below = lax.optimization_barrier((mine, from_above, from_below))
    tokens_grad, layer_out = vmem_call(
        exit_kernel,
        [struct(pos, model, dtype=bf16)] * 2,
        [place],
        [act_grad, from_above, from_below, gate_grad, gated, table, in_keep, links],
        [tok, cot, out_t],
    )
    if pair:
        from_y = lax.ppermute(mine, "dp", across)
        from_y, tokens_grad = lax.optimization_barrier((from_y, tokens_grad))
        pieces = [mine, from_y, lax.ppermute(mine, "dp", swap), lax.ppermute(from_y, "dp", swap)]
    else:
        pieces = list(lax.all_gather(mine, "dp"))
    gain, shift, inproj, kernel, offset, select, stepproj, stepbias, decay, skip, outproj = vmem_call(
        functools.partial(deal_kernel, members=len(pieces), pair=pair),
        [
            struct(model), struct(model), struct(model, 2 * inner_width), struct(3, 3, inner_width),
            struct(inner_width), struct(rank + 2 * states, inner_width), struct(rank, inner_width),
            struct(inner_width), struct(states, inner_width), struct(inner_width), struct(model, inner_width),
        ],
        [group],
        pieces,
        (),
        [pltpu.VMEM((whole, 128), f32)],
    )
    shape = tokens.shape
    return (
        layer_out.reshape(shape), tokens_grad.reshape(shape), gain, shift, inproj, kernel, offset, select.T,
        stepproj, stepbias, decay.T, skip, outproj.T,
    )


def solution(mesh):
    tile, whole = (P("dp", "seq", None, None), P())
    return jax.shard_map(
        on_device,
        mesh=mesh,
        in_specs=(tile, P("dp", None), tile) + (whole,) * 11,
        out_specs=(tile, tile) + (whole,) * 11,
        check_vma=False,
    )
```

```python
import functools

import jax
import jax.numpy as jnp
from jax import lax
from jax.experimental import pallas as pl
from jax.experimental.pallas import tpu as pltpu
from jax.sharding import PartitionSpec as P

epsilon = 1e-05
f32, bf16 = (jnp.float32, jnp.bfloat16)
ONE, IN, OUT, PROJ = (12, 16, 32, 48)
BIAS, SKIP, GAIN, SHIFT, STEP, DECAY, TABLE = (9, 10, 11, 12, 16, 32, 48)
STEP_AT, DECAY_AT, TAPS_AT, OFFSET_AT, SKIP_AT, NORM_AT, SMALL = (48, 64, 80, 89, 90, 95, 96)


def dot(a, b, over):
    return lax.dot_general(a, b, (((over[0],), (over[1],)), ((), ())), preferred_element_type=f32)


def split(value):
    high = value.astype(bf16)
    return (high, (value - high.astype(f32)).astype(bf16))


def fine_dot(a, b, over):
    (a_high, a_low), (b_high, b_low) = (split(a), split(b))
    return dot(a_high, b_high, over) + (dot(a_low, b_high, over) + dot(a_high, b_low, over))


def iota(shape, dim):
    return lax.broadcasted_iota(jnp.int32, shape, dim)


def sigmoid(v):
    return 1.0 / (1.0 + jnp.exp(-v))


def links_up(heights, row):
    if row == 0:
        return 0.0
    end = jnp.int32(0)
    same = True
    for k in range(heights.shape[1]):
        end = end + heights[0, k]
        same = same & (end != row)
    return jnp.where(same, 1.0, 0.0).astype(f32)


def row_masks(links, place):
    lane = iota((1, 128), 1)
    flags = [links[2 * place + k, 0:1] for k in range(3)]
    return (jnp.where(lane < 64, flags[0], flags[1]), jnp.where(lane < 64, flags[1], flags[2]))


def rows_around(own, halo):
    lane = iota((1, 128), 1)
    upper = pltpu.roll(jnp.where(lane < 64, own, halo), 64, 1)
    lower = pltpu.roll(jnp.where(lane < 64, halo, own), 64, 1)
    return (upper, lower)


def from_left(tile):
    place = iota((1, 128), 1) & 63
    wrapped = jnp.where(place == 0, 0.0, pltpu.roll(tile, 73, 1))
    return jnp.where(place < 8, wrapped, pltpu.roll(tile, 8, 1))


def from_right(tile):
    place = iota((1, 128), 1) & 63
    wrapped = jnp.where(place == 63, 0.0, pltpu.roll(tile, 55, 1))
    return jnp.where(place >= 56, wrapped, pltpu.roll(tile, 120, 1))


def conv_tile(upper, own, lower, taps):
    left, middle, right = [
        taps[0][b] * upper + taps[1][b] * own + taps[2][b] * lower for b in range(3)
    ]
    return middle + (from_left(left) + from_right(right))


def normalized(x):
    centred = x - jnp.mean(x, axis=0, keepdims=True)
    inverse = lax.rsqrt(jnp.mean(centred * centred, axis=0, keepdims=True) + epsilon)
    return (centred * inverse, inverse)


def eye(size):
    return (iota((size, size), 0) == iota((size, size), 1)).astype(bf16)


def flipped(value):
    pieces = [value[:, k : k + 128] for k in range(0, value.shape[1], 128)]
    return jnp.concatenate([dot(eye(piece.shape[1]), piece, (1, 1)) for piece in pieces], axis=0)


def flipped_fine(value):
    high, low = split(value)
    rest = (value - high.astype(f32) - low.astype(f32)).astype(bf16)
    return flipped(high) + (flipped(low) + flipped(rest))


def patch_sums(value):
    high, low = split(value)
    ones = jnp.ones((8, value.shape[1]), bf16)
    return (dot(ones, high, (1, 1)) + dot(ones, low, (1, 1)))[0:1]


def put_blocks(ref, start, value):
    for k in range(value.shape[1] // 128):
        ref[start + k * value.shape[0] : start + (k + 1) * value.shape[0]] = value[:, k * 128 : (k + 1) * 128]


def column_order(pos):
    new, old = (iota((pos, pos), 0), iota((pos, pos), 1))
    source = (new & ~63) | ((new & 7) << 3) | ((new >> 3) & 7)
    return (source == old).astype(bf16)


def lane_maps(part, states, width):
    lane = iota((1, width), 1)
    channel = jnp.floor((lane.astype(f32) + 0.5) * (1.0 / states)).astype(jnp.int32)
    return (channel, lane - channel * states, channel < part)


def entered(rows):
    return dot(flipped(rows).astype(bf16), column_order(rows.shape[0]), (1, 0))


def own_kernel(
    heights, place, tok, cot, in_w, out_t, select_t, conv_kernel, conv_bias, step_weight, step_bias, decay_t, skip_gain,
    norm_gain, norm_bias,
    conv_out, gate_out, grad_out, mix_out, low_out, cot_out, conv_rows, select_rows, table, table_t, in_keep, links,
    taps_wide, spread_e, spread_bc, by_state, one_channel, rates, step_three,
):
    model, inner_width = out_t.shape
    states = decay_t.shape[0]
    rank = step_weight.shape[0]
    in_keep[...] = in_w[...]
    for row in range(links.shape[0]):
        links[row] = jnp.full(links.shape[1:], links_up(heights, row), f32)
    in_rows = flipped(in_w[...]).astype(bf16)
    conv_rows[...] = in_rows[:inner_width]
    out_rows = flipped(out_t[...]).astype(bf16)
    chosen = iota((PROJ, select_t.shape[0]), 0)
    chosen = jnp.where(chosen < rank, chosen, jnp.where(chosen < IN, -1, chosen - IN + rank))
    chosen = (chosen == iota((PROJ, select_t.shape[0]), 1)).astype(bf16)
    select_rows[...] = flipped(dot(chosen, select_t[...], (1, 0)).astype(bf16)).astype(bf16)
    table_t[...] = jnp.zeros_like(table_t)
    for k in range(3):
        table_t[3 * k : 3 * k + 3] = conv_kernel[k]
    table_t[BIAS : BIAS + 1] = conv_bias[...].reshape(1, inner_width)
    table_t[SKIP : SKIP + 1] = skip_gain[...].reshape(1, inner_width)
    table_t[GAIN : GAIN + 1, :model] = norm_gain[...].reshape(1, model)
    table_t[SHIFT : SHIFT + 1, :model] = norm_bias[...].reshape(1, model)
    table_t[STEP : STEP + rank] = step_weight[...]
    table_t[STEP + ONE : STEP + ONE + 1] = step_bias[...].reshape(1, inner_width)
    table_t[DECAY : DECAY + states] = decay_t[...]
    columns = flipped_fine(table_t[...])
    table[...] = columns
    for k in range(taps_wide.shape[0]):
        taps_wide[k] = jnp.broadcast_to(columns[:, k : k + 1], taps_wide.shape[1:])
    gain, shift = (columns[:model, GAIN : GAIN + 1], columns[:model, SHIFT : SHIFT + 1])
    low = (normalized(entered(tok[...]))[0] * gain + shift).astype(bf16)
    cot_in = entered(cot[...]).astype(bf16)
    low_out[...] = low
    cot_out[...] = cot_in
    both = dot(in_rows, low, (1, 0))
    conv_out[...] = both[:inner_width]
    gate = both[inner_width:]
    gated_grad = dot(out_rows, cot_in, (1, 0))
    gate_out[...] = gate
    grad_out[...] = gated_grad
    mix_out[...] = gated_grad * (gate * sigmoid(gate))

    part, width = one_channel.shape
    own_rows = table[pl.ds(pl.multiple_of(place[0] * part, 4), part), :]
    channel, state, live = lane_maps(part, states, width)
    twice = iota((2 * part, 1), 0)
    twice = jnp.where(twice >= part, twice - part, twice)
    spread_e[...] = ((twice == channel) & live).astype(bf16)
    coef = iota((2 * PROJ, 1), 0)
    coef = jnp.where(coef >= PROJ, coef - PROJ, coef)
    first = state[:, :128]
    spread_bc[...] = jnp.concatenate([coef - IN == first, coef - OUT == first], axis=1).astype(bf16)
    of_state = ((iota((states, 1), 0) == state) & live).astype(bf16)
    by_state[...] = of_state
    mask = ((iota((part, 1), 0) == channel) & live).astype(f32)
    one_channel[...] = mask
    rate = -jnp.exp(own_rows[:, DECAY : DECAY + states])
    rate_high, rate_low = split(rate)
    rate_rest = split(rate - rate_high.astype(f32) - rate_low.astype(f32))[0]
    rate_row = sum(dot(piece, of_state, (1, 0)) for piece in (rate_high, rate_low, rate_rest))
    rate_row = jnp.sum(rate_row * mask, axis=0, keepdims=True)
    rates[...] = jnp.where(iota((8, 1), 0) == 0, rate_row, rate_row * 1.4426950408889634)
    step_high, step_low = split(own_rows[:, STEP : STEP + 16])
    step_three[...] = jnp.concatenate([step_high, step_high, step_low], axis=1)


def entry_kernel(
    place, above, below, conv_own, mix, conv_rows, select_rows, table, links, taps_wide,
    send, halo_out, pre_out, low_halo_out,
):
    devices = send.shape[0]
    inner_width = conv_own.shape[0]
    model = conv_rows.shape[1]
    part = inner_width // devices
    gain, shift = (table[:model, GAIN : GAIN + 1], table[:model, SHIFT : SHIFT + 1])
    even = place[0] % 2 == 0
    halo = jnp.concatenate(
        [jnp.where(even, below[...], above[...]), jnp.where(even, above[...], below[...])], axis=0
    ).astype(bf16)
    low_halo = (normalized(entered(halo))[0] * gain + shift).astype(bf16)
    low_halo_out[...] = low_halo
    around = dot(conv_rows[...], low_halo, (1, 0))
    halo_out[...] = around
    conv_in = conv_own[...]
    prev, following = row_masks(links, place[0])
    upper, lower = rows_around(conv_in, around)
    taps = [[taps_wide[3 * a + b] for b in range(3)] for a in range(3)]
    pre_act = taps_wide[BIAS] + conv_tile(upper * prev, conv_in, lower * following, taps)
    inner = (pre_act * sigmoid(pre_act)).astype(bf16)
    proj = dot(flipped(select_rows[...]).astype(bf16), inner, (1, 0))
    proj = jnp.where(iota(proj.shape, 0) == ONE, 1.0, proj)
    pre_out[...] = pre_act
    inner = inner.astype(f32)
    for k in range(devices):
        send[k, :part] = inner[k * part : (k + 1) * part]
        send[k, part : 2 * part] = mix[k * part : (k + 1) * part]
        send[k, 2 * part :] = proj


def scan_kernel(
    place, got, table, links, spread_e, spread_bc, by_state, one_channel, rates, step_three,
    send, small,
    a_ref, s_ref, g_ref, down_ref, up_ref, source_ref, mix_ref, col_h, col_m, row_h, row_m,
    prod, end_lr, end_rl, back_lr, back_rl, in_lr, in_rl, tail_lr, tail_rl,
    lhs_d, lhs_u, lhs_m, coef_keep, step_keep, delta_keep, y_keep, steps_keep, sums_keep, coefs_keep, decay_acc, *, part, states, span, group,
):
    devices, _, pos = got.shape
    rows = 2 * devices
    width = a_ref.shape[1]
    rate_row, rate_two = (rates[0:1], rates[1:2])
    step_own = table[pl.ds(pl.multiple_of(place[0] * part, 4), part), STEP : STEP + 16]

    def turned(value):
        return jnp.transpose(jnp.concatenate(split(value), axis=0))

    for tile in range(devices):
        lines = slice(tile * pos, (tile + 1) * pos)
        inner_own = got[tile, :part]
        proj = got[tile, 2 * part :]
        high, low = split(proj[:16])
        pre_step = dot(step_three[...], jnp.concatenate([high, low, high], axis=0), (1, 0))
        tail = jnp.exp(-jnp.abs(pre_step))
        tail = jnp.where(tail < 1e-3, tail * (1.0 - 0.5 * tail), jnp.log(1.0 + tail))
        delta = jnp.maximum(pre_step, 0.0) + tail
        step_keep[tile] = sigmoid(pre_step)
        delta_keep[tile] = delta
        lhs_d[lines, :] = turned(delta)
        lhs_u[lines, :] = turned(delta * inner_own)
        lhs_m[lines, :] = turned(got[tile, part : 2 * part])
        coef_keep[lines, :] = dot(turned(proj), spread_bc[...], (1, 0))

    for k in range(width // span):
        lanes = slice(k * span, (k + 1) * span)

        def prepare(tile, carry):
            lines = pl.ds(pl.multiple_of(tile * pos, pos), pos)
            of_delta, of_source, of_mix = (lhs_d[lines, :], lhs_u[lines, :], lhs_m[lines, :])
            a_ref[lines, lanes] = jnp.exp2(dot(of_delta, spread_e[:, lanes], (1, 0)) * rate_two[:, lanes])
            source = dot(of_source, spread_e[:, lanes], (1, 0))
            mix = dot(of_mix, spread_e[:, lanes], (1, 0))
            source_ref[lines, lanes] = source
            mix_ref[lines, lanes] = mix
            for j in range(span // 128):
                tile_lanes = slice(k * span + j * 128, k * span + (j + 1) * 128)
                piece = slice(j * 128, (j + 1) * 128)
                s_ref[lines, tile_lanes] = source[:, piece] * coef_keep[lines, :128]
                g_ref[lines, tile_lanes] = mix[:, piece] * coef_keep[lines, 128:]
            return carry

        lax.fori_loop(0, devices, prepare, 0, unroll=8)
    down_ref[:64] = jnp.zeros((64, width), f32)
    col_m[...] = jnp.zeros_like(col_m)
    right, left = (range(8), range(7, -1, -1))
    nothing = jnp.zeros((8, 128), f32)

    def packed(row, piece):
        return pl.ds(row * 64 + piece, 8, stride=8)

    def chain(state, row, order, ends, starts):
        for c in order:
            line = pl.ds(pl.multiple_of(row * 64 + c * 8, 8), 8)
            starts[line, :] = state
            state = prod[line, :] * state + ends[line, :]
        return state

    def link(row):
        return links[row]

    def carry_on(held, row, odd):
        ahead, behind = held
        ahead = ahead * link(row)
        if odd:
            ahead = chain(ahead, row, left, end_rl, in_rl)
            behind = chain(behind, row, left, back_lr, tail_lr)
        else:
            ahead = chain(ahead, row, right, end_lr, in_lr)
            behind = chain(behind, row, right, back_rl, tail_rl)
        return (ahead, behind * link(row + 1))

    def carry_back(held, row, odd):
        behind, ahead = held
        behind = behind * link(row + 1)
        if odd:
            behind = chain(behind, row, right, end_lr, in_lr)
            ahead = chain(ahead, row, right, back_rl, tail_rl)
        else:
            behind = chain(behind, row, left, end_rl, in_rl)
            ahead = chain(ahead, row, left, back_lr, tail_lr)
        return (behind, ahead * link(row))

    def wide_link(row):
        return jnp.concatenate([links[row]] * (group // 128), axis=1)

    def ascend(row):
        keep = wide_link(row)
        for k in range(width // group):
            lanes = slice(k * group, (k + 1) * group)
            whole = lr = rl = mlr = mrl = None
            for c in range(8):
                lines = pl.ds(pl.multiple_of(row * 64 + c * 8, 8), 8)
                spot = slice(c * 8, c * 8 + 8)
                a, s, g = (a_ref[lines, lanes], s_ref[lines, lanes], g_ref[lines, lanes])
                before, here = [
                    pl.ds(pl.multiple_of((row + step) * 64 + c * 8, 8), 8) for step in range(2)
                ]
                state_h = a * (down_ref[before, lanes] * keep) + s
                down_ref[here, lanes] = state_h
                lam = g + col_m[spot, lanes] * keep
                col_m[spot, lanes] = a * lam
                up_ref[lines, lanes] = lam
                if c == 0:
                    whole, lr, rl, mlr, mrl = (a, s, s, a * g, a * g)
                else:
                    lr = a * lr + s
                    rl = rl + whole * s
                    whole = whole * a
                    mlr = mlr + whole * g
                    mrl = a * (mrl + g)
            for j in range(group // 128):
                spot = packed(row, k * (group // 128) + j)
                piece = slice(j * 128, (j + 1) * 128)
                prod[spot, :] = whole[:, piece]
                end_lr[spot, :] = lr[:, piece]
                end_rl[spot, :] = rl[:, piece]
                back_lr[spot, :] = mlr[:, piece]
                back_rl[spot, :] = mrl[:, piece]

    def ascend_two(step, held):
        row = 2 * step + 1
        held = carry_on(held, row - 1, False)
        ascend(row)
        held = carry_on(held, row, True)
        ascend(row + 1)
        return held

    ascend(0)
    at_once = 7 if (devices - 1) % 7 == 0 else 1
    held = lax.fori_loop(0, devices - 1, ascend_two, (nothing,) * 2, unroll=at_once)
    held = carry_on(held, rows - 2, False)
    ascend(rows - 1)
    carry_on(held, rows - 1, True)
    col_h[...] = jnp.zeros_like(col_h)
    col_m[...] = jnp.zeros_like(col_m)

    def descend(row):
        keep = wide_link(row + 1)

        def edge(ref, k):
            pieces = [ref[packed(row, k * (group // 128) + j), :] for j in range(group // 128)]
            return pieces[0] if len(pieces) == 1 else jnp.concatenate(pieces, axis=1)

        for k in range(width // group):
            lanes = slice(k * group, (k + 1) * group)
            h_right, m_left = (edge(in_lr, k), edge(tail_rl, k))
            for c in range(8):
                lines = pl.ds(pl.multiple_of(row * 64 + c * 8, 8), 8)
                spot = slice(c * 8, c * 8 + 8)
                a, s, g = (a_ref[lines, lanes], s_ref[lines, lanes], g_ref[lines, lanes])
                h_right = a * h_right + s
                lam = g + m_left
                m_left = a * lam
                row_h[spot, lanes] = h_right
                row_m[spot, lanes] = lam
            h_left, m_right = (edge(in_rl, k), edge(tail_lr, k))
            for c in range(7, -1, -1):
                lines = pl.ds(pl.multiple_of(row * 64 + c * 8, 8), 8)
                spot = slice(c * 8, c * 8 + 8)
                a, s, g = (a_ref[lines, lanes], s_ref[lines, lanes], g_ref[lines, lanes])
                h_left = a * h_left + s
                lam_lr = g + m_right
                m_right = a * lam_lr
                here = pl.ds(pl.multiple_of((row + 1) * 64 + c * 8, 8), 8)
                h_down, lam_up = (down_ref[here, lanes], up_ref[lines, lanes])
                h_up = a * (col_h[spot, lanes] * keep) + s
                col_h[spot, lanes] = h_up
                lam_down = g + col_m[spot, lanes] * keep
                col_m[spot, lanes] = a * lam_down
                h_right, lam_rl = (row_h[spot, lanes], row_m[spot, lanes])
                lam_sum = (lam_lr + lam_rl) + (lam_down + lam_up)
                s_ref[lines, lanes] = (h_right + h_left) + (h_down + h_up)
                up_ref[lines, lanes] = lam_sum
                g_ref[lines, lanes] = (
                    (lam_lr * h_right + lam_rl * h_left)
                    + (lam_down * h_down + lam_up * h_up)
                    - s * lam_sum
                )

    def descend_two(step, held):
        row = rows - 1 - 2 * step
        held = carry_back(held, row - 1, False)
        descend(row)
        held = carry_back(held, row - 2, True)
        descend(row - 1)
        return held

    held = carry_back((nothing,) * 2, rows - 1, True)
    held = lax.fori_loop(0, devices - 1, descend_two, held, unroll=at_once)
    carry_back(held, 0, False)
    descend(1)
    descend(0)
    decay_acc[...] = jnp.zeros_like(decay_acc)
    gather_e, gather_b, gather_c = (spread_e[:part], spread_bc[:PROJ, :128], spread_bc[:PROJ, 128:])

    def finish(tile, carry):
        lines = pl.ds(pl.multiple_of(tile * pos, pos), pos)
        delta = delta_keep[tile]
        delta_low = delta.astype(bf16)
        of_b, of_c = (coef_keep[lines, :128], coef_keep[lines, 128:])
        grad_b = grad_c = None
        of_y, of_step, of_sum = ([], [], [])
        for k in range(width // 128):
            lanes = slice(k * 128, (k + 1) * 128)
            h_sum, lam_sum = (s_ref[lines, lanes], up_ref[lines, lanes])
            of_step.append((g_ref[lines, lanes] * rate_row[:, lanes]).astype(bf16))
            of_y.append((h_sum * of_c).astype(bf16))
            of_sum.append((lam_sum * of_b).astype(bf16))
            term_b, term_c = (lam_sum * source_ref[lines, lanes], h_sum * mix_ref[lines, lanes])
            grad_b = term_b if grad_b is None else grad_b + term_b
            grad_c = term_c if grad_c is None else grad_c + term_c
        of_y, of_step, of_sum = [jnp.concatenate(x, axis=1) for x in (of_y, of_step, of_sum)]
        decay_acc[...] += dot(delta_low, of_step, (1, 0))
        y_keep[tile] = jnp.transpose(dot(of_y, gather_e, (1, 1)))
        steps_keep[tile] = jnp.transpose(dot(of_step, gather_e, (1, 1)))
        sums_keep[tile] = jnp.transpose(dot(of_sum, gather_e, (1, 1)))
        coefs_keep[tile] = dot(gather_b, grad_b.astype(bf16), (1, 1)) + dot(gather_c, grad_c.astype(bf16), (1, 1))
        return carry

    lax.fori_loop(0, devices, finish, 0, unroll=8)
    pre_grads = []
    for tile in range(devices):
        sums = sums_keep[tile]
        pre_grads.append((steps_keep[tile] + got[tile, :part] * sums) * step_keep[tile])
        send[tile, :part] = y_keep[tile]
        send[tile, part : 2 * part] = delta_keep[tile] * sums
        send[tile, 2 * part + 16 :] = coefs_keep[tile, 16:]
    pre_grads = jnp.concatenate(pre_grads, axis=1)
    ranks = jnp.concatenate([got[tile, 2 * part : 2 * part + 16] for tile in range(devices)], axis=1)
    rank_grad = fine_dot(step_own, pre_grads, (0, 0))
    for tile in range(devices):
        send[tile, 2 * part : 2 * part + 16] = coefs_keep[tile, :16] + rank_grad[:, tile * pos : (tile + 1) * pos]
    step_grad = fine_dot(pre_grads, ranks, (1, 1))
    decay_grad = decay_acc[...] * one_channel[...]
    decay_high, decay_low = split(decay_grad)
    decay_grad = dot(decay_high, by_state[...], (1, 1)) + dot(decay_low, by_state[...], (1, 1))
    spot = (iota((part, small.shape[1]), 1) == iota((part, small.shape[1]), 0) + place[0] * part).astype(bf16)
    for at, value in ((0, step_grad), (16, decay_grad)):
        high, low = split(value)
        small[at : at + 16] = dot(high, spot, (0, 0)) + dot(low, spot, (0, 0))


def mix_kernel(
    place, group, got, small_in, low, low_halo, cot, conv_own, conv_halo, pre, gate_in, grad_in,
    select_rows, table, table_t, in_w, links,
    act_out, near, far, gate_grad_out, gated_ref, keep, give,
    grads, inner_ref, moved_ref, sums_ref, *, pair,
):
    devices, length, pos = got.shape
    model, inner_width = (low.shape[0], pre.shape[0])
    part = inner_width // devices
    lane = iota((1, pos), 1)
    prev, following = row_masks(links, place[0])
    proj_grad = got[0, 2 * part :]
    for k in range(1, devices):
        proj_grad = proj_grad + got[k, 2 * part :]
    proj_grad = proj_grad.astype(bf16)
    together = max(1, 48 // part)
    for first in range(0, devices, together):
        members = range(first, first + together)
        rows = slice(first * part, (first + together) * part)
        y = jnp.concatenate([got[k, :part] for k in members], axis=0)
        inner_grad = jnp.concatenate([got[k, part : 2 * part] for k in members], axis=0)
        pre_act, gate, gated_grad = (pre[rows], gate_in[rows], grad_in[rows])
        skip = table[rows, SKIP : SKIP + 1]
        sig_pre, sig_gate = (sigmoid(pre_act), sigmoid(gate))
        inner = (pre_act * sig_pre).astype(bf16)
        inner_ref[rows] = inner
        inner = inner.astype(f32)
        silu_gate = gate * sig_gate
        mix_grad = gated_grad * silu_gate
        inner_grad = inner_grad + mix_grad * skip + dot(select_rows[rows], proj_grad, (1, 0))
        act_grad = inner_grad * (sig_pre * (1.0 + pre_act * (1.0 - sig_pre)))
        act_out[rows] = act_grad
        y_all = y + skip * inner
        gated_ref[rows] = (y_all * silu_gate).astype(bf16)
        gate_grad_out[rows] = (gated_grad * y_all * (sig_gate * (1.0 + gate * (1.0 - sig_gate)))).astype(bf16)
        field = conv_own[rows]
        upper, lower = rows_around(field, conv_halo[rows])
        fields = (upper * prev, field, lower * following)
        sums = jnp.where(lane == 9, jnp.sum(act_grad, axis=1, keepdims=True), 0.0)
        sums = jnp.where(lane == 10, jnp.sum(mix_grad * inner, axis=1, keepdims=True), sums)
        for b, moved in enumerate((from_right(act_grad), act_grad, from_left(act_grad))):
            moved_ref[b, rows] = moved.astype(bf16)
            for a in range(3):
                sums = jnp.where(lane == 3 * a + b, jnp.sum(moved * fields[a], axis=1, keepdims=True), sums)
        sums_ref[rows] = sums
    conv_w = in_w[:, :inner_width].astype(f32)
    beyond = None
    for b in range(3):
        weights = [conv_w * table_t[3 * a + b : 3 * a + b + 1] for a in (0, 2)]
        term = dot(jnp.concatenate(weights, axis=0).astype(bf16), moved_ref[b], (1, 0))
        beyond = term if beyond is None else beyond + term
    beyond = jnp.where(lane < 64, beyond[:model] * prev, beyond[model:] * following)
    top, bottom = (beyond[: model // 2], beyond[model // 2 :])
    up = jnp.where(lane < 64, top, pltpu.roll(bottom, 64, 1))
    down = jnp.where(lane < 64, pltpu.roll(top, 64, 1), bottom)
    even = place[0] % 2 == 0
    near[...] = jnp.where(even, down, up)
    far[...] = jnp.where(even, up, down)
    gated, gate_grad = (gated_ref[...], gate_grad_out[...])

    low_in = low[...]
    upper, lower = rows_around(low_in.astype(f32), low_halo[...].astype(f32))
    which = iota((16, 1), 0)
    masks = jnp.where(which == 0, prev, jnp.where(which == 1, 1.0, following))
    left_hand = jnp.concatenate(
        [(upper * prev).astype(bf16), low_in, (lower * following).astype(bf16), masks.astype(bf16)], axis=0
    )
    blocks = inner_width // 128
    gate_at, out_at, small_at = [k * blocks * model for k in (1, 2, 3)]
    ones = jnp.ones((16, pos), bf16)
    totals = [[], []]
    gain_sum = jnp.zeros((model, 128), f32)
    for n in range(blocks):
        columns = slice(n * 128, (n + 1) * 128)
        in_conv = conv_total = None
        for b in range(3):
            part_b = dot(left_hand, moved_ref[b, columns], (1, 1))
            for a in range(3):
                tap = table_t[3 * a + b : 3 * a + b + 1, columns]
                term = tap * part_b[a * model : (a + 1) * model]
                total = tap * part_b[3 * model + a : 3 * model + a + 1]
                in_conv = term if in_conv is None else in_conv + term
                conv_total = total if conv_total is None else conv_total + total
        in_gate = dot(low_in, gate_grad[columns], (1, 1))
        grads[n * model : (n + 1) * model] = in_conv
        grads[gate_at + n * model : gate_at + (n + 1) * model] = in_gate
        grads[out_at + n * model : out_at + (n + 1) * model] = dot(cot[...], gated[columns], (1, 1))
        totals[0].append(conv_total)
        totals[1].append(dot(ones, gate_grad[columns], (1, 1))[0:1])
        conv_w = in_w[:, columns].astype(f32)
        gate_w = in_w[:, inner_width + n * 128 : inner_width + (n + 1) * 128].astype(f32)
        gain_sum = gain_sum + (conv_w * in_conv + gate_w * in_gate)
    sums = jnp.broadcast_to(jnp.concatenate(totals[0] + totals[1], axis=1), (16, 2 * inner_width))
    sums_high, sums_low = split(sums)
    shift_row = (dot(sums_high, in_w[...], (1, 1)) + dot(sums_low, in_w[...], (1, 1)))[0:1]
    gain_row = patch_sums(gain_sum)
    gain, shift = (table_t[GAIN : GAIN + 1, :model], table_t[SHIFT : SHIFT + 1, :model])
    gain_row = (gain_row - shift * shift_row) / gain
    high, mid = split(sums_ref[...])
    rest = (sums_ref[...] - high.astype(f32) - mid.astype(f32)).astype(bf16)
    chosen = (iota((16, pos), 0) == iota((16, pos), 1)).astype(bf16)
    sums = dot(chosen, high, (1, 1)) + (dot(chosen, mid, (1, 1)) + dot(chosen, rest, (1, 1)))
    norms = jnp.concatenate([gain_row, shift_row], axis=1)
    sums = jnp.where(iota((16, 1), 0) == NORM_AT - TAPS_AT, norms, sums)
    smalls = jnp.concatenate([dot(proj_grad, inner_ref[...], (1, 1)), small_in[...], sums], axis=0)
    put_blocks(grads, small_at, smalls)
    small_at = small_at + blocks * SMALL
    grads[small_at:] = jnp.zeros((grads.shape[0] - small_at, 128), f32)
    own = group[0] % 2
    if pair:
        count = keep.shape[0] // 2
        height = group[0] // 2
        for ref, side in ((keep, own), (give, 1 - own)):
            for k, at in enumerate((height, 1 - height)):
                ref[k * count : (k + 1) * count] = grads[pl.ds(pl.multiple_of((2 * side + at) * count, count), count)]
    else:
        count = keep.shape[0]
        keep[...] = grads[pl.ds(pl.multiple_of(own * count, count), count)]
        give[...] = grads[pl.ds(pl.multiple_of((1 - own) * count, count), count)]


def exit_kernel(
    place, act, from_above, from_below, gate_grad, gated, table, in_w, links, tok, cot, out_t,
    tokens_grad, layer_out,
):
    inner_width, pos = act.shape
    model = in_w.shape[0]
    lane = iota((1, pos), 1)
    even = place[0] % 2 == 0
    above, below = (
        jnp.where(even, from_above[...], from_below[...]), jnp.where(even, from_below[...], from_above[...])
    )
    top = jnp.where(lane < 64, above, pltpu.roll(below, 64, 1))
    bottom = jnp.where(lane < 64, pltpu.roll(above, 64, 1), below)
    beyond_high, beyond_low = split(jnp.concatenate([top, bottom], axis=0))
    act_grad = act[...]
    prev, following = row_masks(links, place[0])
    upper, lower = rows_around(act_grad, jnp.zeros_like(act_grad))
    columns = table[...]
    taps = [[columns[:, 8 - 3 * a - b : 9 - 3 * a - b] for b in range(3)] for a in range(3)]
    conv_grad = conv_tile(upper * prev, act_grad, lower * following, taps).astype(bf16)
    natural = jnp.concatenate([conv_grad, gate_grad[...], gated[...]], axis=0)
    order = column_order(pos)
    natural = dot(natural, order, (1, 0)).astype(bf16)
    layer = jnp.transpose(dot(out_t[...], natural[2 * inner_width :], (1, 0)))
    layer_out[...] = (tok[...].astype(f32) + layer).astype(bf16)
    normed_grad = dot(in_w[...], natural[: 2 * inner_width], (1, 0))
    normed_grad = normed_grad + (dot(beyond_high, order, (1, 0)) + dot(beyond_low, order, (1, 0)))
    xhat, inverse = normalized(flipped(tok[...]))
    scaled = normed_grad * columns[:model, GAIN : GAIN + 1]
    x_grad = (
        scaled
        - jnp.mean(scaled, axis=0, keepdims=True)
        - xhat * jnp.mean(scaled * xhat, axis=0, keepdims=True)
    ) * inverse
    x_grad = jnp.transpose(x_grad)
    tokens_grad[...] = (x_grad + cot[...].astype(f32)).astype(bf16)


def deal_kernel(group, *refs, members, pair):
    pieces, ordered = (refs[:members], refs[-1])
    (
        gain_grad, shift_grad, inproj, kernel_grad, offset, select, stepproj, stepbias, decay, skip, outproj,
    ) = refs[members:-1]
    model, inner_width = outproj.shape
    blocks = inner_width // 128
    rank = stepproj.shape[0]
    states = decay.shape[0]
    count = pieces[0].shape[0]
    for k, piece in enumerate(pieces):
        if pair:
            core, height = (group[0] % 2, group[0] // 2)
            core = 1 - core if k // 2 else core
            height = 1 - height if k % 2 else height
            slot = core * 2 + height
        else:
            slot = k % 2 * (members // 2) + k // 2
        ordered[pl.ds(pl.multiple_of(slot * count, count), count)] = piece[...]

    def rows(start, count):
        return ordered[start : start + count]

    for k in range(2 * blocks):
        inproj[:, k * 128 : (k + 1) * 128] = rows(k * model, model)
    start = 2 * blocks * model
    for k in range(blocks):
        outproj[:, k * 128 : (k + 1) * 128] = rows(start + k * model, model)
    start = start + blocks * model
    small = jnp.concatenate([rows(start + k * SMALL, SMALL) for k in range(blocks)], axis=1)
    select[:rank] = small[:rank]
    select[rank:] = small[IN:PROJ]
    stepproj[...] = small[STEP_AT : STEP_AT + rank]
    stepbias[...] = small[STEP_AT + ONE : STEP_AT + ONE + 1].reshape(stepbias.shape)
    decay[...] = small[DECAY_AT : DECAY_AT + states]
    for k in range(3):
        kernel_grad[k] = small[TAPS_AT + 3 * k : TAPS_AT + 3 * k + 3]
    offset[...] = small[OFFSET_AT : OFFSET_AT + 1].reshape(offset.shape)
    skip[...] = small[SKIP_AT : SKIP_AT + 1].reshape(skip.shape)
    norms = small[NORM_AT : NORM_AT + 1]
    gain_grad[...] = norms[:, :model].reshape(gain_grad.shape)
    shift_grad[...] = norms[:, model:].reshape(shift_grad.shape)


def vmem_call(kernel, out_shape, scalars, arrays, weights=(), scratch=(), limit=16):
    scalars = [pltpu.with_memory_space_constraint(x, pltpu.HBM) if x.ndim == 2 else x for x in scalars]
    arrays = [pltpu.with_memory_space_constraint(x, pltpu.VMEM) for x in arrays]
    arrays += [pltpu.with_memory_space_constraint(x, pltpu.HBM) for x in weights]
    return pl.pallas_call(
        kernel,
        out_shape=out_shape,
        in_specs=[pl.BlockSpec(memory_space=pltpu.SMEM)] * len(scalars)
        + [pl.BlockSpec(memory_space=pltpu.VMEM)] * len(arrays),
        out_specs=[pl.BlockSpec(memory_space=pltpu.VMEM)] * len(out_shape),
        scratch_shapes=list(scratch),
        compiler_params=pltpu.CompilerParams(vmem_limit_bytes=limit * 1024 * 1024),
    )(*scalars, *arrays)


def struct(*shape, dtype=f32):
    return jax.ShapeDtypeStruct(shape, dtype)


def inside(*shape, dtype=f32):
    return pltpu.VMEM(shape, dtype)


def scan_call(place, got, table, links, maps, states):
    devices, length, pos = got.shape
    inner_width = table.shape[0]
    part = inner_width // devices
    width = -(-part * states // 128) * 128
    total = devices * pos
    span = 256 if width % 256 == 0 else 128
    group = 768 if width % 768 == 0 else span
    big = pltpu.VMEM((total, width), f32)
    line = pltpu.VMEM(((2 * devices + 1) * 64, 128), f32)
    column = pltpu.VMEM((pos // 2, width), f32)
    own = pltpu.VMEM((devices, part, pos), f32)
    return vmem_call(
        functools.partial(scan_kernel, part=part, states=states, span=span, group=group),
        [inside(devices, length, pos), inside(32, inner_width)],
        [place],
        [got, table, links, *maps],
        (),
        [big] * 3
        + [pltpu.VMEM((total + pos // 2, width), f32)]
        + [big] * 3
        + [column] * 4
        + [line] * 9
        + [pltpu.VMEM((total, 2 * part), bf16)] * 3
        + [pltpu.VMEM((total, 256), f32)]
        + [own] * 5
        + [pltpu.VMEM((devices, PROJ, pos), f32), pltpu.VMEM((part, width), f32)],
        limit=36 if total <= 1024 else 60,
    )


def on_device(
    tokens, heights, cotangent, norm_gain, norm_bias, in_weight, conv_kernel, conv_bias, select_weight,
    step_weight, step_bias, decay_log, skip_gain, out_weight,
):
    _, tile_rows, grid_cols, model = tokens.shape
    inner_width = out_weight.shape[0]
    states = decay_log.shape[1]
    rank = step_weight.shape[0]
    devices = lax.axis_size("seq")
    groups = lax.axis_size("dp")
    place = lax.axis_index("seq").reshape(1)
    group = lax.axis_index("dp").reshape(1)
    pair = groups == 4
    pos = tile_rows * grid_cols
    part = inner_width // devices
    width = -(-part * states // 128) * 128
    length = 2 * part + PROJ
    near_pairs = [(i, i ^ 1) for i in range(devices)]
    far_pairs = [(i, (i - 1 + 2 * (i % 2)) % devices) for i in range(devices)]

    tok, cot = (tokens.reshape(pos, model), cotangent.reshape(pos, model))
    even = place[0] % 2 == 0
    upper, lower = (tok[:grid_cols].astype(f32), tok[grid_cols:].astype(f32))
    above = lax.ppermute(jnp.where(even, upper, lower), "seq", far_pairs)
    below = lax.ppermute(jnp.where(even, lower, upper), "seq", near_pairs)
    above, group = lax.optimization_barrier((above, group))
    out_t = out_weight.T
    channels = inside(inner_width, pos)
    narrow = inside(model, pos, dtype=bf16)
    conv_own, gate, gated_grad, mix, low, cot_in, conv_rows, select_rows, table, table_t, in_keep, links, taps_wide, *maps = vmem_call(
        own_kernel,
        [channels] * 4
        + [narrow] * 2
        + [
            inside(inner_width, model, dtype=bf16), inside(inner_width, PROJ, dtype=bf16), inside(inner_width, TABLE),
            inside(TABLE, inner_width), inside(model, 2 * inner_width, dtype=bf16),
            inside(2 * devices + 1, 8, 128), inside(BIAS + 1, inner_width, pos),
            inside(2 * part, width, dtype=bf16), inside(2 * PROJ, 256, dtype=bf16), inside(states, width, dtype=bf16),
            inside(part, width), inside(8, width), inside(part, 48, dtype=bf16),
        ],
        [heights, place],
        [],
        [
            tok, cot, in_weight, out_t, select_weight.T, conv_kernel, conv_bias, step_weight, step_bias,
            decay_log.T, skip_gain, norm_gain, norm_bias,
        ],
    )
    sent, conv_halo, pre_act, low_halo = vmem_call(
        entry_kernel,
        [inside(devices, length, pos), channels, channels, narrow],
        [place],
        [above, below, conv_own, mix, conv_rows, select_rows, table, links, taps_wide],
    )
    got = lax.all_to_all(sent, "seq", 0, 0, tiled=True)
    sent, small = scan_call(place, got, table, links, maps, states)
    got = lax.all_to_all(sent, "seq", 0, 0, tiled=True)
    blocks = inner_width // 128
    whole = -(-blocks * (3 * model + SMALL) // 2048) * 2048
    half = whole // 2
    act_grad, near, far, gate_grad, gated, keep, give = vmem_call(
        functools.partial(mix_kernel, pair=pair),
        [channels]
        + [inside(model // 2, pos)] * 2
        + [inside(inner_width, pos, dtype=bf16)] * 2
        + [inside(half, 128)] * 2,
        [place, group],
        [
            got, small, low, low_halo, cot_in, conv_own, conv_halo, pre_act, gate, gated_grad, select_rows, table,
            table_t, in_keep, links,
        ],
        (),
        [
            pltpu.VMEM((whole, 128), f32), pltpu.VMEM((inner_width, pos), bf16),
            pltpu.VMEM((3, inner_width, pos), bf16), pltpu.VMEM((inner_width, pos), f32),
        ],
    )
    from_above = lax.ppermute(far, "seq", far_pairs)
    from_below = lax.ppermute(near, "seq", near_pairs)
    swap = [(i, i ^ 1) for i in range(groups)]
    taken = lax.ppermute(give, "dp", swap)
    count = half // (groups // 2)
    if pair:
        across = [(i, i ^ 2) for i in range(groups)]
        other = lax.ppermute(keep[count:] + taken[count:], "dp", across)
        piece = keep[:count] + taken[:count]
    else:
        same_core = [list(range(c, groups, 2)) for c in range(2)]
        pieces = (keep + taken).reshape(groups // 2, count, 128)
        pieces = lax.all_to_all(pieces, "dp", 0, 0, tiled=True, axis_index_groups=same_core)
        piece, other = (pieces[0], jnp.sum(pieces[1:], axis=0))
    other, from_above, from_below = lax.optimization_barrier((other, from_above, from_below))
    shares = (piece + other).reshape(devices, count // devices, 128)
    shares = lax.all_to_all(shares, "seq", 0, 0, tiled=True)
    share = jnp.broadcast_to(jnp.sum(shares, axis=0), shares.shape)
    mine = lax.all_to_all(share, "seq", 0, 0, tiled=True).reshape(count, 128)
    mine, from_above, from_below = lax.optimization_barrier((mine, from_above, from_below))
    tokens_grad, layer_out = vmem_call(
        exit_kernel,
        [struct(pos, model, dtype=bf16)] * 2,
        [place],
        [act_grad, from_above, from_below, gate_grad, gated, table, in_keep, links],
        [tok, cot, out_t],
    )
    if pair:
        from_y = lax.ppermute(mine, "dp", across)
        from_y, tokens_grad = lax.optimization_barrier((from_y, tokens_grad))
        pieces = [mine, from_y, lax.ppermute(mine, "dp", swap), lax.ppermute(from_y, "dp", swap)]
    else:
        pieces = list(lax.all_gather(mine, "dp"))
    gain, shift, inproj, kernel, offset, select, stepproj, stepbias, decay, skip, outproj = vmem_call(
        functools.partial(deal_kernel, members=len(pieces), pair=pair),
        [
            struct(model), struct(model), struct(model, 2 * inner_width), struct(3, 3, inner_width),
            struct(inner_width), struct(rank + 2 * states, inner_width), struct(rank, inner_width),
            struct(inner_width), struct(states, inner_width), struct(inner_width), struct(model, inner_width),
        ],
        [group],
        pieces,
        (),
        [pltpu.VMEM((whole, 128), f32)],
    )
    shape = tokens.shape
    return (
        layer_out.reshape(shape), tokens_grad.reshape(shape), gain, shift, inproj, kernel, offset, select.T,
        stepproj, stepbias, decay.T, skip, outproj.T,
    )


def solution(mesh):
    tile, whole = (P("dp", "seq", None, None), P())
    return jax.shard_map(
        on_device,
        mesh=mesh,
        in_specs=(tile, P("dp", None), tile) + (whole,) * 11,
        out_specs=(tile, tile) + (whole,) * 11,
        check_vma=False,
    )
```

```python
import functools

import jax
import jax.numpy as jnp
from jax import lax
from jax.experimental import pallas as pl
from jax.experimental.pallas import tpu as pltpu
from jax.sharding import PartitionSpec as P

epsilon = 1e-05
f32, bf16 = (jnp.float32, jnp.bfloat16)
ONE, IN, OUT, PROJ = (12, 16, 32, 48)
BIAS, SKIP, GAIN, SHIFT, STEP, DECAY, TABLE = (9, 10, 11, 12, 16, 32, 48)
STEP_AT, DECAY_AT, TAPS_AT, OFFSET_AT, SKIP_AT, NORM_AT, SMALL = (48, 64, 80, 89, 90, 95, 96)


def dot(a, b, over):
    return lax.dot_general(a, b, (((over[0],), (over[1],)), ((), ())), preferred_element_type=f32)


def split(value):
    high = value.astype(bf16)
    return (high, (value - high.astype(f32)).astype(bf16))


def fine_dot(a, b, over):
    (a_high, a_low), (b_high, b_low) = (split(a), split(b))
    return dot(a_high, b_high, over) + (dot(a_low, b_high, over) + dot(a_high, b_low, over))


def iota(shape, dim):
    return lax.broadcasted_iota(jnp.int32, shape, dim)


def sigmoid(v):
    return 1.0 / (1.0 + jnp.exp(-v))


def links_up(heights, row):
    if row == 0:
        return 0.0
    end = jnp.int32(0)
    same = True
    for k in range(heights.shape[1]):
        end = end + heights[0, k]
        same = same & (end != row)
    return jnp.where(same, 1.0, 0.0).astype(f32)


def row_masks(links, place):
    lane = iota((1, 128), 1)
    flags = [links[2 * place + k, 0:1] for k in range(3)]
    return (jnp.where(lane < 64, flags[0], flags[1]), jnp.where(lane < 64, flags[1], flags[2]))


def rows_around(own, halo):
    lane = iota((1, 128), 1)
    upper = pltpu.roll(jnp.where(lane < 64, own, halo), 64, 1)
    lower = pltpu.roll(jnp.where(lane < 64, halo, own), 64, 1)
    return (upper, lower)


def from_left(tile):
    place = iota((1, 128), 1) & 63
    wrapped = jnp.where(place == 0, 0.0, pltpu.roll(tile, 73, 1))
    return jnp.where(place < 8, wrapped, pltpu.roll(tile, 8, 1))


def from_right(tile):
    place = iota((1, 128), 1) & 63
    wrapped = jnp.where(place == 63, 0.0, pltpu.roll(tile, 55, 1))
    return jnp.where(place >= 56, wrapped, pltpu.roll(tile, 120, 1))


def conv_tile(upper, own, lower, taps):
    left, middle, right = [
        taps[0][b] * upper + taps[1][b] * own + taps[2][b] * lower for b in range(3)
    ]
    return middle + (from_left(left) + from_right(right))


def normalized(x):
    centred = x - jnp.mean(x, axis=0, keepdims=True)
    inverse = lax.rsqrt(jnp.mean(centred * centred, axis=0, keepdims=True) + epsilon)
    return (centred * inverse, inverse)


def eye(size):
    return (iota((size, size), 0) == iota((size, size), 1)).astype(bf16)


def flipped(value):
    pieces = [value[:, k : k + 128] for k in range(0, value.shape[1], 128)]
    return jnp.concatenate([dot(eye(piece.shape[1]), piece, (1, 1)) for piece in pieces], axis=0)


def flipped_fine(value):
    high, low = split(value)
    rest = (value - high.astype(f32) - low.astype(f32)).astype(bf16)
    return flipped(high) + (flipped(low) + flipped(rest))


def patch_sums(value):
    high, low = split(value)
    ones = jnp.ones((8, value.shape[1]), bf16)
    return (dot(ones, high, (1, 1)) + dot(ones, low, (1, 1)))[0:1]


def put_blocks(ref, start, value):
    for k in range(value.shape[1] // 128):
        ref[start + k * value.shape[0] : start + (k + 1) * value.shape[0]] = value[:, k * 128 : (k + 1) * 128]


def column_order(pos):
    new, old = (iota((pos, pos), 0), iota((pos, pos), 1))
    source = (new & ~63) | ((new & 7) << 3) | ((new >> 3) & 7)
    return (source == old).astype(bf16)


def lane_maps(part, states, width):
    lane = iota((1, width), 1)
    channel = jnp.floor((lane.astype(f32) + 0.5) * (1.0 / states)).astype(jnp.int32)
    return (channel, lane - channel * states, channel < part)


def entered(rows):
    return dot(flipped(rows).astype(bf16), column_order(rows.shape[0]), (1, 0))


def own_kernel(
    heights, place, tok, cot, in_w, out_t, select_t, conv_kernel, conv_bias, step_weight, step_bias, decay_t, skip_gain,
    norm_gain, norm_bias,
    conv_out, gate_out, grad_out, mix_out, low_out, cot_out, conv_rows, select_rows, table, table_t, in_keep, links,
    taps_wide, spread_e, spread_bc, by_state, one_channel, rates, step_three,
):
    model, inner_width = out_t.shape
    states = decay_t.shape[0]
    rank = step_weight.shape[0]
    in_keep[...] = in_w[...]
    for row in range(links.shape[0]):
        links[row] = jnp.full(links.shape[1:], links_up(heights, row), f32)
    in_rows = flipped(in_w[...]).astype(bf16)
    conv_rows[...] = in_rows[:inner_width]
    out_rows = flipped(out_t[...]).astype(bf16)
    chosen = iota((PROJ, select_t.shape[0]), 0)
    chosen = jnp.where(chosen < rank, chosen, jnp.where(chosen < IN, -1, chosen - IN + rank))
    chosen = (chosen == iota((PROJ, select_t.shape[0]), 1)).astype(bf16)
    select_rows[...] = flipped(dot(chosen, select_t[...], (1, 0)).astype(bf16)).astype(bf16)
    table_t[...] = jnp.zeros_like(table_t)
    for k in range(3):
        table_t[3 * k : 3 * k + 3] = conv_kernel[k]
    table_t[BIAS : BIAS + 1] = conv_bias[...].reshape(1, inner_width)
    table_t[SKIP : SKIP + 1] = skip_gain[...].reshape(1, inner_width)
    table_t[GAIN : GAIN + 1, :model] = norm_gain[...].reshape(1, model)
    table_t[SHIFT : SHIFT + 1, :model] = norm_bias[...].reshape(1, model)
    table_t[STEP : STEP + rank] = step_weight[...]
    table_t[STEP + ONE : STEP + ONE + 1] = step_bias[...].reshape(1, inner_width)
    table_t[DECAY : DECAY + states] = decay_t[...]
    columns = flipped_fine(table_t[...])
    table[...] = columns
    for k in range(taps_wide.shape[0]):
        taps_wide[k] = jnp.broadcast_to(columns[:, k : k + 1], taps_wide.shape[1:])
    gain, shift = (columns[:model, GAIN : GAIN + 1], columns[:model, SHIFT : SHIFT + 1])
    low = (normalized(entered(tok[...]))[0] * gain + shift).astype(bf16)
    cot_in = entered(cot[...]).astype(bf16)
    low_out[...] = low
    cot_out[...] = cot_in
    both = dot(in_rows, low, (1, 0))
    conv_out[...] = both[:inner_width]
    gate = both[inner_width:]
    gated_grad = dot(out_rows, cot_in, (1, 0))
    gate_out[...] = gate
    grad_out[...] = gated_grad
    mix_out[...] = gated_grad * (gate * sigmoid(gate))

    part, width = one_channel.shape
    own_rows = table[pl.ds(pl.multiple_of(place[0] * part, 4), part), :]
    channel, state, live = lane_maps(part, states, width)
    twice = iota((2 * part, 1), 0)
    twice = jnp.where(twice >= part, twice - part, twice)
    spread_e[...] = ((twice == channel) & live).astype(bf16)
    coef = iota((2 * PROJ, 1), 0)
    coef = jnp.where(coef >= PROJ, coef - PROJ, coef)
    first = state[:, :128]
    spread_bc[...] = jnp.concatenate([coef - IN == first, coef - OUT == first], axis=1).astype(bf16)
    of_state = ((iota((states, 1), 0) == state) & live).astype(bf16)
    by_state[...] = of_state
    mask = ((iota((part, 1), 0) == channel) & live).astype(f32)
    one_channel[...] = mask
    rate = -jnp.exp(own_rows[:, DECAY : DECAY + states])
    rate_high, rate_low = split(rate)
    rate_rest = split(rate - rate_high.astype(f32) - rate_low.astype(f32))[0]
    rate_row = sum(dot(piece, of_state, (1, 0)) for piece in (rate_high, rate_low, rate_rest))
    rate_row = jnp.sum(rate_row * mask, axis=0, keepdims=True)
    rates[...] = jnp.where(iota((8, 1), 0) == 0, rate_row, rate_row * 1.4426950408889634)
    step_high, step_low = split(own_rows[:, STEP : STEP + 16])
    step_three[...] = jnp.concatenate([step_high, step_high, step_low], axis=1)


def entry_kernel(
    place, above, below, conv_own, mix, conv_rows, select_rows, table, links, taps_wide,
    send, halo_out, pre_out, low_halo_out,
):
    devices = send.shape[0]
    inner_width = conv_own.shape[0]
    model = conv_rows.shape[1]
    part = inner_width // devices
    gain, shift = (table[:model, GAIN : GAIN + 1], table[:model, SHIFT : SHIFT + 1])
    even = place[0] % 2 == 0
    halo = jnp.concatenate(
        [jnp.where(even, below[...], above[...]), jnp.where(even, above[...], below[...])], axis=0
    ).astype(bf16)
    low_halo = (normalized(entered(halo))[0] * gain + shift).astype(bf16)
    low_halo_out[...] = low_halo
    around = dot(conv_rows[...], low_halo, (1, 0))
    halo_out[...] = around
    conv_in = conv_own[...]
    prev, following = row_masks(links, place[0])
    upper, lower = rows_around(conv_in, around)
    taps = [[taps_wide[3 * a + b] for b in range(3)] for a in range(3)]
    pre_act = taps_wide[BIAS] + conv_tile(upper * prev, conv_in, lower * following, taps)
    inner = (pre_act * sigmoid(pre_act)).astype(bf16)
    proj = dot(flipped(select_rows[...]).astype(bf16), inner, (1, 0))
    proj = jnp.where(iota(proj.shape, 0) == ONE, 1.0, proj)
    pre_out[...] = pre_act
    inner = inner.astype(f32)
    for k in range(devices):
        send[k, :part] = inner[k * part : (k + 1) * part]
        send[k, part : 2 * part] = mix[k * part : (k + 1) * part]
        send[k, 2 * part :] = proj


def scan_kernel(
    place, got, table, links, spread_e, spread_bc, by_state, one_channel, rates, step_three,
    send, small,
    a_ref, s_ref, g_ref, down_ref, up_ref, source_ref, mix_ref, col_h, col_m, row_h, row_m,
    prod, end_lr, end_rl, back_lr, back_rl, in_lr, in_rl, tail_lr, tail_rl,
    lhs_d, lhs_u, lhs_m, coef_keep, step_keep, delta_keep, y_keep, steps_keep, sums_keep, coefs_keep, decay_acc, *, part, states, span, group,
):
    devices, _, pos = got.shape
    rows = 2 * devices
    width = a_ref.shape[1]
    rate_row, rate_two = (rates[0:1], rates[1:2])
    step_own = table[pl.ds(pl.multiple_of(place[0] * part, 4), part), STEP : STEP + 16]

    def turned(value):
        return jnp.transpose(jnp.concatenate(split(value), axis=0))

    for tile in range(devices):
        lines = slice(tile * pos, (tile + 1) * pos)
        inner_own = got[tile, :part]
        proj = got[tile, 2 * part :]
        high, low = split(proj[:16])
        pre_step = dot(step_three[...], jnp.concatenate([high, low, high], axis=0), (1, 0))
        tail = jnp.exp(-jnp.abs(pre_step))
        tail = jnp.where(tail < 1e-3, tail * (1.0 - 0.5 * tail), jnp.log(1.0 + tail))
        delta = jnp.maximum(pre_step, 0.0) + tail
        step_keep[tile] = sigmoid(pre_step)
        delta_keep[tile] = delta
        lhs_d[lines, :] = turned(delta)
        lhs_u[lines, :] = turned(delta * inner_own)
        lhs_m[lines, :] = turned(got[tile, part : 2 * part])
        coef_keep[lines, :] = dot(turned(proj), spread_bc[...], (1, 0))

    for k in range(width // span):
        lanes = slice(k * span, (k + 1) * span)

        def prepare(tile, carry):
            lines = pl.ds(pl.multiple_of(tile * pos, pos), pos)
            of_delta, of_source, of_mix = (lhs_d[lines, :], lhs_u[lines, :], lhs_m[lines, :])
            a_ref[lines, lanes] = jnp.exp2(dot(of_delta, spread_e[:, lanes], (1, 0)) * rate_two[:, lanes])
            source = dot(of_source, spread_e[:, lanes], (1, 0))
            mix = dot(of_mix, spread_e[:, lanes], (1, 0))
            source_ref[lines, lanes] = source
            mix_ref[lines, lanes] = mix
            for j in range(span // 128):
                tile_lanes = slice(k * span + j * 128, k * span + (j + 1) * 128)
                piece = slice(j * 128, (j + 1) * 128)
                s_ref[lines, tile_lanes] = source[:, piece] * coef_keep[lines, :128]
                g_ref[lines, tile_lanes] = mix[:, piece] * coef_keep[lines, 128:]
            return carry

        lax.fori_loop(0, devices, prepare, 0, unroll=8)
    down_ref[:64] = jnp.zeros((64, width), f32)
    col_m[...] = jnp.zeros_like(col_m)
    right, left = (range(8), range(7, -1, -1))
    nothing = jnp.zeros((8, 128), f32)

    def packed(row, piece):
        return pl.ds(row * 64 + piece, 8, stride=8)

    def chain(state, row, order, ends, starts):
        for c in order:
            line = pl.ds(pl.multiple_of(row * 64 + c * 8, 8), 8)
            starts[line, :] = state
            state = prod[line, :] * state + ends[line, :]
        return state

    def link(row):
        return links[row]

    def carry_on(held, row, odd):
        ahead, behind = held
        ahead = ahead * link(row)
        if odd:
            ahead = chain(ahead, row, left, end_rl, in_rl)
            behind = chain(behind, row, left, back_lr, tail_lr)
        else:
            ahead = chain(ahead, row, right, end_lr, in_lr)
            behind = chain(behind, row, right, back_rl, tail_rl)
        return (ahead, behind * link(row + 1))

    def carry_back(held, row, odd):
        behind, ahead = held
        behind = behind * link(row + 1)
        if odd:
            behind = chain(behind, row, right, end_lr, in_lr)
            ahead = chain(ahead, row, right, back_rl, tail_rl)
        else:
            behind = chain(behind, row, left, end_rl, in_rl)
            ahead = chain(ahead, row, left, back_lr, tail_lr)
        return (behind, ahead * link(row))

    def wide_link(row):
        return jnp.concatenate([links[row]] * (group // 128), axis=1)

    def ascend(row):
        keep = wide_link(row)
        for k in range(width // group):
            lanes = slice(k * group, (k + 1) * group)
            whole = lr = rl = mlr = mrl = None
            for c in range(8):
                lines = pl.ds(pl.multiple_of(row * 64 + c * 8, 8), 8)
                spot = slice(c * 8, c * 8 + 8)
                a, s, g = (a_ref[lines, lanes], s_ref[lines, lanes], g_ref[lines, lanes])
                before, here = [
                    pl.ds(pl.multiple_of((row + step) * 64 + c * 8, 8), 8) for step in range(2)
                ]
                state_h = a * (down_ref[before, lanes] * keep) + s
                down_ref[here, lanes] = state_h
                lam = g + col_m[spot, lanes] * keep
                col_m[spot, lanes] = a * lam
                up_ref[lines, lanes] = lam
                if c == 0:
                    whole, lr, rl, mlr, mrl = (a, s, s, a * g, a * g)
                else:
                    lr = a * lr + s
                    rl = rl + whole * s
                    whole = whole * a
                    mlr = mlr + whole * g
                    mrl = a * (mrl + g)
            for j in range(group // 128):
                spot = packed(row, k * (group // 128) + j)
                piece = slice(j * 128, (j + 1) * 128)
                prod[spot, :] = whole[:, piece]
                end_lr[spot, :] = lr[:, piece]
                end_rl[spot, :] = rl[:, piece]
                back_lr[spot, :] = mlr[:, piece]
                back_rl[spot, :] = mrl[:, piece]

    def ascend_two(step, held):
        row = 2 * step + 1
        held = carry_on(held, row - 1, False)
        ascend(row)
        held = carry_on(held, row, True)
        ascend(row + 1)
        return held

    ascend(0)
    at_once = 7 if (devices - 1) % 7 == 0 else 1
    held = lax.fori_loop(0, devices - 1, ascend_two, (nothing,) * 2, unroll=at_once)
    held = carry_on(held, rows - 2, False)
    ascend(rows - 1)
    carry_on(held, rows - 1, True)
    col_h[...] = jnp.zeros_like(col_h)
    col_m[...] = jnp.zeros_like(col_m)

    def descend(row):
        keep = wide_link(row + 1)

        def edge(ref, k):
            pieces = [ref[packed(row, k * (group // 128) + j), :] for j in range(group // 128)]
            return pieces[0] if len(pieces) == 1 else jnp.concatenate(pieces, axis=1)

        for k in range(width // group):
            lanes = slice(k * group, (k + 1) * group)
            h_right, m_left = (edge(in_lr, k), edge(tail_rl, k))
            for c in range(8):
                lines = pl.ds(pl.multiple_of(row * 64 + c * 8, 8), 8)
                spot = slice(c * 8, c * 8 + 8)
                a, s, g = (a_ref[lines, lanes], s_ref[lines, lanes], g_ref[lines, lanes])
                h_right = a * h_right + s
                lam = g + m_left
                m_left = a * lam
                row_h[spot, lanes] = h_right
                row_m[spot, lanes] = lam
            h_left, m_right = (edge(in_rl, k), edge(tail_lr, k))
            for c in range(7, -1, -1):
                lines = pl.ds(pl.multiple_of(row * 64 + c * 8, 8), 8)
                spot = slice(c * 8, c * 8 + 8)
                a, s, g = (a_ref[lines, lanes], s_ref[lines, lanes], g_ref[lines, lanes])
                h_left = a * h_left + s
                lam_lr = g + m_right
                m_right = a * lam_lr
                here = pl.ds(pl.multiple_of((row + 1) * 64 + c * 8, 8), 8)
                h_down, lam_up = (down_ref[here, lanes], up_ref[lines, lanes])
                h_up = a * (col_h[spot, lanes] * keep) + s
                col_h[spot, lanes] = h_up
                lam_down = g + col_m[spot, lanes] * keep
                col_m[spot, lanes] = a * lam_down
                h_right, lam_rl = (row_h[spot, lanes], row_m[spot, lanes])
                lam_sum = (lam_lr + lam_rl) + (lam_down + lam_up)
                s_ref[lines, lanes] = (h_right + h_left) + (h_down + h_up)
                up_ref[lines, lanes] = lam_sum
                g_ref[lines, lanes] = (
                    (lam_lr * h_right + lam_rl * h_left)
                    + (lam_down * h_down + lam_up * h_up)
                    - s * lam_sum
                )

    def descend_two(step, held):
        row = rows - 1 - 2 * step
        held = carry_back(held, row - 1, False)
        descend(row)
        held = carry_back(held, row - 2, True)
        descend(row - 1)
        return held

    held = carry_back((nothing,) * 2, rows - 1, True)
    held = lax.fori_loop(0, devices - 1, descend_two, held, unroll=at_once)
    carry_back(held, 0, False)
    descend(1)
    descend(0)
    decay_acc[...] = jnp.zeros_like(decay_acc)
    gather_e, gather_b, gather_c = (spread_e[:part], spread_bc[:PROJ, :128], spread_bc[:PROJ, 128:])

    def finish(tile, carry):
        lines = pl.ds(pl.multiple_of(tile * pos, pos), pos)
        delta = delta_keep[tile]
        delta_low = delta.astype(bf16)
        of_b, of_c = (coef_keep[lines, :128], coef_keep[lines, 128:])
        grad_b = grad_c = None
        of_y, of_step, of_sum = ([], [], [])
        for k in range(width // 128):
            lanes = slice(k * 128, (k + 1) * 128)
            h_sum, lam_sum = (s_ref[lines, lanes], up_ref[lines, lanes])
            of_step.append((g_ref[lines, lanes] * rate_row[:, lanes]).astype(bf16))
            of_y.append((h_sum * of_c).astype(bf16))
            of_sum.append((lam_sum * of_b).astype(bf16))
            term_b, term_c = (lam_sum * source_ref[lines, lanes], h_sum * mix_ref[lines, lanes])
            grad_b = term_b if grad_b is None else grad_b + term_b
            grad_c = term_c if grad_c is None else grad_c + term_c
        of_y, of_step, of_sum = [jnp.concatenate(x, axis=1) for x in (of_y, of_step, of_sum)]
        decay_acc[...] += dot(delta_low, of_step, (1, 0))
        y_keep[tile] = jnp.transpose(dot(of_y, gather_e, (1, 1)))
        steps_keep[tile] = jnp.transpose(dot(of_step, gather_e, (1, 1)))
        sums_keep[tile] = jnp.transpose(dot(of_sum, gather_e, (1, 1)))
        coefs_keep[tile] = dot(gather_b, grad_b.astype(bf16), (1, 1)) + dot(gather_c, grad_c.astype(bf16), (1, 1))
        return carry

    lax.fori_loop(0, devices, finish, 0, unroll=8)
    pre_grads = []
    for tile in range(devices):
        sums = sums_keep[tile]
        pre_grads.append((steps_keep[tile] + got[tile, :part] * sums) * step_keep[tile])
        send[tile, :part] = y_keep[tile]
        send[tile, part : 2 * part] = delta_keep[tile] * sums
        send[tile, 2 * part + 16 :] = coefs_keep[tile, 16:]
    pre_grads = jnp.concatenate(pre_grads, axis=1)
    ranks = jnp.concatenate([got[tile, 2 * part : 2 * part + 16] for tile in range(devices)], axis=1)
    rank_grad = fine_dot(step_own, pre_grads, (0, 0))
    for tile in range(devices):
        send[tile, 2 * part : 2 * part + 16] = coefs_keep[tile, :16] + rank_grad[:, tile * pos : (tile + 1) * pos]
    step_grad = fine_dot(pre_grads, ranks, (1, 1))
    decay_grad = decay_acc[...] * one_channel[...]
    decay_high, decay_low = split(decay_grad)
    decay_grad = dot(decay_high, by_state[...], (1, 1)) + dot(decay_low, by_state[...], (1, 1))
    spot = (iota((part, small.shape[1]), 1) == iota((part, small.shape[1]), 0) + place[0] * part).astype(bf16)
    for at, value in ((0, step_grad), (16, decay_grad)):
        high, low = split(value)
        small[at : at + 16] = dot(high, spot, (0, 0)) + dot(low, spot, (0, 0))


def mix_kernel(
    place, group, got, small_in, low, low_halo, cot, conv_own, conv_halo, pre, gate_in, grad_in,
    select_rows, table, table_t, in_w, links,
    act_out, moved_ref, gate_grad_out, gated_ref, keep, give,
    grads, inner_ref, sums_ref, *, pair,
):
    devices, length, pos = got.shape
    model, inner_width = (low.shape[0], pre.shape[0])
    part = inner_width // devices
    lane = iota((1, pos), 1)
    prev, following = row_masks(links, place[0])
    proj_grad = got[0, 2 * part :]
    for k in range(1, devices):
        proj_grad = proj_grad + got[k, 2 * part :]
    proj_grad = proj_grad.astype(bf16)
    together = max(1, 48 // part)
    for first in range(0, devices, together):
        members = range(first, first + together)
        rows = slice(first * part, (first + together) * part)
        y = jnp.concatenate([got[k, :part] for k in members], axis=0)
        inner_grad = jnp.concatenate([got[k, part : 2 * part] for k in members], axis=0)
        pre_act, gate, gated_grad = (pre[rows], gate_in[rows], grad_in[rows])
        skip = table[rows, SKIP : SKIP + 1]
        sig_pre, sig_gate = (sigmoid(pre_act), sigmoid(gate))
        inner = (pre_act * sig_pre).astype(bf16)
        inner_ref[rows] = inner
        inner = inner.astype(f32)
        silu_gate = gate * sig_gate
        mix_grad = gated_grad * silu_gate
        inner_grad = inner_grad + mix_grad * skip + dot(select_rows[rows], proj_grad, (1, 0))
        act_grad = inner_grad * (sig_pre * (1.0 + pre_act * (1.0 - sig_pre)))
        act_out[rows] = act_grad
        y_all = y + skip * inner
        gated_ref[rows] = (y_all * silu_gate).astype(bf16)
        gate_grad_out[rows] = (gated_grad * y_all * (sig_gate * (1.0 + gate * (1.0 - sig_gate)))).astype(bf16)
        field = conv_own[rows]
        upper, lower = rows_around(field, conv_halo[rows])
        fields = (upper * prev, field, lower * following)
        sums = jnp.where(lane == 9, jnp.sum(act_grad, axis=1, keepdims=True), 0.0)
        sums = jnp.where(lane == 10, jnp.sum(mix_grad * inner, axis=1, keepdims=True), sums)
        for b, moved in enumerate((from_right(act_grad), act_grad, from_left(act_grad))):
            moved_ref[b, rows] = moved.astype(bf16)
            for a in range(3):
                sums = jnp.where(lane == 3 * a + b, jnp.sum(moved * fields[a], axis=1, keepdims=True), sums)
        sums_ref[rows] = sums
    gated, gate_grad = (gated_ref[...], gate_grad_out[...])

    low_in = low[...]
    upper, lower = rows_around(low_in.astype(f32), low_halo[...].astype(f32))
    which = iota((16, 1), 0)
    masks = jnp.where(which == 0, prev, jnp.where(which == 1, 1.0, following))
    left_hand = jnp.concatenate(
        [(upper * prev).astype(bf16), low_in, (lower * following).astype(bf16), masks.astype(bf16)], axis=0
    )
    blocks = inner_width // 128
    gate_at, out_at, small_at = [k * blocks * model for k in (1, 2, 3)]
    ones = jnp.ones((16, pos), bf16)
    totals = [[], []]
    gain_sum = jnp.zeros((model, 128), f32)
    for n in range(blocks):
        columns = slice(n * 128, (n + 1) * 128)
        in_conv = conv_total = None
        for b in range(3):
            part_b = dot(left_hand, moved_ref[b, columns], (1, 1))
            for a in range(3):
                tap = table_t[3 * a + b : 3 * a + b + 1, columns]
                term = tap * part_b[a * model : (a + 1) * model]
                total = tap * part_b[3 * model + a : 3 * model + a + 1]
                in_conv = term if in_conv is None else in_conv + term
                conv_total = total if conv_total is None else conv_total + total
        in_gate = dot(low_in, gate_grad[columns], (1, 1))
        grads[n * model : (n + 1) * model] = in_conv
        grads[gate_at + n * model : gate_at + (n + 1) * model] = in_gate
        grads[out_at + n * model : out_at + (n + 1) * model] = dot(cot[...], gated[columns], (1, 1))
        totals[0].append(conv_total)
        totals[1].append(dot(ones, gate_grad[columns], (1, 1))[0:1])
        conv_w = in_w[:, columns].astype(f32)
        gate_w = in_w[:, inner_width + n * 128 : inner_width + (n + 1) * 128].astype(f32)
        gain_sum = gain_sum + (conv_w * in_conv + gate_w * in_gate)
    sums = jnp.broadcast_to(jnp.concatenate(totals[0] + totals[1], axis=1), (16, 2 * inner_width))
    sums_high, sums_low = split(sums)
    shift_row = (dot(sums_high, in_w[...], (1, 1)) + dot(sums_low, in_w[...], (1, 1)))[0:1]
    gain_row = patch_sums(gain_sum)
    gain, shift = (table_t[GAIN : GAIN + 1, :model], table_t[SHIFT : SHIFT + 1, :model])
    gain_row = (gain_row - shift * shift_row) / gain
    high, mid = split(sums_ref[...])
    rest = (sums_ref[...] - high.astype(f32) - mid.astype(f32)).astype(bf16)
    chosen = (iota((16, pos), 0) == iota((16, pos), 1)).astype(bf16)
    sums = dot(chosen, high, (1, 1)) + (dot(chosen, mid, (1, 1)) + dot(chosen, rest, (1, 1)))
    norms = jnp.concatenate([gain_row, shift_row], axis=1)
    sums = jnp.where(iota((16, 1), 0) == NORM_AT - TAPS_AT, norms, sums)
    smalls = jnp.concatenate([dot(proj_grad, inner_ref[...], (1, 1)), small_in[...], sums], axis=0)
    put_blocks(grads, small_at, smalls)
    small_at = small_at + blocks * SMALL
    grads[small_at:] = jnp.zeros((grads.shape[0] - small_at, 128), f32)
    own = group[0] % 2
    if pair:
        count = keep.shape[0] // 2
        height = group[0] // 2
        for ref, side in ((keep, own), (give, 1 - own)):
            for k, at in enumerate((height, 1 - height)):
                ref[k * count : (k + 1) * count] = grads[pl.ds(pl.multiple_of((2 * side + at) * count, count), count)]
    else:
        count = keep.shape[0]
        keep[...] = grads[pl.ds(pl.multiple_of(own * count, count), count)]
        give[...] = grads[pl.ds(pl.multiple_of((1 - own) * count, count), count)]


def beyond_kernel(place, moved, table_t, in_w, links, near, far):
    model = in_w.shape[0]
    inner_width, pos = moved.shape[1:]
    lane = iota((1, pos), 1)
    prev, following = row_masks(links, place[0])
    conv_w = in_w[:, :inner_width].astype(f32)
    beyond = None
    for b in range(3):
        weights = [conv_w * table_t[3 * a + b : 3 * a + b + 1] for a in (0, 2)]
        term = dot(jnp.concatenate(weights, axis=0).astype(bf16), moved[b], (1, 0))
        beyond = term if beyond is None else beyond + term
    beyond = jnp.where(lane < 64, beyond[:model] * prev, beyond[model:] * following)
    top, bottom = (beyond[: model // 2], beyond[model // 2 :])
    up = jnp.where(lane < 64, top, pltpu.roll(bottom, 64, 1))
    down = jnp.where(lane < 64, pltpu.roll(top, 64, 1), bottom)
    even = place[0] % 2 == 0
    near[...] = jnp.where(even, down, up)
    far[...] = jnp.where(even, up, down)


def exit_kernel(
    place, act, from_above, from_below, gate_grad, gated, table, in_w, links, tok, cot, out_t,
    tokens_grad, layer_out,
):
    inner_width, pos = act.shape
    model = in_w.shape[0]
    lane = iota((1, pos), 1)
    even = place[0] % 2 == 0
    above, below = (
        jnp.where(even, from_above[...], from_below[...]), jnp.where(even, from_below[...], from_above[...])
    )
    top = jnp.where(lane < 64, above, pltpu.roll(below, 64, 1))
    bottom = jnp.where(lane < 64, pltpu.roll(above, 64, 1), below)
    beyond_high, beyond_low = split(jnp.concatenate([top, bottom], axis=0))
    act_grad = act[...]
    prev, following = row_masks(links, place[0])
    upper, lower = rows_around(act_grad, jnp.zeros_like(act_grad))
    columns = table[...]
    taps = [[columns[:, 8 - 3 * a - b : 9 - 3 * a - b] for b in range(3)] for a in range(3)]
    conv_grad = conv_tile(upper * prev, act_grad, lower * following, taps).astype(bf16)
    natural = jnp.concatenate([conv_grad, gate_grad[...], gated[...]], axis=0)
    order = column_order(pos)
    natural = dot(natural, order, (1, 0)).astype(bf16)
    layer = jnp.transpose(dot(out_t[...], natural[2 * inner_width :], (1, 0)))
    layer_out[...] = (tok[...].astype(f32) + layer).astype(bf16)
    normed_grad = dot(in_w[...], natural[: 2 * inner_width], (1, 0))
    normed_grad = normed_grad + (dot(beyond_high, order, (1, 0)) + dot(beyond_low, order, (1, 0)))
    xhat, inverse = normalized(flipped(tok[...]))
    scaled = normed_grad * columns[:model, GAIN : GAIN + 1]
    x_grad = (
        scaled
        - jnp.mean(scaled, axis=0, keepdims=True)
        - xhat * jnp.mean(scaled * xhat, axis=0, keepdims=True)
    ) * inverse
    x_grad = jnp.transpose(x_grad)
    tokens_grad[...] = (x_grad + cot[...].astype(f32)).astype(bf16)


def deal_kernel(group, *refs, members, pair):
    pieces, ordered = (refs[:members], refs[-1])
    (
        gain_grad, shift_grad, inproj, kernel_grad, offset, select, stepproj, stepbias, decay, skip, outproj,
    ) = refs[members:-1]
    model, inner_width = outproj.shape
    blocks = inner_width // 128
    rank = stepproj.shape[0]
    states = decay.shape[0]
    count = pieces[0].shape[0]
    for k, piece in enumerate(pieces):
        if pair:
            core, height = (group[0] % 2, group[0] // 2)
            core = 1 - core if k // 2 else core
            height = 1 - height if k % 2 else height
            slot = core * 2 + height
        else:
            slot = k % 2 * (members // 2) + k // 2
        ordered[pl.ds(pl.multiple_of(slot * count, count), count)] = piece[...]

    def rows(start, count):
        return ordered[start : start + count]

    for k in range(2 * blocks):
        inproj[:, k * 128 : (k + 1) * 128] = rows(k * model, model)
    start = 2 * blocks * model
    for k in range(blocks):
        outproj[:, k * 128 : (k + 1) * 128] = rows(start + k * model, model)
    start = start + blocks * model
    small = jnp.concatenate([rows(start + k * SMALL, SMALL) for k in range(blocks)], axis=1)
    select[:rank] = small[:rank]
    select[rank:] = small[IN:PROJ]
    stepproj[...] = small[STEP_AT : STEP_AT + rank]
    stepbias[...] = small[STEP_AT + ONE : STEP_AT + ONE + 1].reshape(stepbias.shape)
    decay[...] = small[DECAY_AT : DECAY_AT + states]
    for k in range(3):
        kernel_grad[k] = small[TAPS_AT + 3 * k : TAPS_AT + 3 * k + 3]
    offset[...] = small[OFFSET_AT : OFFSET_AT + 1].reshape(offset.shape)
    skip[...] = small[SKIP_AT : SKIP_AT + 1].reshape(skip.shape)
    norms = small[NORM_AT : NORM_AT + 1]
    gain_grad[...] = norms[:, :model].reshape(gain_grad.shape)
    shift_grad[...] = norms[:, model:].reshape(shift_grad.shape)


def vmem_call(kernel, out_shape, scalars, arrays, weights=(), scratch=(), limit=16):
    scalars = [pltpu.with_memory_space_constraint(x, pltpu.HBM) if x.ndim == 2 else x for x in scalars]
    arrays = [pltpu.with_memory_space_constraint(x, pltpu.VMEM) for x in arrays]
    arrays += [pltpu.with_memory_space_constraint(x, pltpu.HBM) for x in weights]
    return pl.pallas_call(
        kernel,
        out_shape=out_shape,
        in_specs=[pl.BlockSpec(memory_space=pltpu.SMEM)] * len(scalars)
        + [pl.BlockSpec(memory_space=pltpu.VMEM)] * len(arrays),
        out_specs=[pl.BlockSpec(memory_space=pltpu.VMEM)] * len(out_shape),
        scratch_shapes=list(scratch),
        compiler_params=pltpu.CompilerParams(vmem_limit_bytes=limit * 1024 * 1024),
    )(*scalars, *arrays)


def struct(*shape, dtype=f32):
    return jax.ShapeDtypeStruct(shape, dtype)


def inside(*shape, dtype=f32):
    return pltpu.VMEM(shape, dtype)


def scan_call(place, got, table, links, maps, states):
    devices, length, pos = got.shape
    inner_width = table.shape[0]
    part = inner_width // devices
    width = -(-part * states // 128) * 128
    total = devices * pos
    span = 256 if width % 256 == 0 else 128
    group = 768 if width % 768 == 0 else span
    big = pltpu.VMEM((total, width), f32)
    line = pltpu.VMEM(((2 * devices + 1) * 64, 128), f32)
    column = pltpu.VMEM((pos // 2, width), f32)
    own = pltpu.VMEM((devices, part, pos), f32)
    return vmem_call(
        functools.partial(scan_kernel, part=part, states=states, span=span, group=group),
        [inside(devices, length, pos), inside(32, inner_width)],
        [place],
        [got, table, links, *maps],
        (),
        [big] * 3
        + [pltpu.VMEM((total + pos // 2, width), f32)]
        + [big] * 3
        + [column] * 4
        + [line] * 9
        + [pltpu.VMEM((total, 2 * part), bf16)] * 3
        + [pltpu.VMEM((total, 256), f32)]
        + [own] * 5
        + [pltpu.VMEM((devices, PROJ, pos), f32), pltpu.VMEM((part, width), f32)],
        limit=36 if total <= 1024 else 60,
    )


def on_device(
    tokens, heights, cotangent, norm_gain, norm_bias, in_weight, conv_kernel, conv_bias, select_weight,
    step_weight, step_bias, decay_log, skip_gain, out_weight,
):
    _, tile_rows, grid_cols, model = tokens.shape
    inner_width = out_weight.shape[0]
    states = decay_log.shape[1]
    rank = step_weight.shape[0]
    devices = lax.axis_size("seq")
    groups = lax.axis_size("dp")
    place = lax.axis_index("seq").reshape(1)
    group = lax.axis_index("dp").reshape(1)
    pair = groups == 4
    pos = tile_rows * grid_cols
    part = inner_width // devices
    width = -(-part * states // 128) * 128
    length = 2 * part + PROJ
    near_pairs = [(i, i ^ 1) for i in range(devices)]
    far_pairs = [(i, (i - 1 + 2 * (i % 2)) % devices) for i in range(devices)]

    tok, cot = (tokens.reshape(pos, model), cotangent.reshape(pos, model))
    even = place[0] % 2 == 0
    upper, lower = (tok[:grid_cols].astype(f32), tok[grid_cols:].astype(f32))
    above = lax.ppermute(jnp.where(even, upper, lower), "seq", far_pairs)
    below = lax.ppermute(jnp.where(even, lower, upper), "seq", near_pairs)
    above, group = lax.optimization_barrier((above, group))
    out_t = out_weight.T
    channels = inside(inner_width, pos)
    narrow = inside(model, pos, dtype=bf16)
    conv_own, gate, gated_grad, mix, low, cot_in, conv_rows, select_rows, table, table_t, in_keep, links, taps_wide, *maps = vmem_call(
        own_kernel,
        [channels] * 4
        + [narrow] * 2
        + [
            inside(inner_width, model, dtype=bf16), inside(inner_width, PROJ, dtype=bf16), inside(inner_width, TABLE),
            inside(TABLE, inner_width), inside(model, 2 * inner_width, dtype=bf16),
            inside(2 * devices + 1, 8, 128), inside(BIAS + 1, inner_width, pos),
            inside(2 * part, width, dtype=bf16), inside(2 * PROJ, 256, dtype=bf16), inside(states, width, dtype=bf16),
            inside(part, width), inside(8, width), inside(part, 48, dtype=bf16),
        ],
        [heights, place],
        [],
        [
            tok, cot, in_weight, out_t, select_weight.T, conv_kernel, conv_bias, step_weight, step_bias,
            decay_log.T, skip_gain, norm_gain, norm_bias,
        ],
    )
    sent, conv_halo, pre_act, low_halo = vmem_call(
        entry_kernel,
        [inside(devices, length, pos), channels, channels, narrow],
        [place],
        [above, below, conv_own, mix, conv_rows, select_rows, table, links, taps_wide],
    )
    got = lax.all_to_all(sent, "seq", 0, 0, tiled=True)
    sent, small = scan_call(place, got, table, links, maps, states)
    got = lax.all_to_all(sent, "seq", 0, 0, tiled=True)
    blocks = inner_width // 128
    whole = -(-blocks * (3 * model + SMALL) // 2048) * 2048
    half = whole // 2
    act_grad, moved, gate_grad, gated, keep, give = vmem_call(
        functools.partial(mix_kernel, pair=pair),
        [channels, inside(3, inner_width, pos, dtype=bf16)]
        + [inside(inner_width, pos, dtype=bf16)] * 2
        + [inside(half, 128)] * 2,
        [place, group],
        [
            got, small, low, low_halo, cot_in, conv_own, conv_halo, pre_act, gate, gated_grad, select_rows, table,
            table_t, in_keep, links,
        ],
        (),
        [
            pltpu.VMEM((whole, 128), f32), pltpu.VMEM((inner_width, pos), bf16), pltpu.VMEM((inner_width, pos), f32),
        ],
    )
    near, far = vmem_call(
        beyond_kernel, [inside(model // 2, pos)] * 2, [place], [moved, table_t, in_keep, links]
    )
    keep, near, far = lax.optimization_barrier((keep, near, far))
    from_above = lax.ppermute(far, "seq", far_pairs)
    from_below = lax.ppermute(near, "seq", near_pairs)
    swap = [(i, i ^ 1) for i in range(groups)]
    taken = lax.ppermute(give, "dp", swap)
    count = half // (groups // 2)
    if pair:
        across = [(i, i ^ 2) for i in range(groups)]
        other = lax.ppermute(keep[count:] + taken[count:], "dp", across)
        piece = keep[:count] + taken[:count]
    else:
        same_core = [list(range(c, groups, 2)) for c in range(2)]
        pieces = (keep + taken).reshape(groups // 2, count, 128)
        pieces = lax.all_to_all(pieces, "dp", 0, 0, tiled=True, axis_index_groups=same_core)
        piece, other = (pieces[0], jnp.sum(pieces[1:], axis=0))
    other, from_above, from_below = lax.optimization_barrier((other, from_above, from_below))
    shares = (piece + other).reshape(devices, count // devices, 128)
    shares = lax.all_to_all(shares, "seq", 0, 0, tiled=True)
    share = jnp.broadcast_to(jnp.sum(shares, axis=0), shares.shape)
    mine = lax.all_to_all(share, "seq", 0, 0, tiled=True).reshape(count, 128)
    mine, from_above, from_below = lax.optimization_barrier((mine, from_above, from_below))
    tokens_grad, layer_out = vmem_call(
        exit_kernel,
        [struct(pos, model, dtype=bf16)] * 2,
        [place],
        [act_grad, from_above, from_below, gate_grad, gated, table, in_keep, links],
        [tok, cot, out_t],
    )
    if pair:
        from_y = lax.ppermute(mine, "dp", across)
        from_y, tokens_grad = lax.optimization_barrier((from_y, tokens_grad))
        pieces = [mine, from_y, lax.ppermute(mine, "dp", swap), lax.ppermute(from_y, "dp", swap)]
    else:
        pieces = list(lax.all_gather(mine, "dp"))
    gain, shift, inproj, kernel, offset, select, stepproj, stepbias, decay, skip, outproj = vmem_call(
        functools.partial(deal_kernel, members=len(pieces), pair=pair),
        [
            struct(model), struct(model), struct(model, 2 * inner_width), struct(3, 3, inner_width),
            struct(inner_width), struct(rank + 2 * states, inner_width), struct(rank, inner_width),
            struct(inner_width), struct(states, inner_width), struct(inner_width), struct(model, inner_width),
        ],
        [group],
        pieces,
        (),
        [pltpu.VMEM((whole, 128), f32)],
    )
    shape = tokens.shape
    return (
        layer_out.reshape(shape), tokens_grad.reshape(shape), gain, shift, inproj, kernel, offset, select.T,
        stepproj, stepbias, decay.T, skip, outproj.T,
    )


def solution(mesh):
    tile, whole = (P("dp", "seq", None, None), P())
    return jax.shard_map(
        on_device,
        mesh=mesh,
        in_specs=(tile, P("dp", None), tile) + (whole,) * 11,
        out_specs=(tile, tile) + (whole,) * 11,
        check_vma=False,
    )
```

```python
import functools

import jax
import jax.numpy as jnp
from jax import lax
from jax.experimental import pallas as pl
from jax.experimental.pallas import tpu as pltpu
from jax.sharding import PartitionSpec as P

epsilon = 1e-05
f32, bf16 = (jnp.float32, jnp.bfloat16)
ONE, IN, OUT, PROJ = (12, 16, 32, 48)
BIAS, SKIP, GAIN, SHIFT, STEP, DECAY, TABLE = (9, 10, 11, 12, 16, 32, 48)
STEP_AT, DECAY_AT, TAPS_AT, OFFSET_AT, SKIP_AT, NORM_AT, SMALL = (48, 64, 80, 89, 90, 95, 96)


def dot(a, b, over):
    return lax.dot_general(a, b, (((over[0],), (over[1],)), ((), ())), preferred_element_type=f32)


def split(value):
    high = value.astype(bf16)
    return (high, (value - high.astype(f32)).astype(bf16))


def fine_dot(a, b, over):
    (a_high, a_low), (b_high, b_low) = (split(a), split(b))
    return dot(a_high, b_high, over) + (dot(a_low, b_high, over) + dot(a_high, b_low, over))


def iota(shape, dim):
    return lax.broadcasted_iota(jnp.int32, shape, dim)


def sigmoid(v):
    return 1.0 / (1.0 + jnp.exp(-v))


def links_up(heights, row):
    if row == 0:
        return 0.0
    end = jnp.int32(0)
    same = True
    for k in range(heights.shape[1]):
        end = end + heights[0, k]
        same = same & (end != row)
    return jnp.where(same, 1.0, 0.0).astype(f32)


def row_masks(links, place):
    lane = iota((1, 128), 1)
    flags = [links[2 * place + k, 0:1] for k in range(3)]
    return (jnp.where(lane < 64, flags[0], flags[1]), jnp.where(lane < 64, flags[1], flags[2]))


def rows_around(own, halo):
    lane = iota((1, 128), 1)
    upper = pltpu.roll(jnp.where(lane < 64, own, halo), 64, 1)
    lower = pltpu.roll(jnp.where(lane < 64, halo, own), 64, 1)
    return (upper, lower)


def from_left(tile):
    place = iota((1, 128), 1) & 63
    wrapped = jnp.where(place == 0, 0.0, pltpu.roll(tile, 73, 1))
    return jnp.where(place < 8, wrapped, pltpu.roll(tile, 8, 1))


def from_right(tile):
    place = iota((1, 128), 1) & 63
    wrapped = jnp.where(place == 63, 0.0, pltpu.roll(tile, 55, 1))
    return jnp.where(place >= 56, wrapped, pltpu.roll(tile, 120, 1))


def conv_tile(upper, own, lower, taps):
    left, middle, right = [
        taps[0][b] * upper + taps[1][b] * own + taps[2][b] * lower for b in range(3)
    ]
    return middle + (from_left(left) + from_right(right))


def normalized(x):
    centred = x - jnp.mean(x, axis=0, keepdims=True)
    inverse = lax.rsqrt(jnp.mean(centred * centred, axis=0, keepdims=True) + epsilon)
    return (centred * inverse, inverse)


def eye(size):
    return (iota((size, size), 0) == iota((size, size), 1)).astype(bf16)


def flipped(value):
    pieces = [value[:, k : k + 128] for k in range(0, value.shape[1], 128)]
    return jnp.concatenate([dot(eye(piece.shape[1]), piece, (1, 1)) for piece in pieces], axis=0)


def flipped_fine(value):
    high, low = split(value)
    rest = (value - high.astype(f32) - low.astype(f32)).astype(bf16)
    return flipped(high) + (flipped(low) + flipped(rest))


def patch_sums(value):
    high, low = split(value)
    ones = jnp.ones((8, value.shape[1]), bf16)
    return (dot(ones, high, (1, 1)) + dot(ones, low, (1, 1)))[0:1]


def put_blocks(ref, start, value):
    for k in range(value.shape[1] // 128):
        ref[start + k * value.shape[0] : start + (k + 1) * value.shape[0]] = value[:, k * 128 : (k + 1) * 128]


def column_order(pos):
    new, old = (iota((pos, pos), 0), iota((pos, pos), 1))
    source = (new & ~63) | ((new & 7) << 3) | ((new >> 3) & 7)
    return (source == old).astype(bf16)


def lane_maps(part, states, width):
    lane = iota((1, width), 1)
    channel = jnp.floor((lane.astype(f32) + 0.5) * (1.0 / states)).astype(jnp.int32)
    return (channel, lane - channel * states, channel < part)


def entered(rows):
    return dot(flipped(rows).astype(bf16), column_order(rows.shape[0]), (1, 0))


def own_kernel(
    heights, place, tok, cot, in_w, out_t, select_t, conv_kernel, conv_bias, step_weight, step_bias, decay_t, skip_gain,
    norm_gain, norm_bias,
    conv_out, gate_out, grad_out, mix_out, low_out, cot_out, conv_rows, select_rows, table, table_t, in_keep, links,
    taps_wide, spread_e, spread_bc, by_state, one_channel, rates, step_three,
):
    model, inner_width = out_t.shape
    states = decay_t.shape[0]
    rank = step_weight.shape[0]
    in_keep[...] = in_w[...]
    for row in range(links.shape[0]):
        links[row] = jnp.full(links.shape[1:], links_up(heights, row), f32)
    in_rows = flipped(in_w[...]).astype(bf16)
    conv_rows[...] = in_rows[:inner_width]
    out_rows = flipped(out_t[...]).astype(bf16)
    chosen = iota((PROJ, select_t.shape[0]), 0)
    chosen = jnp.where(chosen < rank, chosen, jnp.where(chosen < IN, -1, chosen - IN + rank))
    chosen = (chosen == iota((PROJ, select_t.shape[0]), 1)).astype(bf16)
    select_rows[...] = flipped(dot(chosen, select_t[...], (1, 0)).astype(bf16)).astype(bf16)
    table_t[...] = jnp.zeros_like(table_t)
    for k in range(3):
        table_t[3 * k : 3 * k + 3] = conv_kernel[k]
    table_t[BIAS : BIAS + 1] = conv_bias[...].reshape(1, inner_width)
    table_t[SKIP : SKIP + 1] = skip_gain[...].reshape(1, inner_width)
    table_t[GAIN : GAIN + 1, :model] = norm_gain[...].reshape(1, model)
    table_t[SHIFT : SHIFT + 1, :model] = norm_bias[...].reshape(1, model)
    table_t[STEP : STEP + rank] = step_weight[...]
    table_t[STEP + ONE : STEP + ONE + 1] = step_bias[...].reshape(1, inner_width)
    table_t[DECAY : DECAY + states] = decay_t[...]
    columns = flipped_fine(table_t[...])
    table[...] = columns
    for k in range(taps_wide.shape[0]):
        taps_wide[k] = jnp.broadcast_to(columns[:, k : k + 1], taps_wide.shape[1:])
    gain, shift = (columns[:model, GAIN : GAIN + 1], columns[:model, SHIFT : SHIFT + 1])
    low = (normalized(entered(tok[...]))[0] * gain + shift).astype(bf16)
    cot_in = entered(cot[...]).astype(bf16)
    low_out[...] = low
    cot_out[...] = cot_in
    both = dot(in_rows, low, (1, 0))
    conv_out[...] = both[:inner_width]
    gate = both[inner_width:]
    gated_grad = dot(out_rows, cot_in, (1, 0))
    gate_out[...] = gate
    grad_out[...] = gated_grad
    mix_out[...] = gated_grad * (gate * sigmoid(gate))

    part, width = one_channel.shape
    own_rows = table[pl.ds(pl.multiple_of(place[0] * part, 4), part), :]
    channel, state, live = lane_maps(part, states, width)
    twice = iota((2 * part, 1), 0)
    twice = jnp.where(twice >= part, twice - part, twice)
    spread_e[...] = ((twice == channel) & live).astype(bf16)
    coef = iota((2 * PROJ, 1), 0)
    coef = jnp.where(coef >= PROJ, coef - PROJ, coef)
    first = state[:, :128]
    spread_bc[...] = jnp.concatenate([coef - IN == first, coef - OUT == first], axis=1).astype(bf16)
    of_state = ((iota((states, 1), 0) == state) & live).astype(bf16)
    by_state[...] = of_state
    mask = ((iota((part, 1), 0) == channel) & live).astype(f32)
    one_channel[...] = mask
    rate = -jnp.exp(own_rows[:, DECAY : DECAY + states])
    rate_high, rate_low = split(rate)
    rate_rest = split(rate - rate_high.astype(f32) - rate_low.astype(f32))[0]
    rate_row = sum(dot(piece, of_state, (1, 0)) for piece in (rate_high, rate_low, rate_rest))
    rate_row = jnp.sum(rate_row * mask, axis=0, keepdims=True)
    rates[...] = jnp.where(iota((8, 1), 0) == 0, rate_row, rate_row * 1.4426950408889634)
    step_high, step_low = split(own_rows[:, STEP : STEP + 16])
    step_three[...] = jnp.concatenate([step_high, step_high, step_low], axis=1)


def entry_kernel(
    place, above, below, conv_own, mix, conv_rows, select_rows, table, links, taps_wide,
    send, halo_out, pre_out, low_halo_out,
):
    devices = send.shape[0]
    inner_width = conv_own.shape[0]
    model = conv_rows.shape[1]
    part = inner_width // devices
    gain, shift = (table[:model, GAIN : GAIN + 1], table[:model, SHIFT : SHIFT + 1])
    even = place[0] % 2 == 0
    rows = [jnp.where(even, below[...], above[...]), jnp.where(even, above[...], below[...])]
    rows = [
        jnp.concatenate([x[:64], jnp.concatenate([x[64:, :64], x[64:, 64:]], axis=0)], axis=1) for x in rows
    ]
    halo = jnp.concatenate(rows, axis=0).astype(bf16)
    low_halo = (normalized(entered(halo))[0] * gain + shift).astype(bf16)
    low_halo_out[...] = low_halo
    around = dot(conv_rows[...], low_halo, (1, 0))
    halo_out[...] = around
    conv_in = conv_own[...]
    prev, following = row_masks(links, place[0])
    upper, lower = rows_around(conv_in, around)
    taps = [[taps_wide[3 * a + b] for b in range(3)] for a in range(3)]
    pre_act = taps_wide[BIAS] + conv_tile(upper * prev, conv_in, lower * following, taps)
    inner = (pre_act * sigmoid(pre_act)).astype(bf16)
    proj = dot(flipped(select_rows[...]).astype(bf16), inner, (1, 0))
    proj = jnp.where(iota(proj.shape, 0) == ONE, 1.0, proj)
    pre_out[...] = pre_act
    inner = inner.astype(f32)
    for k in range(devices):
        send[k, :part] = inner[k * part : (k + 1) * part]
        send[k, part : 2 * part] = mix[k * part : (k + 1) * part]
        send[k, 2 * part :] = proj


def scan_kernel(
    place, got, table, links, spread_e, spread_bc, by_state, one_channel, rates, step_three,
    send, small,
    a_ref, s_ref, g_ref, down_ref, up_ref, source_ref, mix_ref, col_h, col_m, row_h, row_m,
    prod, end_lr, end_rl, back_lr, back_rl, in_lr, in_rl, tail_lr, tail_rl,
    lhs_d, lhs_u, lhs_m, coef_keep, step_keep, delta_keep, y_keep, steps_keep, sums_keep, coefs_keep, decay_acc, *, part, states, span, group,
):
    devices, _, pos = got.shape
    rows = 2 * devices
    width = a_ref.shape[1]
    rate_row, rate_two = (rates[0:1], rates[1:2])
    step_own = table[pl.ds(pl.multiple_of(place[0] * part, 4), part), STEP : STEP + 16]

    def turned(value):
        return jnp.transpose(jnp.concatenate(split(value), axis=0))

    for tile in range(devices):
        lines = slice(tile * pos, (tile + 1) * pos)
        inner_own = got[tile, :part]
        proj = got[tile, 2 * part :]
        high, low = split(proj[:16])
        pre_step = dot(step_three[...], jnp.concatenate([high, low, high], axis=0), (1, 0))
        tail = jnp.exp(-jnp.abs(pre_step))
        tail = jnp.where(tail < 1e-3, tail * (1.0 - 0.5 * tail), jnp.log(1.0 + tail))
        delta = jnp.maximum(pre_step, 0.0) + tail
        step_keep[tile] = sigmoid(pre_step)
        delta_keep[tile] = delta
        lhs_d[lines, :] = turned(delta)
        lhs_u[lines, :] = turned(delta * inner_own)
        lhs_m[lines, :] = turned(got[tile, part : 2 * part])
        coef_keep[lines, :] = dot(turned(proj), spread_bc[...], (1, 0))

    for k in range(width // span):
        lanes = slice(k * span, (k + 1) * span)

        def prepare(tile, carry):
            lines = pl.ds(pl.multiple_of(tile * pos, pos), pos)
            of_delta, of_source, of_mix = (lhs_d[lines, :], lhs_u[lines, :], lhs_m[lines, :])
            a_ref[lines, lanes] = jnp.exp2(dot(of_delta, spread_e[:, lanes], (1, 0)) * rate_two[:, lanes])
            source = dot(of_source, spread_e[:, lanes], (1, 0))
            mix = dot(of_mix, spread_e[:, lanes], (1, 0))
            source_ref[lines, lanes] = source
            mix_ref[lines, lanes] = mix
            for j in range(span // 128):
                tile_lanes = slice(k * span + j * 128, k * span + (j + 1) * 128)
                piece = slice(j * 128, (j + 1) * 128)
                s_ref[lines, tile_lanes] = source[:, piece] * coef_keep[lines, :128]
                g_ref[lines, tile_lanes] = mix[:, piece] * coef_keep[lines, 128:]
            return carry

        lax.fori_loop(0, devices, prepare, 0, unroll=8)
    down_ref[:64] = jnp.zeros((64, width), f32)
    col_m[...] = jnp.zeros_like(col_m)
    right, left = (range(8), range(7, -1, -1))
    nothing = jnp.zeros((8, 128), f32)

    def packed(row, piece):
        return pl.ds(row * 64 + piece, 8, stride=8)

    def chain(state, row, order, ends, starts):
        for c in order:
            line = pl.ds(pl.multiple_of(row * 64 + c * 8, 8), 8)
            starts[line, :] = state
            state = prod[line, :] * state + ends[line, :]
        return state

    def link(row):
        return links[row]

    def carry_on(held, row, odd):
        ahead, behind = held
        ahead = ahead * link(row)
        if odd:
            ahead = chain(ahead, row, left, end_rl, in_rl)
            behind = chain(behind, row, left, back_lr, tail_lr)
        else:
            ahead = chain(ahead, row, right, end_lr, in_lr)
            behind = chain(behind, row, right, back_rl, tail_rl)
        return (ahead, behind * link(row + 1))

    def carry_back(held, row, odd):
        behind, ahead = held
        behind = behind * link(row + 1)
        if odd:
            behind = chain(behind, row, right, end_lr, in_lr)
            ahead = chain(ahead, row, right, back_rl, tail_rl)
        else:
            behind = chain(behind, row, left, end_rl, in_rl)
            ahead = chain(ahead, row, left, back_lr, tail_lr)
        return (behind, ahead * link(row))

    def wide_link(row):
        return jnp.concatenate([links[row]] * (group // 128), axis=1)

    def ascend(row):
        keep = wide_link(row)
        for k in range(width // group):
            lanes = slice(k * group, (k + 1) * group)
            whole = lr = rl = mlr = mrl = None
            for c in range(8):
                lines = pl.ds(pl.multiple_of(row * 64 + c * 8, 8), 8)
                spot = slice(c * 8, c * 8 + 8)
                a, s, g = (a_ref[lines, lanes], s_ref[lines, lanes], g_ref[lines, lanes])
                before, here = [
                    pl.ds(pl.multiple_of((row + step) * 64 + c * 8, 8), 8) for step in range(2)
                ]
                state_h = a * (down_ref[before, lanes] * keep) + s
                down_ref[here, lanes] = state_h
                lam = g + col_m[spot, lanes] * keep
                col_m[spot, lanes] = a * lam
                up_ref[lines, lanes] = lam
                if c == 0:
                    whole, lr, rl, mlr, mrl = (a, s, s, a * g, a * g)
                else:
                    lr = a * lr + s
                    rl = rl + whole * s
                    whole = whole * a
                    mlr = mlr + whole * g
                    mrl = a * (mrl + g)
            for j in range(group // 128):
                spot = packed(row, k * (group // 128) + j)
                piece = slice(j * 128, (j + 1) * 128)
                prod[spot, :] = whole[:, piece]
                end_lr[spot, :] = lr[:, piece]
                end_rl[spot, :] = rl[:, piece]
                back_lr[spot, :] = mlr[:, piece]
                back_rl[spot, :] = mrl[:, piece]

    def ascend_two(step, held):
        row = 2 * step + 1
        held = carry_on(held, row - 1, False)
        ascend(row)
        held = carry_on(held, row, True)
        ascend(row + 1)
        return held

    ascend(0)
    at_once = 7 if (devices - 1) % 7 == 0 else 1
    held = lax.fori_loop(0, devices - 1, ascend_two, (nothing,) * 2, unroll=at_once)
    held = carry_on(held, rows - 2, False)
    ascend(rows - 1)
    carry_on(held, rows - 1, True)
    col_h[...] = jnp.zeros_like(col_h)
    col_m[...] = jnp.zeros_like(col_m)

    def descend(row):
        keep = wide_link(row + 1)

        def edge(ref, k):
            pieces = [ref[packed(row, k * (group // 128) + j), :] for j in range(group // 128)]
            return pieces[0] if len(pieces) == 1 else jnp.concatenate(pieces, axis=1)

        for k in range(width // group):
            lanes = slice(k * group, (k + 1) * group)
            h_right, m_left = (edge(in_lr, k), edge(tail_rl, k))
            for c in range(8):
                lines = pl.ds(pl.multiple_of(row * 64 + c * 8, 8), 8)
                spot = slice(c * 8, c * 8 + 8)
                a, s, g = (a_ref[lines, lanes], s_ref[lines, lanes], g_ref[lines, lanes])
                h_right = a * h_right + s
                lam = g + m_left
                m_left = a * lam
                row_h[spot, lanes] = h_right
                row_m[spot, lanes] = lam
            h_left, m_right = (edge(in_rl, k), edge(tail_lr, k))
            for c in range(7, -1, -1):
                lines = pl.ds(pl.multiple_of(row * 64 + c * 8, 8), 8)
                spot = slice(c * 8, c * 8 + 8)
                a, s, g = (a_ref[lines, lanes], s_ref[lines, lanes], g_ref[lines, lanes])
                h_left = a * h_left + s
                lam_lr = g + m_right
                m_right = a * lam_lr
                here = pl.ds(pl.multiple_of((row + 1) * 64 + c * 8, 8), 8)
                h_down, lam_up = (down_ref[here, lanes], up_ref[lines, lanes])
                h_up = a * (col_h[spot, lanes] * keep) + s
                col_h[spot, lanes] = h_up
                lam_down = g + col_m[spot, lanes] * keep
                col_m[spot, lanes] = a * lam_down
                h_right, lam_rl = (row_h[spot, lanes], row_m[spot, lanes])
                lam_sum = (lam_lr + lam_rl) + (lam_down + lam_up)
                s_ref[lines, lanes] = (h_right + h_left) + (h_down + h_up)
                up_ref[lines, lanes] = lam_sum
                g_ref[lines, lanes] = (
                    (lam_lr * h_right + lam_rl * h_left)
                    + (lam_down * h_down + lam_up * h_up)
                    - s * lam_sum
                )

    def descend_two(step, held):
        row = rows - 1 - 2 * step
        held = carry_back(held, row - 1, False)
        descend(row)
        held = carry_back(held, row - 2, True)
        descend(row - 1)
        return held

    held = carry_back((nothing,) * 2, rows - 1, True)
    held = lax.fori_loop(0, devices - 1, descend_two, held, unroll=at_once)
    carry_back(held, 0, False)
    descend(1)
    descend(0)
    decay_acc[...] = jnp.zeros_like(decay_acc)
    gather_e, gather_b, gather_c = (spread_e[:part], spread_bc[:PROJ, :128], spread_bc[:PROJ, 128:])

    def finish(tile, carry):
        lines = pl.ds(pl.multiple_of(tile * pos, pos), pos)
        delta = delta_keep[tile]
        delta_low = delta.astype(bf16)
        of_b, of_c = (coef_keep[lines, :128], coef_keep[lines, 128:])
        grad_b = grad_c = None
        of_y, of_step, of_sum = ([], [], [])
        for k in range(width // 128):
            lanes = slice(k * 128, (k + 1) * 128)
            h_sum, lam_sum = (s_ref[lines, lanes], up_ref[lines, lanes])
            of_step.append((g_ref[lines, lanes] * rate_row[:, lanes]).astype(bf16))
            of_y.append((h_sum * of_c).astype(bf16))
            of_sum.append((lam_sum * of_b).astype(bf16))
            term_b, term_c = (lam_sum * source_ref[lines, lanes], h_sum * mix_ref[lines, lanes])
            grad_b = term_b if grad_b is None else grad_b + term_b
            grad_c = term_c if grad_c is None else grad_c + term_c
        of_y, of_step, of_sum = [jnp.concatenate(x, axis=1) for x in (of_y, of_step, of_sum)]
        decay_acc[...] += dot(delta_low, of_step, (1, 0))
        y_keep[tile] = jnp.transpose(dot(of_y, gather_e, (1, 1)))
        steps_keep[tile] = jnp.transpose(dot(of_step, gather_e, (1, 1)))
        sums_keep[tile] = jnp.transpose(dot(of_sum, gather_e, (1, 1)))
        coefs_keep[tile] = dot(gather_b, grad_b.astype(bf16), (1, 1)) + dot(gather_c, grad_c.astype(bf16), (1, 1))
        return carry

    lax.fori_loop(0, devices, finish, 0, unroll=8)
    pre_grads = []
    for tile in range(devices):
        sums = sums_keep[tile]
        pre_grads.append((steps_keep[tile] + got[tile, :part] * sums) * step_keep[tile])
        send[tile, :part] = y_keep[tile]
        send[tile, part : 2 * part] = delta_keep[tile] * sums
        send[tile, 2 * part + 16 :] = coefs_keep[tile, 16:]
    pre_grads = jnp.concatenate(pre_grads, axis=1)
    ranks = jnp.concatenate([got[tile, 2 * part : 2 * part + 16] for tile in range(devices)], axis=1)
    rank_grad = fine_dot(step_own, pre_grads, (0, 0))
    for tile in range(devices):
        send[tile, 2 * part : 2 * part + 16] = coefs_keep[tile, :16] + rank_grad[:, tile * pos : (tile + 1) * pos]
    step_grad = fine_dot(pre_grads, ranks, (1, 1))
    decay_grad = decay_acc[...] * one_channel[...]
    decay_high, decay_low = split(decay_grad)
    decay_grad = dot(decay_high, by_state[...], (1, 1)) + dot(decay_low, by_state[...], (1, 1))
    spot = (iota((part, small.shape[1]), 1) == iota((part, small.shape[1]), 0) + place[0] * part).astype(bf16)
    for at, value in ((0, step_grad), (16, decay_grad)):
        high, low = split(value)
        small[at : at + 16] = dot(high, spot, (0, 0)) + dot(low, spot, (0, 0))


def mix_kernel(
    place, group, got, small_in, low, low_halo, cot, conv_own, conv_halo, pre, gate_in, grad_in,
    select_rows, table, table_t, in_w, links,
    act_out, moved_ref, gate_grad_out, gated_ref, keep, give,
    grads, inner_ref, sums_ref, *, pair,
):
    devices, length, pos = got.shape
    model, inner_width = (low.shape[0], pre.shape[0])
    part = inner_width // devices
    lane = iota((1, pos), 1)
    prev, following = row_masks(links, place[0])
    proj_grad = got[0, 2 * part :]
    for k in range(1, devices):
        proj_grad = proj_grad + got[k, 2 * part :]
    proj_grad = proj_grad.astype(bf16)
    together = max(1, 48 // part)
    for first in range(0, devices, together):
        members = range(first, first + together)
        rows = slice(first * part, (first + together) * part)
        y = jnp.concatenate([got[k, :part] for k in members], axis=0)
        inner_grad = jnp.concatenate([got[k, part : 2 * part] for k in members], axis=0)
        pre_act, gate, gated_grad = (pre[rows], gate_in[rows], grad_in[rows])
        skip = table[rows, SKIP : SKIP + 1]
        sig_pre, sig_gate = (sigmoid(pre_act), sigmoid(gate))
        inner = (pre_act * sig_pre).astype(bf16)
        inner_ref[rows] = inner
        inner = inner.astype(f32)
        silu_gate = gate * sig_gate
        mix_grad = gated_grad * silu_gate
        inner_grad = inner_grad + mix_grad * skip + dot(select_rows[rows], proj_grad, (1, 0))
        act_grad = inner_grad * (sig_pre * (1.0 + pre_act * (1.0 - sig_pre)))
        act_out[rows] = act_grad
        y_all = y + skip * inner
        gated_ref[rows] = (y_all * silu_gate).astype(bf16)
        gate_grad_out[rows] = (gated_grad * y_all * (sig_gate * (1.0 + gate * (1.0 - sig_gate)))).astype(bf16)
        field = conv_own[rows]
        upper, lower = rows_around(field, conv_halo[rows])
        fields = (upper * prev, field, lower * following)
        sums = jnp.where(lane == 9, jnp.sum(act_grad, axis=1, keepdims=True), 0.0)
        sums = jnp.where(lane == 10, jnp.sum(mix_grad * inner, axis=1, keepdims=True), sums)
        for b, moved in enumerate((from_right(act_grad), act_grad, from_left(act_grad))):
            moved_ref[b, rows] = moved.astype(bf16)
            for a in range(3):
                sums = jnp.where(lane == 3 * a + b, jnp.sum(moved * fields[a], axis=1, keepdims=True), sums)
        sums_ref[rows] = sums
    gated, gate_grad = (gated_ref[...], gate_grad_out[...])

    low_in = low[...]
    upper, lower = rows_around(low_in.astype(f32), low_halo[...].astype(f32))
    which = iota((16, 1), 0)
    masks = jnp.where(which == 0, prev, jnp.where(which == 1, 1.0, following))
    left_hand = jnp.concatenate(
        [(upper * prev).astype(bf16), low_in, (lower * following).astype(bf16), masks.astype(bf16)], axis=0
    )
    blocks = inner_width // 128
    gate_at, out_at, small_at = [k * blocks * model for k in (1, 2, 3)]
    ones = jnp.ones((16, pos), bf16)
    totals = [[], []]
    gain_sum = jnp.zeros((model, 128), f32)
    for n in range(blocks):
        columns = slice(n * 128, (n + 1) * 128)
        in_conv = conv_total = None
        for b in range(3):
            part_b = dot(left_hand, moved_ref[b, columns], (1, 1))
            for a in range(3):
                tap = table_t[3 * a + b : 3 * a + b + 1, columns]
                term = tap * part_b[a * model : (a + 1) * model]
                total = tap * part_b[3 * model + a : 3 * model + a + 1]
                in_conv = term if in_conv is None else in_conv + term
                conv_total = total if conv_total is None else conv_total + total
        in_gate = dot(low_in, gate_grad[columns], (1, 1))
        grads[n * model : (n + 1) * model] = in_conv
        grads[gate_at + n * model : gate_at + (n + 1) * model] = in_gate
        grads[out_at + n * model : out_at + (n + 1) * model] = dot(cot[...], gated[columns], (1, 1))
        totals[0].append(conv_total)
        totals[1].append(dot(ones, gate_grad[columns], (1, 1))[0:1])
        conv_w = in_w[:, columns].astype(f32)
        gate_w = in_w[:, inner_width + n * 128 : inner_width + (n + 1) * 128].astype(f32)
        gain_sum = gain_sum + (conv_w * in_conv + gate_w * in_gate)
    sums = jnp.broadcast_to(jnp.concatenate(totals[0] + totals[1], axis=1), (16, 2 * inner_width))
    sums_high, sums_low = split(sums)
    shift_row = (dot(sums_high, in_w[...], (1, 1)) + dot(sums_low, in_w[...], (1, 1)))[0:1]
    gain_row = patch_sums(gain_sum)
    gain, shift = (table_t[GAIN : GAIN + 1, :model], table_t[SHIFT : SHIFT + 1, :model])
    gain_row = (gain_row - shift * shift_row) / gain
    high, mid = split(sums_ref[...])
    rest = (sums_ref[...] - high.astype(f32) - mid.astype(f32)).astype(bf16)
    chosen = (iota((16, pos), 0) == iota((16, pos), 1)).astype(bf16)
    sums = dot(chosen, high, (1, 1)) + (dot(chosen, mid, (1, 1)) + dot(chosen, rest, (1, 1)))
    norms = jnp.concatenate([gain_row, shift_row], axis=1)
    sums = jnp.where(iota((16, 1), 0) == NORM_AT - TAPS_AT, norms, sums)
    smalls = jnp.concatenate([dot(proj_grad, inner_ref[...], (1, 1)), small_in[...], sums], axis=0)
    put_blocks(grads, small_at, smalls)
    small_at = small_at + blocks * SMALL
    grads[small_at:] = jnp.zeros((grads.shape[0] - small_at, 128), f32)
    own = group[0] % 2
    if pair:
        count = keep.shape[0] // 2
        height = group[0] // 2
        for ref, side in ((keep, own), (give, 1 - own)):
            for k, at in enumerate((height, 1 - height)):
                ref[k * count : (k + 1) * count] = grads[pl.ds(pl.multiple_of((2 * side + at) * count, count), count)]
    else:
        count = keep.shape[0]
        keep[...] = grads[pl.ds(pl.multiple_of(own * count, count), count)]
        give[...] = grads[pl.ds(pl.multiple_of((1 - own) * count, count), count)]


def beyond_kernel(place, moved, table_t, in_w, links, near, far):
    model = in_w.shape[0]
    inner_width, pos = moved.shape[1:]
    lane = iota((1, pos), 1)
    prev, following = row_masks(links, place[0])
    conv_w = in_w[:, :inner_width].astype(f32)
    beyond = None
    for b in range(3):
        weights = [conv_w * table_t[3 * a + b : 3 * a + b + 1] for a in (0, 2)]
        term = dot(jnp.concatenate(weights, axis=0).astype(bf16), moved[b], (1, 0))
        beyond = term if beyond is None else beyond + term
    beyond = jnp.where(lane < 64, beyond[:model] * prev, beyond[model:] * following)
    top, bottom = (beyond[: model // 2], beyond[model // 2 :])
    up = jnp.where(lane < 64, top, pltpu.roll(bottom, 64, 1))
    down = jnp.where(lane < 64, pltpu.roll(top, 64, 1), bottom)
    even = place[0] % 2 == 0
    near[...] = jnp.where(even, down, up)
    far[...] = jnp.where(even, up, down)


def exit_kernel(
    place, act, from_above, from_below, gate_grad, gated, table, in_w, links, tok, cot, out_t,
    tokens_grad, layer_out,
):
    inner_width, pos = act.shape
    model = in_w.shape[0]
    lane = iota((1, pos), 1)
    even = place[0] % 2 == 0
    above, below = (
        jnp.where(even, from_above[...], from_below[...]), jnp.where(even, from_below[...], from_above[...])
    )
    top = jnp.where(lane < 64, above, pltpu.roll(below, 64, 1))
    bottom = jnp.where(lane < 64, pltpu.roll(above, 64, 1), below)
    beyond_high, beyond_low = split(jnp.concatenate([top, bottom], axis=0))
    act_grad = act[...]
    prev, following = row_masks(links, place[0])
    upper, lower = rows_around(act_grad, jnp.zeros_like(act_grad))
    columns = table[...]
    taps = [[columns[:, 8 - 3 * a - b : 9 - 3 * a - b] for b in range(3)] for a in range(3)]
    conv_grad = conv_tile(upper * prev, act_grad, lower * following, taps).astype(bf16)
    natural = jnp.concatenate([conv_grad, gate_grad[...], gated[...]], axis=0)
    order = column_order(pos)
    natural = dot(natural, order, (1, 0)).astype(bf16)
    layer = jnp.transpose(dot(out_t[...], natural[2 * inner_width :], (1, 0)))
    layer_out[...] = (tok[...].astype(f32) + layer).astype(bf16)
    normed_grad = dot(in_w[...], natural[: 2 * inner_width], (1, 0))
    normed_grad = normed_grad + (dot(beyond_high, order, (1, 0)) + dot(beyond_low, order, (1, 0)))
    xhat, inverse = normalized(flipped(tok[...]))
    scaled = normed_grad * columns[:model, GAIN : GAIN + 1]
    x_grad = (
        scaled
        - jnp.mean(scaled, axis=0, keepdims=True)
        - xhat * jnp.mean(scaled * xhat, axis=0, keepdims=True)
    ) * inverse
    x_grad = jnp.transpose(x_grad)
    tokens_grad[...] = (x_grad + cot[...].astype(f32)).astype(bf16)


def deal_kernel(group, *refs, members, pair):
    pieces, ordered = (refs[:members], refs[-1])
    (
        gain_grad, shift_grad, inproj, kernel_grad, offset, select, stepproj, stepbias, decay, skip, outproj,
    ) = refs[members:-1]
    model, inner_width = outproj.shape
    blocks = inner_width // 128
    rank = stepproj.shape[0]
    states = decay.shape[0]
    count = pieces[0].shape[0]
    for k, piece in enumerate(pieces):
        if pair:
            core, height = (group[0] % 2, group[0] // 2)
            core = 1 - core if k // 2 else core
            height = 1 - height if k % 2 else height
            slot = core * 2 + height
        else:
            slot = k % 2 * (members // 2) + k // 2
        ordered[pl.ds(pl.multiple_of(slot * count, count), count)] = piece[...]

    def rows(start, count):
        return ordered[start : start + count]

    for k in range(2 * blocks):
        inproj[:, k * 128 : (k + 1) * 128] = rows(k * model, model)
    start = 2 * blocks * model
    for k in range(blocks):
        outproj[:, k * 128 : (k + 1) * 128] = rows(start + k * model, model)
    start = start + blocks * model
    small = jnp.concatenate([rows(start + k * SMALL, SMALL) for k in range(blocks)], axis=1)
    select[:rank] = small[:rank]
    select[rank:] = small[IN:PROJ]
    stepproj[...] = small[STEP_AT : STEP_AT + rank]
    stepbias[...] = small[STEP_AT + ONE : STEP_AT + ONE + 1].reshape(stepbias.shape)
    decay[...] = small[DECAY_AT : DECAY_AT + states]
    for k in range(3):
        kernel_grad[k] = small[TAPS_AT + 3 * k : TAPS_AT + 3 * k + 3]
    offset[...] = small[OFFSET_AT : OFFSET_AT + 1].reshape(offset.shape)
    skip[...] = small[SKIP_AT : SKIP_AT + 1].reshape(skip.shape)
    norms = small[NORM_AT : NORM_AT + 1]
    gain_grad[...] = norms[:, :model].reshape(gain_grad.shape)
    shift_grad[...] = norms[:, model:].reshape(shift_grad.shape)


def vmem_call(kernel, out_shape, scalars, arrays, weights=(), scratch=(), limit=16):
    scalars = [pltpu.with_memory_space_constraint(x, pltpu.HBM) if x.ndim == 2 else x for x in scalars]
    arrays = [pltpu.with_memory_space_constraint(x, pltpu.VMEM) for x in arrays]
    arrays += [pltpu.with_memory_space_constraint(x, pltpu.HBM) for x in weights]
    return pl.pallas_call(
        kernel,
        out_shape=out_shape,
        in_specs=[pl.BlockSpec(memory_space=pltpu.SMEM)] * len(scalars)
        + [pl.BlockSpec(memory_space=pltpu.VMEM)] * len(arrays),
        out_specs=[pl.BlockSpec(memory_space=pltpu.VMEM)] * len(out_shape),
        scratch_shapes=list(scratch),
        compiler_params=pltpu.CompilerParams(vmem_limit_bytes=limit * 1024 * 1024),
    )(*scalars, *arrays)


def struct(*shape, dtype=f32):
    return jax.ShapeDtypeStruct(shape, dtype)


def inside(*shape, dtype=f32):
    return pltpu.VMEM(shape, dtype)


def scan_call(place, got, table, links, maps, states):
    devices, length, pos = got.shape
    inner_width = table.shape[0]
    part = inner_width // devices
    width = -(-part * states // 128) * 128
    total = devices * pos
    span = 256 if width % 256 == 0 else 128
    group = 768 if width % 768 == 0 else span
    big = pltpu.VMEM((total, width), f32)
    line = pltpu.VMEM(((2 * devices + 1) * 64, 128), f32)
    column = pltpu.VMEM((pos // 2, width), f32)
    own = pltpu.VMEM((devices, part, pos), f32)
    return vmem_call(
        functools.partial(scan_kernel, part=part, states=states, span=span, group=group),
        [inside(devices, length, pos), inside(32, inner_width)],
        [place],
        [got, table, links, *maps],
        (),
        [big] * 3
        + [pltpu.VMEM((total + pos // 2, width), f32)]
        + [big] * 3
        + [column] * 4
        + [line] * 9
        + [pltpu.VMEM((total, 2 * part), bf16)] * 3
        + [pltpu.VMEM((total, 256), f32)]
        + [own] * 5
        + [pltpu.VMEM((devices, PROJ, pos), f32), pltpu.VMEM((part, width), f32)],
        limit=36 if total <= 1024 else 60,
    )


def on_device(
    tokens, heights, cotangent, norm_gain, norm_bias, in_weight, conv_kernel, conv_bias, select_weight,
    step_weight, step_bias, decay_log, skip_gain, out_weight,
):
    _, tile_rows, grid_cols, model = tokens.shape
    inner_width = out_weight.shape[0]
    states = decay_log.shape[1]
    rank = step_weight.shape[0]
    devices = lax.axis_size("seq")
    groups = lax.axis_size("dp")
    place = lax.axis_index("seq").reshape(1)
    group = lax.axis_index("dp").reshape(1)
    pair = groups == 4
    pos = tile_rows * grid_cols
    part = inner_width // devices
    width = -(-part * states // 128) * 128
    length = 2 * part + PROJ
    near_pairs = [(i, i ^ 1) for i in range(devices)]
    far_pairs = [(i, (i - 1 + 2 * (i % 2)) % devices) for i in range(devices)]

    tok, cot = (tokens.reshape(pos, model), cotangent.reshape(pos, model))
    even = place[0] % 2 == 0
    upper, lower = (tok[:grid_cols].astype(f32), tok[grid_cols:].astype(f32))

    def dense(rows):
        rest = rows[:, 128:].reshape(2, grid_cols // 2, model - 128)
        return jnp.concatenate([rows[:, :128], jnp.concatenate([rest[0], rest[1]], axis=1)], axis=0)

    above = lax.ppermute(dense(jnp.where(even, upper, lower)), "seq", far_pairs)
    below = lax.ppermute(dense(jnp.where(even, lower, upper)), "seq", near_pairs)
    above, group = lax.optimization_barrier((above, group))
    out_t = out_weight.T
    channels = inside(inner_width, pos)
    narrow = inside(model, pos, dtype=bf16)
    conv_own, gate, gated_grad, mix, low, cot_in, conv_rows, select_rows, table, table_t, in_keep, links, taps_wide, *maps = vmem_call(
        own_kernel,
        [channels] * 4
        + [narrow] * 2
        + [
            inside(inner_width, model, dtype=bf16), inside(inner_width, PROJ, dtype=bf16), inside(inner_width, TABLE),
            inside(TABLE, inner_width), inside(model, 2 * inner_width, dtype=bf16),
            inside(2 * devices + 1, 8, 128), inside(BIAS + 1, inner_width, pos),
            inside(2 * part, width, dtype=bf16), inside(2 * PROJ, 256, dtype=bf16), inside(states, width, dtype=bf16),
            inside(part, width), inside(8, width), inside(part, 48, dtype=bf16),
        ],
        [heights, place],
        [],
        [
            tok, cot, in_weight, out_t, select_weight.T, conv_kernel, conv_bias, step_weight, step_bias,
            decay_log.T, skip_gain, norm_gain, norm_bias,
        ],
    )
    sent, conv_halo, pre_act, low_halo = vmem_call(
        entry_kernel,
        [inside(devices, length, pos), channels, channels, narrow],
        [place],
        [above, below, conv_own, mix, conv_rows, select_rows, table, links, taps_wide],
    )
    got = lax.all_to_all(sent, "seq", 0, 0, tiled=True)
    sent, small = scan_call(place, got, table, links, maps, states)
    got = lax.all_to_all(sent, "seq", 0, 0, tiled=True)
    blocks = inner_width // 128
    whole = -(-blocks * (3 * model + SMALL) // 2048) * 2048
    half = whole // 2
    act_grad, moved, gate_grad, gated, keep, give = vmem_call(
        functools.partial(mix_kernel, pair=pair),
        [channels, inside(3, inner_width, pos, dtype=bf16)]
        + [inside(inner_width, pos, dtype=bf16)] * 2
        + [inside(half, 128)] * 2,
        [place, group],
        [
            got, small, low, low_halo, cot_in, conv_own, conv_halo, pre_act, gate, gated_grad, select_rows, table,
            table_t, in_keep, links,
        ],
        (),
        [
            pltpu.VMEM((whole, 128), f32), pltpu.VMEM((inner_width, pos), bf16), pltpu.VMEM((inner_width, pos), f32),
        ],
    )
    near, far = vmem_call(
        beyond_kernel, [inside(model // 2, pos)] * 2, [place], [moved, table_t, in_keep, links]
    )
    keep, near, far = lax.optimization_barrier((keep, near, far))
    from_above = lax.ppermute(far, "seq", far_pairs)
    from_below = lax.ppermute(near, "seq", near_pairs)
    swap = [(i, i ^ 1) for i in range(groups)]
    taken = lax.ppermute(give, "dp", swap)
    count = half // (groups // 2)
    if pair:
        across = [(i, i ^ 2) for i in range(groups)]
        other = lax.ppermute(keep[count:] + taken[count:], "dp", across)
        piece = keep[:count] + taken[:count]
    else:
        same_core = [list(range(c, groups, 2)) for c in range(2)]
        pieces = (keep + taken).reshape(groups // 2, count, 128)
        pieces = lax.all_to_all(pieces, "dp", 0, 0, tiled=True, axis_index_groups=same_core)
        piece, other = (pieces[0], jnp.sum(pieces[1:], axis=0))
    other, from_above, from_below = lax.optimization_barrier((other, from_above, from_below))
    shares = (piece + other).reshape(devices, count // devices, 128)
    shares = lax.all_to_all(shares, "seq", 0, 0, tiled=True)
    share = jnp.broadcast_to(jnp.sum(shares, axis=0), shares.shape)
    mine = lax.all_to_all(share, "seq", 0, 0, tiled=True).reshape(count, 128)
    mine, from_above, from_below = lax.optimization_barrier((mine, from_above, from_below))
    tokens_grad, layer_out = vmem_call(
        exit_kernel,
        [struct(pos, model, dtype=bf16)] * 2,
        [place],
        [act_grad, from_above, from_below, gate_grad, gated, table, in_keep, links],
        [tok, cot, out_t],
    )
    if pair:
        from_y = lax.ppermute(mine, "dp", across)
        from_y, tokens_grad = lax.optimization_barrier((from_y, tokens_grad))
        pieces = [mine, from_y, lax.ppermute(mine, "dp", swap), lax.ppermute(from_y, "dp", swap)]
    else:
        pieces = list(lax.all_gather(mine, "dp"))
    gain, shift, inproj, kernel, offset, select, stepproj, stepbias, decay, skip, outproj = vmem_call(
        functools.partial(deal_kernel, members=len(pieces), pair=pair),
        [
            struct(model), struct(model), struct(model, 2 * inner_width), struct(3, 3, inner_width),
            struct(inner_width), struct(rank + 2 * states, inner_width), struct(rank, inner_width),
            struct(inner_width), struct(states, inner_width), struct(inner_width), struct(model, inner_width),
        ],
        [group],
        pieces,
        (),
        [pltpu.VMEM((whole, 128), f32)],
    )
    shape = tokens.shape
    return (
        layer_out.reshape(shape), tokens_grad.reshape(shape), gain, shift, inproj, kernel, offset, select.T,
        stepproj, stepbias, decay.T, skip, outproj.T,
    )


def solution(mesh):
    tile, whole = (P("dp", "seq", None, None), P())
    return jax.shard_map(
        on_device,
        mesh=mesh,
        in_specs=(tile, P("dp", None), tile) + (whole,) * 11,
        out_specs=(tile, tile) + (whole,) * 11,
        check_vma=False,
    )
```
